32 devices in a mesh: rows: 4 (over z), cols: 8 (over y, x, core).
Axes of the slice: x: 2, y: 2, z: 4, core: 2. Of those that a mesh axis runs over, the one named last changes fastest.
Arguments:
- features: bfloat16 [64, 512, 180], P('rows', 'cols'), may hold values from -8 to 8
- gain_one: float32 [180], replicated, may hold values from 0.1 to 1.9
- qkv_weight: bfloat16 [180, 540], replicated, may hold values from -4 to 4
- bias_table: float32 [1521, 6], replicated, may hold values from -4 to 4
- proj_weight: bfloat16 [180, 180], replicated, may hold values from -0.4375 to 0.4375
- gain_two: float32 [180], replicated, may hold values from 0.1 to 1.9
- hidden_weight: bfloat16 [180, 360], replicated, may hold values from -0.4375 to 0.4375
- output_weight: bfloat16 [360, 180], replicated, may hold values from -0.3125 to 0.3125
- group_conv: bfloat16 [3, 3, 180, 180], replicated, may hold values from -0.15625 to 0.15625
- before_conv: bfloat16 [3, 3, 180, 64], replicated, may hold values from -0.15625 to 0.15625
- upsample_conv: bfloat16 [3, 3, 64, 256], replicated, may hold values from -0.25 to 0.25
Outputs:
- upscaled: bfloat16 [64, 128, 1024], P(None, 'rows', 'cols')
The draws below stay inside these ranges and needn't reach their ends.
All inputs are finite; a program needn't handle non-finite values.
Results may differ from the reference program's by a relative error of at most 0.017.
Values may be sent and summed in bfloat16 or wider, within the bound.
No kernel may reach another device: no remote copies, remote signals or barrier semaphores. Data moves between devices by JAX's collectives and lax.ppermute only.
A program may use at most 128 MiB of HBM per device.

```python
import jax
import jax.numpy as jnp
import numpy as np
from jax import lax

C = 180
HEADS = 6
MLP = 360
NF = 64
WIN = 16
KWIN = 24
TABLE = 1521
NR = 64
NC = 512


def draw_features(key, part):
    key = jax.random.fold_in(key, 3)
    noise = jax.random.normal(jax.random.fold_in(key, 1), (NR, NC, C), jnp.float32)
    values = noise
    return jnp.clip(values, -8.0, 8.0).astype(jnp.bfloat16)


def draw_qkv_weight(key, part):
    key = jax.random.fold_in(key, 7)
    weight = jax.random.normal(jax.random.fold_in(key, 1), (C, 3 * C), jnp.float32) / jnp.sqrt(jnp.float32(C))
    return jnp.clip(weight, -4.0, 4.0).astype(jnp.bfloat16)


def normal_values(stream_key, shape, scale, bound, dtype=jnp.bfloat16):
    values = scale * jax.random.normal(stream_key, shape, jnp.float32)
    return jnp.clip(values, min=-bound, max=bound).astype(dtype)


def setup_inputs(seed: int = 0) -> dict:
    streams_of = jax.random.split(jax.random.key(seed), 12)
    return {
        "features": draw_features(jax.random.fold_in(streams_of[11], 71), 0),
        "gain_one": jnp.clip(1.0 + 0.18 * jax.random.normal(streams_of[1], (C,), jnp.float32), 0.1, 1.9),
        "qkv_weight": draw_qkv_weight(jax.random.fold_in(streams_of[11], 71), 0),
        "bias_table": normal_values(streams_of[3], (TABLE, HEADS), 1.0, 4.0, jnp.float32),
        "proj_weight": normal_values(streams_of[4], (C, C), C ** -0.5, 0.4375),
        "gain_two": jnp.clip(1.0 + 0.18 * jax.random.normal(streams_of[5], (C,), jnp.float32), 0.1, 1.9),
        "hidden_weight": normal_values(streams_of[6], (C, MLP), C ** -0.5, 0.4375),
        "output_weight": normal_values(streams_of[7], (MLP, C), MLP ** -0.5, 0.3125),
        "group_conv": normal_values(streams_of[8], (3, 3, C, C), (9 * C) ** -0.5, 0.15625),
        "before_conv": normal_values(streams_of[9], (3, 3, C, NF), (9 * C) ** -0.5, 0.15625),
        "upsample_conv": normal_values(streams_of[10], (3, 3, NF, 4 * NF), (9 * NF) ** -0.5, 0.25),
    }


def layer_norm(values, gain):
    center = values - lax.optimization_barrier(jnp.mean(values, axis=-1, keepdims=True))
    spread = lax.optimization_barrier(jnp.mean(center * center, axis=-1, keepdims=True))
    return center * lax.rsqrt(spread + 1e-05) * gain

def bias_indices():
    query_pos = np.arange(WIN)
    key_pos = np.arange(KWIN)
    offset = key_pos[None, :] - query_pos[:, None] + WIN - 1
    side = WIN + KWIN - 1
    full = offset[:, None, :, None] * side + offset[None, :, None, :]
    return full.reshape(WIN * WIN, KWIN * KWIN).astype(np.int32)

def query_windows(values):
    height, width, chans = values.shape
    blocks = values.reshape(height // WIN, WIN, width // WIN, WIN, chans)
    return blocks.transpose(0, 2, 1, 3, 4).reshape(-1, WIN * WIN, chans)

def undo_windows(values, height, width):
    chans = values.shape[-1]
    blocks = values.reshape(height // WIN, width // WIN, WIN, WIN, chans)
    return blocks.transpose(0, 2, 1, 3, 4).reshape(height, width, chans)

def key_windows(padded):
    span = KWIN - WIN
    height, width, chans = padded.shape
    nbr = height // span
    nbc = width // span
    blocks = padded.reshape(nbr, span, nbc, span, chans)
    stacked = jnp.stack([blocks[0:nbr - 1:2], blocks[1:nbr:2], blocks[2:nbr:2]], axis=1)
    stacked = jnp.stack([stacked[:, :, :, 0:nbc - 1:2], stacked[:, :, :, 1:nbc:2], stacked[:, :, :, 2:nbc:2]], axis=4)
    stacked = stacked.transpose(0, 3, 1, 2, 4, 5, 6)
    return stacked.reshape(-1, KWIN * KWIN, chans)

def attend_group(query_block, keyval_block, bias):
    groups = query_block.shape[0]
    chans = query_block.shape[-1]
    head_size = chans // HEADS
    qs = query_block.reshape(groups, WIN * WIN, HEADS, head_size).astype(jnp.float32)
    keys = keyval_block[..., :chans].reshape(groups, KWIN * KWIN, HEADS, head_size).astype(jnp.float32)
    vals = keyval_block[..., chans:].reshape(groups, KWIN * KWIN, HEADS, head_size).astype(jnp.float32)
    scores = jnp.einsum('gqhd,gkhd->ghqk', qs, keys) / jnp.sqrt(jnp.float32(head_size)) + bias[None]
    probs = jax.nn.softmax(scores, axis=-1).astype(jnp.bfloat16)
    result = jnp.einsum('ghqk,gkhd->gqhd', probs.astype(jnp.float32), vals)
    return result.reshape(groups, WIN * WIN, chans).astype(jnp.bfloat16)

def conv_last(padded, weight):
    height = padded.shape[0] - 2
    width = padded.shape[1] - 2
    total = jnp.zeros((height, width, weight.shape[3]), jnp.float32)
    for tap_r in range(3):
        for tap_c in range(3):
            total = total + jnp.dot(padded[tap_r:tap_r + height, tap_c:tap_c + width], weight[tap_r, tap_c], preferred_element_type=jnp.float32)
    return total

def conv_to_first(padded, weight):
    height = padded.shape[0] - 2
    width = padded.shape[1] - 2
    total = jnp.zeros((weight.shape[3], height, width), jnp.float32)
    for tap_r in range(3):
        for tap_c in range(3):
            total = total + jnp.einsum('hwc,co->ohw', padded[tap_r:tap_r + height, tap_c:tap_c + width].astype(jnp.float32), weight[tap_r, tap_c].astype(jnp.float32))
    return total

def conv_first(padded, weight):
    height = padded.shape[1] - 2
    width = padded.shape[2] - 2
    total = jnp.zeros((weight.shape[3], height, width), jnp.float32)
    for tap_r in range(3):
        for tap_c in range(3):
            total = total + jnp.einsum('chw,co->ohw', padded[:, tap_r:tap_r + height, tap_c:tap_c + width].astype(jnp.float32), weight[tap_r, tap_c].astype(jnp.float32))
    return total

def shuffle(expanded):
    chans4, height, width = expanded.shape
    chans = chans4 // 4
    parts = expanded.reshape(chans, 2, 2, height, width).transpose(0, 3, 1, 4, 2)
    return parts.reshape(chans, 2 * height, 2 * width)

def reference(features, gain_one, qkv_weight, bias_table, proj_weight, gain_two, hidden_weight, output_weight, group_conv, before_conv, upsample_conv):
    height, width, chans = features.shape
    rim = (KWIN - WIN) // 2
    base = features.astype(jnp.float32)
    normed = layer_norm(base, gain_one).astype(jnp.bfloat16)
    projected = jnp.dot(normed, qkv_weight, preferred_element_type=jnp.float32)
    queries = projected[..., :chans].astype(jnp.bfloat16)
    keyvals = projected[..., chans:].astype(jnp.bfloat16)
    padded = jnp.pad(keyvals, ((rim, rim), (rim, rim), (0, 0)))
    bias = jnp.take(bias_table, jnp.asarray(bias_indices()), axis=0).transpose(2, 0, 1)
    query_win = query_windows(queries)
    keyval_win = key_windows(padded)
    count = query_win.shape[0]
    group = 8 if count % 8 == 0 else 1
    attended = lax.map(lambda pair: attend_group(pair[0], pair[1], bias), (query_win.reshape(count // group, group, WIN * WIN, chans), keyval_win.reshape(count // group, group, KWIN * KWIN, 2 * chans)))
    attended = undo_windows(attended.reshape(count, WIN * WIN, chans), height, width)
    first = base + jnp.dot(attended, proj_weight, preferred_element_type=jnp.float32)
    second_norm = layer_norm(first, gain_two).astype(jnp.bfloat16)
    inner = jax.nn.gelu(jnp.dot(second_norm, hidden_weight, preferred_element_type=jnp.float32), approximate=False).astype(jnp.bfloat16)
    mixed = (first + jnp.dot(inner, output_weight, preferred_element_type=jnp.float32)).astype(jnp.bfloat16)
    grouped = (base + conv_last(jnp.pad(mixed, ((1, 1), (1, 1), (0, 0))), group_conv)).astype(jnp.bfloat16)
    lowfeat = jax.nn.leaky_relu(conv_to_first(jnp.pad(grouped, ((1, 1), (1, 1), (0, 0))), before_conv), 0.01).astype(jnp.bfloat16)
    expanded = conv_first(jnp.pad(lowfeat, ((0, 0), (1, 1), (1, 1))), upsample_conv)
    return shuffle(expanded).astype(jnp.bfloat16)
```

```python
import functools

import jax
import jax.numpy as jnp
import numpy as np
from jax import lax
from jax.experimental import pallas as pl
from jax.experimental.pallas import tpu as pltpu
from jax.sharding import PartitionSpec as P

HEADS = 6
HD = 30
HP = 32
WIN = 16
KWIN = 24
KEYS = KWIN * KWIN
CHUNKS = 3
CHUNK = KEYS // CHUNKS
SIDE = WIN + KWIN - 1
RIM = (KWIN - WIN) // 2
EDGE = WIN + 2 * RIM
STRIP = 8
LOG2E = 1.4426950408889634
F32 = jnp.float32
BF16 = jnp.bfloat16
NT = (((1,), (1,)), ((), ()))
TN = (((0,), (0,)), ((), ()))


def dot(a, b):
    return jnp.dot(a, b, preferred_element_type=F32)


def dot_nt(a, b):
    return lax.dot_general(a, b, NT, preferred_element_type=F32)


def layer_norm(values, gain):
    center = values - jnp.mean(values, axis=-1, keepdims=True)
    spread = jnp.mean(center * center, axis=-1, keepdims=True)
    return center * lax.rsqrt(spread + 1e-05) * gain


def call(kernel, out_shape, scratch, flops, bytes_accessed, smem=0):
    def run(*args):
        specs = [pl.BlockSpec(memory_space=pltpu.VMEM)] * len(args)
        for index in range(smem):
            specs[index] = pl.BlockSpec(memory_space=pltpu.SMEM)
        return pl.pallas_call(
            kernel,
            out_shape=out_shape,
            in_specs=specs,
            scratch_shapes=scratch,
            compiler_params=pltpu.CompilerParams(vmem_limit_bytes=24 * 2**20),
            cost_estimate=pl.CostEstimate(
                flops=flops, bytes_accessed=bytes_accessed, transcendentals=0
            ),
        )(*args)

    return run


def bias_kernel(table_ref, left_ref, border_ref, right_ref, middle_ref, t_scr, e_scr, w_scr, x_scr):
    for d in range(SIDE):
        t_scr[8 * d : 8 * d + HEADS, 0:SIDE] = jnp.exp(table_ref[:, SIDE * d : SIDE * (d + 1)])

    def head(h, carry):
        values = t_scr[pl.ds(h, SIDE, stride=8), 0:SIDE].astype(BF16)

        def expand(cols, first):
            width = -(-SIDE * cols // 128) * 128
            spot = lax.broadcasted_iota(jnp.int32, (SIDE, width), 1) // cols
            row = lax.broadcasted_iota(jnp.int32, (SIDE, width), 0)
            pick = (spot == SIDE - 1 - row).astype(F32).astype(BF16)
            e_scr[0:SIDE, 0:width] = lax.dot_general(values, pick, TN, preferred_element_type=F32)
            lane = lax.broadcasted_iota(jnp.int32, (KWIN, width), 1) % cols
            out = jnp.zeros((KWIN, width), F32)
            for jj in range(cols):
                start = WIN - 1 - first - jj
                out = jnp.where(lane == jj, e_scr[start : start + KWIN, 0:width], out)
            w_scr[:, 0:width] = out

        lanes = lax.broadcasted_iota(jnp.int32, (KWIN, 128), 1)
        expand(WIN, 0)
        for p in range(KWIN):
            rows = slice(p * KWIN, (p + 1) * KWIN)
            low = w_scr[:, (23 - p) * WIN : (23 - p) * WIN + 128]
            high = w_scr[:, (31 - p) * WIN : (31 - p) * WIN + 128]
            x_scr[0, rows] = jnp.where(lanes < 64, low, high)
            x_scr[1, rows] = w_scr[:, (27 - p) * WIN : (27 - p) * WIN + 128]
        border_ref[h] = x_scr[0].astype(BF16)
        middle_ref[h] = x_scr[1].astype(BF16)
        for out_ref, first in ((left_ref, WIN - STRIP), (right_ref, 0)):
            expand(STRIP, first)
            for p in range(KWIN):
                rows = slice(p * KWIN, (p + 1) * KWIN)
                x_scr[0, rows] = w_scr[:, (23 - p) * STRIP : (23 - p) * STRIP + 128]
            out_ref[h] = x_scr[0].astype(BF16)
        return carry

    lax.fori_loop(0, HEADS, head, 0)


def build_bias(bias_table):
    return call(
        bias_kernel,
        [jax.ShapeDtypeStruct((HEADS, KEYS, 128), BF16)] * 4,
        [
            pltpu.VMEM((8 * SIDE, 128), F32),
            pltpu.VMEM((SIDE + 1, 640), F32),
            pltpu.VMEM((KWIN, 640), F32),
            pltpu.VMEM((2, KEYS, 128), F32),
        ],
        4_000_000_000,
        4_000_000,
    )(bias_table.T)


def one_hot(shape, row_of, col_of):
    row = lax.broadcasted_iota(jnp.int32, shape, 0)
    col = lax.broadcasted_iota(jnp.int32, shape, 1)
    return (row_of(row) == col_of(col)).astype(F32).astype(BF16)


def spread_head(place):
    return jnp.where(place % HP < HD, place // HP * HD + place % HP, -1)


def weights_into(qkv_ref, proj_ref, wk_ref, wqv_ref, wp_ref):
    chans = qkv_ref.shape[0]
    width = HEADS * HP
    qkv = qkv_ref[...]
    pick = one_hot(
        (3 * chans, 3 * 128),
        lambda row: row,
        lambda col: jnp.where(
            (col % 128 < 2 * HP) & (col % HP < HD),
            chans + (col // 128 * 2 + col % 128 // HP) * HD + col % HP,
            -1,
        ),
    )
    wk_ref[...] = dot(qkv, pick).astype(BF16)
    pick = one_hot(
        (2 * width, 3 * chans),
        lambda row: jnp.where(
            row % HP < HD, row // HP * HD + row % HP + jnp.where(row < width, 0, chans), -1
        ),
        lambda col: col,
    )
    wqv_ref[...] = dot_nt(pick, qkv).astype(BF16)
    pick = one_hot((width, chans), spread_head, lambda col: col)
    wp_ref[...] = dot(pick, proj_ref[...]).astype(BF16)


def set_queries(q_scr, wqv_ref, groups):
    scale = LOG2E / np.sqrt(HD)
    rows = jnp.concatenate([rows.reshape(128, rows.shape[2]) for rows in groups], axis=0)
    queries = (dot_nt(wqv_ref[0 : HEADS * HP], rows.astype(BF16)) * scale).astype(BF16)
    none = jnp.zeros((HP, 128), BF16)
    for g in range(len(groups)):
        lanes = slice(128 * g, 128 * g + 128)
        for t in range(HEADS // 2):
            one = queries[2 * t * HP : (2 * t + 1) * HP, lanes]
            two = queries[(2 * t + 1) * HP : (2 * t + 2) * HP, lanes]
            q_scr[g, t, 0:HP] = jnp.concatenate([one, none], axis=1)
            q_scr[g, t, HP : 2 * HP] = jnp.concatenate([none, two], axis=1)


class BiasCopies:
    def __init__(self, bias_refs, bias_scr, sem):
        self.copies = [
            pltpu.make_async_copy(ref, bias_scr.at[index], sem.at[index])
            for index, ref in enumerate(bias_refs)
        ]

    def start(self):
        for copy in self.copies:
            copy.start()

    def wait(self):
        for copy in self.copies:
            copy.wait()


def lookup(g, values):
    out = values[0]
    for index in range(1, len(values)):
        out = jnp.where(g >= index, values[index], out)
    return out


def attention(kinds, windows, q_scr, k_ref, v_ref, bias_ref, wp_ref, p_scr, a_scr, o_scr):
    groups = len(windows)
    pairs = HEADS // 2
    stages = [(c, t) for c in range(CHUNKS) for t in range(pairs)]

    def sum_values(g, c, t, slot):
        part = dot(v_ref[lookup(g, windows), c, 2 * t * HP : 2 * (t + 1) * HP], p_scr[slot])
        o_scr[g, t] = part if c == 0 else o_scr[g, t] * a_scr[slot] + part

    p_scr[(len(stages) - 1) % 3] = jnp.zeros((CHUNK, 256), BF16)
    a_scr[(len(stages) - 1) % 3] = jnp.zeros((1, 256), F32)
    o_scr[0, pairs - 1] = jnp.zeros((2 * HP, 256), F32)

    def attend(g, carry):
        window = lookup(g, windows)
        tops = [None] * pairs
        for n, (c, t) in enumerate(stages):
            rows = slice(CHUNK * c, CHUNK * (c + 1))
            s = dot(k_ref[window, rows, 128 * t : 128 * t + 2 * HP], q_scr[g, t])
            top = jnp.max(jnp.max(s.reshape(CHUNK // 8, 8, 256), axis=0), axis=0, keepdims=True)
            if c > 0:
                top = jnp.maximum(top, tops[t])
            if n == 0:
                sum_values(jnp.maximum(g - 1, 0), *stages[-1], (len(stages) - 1) % 3)
            else:
                sum_values(g, *stages[n - 1], (n - 1) % 3)
            if c > 0:
                a_scr[n % 3] = jnp.exp2(tops[t] - top)
            tops[t] = top
            prob = jnp.exp2(s - top).astype(BF16)
            for half in range(2):
                lanes = slice(128 * half, 128 * half + 128)
                head = 2 * t + half
                bias = bias_ref[head, rows] if kinds is None else bias_ref[lookup(g, kinds), head, rows]
                p_scr[n % 3, :, lanes] = prob[:, lanes] * bias
        return carry

    lax.fori_loop(0, groups, attend, 0)
    sum_values(groups - 1, *stages[-1], (len(stages) - 1) % 3)
    attended = []
    for g in range(groups):
        parts = []
        for t in range(pairs):
            for half in range(2):
                lanes = slice(128 * half, 128 * half + 128)
                one = o_scr[g, t, half * HP : (half + 1) * HP, lanes]
                parts.append((one * (1.0 / one[HD : HD + 1])).astype(BF16))
        attended.append(jnp.concatenate(parts, axis=0))
    attended = jnp.concatenate(attended, axis=1)
    return lax.dot_general(attended, wp_ref[...], TN, preferred_element_type=F32)


def feed_forward(first, gain, hidden_ref, output_ref):
    normed = layer_norm(first, gain).astype(BF16)
    inner = dot(normed, hidden_ref[...])
    inner = (0.5 * inner * (1.0 + lax.erf(inner * np.float32(np.sqrt(0.5))))).astype(BF16)
    return first + dot_nt(inner, output_ref[...])


def project(keys, wk_ref, wqv_ref, k_ref, v_ref, index):
    width = HEADS * HP
    one_row = (lax.broadcasted_iota(jnp.int32, (width, 1), 0) % HP == HD).astype(F32)
    keys = keys.reshape(KEYS, keys.shape[2]).astype(BF16)
    k_ref[index] = dot(keys, wk_ref[...]).astype(BF16)
    for c in range(CHUNKS):
        part = keys[CHUNK * c : CHUNK * (c + 1)]
        v_ref[index, c] = (dot_nt(wqv_ref[width : 2 * width], part) + one_row).astype(BF16)


def from_sides(even, first, second):
    first, second = first.astype(F32), second.astype(F32)
    return jnp.where(even, second, first), jnp.where(even, first, second)


def border_rows(ref, c0):
    return jnp.concatenate([ref[0:4, c0 : c0 + WIN], ref[12:16, c0 : c0 + WIN]], axis=0)


def inner_kernel(
    flags,
    own_ref,
    row_one_ref,
    row_two_ref,
    gain_one_ref,
    qkv_ref,
    proj_ref,
    border_bias_ref,
    middle_bias_ref,
    gain_two_ref,
    hidden_ref,
    output_ref,
    nrm_ref,
    wk_ref,
    wqv_ref,
    wp_ref,
    k_ref,
    v_ref,
    border_ref,
    mid_ref,
    q_scr,
    p_scr,
    a_scr,
    o_scr,
    bias_scr,
    sem,
):
    height, cols, chans = own_ref.shape
    inner = cols // WIN - 2
    copies = BiasCopies((border_bias_ref, middle_bias_ref), bias_scr, sem)
    copies.start()
    weights_into(qkv_ref, proj_ref, wk_ref, wqv_ref, wp_ref)
    gain_one = gain_one_ref[...]
    for r in range(RIM):
        above, below = from_sides(flags[4] > 0, row_one_ref[r], row_two_ref[r])
        nrm_ref[r] = layer_norm(above, gain_one)
        nrm_ref[RIM + height + r] = layer_norm(below, gain_one)
    for r in range(height):
        nrm_ref[RIM + r] = layer_norm(own_ref[r].astype(F32), gain_one)
    kinds, windows, first, queries = [], [], [], []
    for w in range(inner):
        c0 = WIN * (w + 1)
        project(nrm_ref[:, c0 - RIM : c0 - RIM + KWIN], wk_ref, wqv_ref, k_ref, v_ref, w)
        first.append(border_rows(own_ref, c0).reshape(128, chans))
        queries.append(border_rows(nrm_ref.at[RIM : RIM + height], c0))
        kinds.append(0)
        windows.append(w)
    for w in range(inner - 1):
        c0 = WIN * (w + 1)
        first.append(own_ref[4:12, c0 : c0 + WIN].reshape(128, chans))
        queries.append(nrm_ref[RIM + 4 : RIM + 12, c0 : c0 + WIN])
        kinds.append(1)
        windows.append(w)
    groups = len(kinds)
    set_queries(q_scr, wqv_ref, queries)
    copies.wait()
    first = jnp.concatenate(first, axis=0).astype(F32) + attention(
        kinds, windows, q_scr, k_ref, v_ref, bias_scr, wp_ref, p_scr, a_scr, o_scr
    )
    mixed = feed_forward(first, gain_two_ref[...], hidden_ref, output_ref)
    mixed = mixed.reshape(groups, 8, WIN, chans)
    for g in range(groups):
        if g < inner:
            border_ref[:, WIN * g : WIN * (g + 1)] = mixed[g]
        else:
            mid_ref[:, WIN * (g - inner) : WIN * (g - inner + 1)] = mixed[g]


def outer_kernel(
    flags,
    own_ref,
    nrm_ref,
    col_one_ref,
    col_two_ref,
    gain_one_ref,
    wk_ref,
    wqv_ref,
    wp_ref,
    inner_k_ref,
    inner_v_ref,
    inner_border_ref,
    left_bias_ref,
    border_bias_ref,
    right_bias_ref,
    gain_two_ref,
    hidden_ref,
    output_ref,
    pay_one_ref,
    pay_two_ref,
    edge_ref,
    side_ref,
    k_ref,
    v_ref,
    side_scr,
    x_scr,
    q_scr,
    p_scr,
    a_scr,
    o_scr,
    bias_scr,
    sem,
    image,
):
    height, cols, chans = own_ref.shape
    inner = cols // WIN - 2
    copies = BiasCopies((left_bias_ref, border_bias_ref, right_bias_ref), bias_scr, sem)
    copies.start()
    gain_one = gain_one_ref[...]
    for r in range(height + 2 * RIM):
        both = from_sides(flags[5] > 0, col_one_ref[r], col_two_ref[r])
        for side in range(2):
            if RIM <= r < RIM + height:
                x_scr[side, r - RIM] = both[side]
            side_scr[side, r, side * EDGE : (side + 1) * EDGE] = layer_norm(both[side], gain_one)
    side_scr[0, :, EDGE : 2 * EDGE] = nrm_ref[:, 0:EDGE]
    side_scr[1, :, 0:EDGE] = nrm_ref[:, cols - EDGE : cols]
    k_ref[2] = inner_k_ref[inner - 1]
    v_ref[2] = inner_v_ref[inner - 1]
    for index, side, c0 in ((0, 0, RIM), (1, 0, RIM + WIN), (3, 1, RIM), (4, 1, RIM + WIN)):
        project(side_scr[side, :, c0 : c0 + KWIN], wk_ref, wqv_ref, k_ref, v_ref, index)
    spots = (EDGE - STRIP, 0, cols - WIN, EDGE)
    first, queries = [], []
    for g in range(4):
        side, c0 = g // 2, spots[g]
        if g in (0, 3):
            x = x_scr[side, :, c0 - side * EDGE : c0 - side * EDGE + STRIP]
            queries.append(side_scr[side, RIM : RIM + height, c0 : c0 + STRIP])
        else:
            x = border_rows(own_ref, c0).astype(F32)
            queries.append(border_rows(nrm_ref.at[RIM : RIM + height], c0))
        first.append(x.reshape(128, chans))
    set_queries(q_scr, wqv_ref, queries)
    copies.wait()
    first = jnp.concatenate(first, axis=0) + attention(
        [0, 1, 1, 2], [0, 1, 3, 4], q_scr, k_ref, v_ref, bias_scr, wp_ref, p_scr, a_scr, o_scr
    )
    image[0:4, STRIP + WIN : STRIP + cols - WIN] = inner_border_ref[0:4]
    image[12:16, STRIP + WIN : STRIP + cols - WIN] = inner_border_ref[4:8]
    for pair in range(2):
        mixed = feed_forward(first[256 * pair : 256 * pair + 256], gain_two_ref[...], hidden_ref, output_ref)
        for s in range(2):
            g = 2 * pair + s
            one = mixed[s * 128 : (s + 1) * 128]
            if g in (0, 3):
                one = jnp.where(flags[g // 3] > 0, 0.0, one).reshape(height, STRIP, chans)
                c0 = 0 if g == 0 else STRIP + cols
                image[:, c0 : c0 + STRIP] = one
            else:
                one = one.reshape(8, WIN, chans)
                c0 = STRIP + spots[g]
                image[0:4, c0 : c0 + WIN] = one[0:4]
                image[12:16, c0 : c0 + WIN] = one[4:8]
    even = flags[4] > 0
    pay_one_ref[...] = jnp.where(even, image[13:16], image[0:3]).astype(BF16)
    pay_two_ref[...] = jnp.where(even, image[0:3], image[13:16]).astype(BF16)
    edge_ref[0:4] = image[0:4]
    edge_ref[4:8] = image[12:16]
    side_ref[:, 0:STRIP] = image[4:12, 0:STRIP]
    side_ref[:, STRIP : 2 * STRIP] = image[4:12, STRIP + cols :]


def middle_kernel(
    own_ref,
    nrm_ref,
    k_ref,
    v_ref,
    wqv_ref,
    wp_ref,
    inner_mid_ref,
    middle_bias_ref,
    gain_two_ref,
    hidden_ref,
    output_ref,
    mid_ref,
    q_scr,
    p_scr,
    a_scr,
    o_scr,
):
    height, cols, chans = own_ref.shape
    spots = (0, cols - 2 * WIN, cols - WIN)
    set_queries(q_scr, wqv_ref, [nrm_ref[RIM + 4 : RIM + 12, c0 : c0 + WIN] for c0 in spots])
    first = [own_ref[4:12, c0 : c0 + WIN].reshape(128, chans) for c0 in spots]
    first = jnp.concatenate(first, axis=0).astype(F32) + attention(
        None, [1, 2, 3], q_scr, k_ref, v_ref, middle_bias_ref, wp_ref, p_scr, a_scr, o_scr
    )
    mixed = feed_forward(first, gain_two_ref[...], hidden_ref, output_ref)
    mixed = mixed.reshape(3, 8, WIN, chans)
    mid_ref[:, WIN : cols - 2 * WIN] = inner_mid_ref[...]
    for g in range(3):
        mid_ref[:, spots[g] : spots[g] + WIN] = mixed[g]


def attention_scratch(groups, kinds):
    scratch = [
        pltpu.VMEM((groups, HEADS // 2, 2 * HP, 256), BF16),
        pltpu.VMEM((3, CHUNK, 256), BF16),
        pltpu.VMEM((3, 1, 256), F32),
        pltpu.VMEM((groups, HEADS // 2, 2 * HP, 256), F32),
    ]
    if kinds:
        scratch.append(pltpu.VMEM((kinds, HEADS, KEYS, 128), BF16))
        scratch.append(pltpu.SemaphoreType.DMA((kinds,)))
    return scratch


def inner_block(*args):
    height, cols, chans = args[1].shape
    inner = cols // WIN - 2
    width = HEADS * HP
    groups = 2 * inner - 1
    return call(
        inner_kernel,
        (
            jax.ShapeDtypeStruct((height + 2 * RIM, cols, chans), F32),
            jax.ShapeDtypeStruct((chans, 3 * 128), BF16),
            jax.ShapeDtypeStruct((2 * width, chans), BF16),
            jax.ShapeDtypeStruct((width, chans), BF16),
            jax.ShapeDtypeStruct((inner, KEYS, 3 * 128), BF16),
            jax.ShapeDtypeStruct((inner, CHUNKS, width, CHUNK), BF16),
            jax.ShapeDtypeStruct((8, WIN * inner, chans), F32),
            jax.ShapeDtypeStruct((8, WIN * (inner - 1), chans), F32),
        ),
        attention_scratch(groups, 2),
        5_000_000_000,
        4_000_000,
        smem=1,
    )(*args)


def outer_block(*args):
    height, cols, chans = args[1].shape
    span = cols + 2 * STRIP
    return call(
        outer_kernel,
        (
            jax.ShapeDtypeStruct((3, span, chans), BF16),
            jax.ShapeDtypeStruct((3, span, chans), BF16),
            jax.ShapeDtypeStruct((8, span, chans), F32),
            jax.ShapeDtypeStruct((8, 2 * STRIP, chans), F32),
            jax.ShapeDtypeStruct((5, KEYS, 3 * 128), BF16),
            jax.ShapeDtypeStruct((5, CHUNKS, HEADS * HP, CHUNK), BF16),
        ),
        [
            pltpu.VMEM((2, height + 2 * RIM, 2 * EDGE, chans), F32),
            pltpu.VMEM((2, height, EDGE, chans), F32),
            *attention_scratch(4, 3),
            pltpu.VMEM((height, span, chans), F32),
        ],
        5_000_000_000,
        4_000_000,
        smem=1,
    )(*args)


def middle_block(*args):
    height, cols, chans = args[0].shape
    return call(
        middle_kernel,
        jax.ShapeDtypeStruct((8, cols, chans), F32),
        attention_scratch(3, 0),
        5_000_000_000,
        4_000_000,
    )(*args)


def conv_kernel(
    flags,
    own_ref,
    row_one_ref,
    row_two_ref,
    col_one_ref,
    col_two_ref,
    back_one_ref,
    back_two_ref,
    edge_ref,
    side_ref,
    mid_ref,
    group_ref,
    before_ref,
    upsample_ref,
    out_ref,
    base,
    image,
    taps,
    grouped,
    sums,
    lowfeat,
    low_taps,
    out_scr,
    wg_scr,
    wb_scr,
    wu_scr,
):
    height, cols, chans = own_ref.shape
    span = cols + 2 * STRIP
    at_left, at_right, at_top, at_bottom = (flags[i] > 0 for i in range(4))
    even_row, even_col = flags[4] > 0, flags[5] > 0

    feats = before_ref.shape[2]
    pad = chans // 16 * 16
    for a in range(3):
        wb_scr[256 * a + pad : 256 * (a + 1)] = jnp.zeros((256 - pad, 3 * feats), BF16)
        wu_scr[256 * a + 3 * feats : 256 * (a + 1)] = jnp.zeros((256 - 3 * feats, 4 * feats), BF16)
        for b in range(3):
            wg_scr[256 * (3 * a + b) + pad : 256 * (3 * a + b + 1)] = jnp.zeros((256 - pad, chans), BF16)
            wg_scr[256 * (3 * a + b) : 256 * (3 * a + b) + chans] = group_ref[a, b]
    same = one_hot((chans, chans), lambda row: row, lambda col: col)
    order = one_hot(
        (4 * feats, 4 * feats), lambda row: row, lambda col: col % feats * 4 + col // feats
    )
    for a in range(3):
        part = before_ref[a].reshape(3 * feats, chans)
        wb_scr[256 * a : 256 * a + chans] = dot_nt(same, part).astype(BF16)
        part = upsample_ref[a].reshape(3 * feats, 4 * feats)
        wu_scr[256 * a : 256 * a + 3 * feats] = dot(part, order).astype(BF16)

    above, below = from_sides(even_row, row_one_ref[...], row_two_ref[...])
    base[0:2, STRIP : STRIP + cols] = above[2:4]
    base[2 : 2 + height, STRIP : STRIP + cols] = own_ref[...].astype(F32)
    base[2 + height : 4 + height, STRIP : STRIP + cols] = below[0:2]
    rows = slice(2, height + 6)
    before_side, after_side = from_sides(even_col, col_one_ref[rows], col_two_ref[rows])
    base[:, 0:STRIP] = before_side[:, EDGE - STRIP :]
    base[:, STRIP + cols : span] = after_side[:, 0:STRIP]
    base[:, span:] = jnp.zeros((height + 4, STRIP, chans), F32)
    image[:, span:] = jnp.zeros((height + 6, STRIP, chans), F32)
    above, below = from_sides(even_row, back_one_ref[...], back_two_ref[...])
    image[0:3, 0:span] = above
    image[3:7, 0:span] = edge_ref[0:4]
    image[7:15, 0:STRIP] = side_ref[:, 0:STRIP]
    image[7:15, STRIP : STRIP + cols] = mid_ref[...]
    image[7:15, STRIP + cols : span] = side_ref[:, STRIP : 2 * STRIP]
    image[15:19, 0:span] = edge_ref[4:8]
    image[19:22, 0:span] = below
    taps[...] = jnp.zeros(taps.shape, BF16)
    grouped[...] = jnp.zeros(grouped.shape, BF16)
    part = 4
    col = lax.broadcasted_iota(jnp.int32, (span, chans), 0) - 2
    keep_grouped = (col < cols + 2) & ((col >= 0) | jnp.logical_not(at_left))
    keep_grouped = keep_grouped & ((col < cols) | jnp.logical_not(at_right))
    low_span = cols + 8
    col = lax.broadcasted_iota(jnp.int32, (low_span, 128), 0) - 1
    keep_low = (col <= cols) & ((col >= 0) | jnp.logical_not(at_left))
    keep_low = keep_low & ((col < cols) | jnp.logical_not(at_right))
    left_half = lax.broadcasted_iota(jnp.int32, (cols, 128), 1) < feats
    spot = lax.broadcasted_iota(jnp.int32, (256, 256), 0)
    place = lax.broadcasted_iota(jnp.int32, (256, 256), 1)
    spread = (spot % 128 // cols == place // 128) & (
        spot % cols * 2 + spot // 128 == place % 128
    )
    spread = spread.astype(F32).astype(BF16)

    def fill_taps(first, last):
        for b in range(3):
            start = STRIP - 3 + b
            taps[first:last, :, 256 * b : 256 * b + chans] = image[
                first:last, start : start + span, :
            ].astype(BF16)

    def group(h):
        lhs = jnp.concatenate(
            [taps[h + a : h + a + part].reshape(part * span, 768) for a in range(3)], axis=1
        )
        total = dot(lhs, wg_scr[...]).reshape(part, span, chans)
        total = total + base[h : h + part, STRIP - 2 : STRIP - 2 + span, :]
        for r in range(part):
            mask = keep_grouped
            if h + r < 2:
                mask = mask & jnp.logical_not(at_top)
            if h + r >= height + 2:
                mask = mask & jnp.logical_not(at_bottom)
            grouped[h + r, 0:span, 0:chans] = jnp.where(mask, total[r], 0.0).astype(BF16)

    def narrow(h, count):
        lhs = jnp.concatenate(
            [grouped[h + a : h + a + count].reshape(count * span, 256) for a in range(3)], axis=1
        )
        slot = h // part % 2
        sums[slot, 0:count, :, 0 : 3 * feats] = dot(lhs, wb_scr[...]).reshape(count, span, 3 * feats)
        for r in range(count):
            total = sums[slot, r, 0:low_span, 0:128]
            total = total + pltpu.roll(sums[slot, r, 1 : low_span + 1, 0:128], feats, 1)
            total = total + sums[slot, r, 2 : low_span + 2, 128:256]
            mask = keep_low
            if h + r == 0:
                mask = mask & jnp.logical_not(at_top)
            if h + r == height + 1:
                mask = mask & jnp.logical_not(at_bottom)
            lowfeat[h + r] = jnp.where(mask, jnp.where(total >= 0, total, 0.01 * total), 0.0)
            low_taps[h + r, :, 0:128] = jnp.where(
                left_half, lowfeat[h + r, 0:cols], pltpu.roll(lowfeat[h + r, 1 : cols + 1], feats, 1)
            ).astype(BF16)
            low_taps[h + r, :, 128:256] = jnp.where(
                left_half, lowfeat[h + r, 2 : cols + 2], 0.0
            ).astype(BF16)

    def expand(h):
        lhs = jnp.concatenate(
            [low_taps[h + a : h + a + part].reshape(part * cols, 256) for a in range(3)], axis=1
        )
        total = dot(lhs, wu_scr[...])
        for pair in range(part // 2):
            turned = total[2 * cols * pair : 2 * cols * (pair + 1)].T.astype(BF16)
            lhs = [
                jnp.concatenate(
                    [turned[(2 * a + b) * feats : (2 * a + b + 1) * feats] for b in range(2)], axis=1
                )
                for a in range(2)
            ]
            final = dot(jnp.concatenate(lhs, axis=0), spread)
            for r in range(2):
                for a in range(2):
                    row = 2 * (h + 2 * pair + r) + a
                    out_scr[pl.ds(row, feats, stride=2 * height), :] = final[
                        a * feats : (a + 1) * feats, 128 * r : 128 * (r + 1)
                    ]

    fill_taps(0, part + 2)
    narrowed = expanded = done = 0
    while expanded < height:
        expand_to, narrow_to = min(narrowed - 2, height), min(done - 2, height + 2)
        if done < height + 4:
            if done + part < height + 4:
                fill_taps(done + part + 2, done + 2 * part + 2)
            group(done)
            done += part
        while narrowed < narrow_to:
            count = min(part, height + 2 - narrowed)
            if narrowed + count > narrow_to:
                break
            narrow(narrowed, count)
            narrowed += count
        while expanded + part <= expand_to:
            expand(expanded)
            expanded += part
    out_ref[...] = out_scr[...].reshape(feats, 2 * height, 128).astype(BF16)


def convs(*args):
    height, cols, chans = args[1].shape
    span = cols + 2 * STRIP
    feats = args[-2].shape[2]
    return call(
        conv_kernel,
        jax.ShapeDtypeStruct((feats, 2 * height, 2 * cols), BF16),
        [
            pltpu.VMEM((height + 4, span + STRIP, chans), F32),
            pltpu.VMEM((height + 6, span + STRIP, chans), F32),
            pltpu.VMEM((height + 6, span, 768), BF16),
            pltpu.VMEM((height + 4, span, 256), BF16),
            pltpu.VMEM((2, 4, span, 256), F32),
            pltpu.VMEM((height + 2, cols + 8, 128), F32),
            pltpu.VMEM((height + 2, cols, 256), BF16),
            pltpu.VMEM((feats * 2 * height, 128), F32),
            pltpu.VMEM((9 * 256, chans), BF16),
            pltpu.VMEM((3 * 256, 3 * feats), BF16),
            pltpu.VMEM((3 * 256, 4 * feats), BF16),
        ],
        8_000_000_000,
        4_000_000,
        smem=1,
    )(*args)


def swapped(axis, first, second):
    count = lax.axis_size(axis)
    out = []
    for start, payload in ((0, first), (1, second)):
        pairs = [(i, i + 1) for i in range(start, count - 1, 2)]
        pairs = pairs + [(b, a) for a, b in pairs]
        out.append(lax.ppermute(payload, axis, pairs))
    return out


def on_device(
    features,
    gain_one,
    qkv_weight,
    bias_table,
    proj_weight,
    gain_two,
    hidden_weight,
    output_weight,
    group_conv,
    before_conv,
    upsample_conv,
):
    height, cols, chans = features.shape
    row, column = lax.axis_index("rows"), lax.axis_index("cols")
    even_row, even_col = row % 2 == 0, column % 2 == 0
    flags = jnp.stack(
        [
            column == 0,
            column == lax.axis_size("cols") - 1,
            row == 0,
            row == lax.axis_size("rows") - 1,
            even_row,
            even_col,
        ]
    ).astype(jnp.int32)

    low, high = features[:RIM], features[height - RIM :]
    row_one, row_two = swapped(
        "rows", jnp.where(even_row, high, low), jnp.where(even_row, low, high)
    )
    above, below = jnp.where(even_row, row_two, row_one), jnp.where(even_row, row_one, row_two)
    low, high = (
        jnp.concatenate([part[:, span] for part in (above, features, below)], axis=0)
        for span in (slice(0, EDGE), slice(cols - EDGE, cols))
    )
    col_one, col_two = swapped(
        "cols", jnp.where(even_col, high, low), jnp.where(even_col, low, high)
    )

    left_bias, border_bias, right_bias, middle_bias = build_bias(bias_table)
    gain_one, gain_two = gain_one.reshape(1, chans), gain_two.reshape(1, chans)
    post = (gain_two, hidden_weight, output_weight.T)
    nrm, wk, wqv, wp, inner_k, inner_v, inner_border, inner_mid = inner_block(
        flags,
        features,
        row_one,
        row_two,
        gain_one,
        qkv_weight,
        proj_weight,
        border_bias,
        middle_bias,
        *post,
    )
    back_one, back_two, edge, side, keys, values = outer_block(
        flags,
        features,
        nrm,
        col_one,
        col_two,
        gain_one,
        wk,
        wqv,
        wp,
        inner_k,
        inner_v,
        inner_border,
        left_bias,
        border_bias,
        right_bias,
        *post,
    )
    back_one, back_two = swapped("rows", back_one, back_two)
    mid = middle_block(features, nrm, keys, values, wqv, wp, inner_mid, middle_bias, *post)
    return convs(
        flags,
        features,
        row_one,
        row_two,
        col_one,
        col_two,
        back_one,
        back_two,
        edge,
        side,
        mid,
        group_conv,
        before_conv.transpose(0, 1, 3, 2),
        upsample_conv,
    )


def solution(mesh):
    placed = (P("rows", "cols", None), P(), P(), P(), P(), P(), P(), P(), P(), P(), P())
    return jax.shard_map(
        on_device, mesh=mesh, in_specs=placed, out_specs=P(None, "rows", "cols"), check_vma=False
    )
```

```python
import functools

import jax
import jax.numpy as jnp
import numpy as np
from jax import lax
from jax.experimental import pallas as pl
from jax.experimental.pallas import tpu as pltpu
from jax.sharding import PartitionSpec as P

HEADS = 6
HD = 30
HP = 32
WIN = 16
KWIN = 24
KEYS = KWIN * KWIN
SIDE = WIN + KWIN - 1
RIM = (KWIN - WIN) // 2
EDGE = WIN + 2 * RIM
STRIP = 8
LOG2E = 1.4426950408889634
F32 = jnp.float32
BF16 = jnp.bfloat16
NT = (((1,), (1,)), ((), ()))
TN = (((0,), (0,)), ((), ()))


def dot(a, b):
    return jnp.dot(a, b, preferred_element_type=F32)


def dot_nt(a, b):
    return lax.dot_general(a, b, NT, preferred_element_type=F32)


def layer_norm(values, gain):
    center = values - jnp.mean(values, axis=-1, keepdims=True)
    spread = jnp.mean(center * center, axis=-1, keepdims=True)
    return center * lax.rsqrt(spread + 1e-05) * gain


def call(kernel, out_shape, scratch, flops, bytes_accessed):
    return pl.pallas_call(
        kernel,
        out_shape=out_shape,
        scratch_shapes=scratch,
        compiler_params=pltpu.CompilerParams(vmem_limit_bytes=24 * 2**20),
        cost_estimate=pl.CostEstimate(
            flops=flops, bytes_accessed=bytes_accessed, transcendentals=0
        ),
    )


def bias_kernel(table_ref, out_ref, t_scr, e_scr, w_scr, x_scr):
    for d in range(SIDE):
        t_scr[8 * d : 8 * d + HEADS, 0:SIDE] = jnp.exp(table_ref[:, SIDE * d : SIDE * (d + 1)])

    def head(h, carry):
        values = t_scr[pl.ds(h, SIDE, stride=8), 0:SIDE].astype(BF16)

        def expand(cols, first):
            width = -(-SIDE * cols // 128) * 128
            spot = lax.broadcasted_iota(jnp.int32, (SIDE, width), 1) // cols
            row = lax.broadcasted_iota(jnp.int32, (SIDE, width), 0)
            pick = (spot == SIDE - 1 - row).astype(F32).astype(BF16)
            e_scr[0:SIDE, 0:width] = lax.dot_general(values, pick, TN, preferred_element_type=F32)
            lane = lax.broadcasted_iota(jnp.int32, (KWIN, width), 1) % cols
            out = jnp.zeros((KWIN, width), F32)
            for jj in range(cols):
                start = WIN - 1 - first - jj
                out = jnp.where(lane == jj, e_scr[start : start + KWIN, 0:width], out)
            w_scr[:, 0:width] = out

        lanes = lax.broadcasted_iota(jnp.int32, (KWIN, 128), 1)
        expand(WIN, 0)
        for p in range(KWIN):
            rows = slice(p * KWIN, (p + 1) * KWIN)
            low = w_scr[:, (23 - p) * WIN : (23 - p) * WIN + 128]
            high = w_scr[:, (31 - p) * WIN : (31 - p) * WIN + 128]
            x_scr[0, rows] = jnp.where(lanes < 64, low, high)
            x_scr[1, rows] = w_scr[:, (27 - p) * WIN : (27 - p) * WIN + 128]
        out_ref[1, h] = x_scr[0].astype(BF16)
        out_ref[3, h] = x_scr[1].astype(BF16)
        for kind, first in ((0, WIN - STRIP), (2, 0)):
            expand(STRIP, first)
            for p in range(KWIN):
                rows = slice(p * KWIN, (p + 1) * KWIN)
                x_scr[0, rows] = w_scr[:, (23 - p) * STRIP : (23 - p) * STRIP + 128]
            out_ref[kind, h] = x_scr[0].astype(BF16)
        return carry

    lax.fori_loop(0, HEADS, head, 0)


def build_bias(bias_table):
    return call(
        bias_kernel,
        jax.ShapeDtypeStruct((4, HEADS, KEYS, 128), BF16),
        [
            pltpu.VMEM((8 * SIDE, 128), F32),
            pltpu.VMEM((SIDE + 1, 640), F32),
            pltpu.VMEM((KWIN, 640), F32),
            pltpu.VMEM((2, KEYS, 128), F32),
        ],
        4_000_000_000,
        4_000_000,
    )(bias_table.T)


def one_hot(shape, row_of, col_of):
    row = lax.broadcasted_iota(jnp.int32, shape, 0)
    col = lax.broadcasted_iota(jnp.int32, shape, 1)
    return (row_of(row) == col_of(col)).astype(F32).astype(BF16)


def spread_head(place):
    return jnp.where(place % HP < HD, place // HP * HD + place % HP, -1)


def weights_into(qkv_ref, proj_ref, wk_ref, wqv_ref, wp_ref):
    chans = qkv_ref.shape[0]
    width = HEADS * HP
    qkv = qkv_ref[...]
    pick = one_hot(
        (3 * chans, 3 * 128),
        lambda row: row,
        lambda col: jnp.where(
            (col % 128 < 2 * HP) & (col % HP < HD),
            chans + (col // 128 * 2 + col % 128 // HP) * HD + col % HP,
            -1,
        ),
    )
    wk_ref[...] = dot(qkv, pick).astype(BF16)
    pick = one_hot(
        (2 * width, 3 * chans),
        lambda row: jnp.where(
            row % HP < HD, row // HP * HD + row % HP + jnp.where(row < width, 0, chans), -1
        ),
        lambda col: col,
    )
    wqv_ref[...] = dot_nt(pick, qkv).astype(BF16)
    pick = one_hot((width, chans), spread_head, lambda col: col)
    wp_ref[...] = dot(pick, proj_ref[...]).astype(BF16)


def set_queries(q_scr, wqv_ref, groups):
    scale = LOG2E / np.sqrt(HD)
    rows = jnp.concatenate([rows.reshape(128, rows.shape[2]) for rows in groups], axis=0)
    queries = (dot_nt(wqv_ref[0 : HEADS * HP], rows.astype(BF16)) * scale).astype(BF16)
    none = jnp.zeros((HP, 128), BF16)
    for g in range(len(groups)):
        lanes = slice(128 * g, 128 * g + 128)
        for t in range(HEADS // 2):
            one = queries[2 * t * HP : (2 * t + 1) * HP, lanes]
            two = queries[(2 * t + 1) * HP : (2 * t + 2) * HP, lanes]
            q_scr[g, t, 0:HP] = jnp.concatenate([one, none], axis=1)
            q_scr[g, t, HP : 2 * HP] = jnp.concatenate([none, two], axis=1)


def lookup(g, values):
    out = values[0]
    for index in range(1, len(values)):
        out = jnp.where(g >= index, values[index], out)
    return out


def attention(kinds, windows, q_scr, k_ref, v_ref, bias_ref, wp_ref, s_scr, m_scr, p_scr, o_scr):
    groups = len(kinds)
    pairs = HEADS // 2
    step = 192

    def keep(g, t, k0, top):
        keys = k_ref[lookup(g, windows), k0 : k0 + step, 128 * t : 128 * t + 2 * HP]
        one = dot(keys, q_scr[g, t])
        s_scr[t, k0 : k0 + step] = one
        part = jnp.max(one.reshape(step // 8, 8, 256), axis=0)
        return part if top is None else jnp.maximum(top, part)

    def sum_values(g, t):
        o_scr[g, t] = dot(v_ref[lookup(g, windows), 2 * t * HP : 2 * (t + 1) * HP], p_scr[t])

    top = None
    for k0 in range(0, KEYS, step):
        top = keep(0, 0, k0, top)
    m_scr[...] = top
    p_scr[pairs - 1] = jnp.zeros((KEYS, 256), BF16)

    def attend(g, carry):
        kind = lookup(g, kinds)
        top = m_scr[...]
        for t in range(pairs):
            top = jnp.max(top, axis=0, keepdims=True)
            if t == 0:
                sum_values(jnp.maximum(g - 1, 0), pairs - 1)
            else:
                sum_values(g, t - 1)
            following = g if t + 1 < pairs else jnp.minimum(g + 1, groups - 1)
            later = None
            for k0 in range(0, KEYS, step):
                prob = jnp.exp2(s_scr[t, k0 : k0 + step] - top).astype(BF16)
                for half in range(2):
                    lanes = slice(128 * half, 128 * half + 128)
                    p_scr[t, k0 : k0 + step, lanes] = (
                        prob[:, lanes] * bias_ref[kind, 2 * t + half, k0 : k0 + step]
                    )
                later = keep(following, (t + 1) % pairs, k0, later)
            top = later
        m_scr[...] = top
        return carry

    lax.fori_loop(0, groups, attend, 0)
    sum_values(groups - 1, pairs - 1)
    attended = []
    for g in range(groups):
        parts = []
        for t in range(pairs):
            for half in range(2):
                lanes = slice(128 * half, 128 * half + 128)
                one = o_scr[g, t, half * HP : (half + 1) * HP, lanes]
                parts.append((one * (1.0 / one[HD : HD + 1])).astype(BF16))
        attended.append(jnp.concatenate(parts, axis=0))
    attended = jnp.concatenate(attended, axis=1)
    return lax.dot_general(attended, wp_ref[...], TN, preferred_element_type=F32)


def feed_forward(first, gain, hidden_ref, output_ref):
    normed = layer_norm(first, gain).astype(BF16)
    inner = dot(normed, hidden_ref[...])
    inner = (0.5 * inner * (1.0 + lax.erf(inner * np.float32(np.sqrt(0.5))))).astype(BF16)
    return first + dot_nt(inner, output_ref[...])


def feed_groups(first, gain, hidden_ref, output_ref):
    groups = range(first.shape[0] // 128)
    return [feed_forward(first[128 * g : 128 * (g + 1)], gain, hidden_ref, output_ref) for g in groups]


def project(keys, wk_ref, wqv_ref, k_ref, v_ref, index):
    width = HEADS * HP
    one_row = (lax.broadcasted_iota(jnp.int32, (width, 1), 0) % HP == HD).astype(F32)
    keys = keys.reshape(KEYS, keys.shape[2]).astype(BF16)
    k_ref[index] = dot(keys, wk_ref[...]).astype(BF16)
    v_ref[index] = (dot_nt(wqv_ref[width : 2 * width], keys) + one_row).astype(BF16)


def at_edges():
    row, column = lax.axis_index("rows"), lax.axis_index("cols")
    return (
        column == 0,
        column == lax.axis_size("cols") - 1,
        row == 0,
        row == lax.axis_size("rows") - 1,
        row % 2 == 0,
        column % 2 == 0,
    )


def from_sides(even, first, second):
    first, second = first.astype(F32), second.astype(F32)
    return jnp.where(even, second, first), jnp.where(even, first, second)


def border_rows(ref, c0):
    return jnp.concatenate([ref[0:4, c0 : c0 + WIN], ref[12:16, c0 : c0 + WIN]], axis=0)


def pack_kernel(own_ref, row_one_ref, row_two_ref, pay_one_ref, pay_two_ref):
    height, cols, chans = own_ref.shape
    even_row, even_col = at_edges()[4:]
    above, below = from_sides(even_row, row_one_ref[...], row_two_ref[...])
    for rows, part in (
        (slice(0, RIM), above),
        (slice(RIM, RIM + height), own_ref[...].astype(F32)),
        (slice(RIM + height, 2 * RIM + height), below),
    ):
        low, high = part[:, 0:EDGE], part[:, cols - EDGE : cols]
        pay_one_ref[rows] = jnp.where(even_col, high, low).astype(BF16)
        pay_two_ref[rows] = jnp.where(even_col, low, high).astype(BF16)


def pack(own, row_one, row_two):
    height, cols, chans = own.shape
    pay = jax.ShapeDtypeStruct((height + 2 * RIM, EDGE, chans), BF16)
    return call(pack_kernel, (pay, pay), [], 1_000_000, 1_000_000)(own, row_one, row_two)


def inner_kernel(
    own_ref,
    row_one_ref,
    row_two_ref,
    gain_one_ref,
    qkv_ref,
    proj_ref,
    bias_ref,
    gain_two_ref,
    hidden_ref,
    output_ref,
    nrm_ref,
    wk_ref,
    wqv_ref,
    wp_ref,
    k_ref,
    v_ref,
    border_ref,
    mid_ref,
    q_scr,
    s_scr,
    m_scr,
    p_scr,
    o_scr,
):
    height, cols, chans = own_ref.shape
    inner = cols // WIN - 2
    flags = at_edges()
    weights_into(qkv_ref, proj_ref, wk_ref, wqv_ref, wp_ref)
    gain_one = gain_one_ref[...]
    for r in range(RIM):
        above, below = from_sides(flags[4], row_one_ref[r], row_two_ref[r])
        nrm_ref[r] = layer_norm(above, gain_one)
        nrm_ref[RIM + height + r] = layer_norm(below, gain_one)
    for r in range(height):
        nrm_ref[RIM + r] = layer_norm(own_ref[r].astype(F32), gain_one)
    kinds, windows, first, queries = [], [], [], []
    for w in range(inner):
        c0 = WIN * (w + 1)
        project(nrm_ref[:, c0 - RIM : c0 - RIM + KWIN], wk_ref, wqv_ref, k_ref, v_ref, w)
        first.append(border_rows(own_ref, c0).reshape(128, chans))
        queries.append(border_rows(nrm_ref.at[RIM : RIM + height], c0))
        kinds.append(1)
        windows.append(w)
    for w in range(inner - 1):
        c0 = WIN * (w + 1)
        first.append(own_ref[4:12, c0 : c0 + WIN].reshape(128, chans))
        queries.append(nrm_ref[RIM + 4 : RIM + 12, c0 : c0 + WIN])
        kinds.append(3)
        windows.append(w)
    groups = len(kinds)
    set_queries(q_scr, wqv_ref, queries)
    first = jnp.concatenate(first, axis=0).astype(F32) + attention(
        kinds, windows, q_scr, k_ref, v_ref, bias_ref, wp_ref, s_scr, m_scr, p_scr, o_scr
    )
    mixed = feed_groups(first, gain_two_ref[...], hidden_ref, output_ref)
    for g in range(groups):
        one = mixed[g].reshape(8, WIN, chans)
        if g < inner:
            border_ref[:, WIN * g : WIN * (g + 1)] = one
        else:
            mid_ref[:, WIN * (g - inner) : WIN * (g - inner + 1)] = one


def outer_kernel(
    own_ref,
    nrm_ref,
    col_one_ref,
    col_two_ref,
    gain_one_ref,
    wk_ref,
    wqv_ref,
    wp_ref,
    inner_k_ref,
    inner_v_ref,
    inner_border_ref,
    bias_ref,
    gain_two_ref,
    hidden_ref,
    output_ref,
    pay_one_ref,
    pay_two_ref,
    edge_ref,
    side_ref,
    k_ref,
    v_ref,
    side_scr,
    x_scr,
    q_scr,
    s_scr,
    m_scr,
    p_scr,
    o_scr,
    image,
):
    height, cols, chans = own_ref.shape
    inner = cols // WIN - 2
    flags = at_edges()
    gain_one = gain_one_ref[...]
    for r in range(height + 2 * RIM):
        both = from_sides(flags[5], col_one_ref[r], col_two_ref[r])
        for side in range(2):
            if RIM <= r < RIM + height:
                x_scr[side, r - RIM] = both[side]
            side_scr[side, r, side * EDGE : (side + 1) * EDGE] = layer_norm(both[side], gain_one)
    side_scr[0, :, EDGE : 2 * EDGE] = nrm_ref[:, 0:EDGE]
    side_scr[1, :, 0:EDGE] = nrm_ref[:, cols - EDGE : cols]
    k_ref[2] = inner_k_ref[inner - 1]
    v_ref[2] = inner_v_ref[inner - 1]
    for index, side, c0 in ((0, 0, RIM), (1, 0, RIM + WIN), (3, 1, RIM), (4, 1, RIM + WIN)):
        project(side_scr[side, :, c0 : c0 + KWIN], wk_ref, wqv_ref, k_ref, v_ref, index)
    spots = (EDGE - STRIP, 0, cols - WIN, EDGE)
    first, queries = [], []
    for g in range(4):
        side, c0 = g // 2, spots[g]
        if g in (0, 3):
            x = x_scr[side, :, c0 - side * EDGE : c0 - side * EDGE + STRIP]
            queries.append(side_scr[side, RIM : RIM + height, c0 : c0 + STRIP])
        else:
            x = border_rows(own_ref, c0).astype(F32)
            queries.append(border_rows(nrm_ref.at[RIM : RIM + height], c0))
        first.append(x.reshape(128, chans))
    set_queries(q_scr, wqv_ref, queries)
    first = jnp.concatenate(first, axis=0) + attention(
        [0, 1, 1, 2], [0, 1, 3, 4], q_scr, k_ref, v_ref, bias_ref, wp_ref, s_scr, m_scr, p_scr, o_scr
    )
    image[0:4, STRIP + WIN : STRIP + cols - WIN] = inner_border_ref[0:4]
    image[12:16, STRIP + WIN : STRIP + cols - WIN] = inner_border_ref[4:8]
    mixed = feed_groups(first, gain_two_ref[...], hidden_ref, output_ref)
    for g in range(4):
        if g in (0, 3):
            one = jnp.where(flags[g // 3], 0.0, mixed[g]).reshape(height, STRIP, chans)
            c0 = 0 if g == 0 else STRIP + cols
            image[:, c0 : c0 + STRIP] = one
        else:
            one = mixed[g].reshape(8, WIN, chans)
            c0 = STRIP + spots[g]
            image[0:4, c0 : c0 + WIN] = one[0:4]
            image[12:16, c0 : c0 + WIN] = one[4:8]
    even = flags[4]
    pay_one_ref[...] = jnp.where(even, image[13:16], image[0:3]).astype(BF16)
    pay_two_ref[...] = jnp.where(even, image[0:3], image[13:16]).astype(BF16)
    edge_ref[0:4] = image[0:4]
    edge_ref[4:8] = image[12:16]
    side_ref[:, 0:STRIP] = image[4:12, 0:STRIP]
    side_ref[:, STRIP : 2 * STRIP] = image[4:12, STRIP + cols :]


def middle_kernel(
    own_ref,
    nrm_ref,
    k_ref,
    v_ref,
    wqv_ref,
    wp_ref,
    inner_mid_ref,
    bias_ref,
    gain_two_ref,
    hidden_ref,
    output_ref,
    mid_ref,
    q_scr,
    s_scr,
    m_scr,
    p_scr,
    o_scr,
):
    height, cols, chans = own_ref.shape
    spots = (0, cols - 2 * WIN, cols - WIN)
    set_queries(q_scr, wqv_ref, [nrm_ref[RIM + 4 : RIM + 12, c0 : c0 + WIN] for c0 in spots])
    first = [own_ref[4:12, c0 : c0 + WIN].reshape(128, chans) for c0 in spots]
    first = jnp.concatenate(first, axis=0).astype(F32) + attention(
        [3, 3, 3], [1, 2, 3], q_scr, k_ref, v_ref, bias_ref, wp_ref, s_scr, m_scr, p_scr, o_scr
    )
    mixed = feed_groups(first, gain_two_ref[...], hidden_ref, output_ref)
    mid_ref[:, WIN : cols - 2 * WIN] = inner_mid_ref[...]
    for g in range(3):
        mid_ref[:, spots[g] : spots[g] + WIN] = mixed[g].reshape(8, WIN, chans)


def attention_scratch(groups):
    return [
        pltpu.VMEM((groups, HEADS // 2, 2 * HP, 256), BF16),
        pltpu.VMEM((HEADS // 2, KEYS, 256), F32),
        pltpu.VMEM((8, 256), F32),
        pltpu.VMEM((HEADS // 2, KEYS, 256), BF16),
        pltpu.VMEM((groups, HEADS // 2, 2 * HP, 256), F32),
    ]


def inner_block(*args):
    height, cols, chans = args[0].shape
    inner = cols // WIN - 2
    width = HEADS * HP
    groups = 2 * inner - 1
    return call(
        inner_kernel,
        (
            jax.ShapeDtypeStruct((height + 2 * RIM, cols, chans), F32),
            jax.ShapeDtypeStruct((chans, 3 * 128), BF16),
            jax.ShapeDtypeStruct((2 * width, chans), BF16),
            jax.ShapeDtypeStruct((width, chans), BF16),
            jax.ShapeDtypeStruct((inner, KEYS, 3 * 128), BF16),
            jax.ShapeDtypeStruct((inner, width, KEYS), BF16),
            jax.ShapeDtypeStruct((8, WIN * inner, chans), F32),
            jax.ShapeDtypeStruct((8, WIN * (inner - 1), chans), F32),
        ),
        attention_scratch(groups),
        5_000_000_000,
        4_000_000,
    )(*args)


def outer_block(*args):
    height, cols, chans = args[0].shape
    span = cols + 2 * STRIP
    return call(
        outer_kernel,
        (
            jax.ShapeDtypeStruct((3, span, chans), BF16),
            jax.ShapeDtypeStruct((3, span, chans), BF16),
            jax.ShapeDtypeStruct((8, span, chans), F32),
            jax.ShapeDtypeStruct((8, 2 * STRIP, chans), F32),
            jax.ShapeDtypeStruct((5, KEYS, 3 * 128), BF16),
            jax.ShapeDtypeStruct((5, HEADS * HP, KEYS), BF16),
        ),
        [
            pltpu.VMEM((2, height + 2 * RIM, 2 * EDGE, chans), F32),
            pltpu.VMEM((2, height, EDGE, chans), F32),
            *attention_scratch(4),
            pltpu.VMEM((height, span, chans), F32),
        ],
        5_000_000_000,
        4_000_000,
    )(*args)


def middle_block(*args):
    height, cols, chans = args[0].shape
    return call(
        middle_kernel,
        jax.ShapeDtypeStruct((8, cols, chans), F32),
        attention_scratch(3),
        5_000_000_000,
        4_000_000,
    )(*args)


def conv_kernel(
    own_ref,
    row_one_ref,
    row_two_ref,
    col_one_ref,
    col_two_ref,
    back_one_ref,
    back_two_ref,
    edge_ref,
    side_ref,
    mid_ref,
    group_ref,
    before_ref,
    upsample_ref,
    out_ref,
    base,
    image,
    taps,
    grouped,
    sums,
    lowfeat,
    low_taps,
    out_scr,
    wg_scr,
    wb_scr,
    wu_scr,
):
    height, cols, chans = own_ref.shape
    span = cols + 2 * STRIP
    at_left, at_right, at_top, at_bottom, even_row, even_col = at_edges()

    feats = before_ref.shape[2]
    pad = chans // 16 * 16
    for a in range(3):
        wb_scr[256 * a + pad : 256 * (a + 1)] = jnp.zeros((256 - pad, 3 * feats), BF16)
        wu_scr[256 * a + 3 * feats : 256 * (a + 1)] = jnp.zeros((256 - 3 * feats, 4 * feats), BF16)
        for b in range(3):
            wg_scr[256 * (3 * a + b) + pad : 256 * (3 * a + b + 1)] = jnp.zeros((256 - pad, chans), BF16)
            wg_scr[256 * (3 * a + b) : 256 * (3 * a + b) + chans] = group_ref[a, b]
    same = one_hot((chans, chans), lambda row: row, lambda col: col)
    order = one_hot(
        (4 * feats, 4 * feats), lambda row: row, lambda col: col % feats * 4 + col // feats
    )
    for a in range(3):
        part = before_ref[a].reshape(3 * feats, chans)
        wb_scr[256 * a : 256 * a + chans] = dot_nt(same, part).astype(BF16)
        part = upsample_ref[a].reshape(3 * feats, 4 * feats)
        wu_scr[256 * a : 256 * a + 3 * feats] = dot(part, order).astype(BF16)

    above, below = from_sides(even_row, row_one_ref[...], row_two_ref[...])
    base[0:2, STRIP : STRIP + cols] = above[2:4]
    base[2 : 2 + height, STRIP : STRIP + cols] = own_ref[...].astype(F32)
    base[2 + height : 4 + height, STRIP : STRIP + cols] = below[0:2]
    rows = slice(2, height + 6)
    before_side, after_side = from_sides(even_col, col_one_ref[rows], col_two_ref[rows])
    base[:, 0:STRIP] = before_side[:, EDGE - STRIP :]
    base[:, STRIP + cols : span] = after_side[:, 0:STRIP]
    base[:, span:] = jnp.zeros((height + 4, STRIP, chans), F32)
    image[:, span:] = jnp.zeros((height + 6, STRIP, chans), F32)
    above, below = from_sides(even_row, back_one_ref[...], back_two_ref[...])
    image[0:3, 0:span] = above
    image[3:7, 0:span] = edge_ref[0:4]
    image[7:15, 0:STRIP] = side_ref[:, 0:STRIP]
    image[7:15, STRIP : STRIP + cols] = mid_ref[...]
    image[7:15, STRIP + cols : span] = side_ref[:, STRIP : 2 * STRIP]
    image[15:19, 0:span] = edge_ref[4:8]
    image[19:22, 0:span] = below
    taps[...] = jnp.zeros(taps.shape, BF16)
    grouped[...] = jnp.zeros(grouped.shape, BF16)
    part = 4
    col = lax.broadcasted_iota(jnp.int32, (span, chans), 0) - 2
    keep_grouped = (col < cols + 2) & ((col >= 0) | jnp.logical_not(at_left))
    keep_grouped = keep_grouped & ((col < cols) | jnp.logical_not(at_right))
    low_span = cols + 8
    col = lax.broadcasted_iota(jnp.int32, (low_span, 128), 0) - 1
    keep_low = (col <= cols) & ((col >= 0) | jnp.logical_not(at_left))
    keep_low = keep_low & ((col < cols) | jnp.logical_not(at_right))
    left_half = lax.broadcasted_iota(jnp.int32, (cols, 128), 1) < feats
    spot = lax.broadcasted_iota(jnp.int32, (256, 256), 0)
    place = lax.broadcasted_iota(jnp.int32, (256, 256), 1)
    spread = (spot % 128 // cols == place // 128) & (
        spot % cols * 2 + spot // 128 == place % 128
    )
    spread = spread.astype(F32).astype(BF16)

    def fill_taps(first, last):
        for b in range(3):
            start = STRIP - 3 + b
            taps[first:last, :, 256 * b : 256 * b + chans] = image[
                first:last, start : start + span, :
            ].astype(BF16)

    def group(h):
        lhs = jnp.concatenate(
            [taps[h + a : h + a + part].reshape(part * span, 768) for a in range(3)], axis=1
        )
        total = dot(lhs, wg_scr[...]).reshape(part, span, chans)
        total = total + base[h : h + part, STRIP - 2 : STRIP - 2 + span, :]
        for r in range(part):
            mask = keep_grouped
            if h + r < 2:
                mask = mask & jnp.logical_not(at_top)
            if h + r >= height + 2:
                mask = mask & jnp.logical_not(at_bottom)
            grouped[h + r, 0:span, 0:chans] = jnp.where(mask, total[r], 0.0).astype(BF16)

    def narrow(h, count):
        lhs = jnp.concatenate(
            [grouped[h + a : h + a + count].reshape(count * span, 256) for a in range(3)], axis=1
        )
        slot = h // part % 2
        sums[slot, 0:count, :, 0 : 3 * feats] = dot(lhs, wb_scr[...]).reshape(count, span, 3 * feats)
        for r in range(count):
            total = sums[slot, r, 0:low_span, 0:128]
            total = total + pltpu.roll(sums[slot, r, 1 : low_span + 1, 0:128], feats, 1)
            total = total + sums[slot, r, 2 : low_span + 2, 128:256]
            mask = keep_low
            if h + r == 0:
                mask = mask & jnp.logical_not(at_top)
            if h + r == height + 1:
                mask = mask & jnp.logical_not(at_bottom)
            lowfeat[h + r] = jnp.where(mask, jnp.where(total >= 0, total, 0.01 * total), 0.0)
            low_taps[h + r, :, 0:128] = jnp.where(
                left_half, lowfeat[h + r, 0:cols], pltpu.roll(lowfeat[h + r, 1 : cols + 1], feats, 1)
            ).astype(BF16)
            low_taps[h + r, :, 128:256] = jnp.where(
                left_half, lowfeat[h + r, 2 : cols + 2], 0.0
            ).astype(BF16)

    def expand(h):
        lhs = jnp.concatenate(
            [low_taps[h + a : h + a + part].reshape(part * cols, 256) for a in range(3)], axis=1
        )
        total = dot(lhs, wu_scr[...])
        for pair in range(part // 2):
            turned = total[2 * cols * pair : 2 * cols * (pair + 1)].T.astype(BF16)
            lhs = [
                jnp.concatenate(
                    [turned[(2 * a + b) * feats : (2 * a + b + 1) * feats] for b in range(2)], axis=1
                )
                for a in range(2)
            ]
            final = dot(jnp.concatenate(lhs, axis=0), spread)
            for r in range(2):
                for a in range(2):
                    row = 2 * (h + 2 * pair + r) + a
                    out_scr[pl.ds(row, feats, stride=2 * height), :] = final[
                        a * feats : (a + 1) * feats, 128 * r : 128 * (r + 1)
                    ]

    fill_taps(0, part + 2)
    narrowed = expanded = done = 0
    while expanded < height:
        expand_to, narrow_to = min(narrowed - 2, height), min(done - 2, height + 2)
        if done < height + 4:
            if done + part < height + 4:
                fill_taps(done + part + 2, done + 2 * part + 2)
            group(done)
            done += part
        while narrowed < narrow_to:
            count = min(part, height + 2 - narrowed)
            if narrowed + count > narrow_to:
                break
            narrow(narrowed, count)
            narrowed += count
        while expanded + part <= expand_to:
            expand(expanded)
            expanded += part
    out_ref[...] = out_scr[...].reshape(feats, 2 * height, 128).astype(BF16)


def convs(*args):
    height, cols, chans = args[0].shape
    span = cols + 2 * STRIP
    feats = args[-2].shape[2]
    return call(
        conv_kernel,
        jax.ShapeDtypeStruct((feats, 2 * height, 2 * cols), BF16),
        [
            pltpu.VMEM((height + 4, span + STRIP, chans), F32),
            pltpu.VMEM((height + 6, span + STRIP, chans), F32),
            pltpu.VMEM((height + 6, span, 768), BF16),
            pltpu.VMEM((height + 4, span, 256), BF16),
            pltpu.VMEM((2, 4, span, 256), F32),
            pltpu.VMEM((height + 2, cols + 8, 128), F32),
            pltpu.VMEM((height + 2, cols, 256), BF16),
            pltpu.VMEM((feats * 2 * height, 128), F32),
            pltpu.VMEM((9 * 256, chans), BF16),
            pltpu.VMEM((3 * 256, 3 * feats), BF16),
            pltpu.VMEM((3 * 256, 4 * feats), BF16),
        ],
        8_000_000_000,
        4_000_000,
    )(*args)


def swapped(axis, first, second):
    count = lax.axis_size(axis)
    out = []
    for start, payload in ((0, first), (1, second)):
        pairs = [(i, i + 1) for i in range(start, count - 1, 2)]
        pairs = pairs + [(b, a) for a, b in pairs]
        out.append(lax.ppermute(payload, axis, pairs))
    return out


def on_device(
    features,
    gain_one,
    qkv_weight,
    bias_table,
    proj_weight,
    gain_two,
    hidden_weight,
    output_weight,
    group_conv,
    before_conv,
    upsample_conv,
):
    height, cols, chans = features.shape
    even_row = lax.axis_index("rows") % 2 == 0
    low, high = features[:RIM], features[height - RIM :]
    row_one, row_two = swapped(
        "rows", jnp.where(even_row, high, low), jnp.where(even_row, low, high)
    )
    col_one, col_two = swapped("cols", *pack(features, row_one, row_two))

    bias = build_bias(bias_table)
    gain_one, gain_two = gain_one.reshape(1, chans), gain_two.reshape(1, chans)
    post = (gain_two, hidden_weight, output_weight.T)
    nrm, wk, wqv, wp, inner_k, inner_v, inner_border, inner_mid = inner_block(
        features,
        row_one,
        row_two,
        gain_one,
        qkv_weight,
        proj_weight,
        bias,
        *post,
    )
    back_one, back_two, edge, side, keys, values = outer_block(
        features,
        nrm,
        col_one,
        col_two,
        gain_one,
        wk,
        wqv,
        wp,
        inner_k,
        inner_v,
        inner_border,
        bias,
        *post,
    )
    back_one, back_two = swapped("rows", back_one, back_two)
    mid = middle_block(features, nrm, keys, values, wqv, wp, inner_mid, bias, *post)
    return convs(
        features,
        row_one,
        row_two,
        col_one,
        col_two,
        back_one,
        back_two,
        edge,
        side,
        mid,
        group_conv,
        before_conv.transpose(0, 1, 3, 2),
        upsample_conv,
    )


def solution(mesh):
    placed = (P("rows", "cols", None), P(), P(), P(), P(), P(), P(), P(), P(), P(), P())
    return jax.shard_map(
        on_device, mesh=mesh, in_specs=placed, out_specs=P(None, "rows", "cols"), check_vma=False
    )
```

```python
import functools

import jax
import jax.numpy as jnp
import numpy as np
from jax import lax
from jax.experimental import pallas as pl
from jax.experimental.pallas import tpu as pltpu
from jax.sharding import PartitionSpec as P

HEADS = 6
HD = 30
HP = 32
WIN = 16
KWIN = 24
KEYS = KWIN * KWIN
SIDE = WIN + KWIN - 1
RIM = (KWIN - WIN) // 2
EDGE = WIN + 2 * RIM
STRIP = 8
LOG2E = 1.4426950408889634
F32 = jnp.float32
BF16 = jnp.bfloat16
NT = (((1,), (1,)), ((), ()))
TN = (((0,), (0,)), ((), ()))


def dot(a, b):
    return jnp.dot(a, b, preferred_element_type=F32)


def dot_nt(a, b):
    return lax.dot_general(a, b, NT, preferred_element_type=F32)


def layer_norm(values, gain):
    center = values - jnp.mean(values, axis=-1, keepdims=True)
    spread = jnp.mean(center * center, axis=-1, keepdims=True)
    return center * lax.rsqrt(spread + 1e-05) * gain


def call(kernel, out_shape, scratch, flops, bytes_accessed):
    return pl.pallas_call(
        kernel,
        out_shape=out_shape,
        scratch_shapes=scratch,
        compiler_params=pltpu.CompilerParams(vmem_limit_bytes=24 * 2**20),
        cost_estimate=pl.CostEstimate(
            flops=flops, bytes_accessed=bytes_accessed, transcendentals=0
        ),
    )


def bias_kernel(table_ref, out_ref, t_scr, e_scr, w_scr, x_scr):
    for d in range(SIDE):
        t_scr[8 * d : 8 * d + HEADS, 0:SIDE] = jnp.exp(table_ref[:, SIDE * d : SIDE * (d + 1)])

    def head(h, carry):
        values = t_scr[pl.ds(h, SIDE, stride=8), 0:SIDE].astype(BF16)

        def expand(cols, first):
            width = -(-SIDE * cols // 128) * 128
            spot = lax.broadcasted_iota(jnp.int32, (SIDE, width), 1) // cols
            row = lax.broadcasted_iota(jnp.int32, (SIDE, width), 0)
            pick = (spot == SIDE - 1 - row).astype(F32).astype(BF16)
            e_scr[0:SIDE, 0:width] = lax.dot_general(values, pick, TN, preferred_element_type=F32)
            lane = lax.broadcasted_iota(jnp.int32, (KWIN, width), 1) % cols
            out = jnp.zeros((KWIN, width), F32)
            for jj in range(cols):
                start = WIN - 1 - first - jj
                out = jnp.where(lane == jj, e_scr[start : start + KWIN, 0:width], out)
            w_scr[:, 0:width] = out

        lanes = lax.broadcasted_iota(jnp.int32, (KWIN, 128), 1)
        expand(WIN, 0)
        for p in range(KWIN):
            rows = slice(p * KWIN, (p + 1) * KWIN)
            low = w_scr[:, (23 - p) * WIN : (23 - p) * WIN + 128]
            high = w_scr[:, (31 - p) * WIN : (31 - p) * WIN + 128]
            x_scr[0, rows] = jnp.where(lanes < 64, low, high)
            x_scr[1, rows] = w_scr[:, (27 - p) * WIN : (27 - p) * WIN + 128]
        out_ref[1, h] = x_scr[0].astype(BF16)
        out_ref[3, h] = x_scr[1].astype(BF16)
        for kind, first in ((0, WIN - STRIP), (2, 0)):
            expand(STRIP, first)
            for p in range(KWIN):
                rows = slice(p * KWIN, (p + 1) * KWIN)
                x_scr[0, rows] = w_scr[:, (23 - p) * STRIP : (23 - p) * STRIP + 128]
            out_ref[kind, h] = x_scr[0].astype(BF16)
        return carry

    lax.fori_loop(0, HEADS, head, 0)


def build_bias(bias_table):
    return call(
        bias_kernel,
        jax.ShapeDtypeStruct((4, HEADS, KEYS, 128), BF16),
        [
            pltpu.VMEM((8 * SIDE, 128), F32),
            pltpu.VMEM((SIDE + 1, 640), F32),
            pltpu.VMEM((KWIN, 640), F32),
            pltpu.VMEM((2, KEYS, 128), F32),
        ],
        4_000_000_000,
        4_000_000,
    )(bias_table.T)


def one_hot(shape, row_of, col_of):
    row = lax.broadcasted_iota(jnp.int32, shape, 0)
    col = lax.broadcasted_iota(jnp.int32, shape, 1)
    return (row_of(row) == col_of(col)).astype(F32).astype(BF16)


def spread_head(place):
    return jnp.where(place % HP < HD, place // HP * HD + place % HP, -1)


def weights_into(qkv_ref, proj_ref, wk_ref, wqv_ref, wp_ref):
    chans = qkv_ref.shape[0]
    width = HEADS * HP
    qkv = qkv_ref[...]
    pick = one_hot(
        (3 * chans, 3 * 128),
        lambda row: row,
        lambda col: jnp.where(
            (col % 128 < 2 * HP) & (col % HP < HD),
            chans + (col // 128 * 2 + col % 128 // HP) * HD + col % HP,
            -1,
        ),
    )
    wk_ref[...] = dot(qkv, pick).astype(BF16)
    pick = one_hot(
        (2 * width, 3 * chans),
        lambda row: jnp.where(
            row % HP < HD, row // HP * HD + row % HP + jnp.where(row < width, 0, chans), -1
        ),
        lambda col: col,
    )
    wqv_ref[...] = dot_nt(pick, qkv).astype(BF16)
    pick = one_hot((width, chans), spread_head, lambda col: col)
    wp_ref[...] = dot(pick, proj_ref[...]).astype(BF16)


def set_queries(q_scr, wqv_ref, groups):
    scale = LOG2E / np.sqrt(HD)
    rows = jnp.concatenate([rows.reshape(128, rows.shape[2]) for rows in groups], axis=0)
    queries = (dot_nt(wqv_ref[0 : HEADS * HP], rows.astype(BF16)) * scale).astype(BF16)
    none = jnp.zeros((HP, 128), BF16)
    for g in range(len(groups)):
        lanes = slice(128 * g, 128 * g + 128)
        for t in range(HEADS // 2):
            one = queries[2 * t * HP : (2 * t + 1) * HP, lanes]
            two = queries[(2 * t + 1) * HP : (2 * t + 2) * HP, lanes]
            q_scr[g, t, 0:HP] = jnp.concatenate([one, none], axis=1)
            q_scr[g, t, HP : 2 * HP] = jnp.concatenate([none, two], axis=1)


def lookup(g, values):
    out = values[0]
    for index in range(1, len(values)):
        out = jnp.where(g >= index, values[index], out)
    return out


def attention(kinds, windows, q_scr, k_ref, v_ref, bias_ref, wp_ref, s_scr, m_scr, p_scr, o_scr):
    groups = len(kinds)
    pairs = HEADS // 2
    step = 192

    def keep(g, t, k0, top):
        keys = k_ref[lookup(g, windows), k0 : k0 + step, 128 * t : 128 * t + 2 * HP]
        one = dot(keys, q_scr[g, t])
        s_scr[t, k0 : k0 + step] = one
        part = jnp.max(one.reshape(step // 8, 8, 256), axis=0)
        return part if top is None else jnp.maximum(top, part)

    def sum_values(g, t):
        o_scr[g, t] = dot(v_ref[lookup(g, windows), 2 * t * HP : 2 * (t + 1) * HP], p_scr[t])

    top = None
    for k0 in range(0, KEYS, step):
        top = keep(0, 0, k0, top)
    m_scr[...] = top
    p_scr[pairs - 1] = jnp.zeros((KEYS, 256), BF16)

    def attend(g, carry):
        kind = lookup(g, kinds)
        top = m_scr[...]
        for t in range(pairs):
            top = jnp.max(top, axis=0, keepdims=True)
            if t == 0:
                sum_values(jnp.maximum(g - 1, 0), pairs - 1)
            else:
                sum_values(g, t - 1)
            following = g if t + 1 < pairs else jnp.minimum(g + 1, groups - 1)
            later = None
            for k0 in range(0, KEYS, step):
                prob = jnp.exp2(s_scr[t, k0 : k0 + step] - top).astype(BF16)
                for half in range(2):
                    lanes = slice(128 * half, 128 * half + 128)
                    p_scr[t, k0 : k0 + step, lanes] = (
                        prob[:, lanes] * bias_ref[kind, 2 * t + half, k0 : k0 + step]
                    )
                later = keep(following, (t + 1) % pairs, k0, later)
            top = later
        m_scr[...] = top
        return carry

    lax.fori_loop(0, groups, attend, 0)
    sum_values(groups - 1, pairs - 1)
    attended = []
    for g in range(groups):
        parts = []
        for t in range(pairs):
            for half in range(2):
                lanes = slice(128 * half, 128 * half + 128)
                one = o_scr[g, t, half * HP : (half + 1) * HP, lanes]
                parts.append((one * (1.0 / one[HD : HD + 1])).astype(BF16))
        attended.append(jnp.concatenate(parts, axis=0))
    attended = jnp.concatenate(attended, axis=1)
    return lax.dot_general(attended, wp_ref[...], TN, preferred_element_type=F32)


def feed_forward(first, gain, hidden_ref, output_ref):
    normed = layer_norm(first, gain).astype(BF16)
    inner = dot(normed, hidden_ref[...])
    inner = (0.5 * inner * (1.0 + lax.erf(inner * np.float32(np.sqrt(0.5))))).astype(BF16)
    return first + dot_nt(inner, output_ref[...])


def feed_groups(first, gain, hidden_ref, output_ref):
    groups = range(first.shape[0] // 128)
    return [feed_forward(first[128 * g : 128 * (g + 1)], gain, hidden_ref, output_ref) for g in groups]


def project(keys, wk_ref, wqv_ref, k_ref, v_ref, index):
    width = HEADS * HP
    one_row = (lax.broadcasted_iota(jnp.int32, (width, 1), 0) % HP == HD).astype(F32)
    keys = keys.reshape(KEYS, keys.shape[2]).astype(BF16)
    k_ref[index] = dot(keys, wk_ref[...]).astype(BF16)
    v_ref[index] = (dot_nt(wqv_ref[width : 2 * width], keys) + one_row).astype(BF16)


def at_edges():
    row, column = lax.axis_index("rows"), lax.axis_index("cols")
    return (
        column == 0,
        column == lax.axis_size("cols") - 1,
        row == 0,
        row == lax.axis_size("rows") - 1,
        row % 2 == 0,
        column % 2 == 0,
    )


def from_sides(even, first, second):
    first, second = first.astype(F32), second.astype(F32)
    return jnp.where(even, second, first), jnp.where(even, first, second)


def border_rows(ref, c0):
    return jnp.concatenate([ref[0:4, c0 : c0 + WIN], ref[12:16, c0 : c0 + WIN]], axis=0)


def halves(wide, count):
    left = lax.broadcasted_iota(jnp.int32, (1, 128), 1) < 64
    rest = wide.shape[0] - count
    out = jnp.where(left, wide[0:rest], pltpu.roll(wide[count:], 64, 1))
    return out if rest == count else jnp.concatenate([out, wide[rest:count]], axis=0)


def unhalve(packed, rows):
    count = packed.shape[0]
    return jnp.concatenate([packed, pltpu.roll(packed[0 : rows - count], 64, 1)], axis=0)


def pack_kernel(own_ref, row_one_ref, row_two_ref, pay_one_ref, pay_two_ref, x_scr, flat):
    height, cols, chans = own_ref.shape
    even_row, even_col = at_edges()[4:]
    above, below = from_sides(even_row, row_one_ref[...], row_two_ref[...])
    x_scr[0:RIM] = above
    x_scr[RIM : RIM + height] = own_ref[...].astype(F32)
    x_scr[RIM + height :] = below
    for side, near, far in ((0, 0, WIN), (1, cols - WIN, cols - WIN - RIM)):
        for r in range(height + 2 * RIM):
            flat[side, WIN * r : WIN * (r + 1), 0:chans] = x_scr[r, near : near + WIN]
            place = WIN * (height + 2 * RIM) + RIM * r
            flat[side, place : place + RIM, 0:chans] = x_scr[r, far : far + RIM]
    count = flat.shape[1]
    for lanes in (slice(0, 128), slice(128, 256)):
        low, high = flat[0, :, lanes], flat[1, :, lanes]
        one, two = jnp.where(even_col, high, low), jnp.where(even_col, low, high)
        rows = slice(0, count)
        if lanes.start:
            one, two = halves(one, count // 2), halves(two, count // 2)
            rows = slice(count, count + count // 2)
        pay_one_ref[rows] = one.astype(BF16)
        pay_two_ref[rows] = two.astype(BF16)


def pack(own, row_one, row_two):
    height, cols, chans = own.shape
    pixels = (height + 2 * RIM) * (WIN + RIM)
    pay = jax.ShapeDtypeStruct((pixels * 3 // 2, 128), BF16)
    return call(
        pack_kernel,
        (pay, pay),
        [
            pltpu.VMEM((height + 2 * RIM, cols, chans), F32),
            pltpu.VMEM((2, pixels, 256), F32),
        ],
        1_000_000,
        1_000_000,
    )(own, row_one, row_two)


def inner_kernel(
    own_ref,
    row_one_ref,
    row_two_ref,
    gain_one_ref,
    qkv_ref,
    proj_ref,
    bias_ref,
    gain_two_ref,
    hidden_ref,
    output_ref,
    nrm_ref,
    wk_ref,
    wqv_ref,
    wp_ref,
    k_ref,
    v_ref,
    border_ref,
    mid_ref,
    q_scr,
    s_scr,
    m_scr,
    p_scr,
    o_scr,
):
    height, cols, chans = own_ref.shape
    inner = cols // WIN - 2
    flags = at_edges()
    weights_into(qkv_ref, proj_ref, wk_ref, wqv_ref, wp_ref)
    gain_one = gain_one_ref[...]
    for r in range(RIM):
        above, below = from_sides(flags[4], row_one_ref[r], row_two_ref[r])
        nrm_ref[r] = layer_norm(above, gain_one)
        nrm_ref[RIM + height + r] = layer_norm(below, gain_one)
    for r in range(height):
        nrm_ref[RIM + r] = layer_norm(own_ref[r].astype(F32), gain_one)
    kinds, windows, first, queries = [], [], [], []
    for w in range(inner):
        c0 = WIN * (w + 1)
        project(nrm_ref[:, c0 - RIM : c0 - RIM + KWIN], wk_ref, wqv_ref, k_ref, v_ref, w)
        first.append(border_rows(own_ref, c0).reshape(128, chans))
        queries.append(border_rows(nrm_ref.at[RIM : RIM + height], c0))
        kinds.append(1)
        windows.append(w)
    for w in range(inner - 1):
        c0 = WIN * (w + 1)
        first.append(own_ref[4:12, c0 : c0 + WIN].reshape(128, chans))
        queries.append(nrm_ref[RIM + 4 : RIM + 12, c0 : c0 + WIN])
        kinds.append(3)
        windows.append(w)
    groups = len(kinds)
    set_queries(q_scr, wqv_ref, queries)
    first = jnp.concatenate(first, axis=0).astype(F32) + attention(
        kinds, windows, q_scr, k_ref, v_ref, bias_ref, wp_ref, s_scr, m_scr, p_scr, o_scr
    )
    mixed = feed_groups(first, gain_two_ref[...], hidden_ref, output_ref)
    for g in range(groups):
        one = mixed[g].reshape(8, WIN, chans)
        if g < inner:
            border_ref[:, WIN * g : WIN * (g + 1)] = one
        else:
            mid_ref[:, WIN * (g - inner) : WIN * (g - inner + 1)] = one


def outer_kernel(
    own_ref,
    nrm_ref,
    col_two_ref,
    col_one_ref,
    gain_one_ref,
    wk_ref,
    wqv_ref,
    wp_ref,
    inner_k_ref,
    inner_v_ref,
    inner_border_ref,
    bias_ref,
    gain_two_ref,
    hidden_ref,
    output_ref,
    pay_one_ref,
    pay_two_ref,
    edge_ref,
    side_ref,
    strip_ref,
    k_ref,
    v_ref,
    side_scr,
    x_scr,
    n_scr,
    b_scr,
    q_scr,
    s_scr,
    m_scr,
    p_scr,
    o_scr,
    image,
):
    height, cols, chans = own_ref.shape
    inner = cols // WIN - 2
    flags = at_edges()
    gain_one = gain_one_ref[...]
    rows = height + 2 * RIM
    pixels = rows * (WIN + RIM)
    both = from_sides(flags[5], col_one_ref[...], col_two_ref[...])
    for side in range(2):
        x_scr[side, :, 0:128] = both[side][0:pixels]
        x_scr[side, :, 128:256] = unhalve(both[side][pixels:], pixels)
        n_scr[...] = layer_norm(x_scr[side, :, 0:chans], gain_one)
        near, far = (EDGE - WIN, EDGE - WIN - RIM) if side == 0 else (EDGE, EDGE + WIN)
        for r in range(rows):
            side_scr[side, r, near : near + WIN] = n_scr[WIN * r : WIN * (r + 1)]
            place = WIN * rows + RIM * r
            side_scr[side, r, far : far + RIM] = n_scr[place : place + RIM]
        c0 = WIN - STRIP if side == 0 else 0
        x = x_scr[side, 0 : WIN * rows, 0:chans].reshape(rows, WIN, chans)
        strip_ref[side] = x[:, c0 : c0 + STRIP]
    side_scr[0, :, EDGE : 2 * EDGE] = nrm_ref[:, 0:EDGE]
    side_scr[1, :, 0:EDGE] = nrm_ref[:, cols - EDGE : cols]
    k_ref[2] = inner_k_ref[inner - 1]
    v_ref[2] = inner_v_ref[inner - 1]
    for index, side, c0 in ((0, 0, RIM), (1, 0, RIM + WIN), (3, 1, RIM), (4, 1, RIM + WIN)):
        project(side_scr[side, :, c0 : c0 + KWIN], wk_ref, wqv_ref, k_ref, v_ref, index)
    spots = (EDGE - STRIP, 0, cols - WIN, EDGE)
    first, queries = [], []
    for g in range(4):
        side, c0 = g // 2, spots[g]
        if g in (0, 3):
            x = strip_ref[side, RIM : RIM + height]
            queries.append(side_scr[side, RIM : RIM + height, c0 : c0 + STRIP])
        else:
            x = border_rows(own_ref, c0).astype(F32)
            queries.append(border_rows(nrm_ref.at[RIM : RIM + height], c0))
        first.append(x.reshape(128, chans))
    set_queries(q_scr, wqv_ref, queries)
    first = jnp.concatenate(first, axis=0) + attention(
        [0, 1, 1, 2], [0, 1, 3, 4], q_scr, k_ref, v_ref, bias_ref, wp_ref, s_scr, m_scr, p_scr, o_scr
    )
    image[0:4, STRIP + WIN : STRIP + cols - WIN] = inner_border_ref[0:4]
    image[12:16, STRIP + WIN : STRIP + cols - WIN] = inner_border_ref[4:8]
    mixed = feed_groups(first, gain_two_ref[...], hidden_ref, output_ref)
    for g in range(4):
        if g in (0, 3):
            one = jnp.where(flags[g // 3], 0.0, mixed[g]).reshape(height, STRIP, chans)
            c0 = 0 if g == 0 else STRIP + cols
            image[:, c0 : c0 + STRIP] = one
        else:
            one = mixed[g].reshape(8, WIN, chans)
            c0 = STRIP + spots[g]
            image[0:4, c0 : c0 + WIN] = one[0:4]
            image[12:16, c0 : c0 + WIN] = one[4:8]
    even = flags[4]
    count = 3 * image.shape[1]
    for pay_ref, rows in (
        (pay_one_ref, jnp.where(even, image[13:16], image[0:3])),
        (pay_two_ref, jnp.where(even, image[0:3], image[13:16])),
    ):
        b_scr[:, 0:chans] = rows.reshape(count, chans)
        pay_ref[0:count] = b_scr[:, 0:128].astype(BF16)
        pay_ref[count:] = halves(b_scr[:, 128:256], 128).astype(BF16)
    edge_ref[0:4] = image[0:4]
    edge_ref[4:8] = image[12:16]
    side_ref[:, 0:STRIP] = image[4:12, 0:STRIP]
    side_ref[:, STRIP : 2 * STRIP] = image[4:12, STRIP + cols :]


def middle_kernel(
    own_ref,
    nrm_ref,
    k_ref,
    v_ref,
    wqv_ref,
    wp_ref,
    inner_mid_ref,
    bias_ref,
    gain_two_ref,
    hidden_ref,
    output_ref,
    mid_ref,
    q_scr,
    s_scr,
    m_scr,
    p_scr,
    o_scr,
):
    height, cols, chans = own_ref.shape
    spots = (0, cols - 2 * WIN, cols - WIN)
    set_queries(q_scr, wqv_ref, [nrm_ref[RIM + 4 : RIM + 12, c0 : c0 + WIN] for c0 in spots])
    first = [own_ref[4:12, c0 : c0 + WIN].reshape(128, chans) for c0 in spots]
    first = jnp.concatenate(first, axis=0).astype(F32) + attention(
        [3, 3, 3], [1, 2, 3], q_scr, k_ref, v_ref, bias_ref, wp_ref, s_scr, m_scr, p_scr, o_scr
    )
    mixed = feed_groups(first, gain_two_ref[...], hidden_ref, output_ref)
    mid_ref[:, WIN : cols - 2 * WIN] = inner_mid_ref[...]
    for g in range(3):
        mid_ref[:, spots[g] : spots[g] + WIN] = mixed[g].reshape(8, WIN, chans)


def attention_scratch(groups):
    return [
        pltpu.VMEM((groups, HEADS // 2, 2 * HP, 256), BF16),
        pltpu.VMEM((HEADS // 2, KEYS, 256), F32),
        pltpu.VMEM((8, 256), F32),
        pltpu.VMEM((HEADS // 2, KEYS, 256), BF16),
        pltpu.VMEM((groups, HEADS // 2, 2 * HP, 256), F32),
    ]


def inner_block(*args):
    height, cols, chans = args[0].shape
    inner = cols // WIN - 2
    width = HEADS * HP
    groups = 2 * inner - 1
    return call(
        inner_kernel,
        (
            jax.ShapeDtypeStruct((height + 2 * RIM, cols, chans), F32),
            jax.ShapeDtypeStruct((chans, 3 * 128), BF16),
            jax.ShapeDtypeStruct((2 * width, chans), BF16),
            jax.ShapeDtypeStruct((width, chans), BF16),
            jax.ShapeDtypeStruct((inner, KEYS, 3 * 128), BF16),
            jax.ShapeDtypeStruct((inner, width, KEYS), BF16),
            jax.ShapeDtypeStruct((8, WIN * inner, chans), F32),
            jax.ShapeDtypeStruct((8, WIN * (inner - 1), chans), F32),
        ),
        attention_scratch(groups),
        5_000_000_000,
        4_000_000,
    )(*args)


def outer_block(*args):
    height, cols, chans = args[0].shape
    span = cols + 2 * STRIP
    return call(
        outer_kernel,
        (
            jax.ShapeDtypeStruct((3 * span + 128, 128), BF16),
            jax.ShapeDtypeStruct((3 * span + 128, 128), BF16),
            jax.ShapeDtypeStruct((8, span, chans), F32),
            jax.ShapeDtypeStruct((8, 2 * STRIP, chans), F32),
            jax.ShapeDtypeStruct((2, height + 2 * RIM, STRIP, chans), F32),
            jax.ShapeDtypeStruct((5, KEYS, 3 * 128), BF16),
            jax.ShapeDtypeStruct((5, HEADS * HP, KEYS), BF16),
        ),
        [
            pltpu.VMEM((2, height + 2 * RIM, 2 * EDGE, chans), F32),
            pltpu.VMEM((2, (height + 2 * RIM) * (WIN + RIM), 256), F32),
            pltpu.VMEM(((height + 2 * RIM) * (WIN + RIM), chans), F32),
            pltpu.VMEM((3 * span, 256), F32),
            *attention_scratch(4),
            pltpu.VMEM((height, span, chans), F32),
        ],
        5_000_000_000,
        4_000_000,
    )(*args)


def middle_block(*args):
    height, cols, chans = args[0].shape
    return call(
        middle_kernel,
        jax.ShapeDtypeStruct((8, cols, chans), F32),
        attention_scratch(3),
        5_000_000_000,
        4_000_000,
    )(*args)


def conv_kernel(
    own_ref,
    row_one_ref,
    row_two_ref,
    strip_ref,
    back_one_ref,
    back_two_ref,
    edge_ref,
    side_ref,
    mid_ref,
    group_ref,
    before_ref,
    upsample_ref,
    out_ref,
    base,
    image,
    taps,
    grouped,
    sums,
    lowfeat,
    low_taps,
    out_scr,
    wg_scr,
    wb_scr,
    wu_scr,
):
    height, cols, chans = own_ref.shape
    span = cols + 2 * STRIP
    at_left, at_right, at_top, at_bottom, even_row, _ = at_edges()

    feats = before_ref.shape[2]
    pad = chans // 16 * 16
    for a in range(3):
        wb_scr[256 * a + pad : 256 * (a + 1)] = jnp.zeros((256 - pad, 3 * feats), BF16)
        wu_scr[256 * a + 3 * feats : 256 * (a + 1)] = jnp.zeros((256 - 3 * feats, 4 * feats), BF16)
        for b in range(3):
            wg_scr[256 * (3 * a + b) + pad : 256 * (3 * a + b + 1)] = jnp.zeros((256 - pad, chans), BF16)
            wg_scr[256 * (3 * a + b) : 256 * (3 * a + b) + chans] = group_ref[a, b]
    same = one_hot((chans, chans), lambda row: row, lambda col: col)
    order = one_hot(
        (4 * feats, 4 * feats), lambda row: row, lambda col: col % feats * 4 + col // feats
    )
    for a in range(3):
        part = before_ref[a].reshape(3 * feats, chans)
        wb_scr[256 * a : 256 * a + chans] = dot_nt(same, part).astype(BF16)
        part = upsample_ref[a].reshape(3 * feats, 4 * feats)
        wu_scr[256 * a : 256 * a + 3 * feats] = dot(part, order).astype(BF16)

    above, below = from_sides(even_row, row_one_ref[...], row_two_ref[...])
    base[0:2, STRIP : STRIP + cols] = above[2:4]
    base[2 : 2 + height, STRIP : STRIP + cols] = own_ref[...].astype(F32)
    base[2 + height : 4 + height, STRIP : STRIP + cols] = below[0:2]
    rows = slice(2, height + 6)
    base[:, 0:STRIP] = strip_ref[0, rows]
    base[:, STRIP + cols : span] = strip_ref[1, rows]
    base[:, span:] = jnp.zeros((height + 4, STRIP, chans), F32)
    image[:, span:] = jnp.zeros((height + 6, STRIP, chans), F32)
    above, below = from_sides(even_row, back_one_ref[...], back_two_ref[...])
    for rows, packed in ((slice(0, 3), above), (slice(19, 22), below)):
        image[rows, 0:span, 0:128] = packed[0 : 3 * span].reshape(3, span, 128)
        rest = unhalve(packed[3 * span :], 3 * span).reshape(3, span, 128)
        image[rows, 0:span, 128:chans] = rest[:, :, 0 : chans - 128]
    image[3:7, 0:span] = edge_ref[0:4]
    image[7:15, 0:STRIP] = side_ref[:, 0:STRIP]
    image[7:15, STRIP : STRIP + cols] = mid_ref[...]
    image[7:15, STRIP + cols : span] = side_ref[:, STRIP : 2 * STRIP]
    image[15:19, 0:span] = edge_ref[4:8]
    taps[...] = jnp.zeros(taps.shape, BF16)
    grouped[...] = jnp.zeros(grouped.shape, BF16)
    part = 4
    col = lax.broadcasted_iota(jnp.int32, (span, chans), 0) - 2
    keep_grouped = (col < cols + 2) & ((col >= 0) | jnp.logical_not(at_left))
    keep_grouped = keep_grouped & ((col < cols) | jnp.logical_not(at_right))
    low_span = cols + 8
    col = lax.broadcasted_iota(jnp.int32, (low_span, 128), 0) - 1
    keep_low = (col <= cols) & ((col >= 0) | jnp.logical_not(at_left))
    keep_low = keep_low & ((col < cols) | jnp.logical_not(at_right))
    left_half = lax.broadcasted_iota(jnp.int32, (cols, 128), 1) < feats
    spot = lax.broadcasted_iota(jnp.int32, (256, 256), 0)
    place = lax.broadcasted_iota(jnp.int32, (256, 256), 1)
    spread = (spot % 128 // cols == place // 128) & (
        spot % cols * 2 + spot // 128 == place % 128
    )
    spread = spread.astype(F32).astype(BF16)

    def fill_taps(first, last):
        for b in range(3):
            start = STRIP - 3 + b
            taps[first:last, :, 256 * b : 256 * b + chans] = image[
                first:last, start : start + span, :
            ].astype(BF16)

    def group(h):
        lhs = jnp.concatenate(
            [taps[h + a : h + a + part].reshape(part * span, 768) for a in range(3)], axis=1
        )
        total = dot(lhs, wg_scr[...]).reshape(part, span, chans)
        total = total + base[h : h + part, STRIP - 2 : STRIP - 2 + span, :]
        for r in range(part):
            mask = keep_grouped
            if h + r < 2:
                mask = mask & jnp.logical_not(at_top)
            if h + r >= height + 2:
                mask = mask & jnp.logical_not(at_bottom)
            grouped[h + r, 0:span, 0:chans] = jnp.where(mask, total[r], 0.0).astype(BF16)

    def narrow(h, count):
        lhs = jnp.concatenate(
            [grouped[h + a : h + a + count].reshape(count * span, 256) for a in range(3)], axis=1
        )
        slot = h // part % 2
        sums[slot, 0:count, :, 0 : 3 * feats] = dot(lhs, wb_scr[...]).reshape(count, span, 3 * feats)
        for r in range(count):
            total = sums[slot, r, 0:low_span, 0:128]
            total = total + pltpu.roll(sums[slot, r, 1 : low_span + 1, 0:128], feats, 1)
            total = total + sums[slot, r, 2 : low_span + 2, 128:256]
            mask = keep_low
            if h + r == 0:
                mask = mask & jnp.logical_not(at_top)
            if h + r == height + 1:
                mask = mask & jnp.logical_not(at_bottom)
            lowfeat[h + r] = jnp.where(mask, jnp.where(total >= 0, total, 0.01 * total), 0.0)
            low_taps[h + r, :, 0:128] = jnp.where(
                left_half, lowfeat[h + r, 0:cols], pltpu.roll(lowfeat[h + r, 1 : cols + 1], feats, 1)
            ).astype(BF16)
            low_taps[h + r, :, 128:256] = jnp.where(
                left_half, lowfeat[h + r, 2 : cols + 2], 0.0
            ).astype(BF16)

    def expand(h):
        lhs = jnp.concatenate(
            [low_taps[h + a : h + a + part].reshape(part * cols, 256) for a in range(3)], axis=1
        )
        total = dot(lhs, wu_scr[...])
        for pair in range(part // 2):
            turned = total[2 * cols * pair : 2 * cols * (pair + 1)].T.astype(BF16)
            lhs = [
                jnp.concatenate(
                    [turned[(2 * a + b) * feats : (2 * a + b + 1) * feats] for b in range(2)], axis=1
                )
                for a in range(2)
            ]
            final = dot(jnp.concatenate(lhs, axis=0), spread)
            for r in range(2):
                for a in range(2):
                    row = 2 * (h + 2 * pair + r) + a
                    out_scr[pl.ds(row, feats, stride=2 * height), :] = final[
                        a * feats : (a + 1) * feats, 128 * r : 128 * (r + 1)
                    ]

    fill_taps(0, part + 2)
    narrowed = expanded = done = 0
    while expanded < height:
        expand_to, narrow_to = min(narrowed - 2, height), min(done - 2, height + 2)
        if done < height + 4:
            if done + part < height + 4:
                fill_taps(done + part + 2, done + 2 * part + 2)
            group(done)
            done += part
        while narrowed < narrow_to:
            count = min(part, height + 2 - narrowed)
            if narrowed + count > narrow_to:
                break
            narrow(narrowed, count)
            narrowed += count
        while expanded + part <= expand_to:
            expand(expanded)
            expanded += part
    out_ref[...] = out_scr[...].reshape(feats, 2 * height, 128).astype(BF16)


def convs(*args):
    height, cols, chans = args[0].shape
    span = cols + 2 * STRIP
    feats = args[-2].shape[2]
    return call(
        conv_kernel,
        jax.ShapeDtypeStruct((feats, 2 * height, 2 * cols), BF16),
        [
            pltpu.VMEM((height + 4, span + STRIP, chans), F32),
            pltpu.VMEM((height + 6, span + STRIP, chans), F32),
            pltpu.VMEM((height + 6, span, 768), BF16),
            pltpu.VMEM((height + 4, span, 256), BF16),
            pltpu.VMEM((2, 4, span, 256), F32),
            pltpu.VMEM((height + 2, cols + 8, 128), F32),
            pltpu.VMEM((height + 2, cols, 256), BF16),
            pltpu.VMEM((feats * 2 * height, 128), F32),
            pltpu.VMEM((9 * 256, chans), BF16),
            pltpu.VMEM((3 * 256, 3 * feats), BF16),
            pltpu.VMEM((3 * 256, 4 * feats), BF16),
        ],
        8_000_000_000,
        4_000_000,
    )(*args)


def swapped(axis, first, second):
    count = lax.axis_size(axis)
    out = []
    for start, payload in ((1, second), (0, first)):
        pairs = [(i, i + 1) for i in range(start, count - 1, 2)]
        pairs = pairs + [(b, a) for a, b in pairs]
        out.append(lax.ppermute(payload, axis, pairs))
    return out[::-1]


def on_device(
    features,
    gain_one,
    qkv_weight,
    bias_table,
    proj_weight,
    gain_two,
    hidden_weight,
    output_weight,
    group_conv,
    before_conv,
    upsample_conv,
):
    height, cols, chans = features.shape
    even_row = lax.axis_index("rows") % 2 == 0
    low, high = features[:RIM], features[height - RIM :]
    row_one, row_two = swapped(
        "rows", jnp.where(even_row, high, low), jnp.where(even_row, low, high)
    )
    col_one, col_two = swapped("cols", *pack(features, row_one, row_two))

    bias = build_bias(bias_table)
    gain_one, gain_two = gain_one.reshape(1, chans), gain_two.reshape(1, chans)
    post = (gain_two, hidden_weight, output_weight.T)
    nrm, wk, wqv, wp, inner_k, inner_v, inner_border, inner_mid = inner_block(
        features,
        row_one,
        row_two,
        gain_one,
        qkv_weight,
        proj_weight,
        bias,
        *post,
    )
    back_one, back_two, edge, side, strips, keys, values = outer_block(
        features,
        nrm,
        col_two,
        col_one,
        gain_one,
        wk,
        wqv,
        wp,
        inner_k,
        inner_v,
        inner_border,
        bias,
        *post,
    )
    back_one, back_two = swapped("rows", back_one, back_two)
    mid = middle_block(features, nrm, keys, values, wqv, wp, inner_mid, bias, *post)
    return convs(
        features,
        row_one,
        row_two,
        strips,
        back_one,
        back_two,
        edge,
        side,
        mid,
        group_conv,
        before_conv.transpose(0, 1, 3, 2),
        upsample_conv,
    )


def solution(mesh):
    placed = (P("rows", "cols", None), P(), P(), P(), P(), P(), P(), P(), P(), P(), P())
    return jax.shard_map(
        on_device, mesh=mesh, in_specs=placed, out_specs=P(None, "rows", "cols"), check_vma=False
    )
```

```python
import functools

import jax
import jax.numpy as jnp
import numpy as np
from jax import lax
from jax.experimental import pallas as pl
from jax.experimental.pallas import tpu as pltpu
from jax.sharding import PartitionSpec as P

HEADS = 6
HD = 30
HP = 32
WIN = 16
KWIN = 24
KEYS = KWIN * KWIN
SIDE = WIN + KWIN - 1
RIM = (KWIN - WIN) // 2
EDGE = WIN + 2 * RIM
STRIP = 8
LOG2E = 1.4426950408889634
F32 = jnp.float32
BF16 = jnp.bfloat16
NT = (((1,), (1,)), ((), ()))
TN = (((0,), (0,)), ((), ()))


def dot(a, b):
    return jnp.dot(a, b, preferred_element_type=F32)


def dot_nt(a, b):
    return lax.dot_general(a, b, NT, preferred_element_type=F32)


def layer_norm(values, gain):
    center = values - jnp.mean(values, axis=-1, keepdims=True)
    spread = jnp.mean(center * center, axis=-1, keepdims=True)
    return center * lax.rsqrt(spread + 1e-05) * gain


def call(kernel, out_shape, scratch, flops, bytes_accessed, in_specs=None):
    more = {} if in_specs is None else {"in_specs": in_specs}
    return pl.pallas_call(
        kernel,
        out_shape=out_shape,
        **more,
        scratch_shapes=scratch,
        compiler_params=pltpu.CompilerParams(vmem_limit_bytes=24 * 2**20),
        cost_estimate=pl.CostEstimate(
            flops=flops, bytes_accessed=bytes_accessed, transcendentals=0
        ),
    )


def bias_kernel(table_ref, out_ref, t_scr, e_scr, w_scr, x_scr):
    for d in range(SIDE):
        t_scr[8 * d : 8 * d + HEADS, 0:SIDE] = jnp.exp(table_ref[:, SIDE * d : SIDE * (d + 1)])

    def head(h, carry):
        values = t_scr[pl.ds(h, SIDE, stride=8), 0:SIDE].astype(BF16)

        def expand(cols, first):
            width = -(-SIDE * cols // 128) * 128
            spot = lax.broadcasted_iota(jnp.int32, (SIDE, width), 1) // cols
            row = lax.broadcasted_iota(jnp.int32, (SIDE, width), 0)
            pick = (spot == SIDE - 1 - row).astype(F32).astype(BF16)
            e_scr[0:SIDE, 0:width] = lax.dot_general(values, pick, TN, preferred_element_type=F32)
            lane = lax.broadcasted_iota(jnp.int32, (KWIN, width), 1) % cols
            out = jnp.zeros((KWIN, width), F32)
            for jj in range(cols):
                start = WIN - 1 - first - jj
                out = jnp.where(lane == jj, e_scr[start : start + KWIN, 0:width], out)
            w_scr[:, 0:width] = out

        lanes = lax.broadcasted_iota(jnp.int32, (KWIN, 128), 1)
        expand(WIN, 0)
        whole = w_scr[...]
        for phase in range(8):
            turned = whole if phase == 0 else pltpu.roll(whole, 640 - WIN * phase, 1)
            for p in range(KWIN):
                rows = slice(p * KWIN, (p + 1) * KWIN)
                if (23 - p) % 8 == phase:
                    at = (23 - p) // 8 * 128
                    low, high = turned[:, at : at + 128], turned[:, at + 128 : at + 256]
                    x_scr[0, rows] = jnp.where(lanes < 64, low, high)
                if (27 - p) % 8 == phase:
                    at = (27 - p) // 8 * 128
                    x_scr[1, rows] = turned[:, at : at + 128]
        out_ref[1, h] = x_scr[0].astype(BF16)
        out_ref[3, h] = x_scr[1].astype(BF16)
        for kind, first in ((0, WIN - STRIP), (2, 0)):
            expand(STRIP, first)
            for p in range(KWIN):
                rows = slice(p * KWIN, (p + 1) * KWIN)
                x_scr[0, rows] = w_scr[:, (23 - p) * STRIP : (23 - p) * STRIP + 128]
            out_ref[kind, h] = x_scr[0].astype(BF16)
        return carry

    lax.fori_loop(0, HEADS, head, 0)


def build_bias(bias_table):
    return call(
        bias_kernel,
        jax.ShapeDtypeStruct((4, HEADS, KEYS, 128), BF16),
        [
            pltpu.VMEM((8 * SIDE, 128), F32),
            pltpu.VMEM((SIDE + 1, 640), F32),
            pltpu.VMEM((KWIN, 640), F32),
            pltpu.VMEM((2, KEYS, 128), F32),
        ],
        4_000_000_000,
        4_000_000,
    )(bias_table.T)


def one_hot(shape, row_of, col_of):
    row = lax.broadcasted_iota(jnp.int32, shape, 0)
    col = lax.broadcasted_iota(jnp.int32, shape, 1)
    return (row_of(row) == col_of(col)).astype(F32).astype(BF16)


def spread_head(place):
    return jnp.where(place % HP < HD, place // HP * HD + place % HP, -1)


def weights_into(qkv_ref, proj_ref, wk_ref, wqv_ref, wp_ref):
    chans = qkv_ref.shape[0]
    width = HEADS * HP
    qkv = qkv_ref[...]
    pick = one_hot(
        (3 * chans, 3 * 128),
        lambda row: row,
        lambda col: jnp.where(
            (col % 128 < 2 * HP) & (col % HP < HD),
            chans + (col // 128 * 2 + col % 128 // HP) * HD + col % HP,
            -1,
        ),
    )
    wk_ref[...] = dot(qkv, pick).astype(BF16)
    pick = one_hot(
        (2 * width, 3 * chans),
        lambda row: jnp.where(
            row % HP < HD, row // HP * HD + row % HP + jnp.where(row < width, 0, chans), -1
        ),
        lambda col: col,
    )
    wqv_ref[...] = dot_nt(pick, qkv).astype(BF16)
    pick = one_hot((width, chans), spread_head, lambda col: col)
    wp_ref[...] = dot(pick, proj_ref[...]).astype(BF16)


def set_queries(q_scr, wqv_ref, groups):
    scale = LOG2E / np.sqrt(HD)
    rows = jnp.concatenate([rows.reshape(128, rows.shape[2]) for rows in groups], axis=0)
    queries = (dot_nt(wqv_ref[0 : HEADS * HP], rows.astype(BF16)) * scale).astype(BF16)
    none = jnp.zeros((HP, 128), BF16)
    for g in range(len(groups)):
        lanes = slice(128 * g, 128 * g + 128)
        for t in range(HEADS // 2):
            one = queries[2 * t * HP : (2 * t + 1) * HP, lanes]
            two = queries[(2 * t + 1) * HP : (2 * t + 2) * HP, lanes]
            q_scr[g, t, 0:HP] = jnp.concatenate([one, none], axis=1)
            q_scr[g, t, HP : 2 * HP] = jnp.concatenate([none, two], axis=1)


def attention(groups, q_scr, k_ref, v_ref, bias_ref, wp_ref, s_scr, p_scr, o_scr, finish):
    pairs = HEADS // 2
    step = 192
    stages = [(g, t) for g in range(len(groups)) for t in range(pairs)]

    def keep(n, k0, top):
        g, t = stages[n]
        keys = k_ref[groups[g][1], k0 : k0 + step, 128 * t : 128 * t + 2 * HP]
        one = dot(keys, q_scr[g, t])
        s_scr[n % 2, k0 : k0 + step] = one
        part = jnp.max(one.reshape(step // 8, 8, 256), axis=0)
        return part if top is None else jnp.maximum(top, part)

    def sum_values(n):
        g, t = stages[n]
        o_scr[n % 6] = dot(v_ref[groups[g][1], 2 * t * HP : 2 * (t + 1) * HP], p_scr[n % 2])

    def project_group(g):
        parts = []
        for t in range(pairs):
            for half in range(2):
                lanes = slice(128 * half, 128 * half + 128)
                one = o_scr[(pairs * g + t) % 6, half * HP : (half + 1) * HP, lanes]
                parts.append((one * (1.0 / one[HD : HD + 1])).astype(BF16))
        attended = jnp.concatenate(parts, axis=0)
        finish(g, lax.dot_general(attended, wp_ref[...], TN, preferred_element_type=F32))

    top = None
    for k0 in range(0, KEYS, step):
        top = keep(0, k0, top)
    for n, (g, t) in enumerate(stages):
        top = jnp.max(top, axis=0, keepdims=True)
        if n > 0:
            sum_values(n - 1)
        later = None
        for k0 in range(0, KEYS, step):
            prob = jnp.exp2(s_scr[n % 2, k0 : k0 + step] - top).astype(BF16)
            for half in range(2):
                lanes = slice(128 * half, 128 * half + 128)
                p_scr[n % 2, k0 : k0 + step, lanes] = (
                    prob[:, lanes] * bias_ref[groups[g][0], 2 * t + half, k0 : k0 + step]
                )
            if n + 1 < len(stages):
                later = keep(n + 1, k0, later)
        top = later
        if t == 0 and g > 0:
            project_group(g - 1)
    sum_values(len(stages) - 1)
    project_group(len(groups) - 1)


def feed_forward(first, gain, hidden_ref, output_ref):
    normed = layer_norm(first, gain).astype(BF16)
    inner = dot(normed, hidden_ref[...])
    inner = (0.5 * inner * (1.0 + lax.erf(inner * np.float32(np.sqrt(0.5))))).astype(BF16)
    return first + dot_nt(inner, output_ref[...])


def project(keys, wk_ref, wqv_ref, k_ref, v_ref, index):
    width = HEADS * HP
    one_row = (lax.broadcasted_iota(jnp.int32, (width, 1), 0) % HP == HD).astype(F32)
    keys = keys.reshape(KEYS, keys.shape[2]).astype(BF16)
    k_ref[index] = dot(keys, wk_ref[...]).astype(BF16)
    v_ref[index] = (dot_nt(wqv_ref[width : 2 * width], keys) + one_row).astype(BF16)


def at_edges():
    row, column = lax.axis_index("rows"), lax.axis_index("cols")
    return (
        column == 0,
        column == lax.axis_size("cols") - 1,
        row == 0,
        row == lax.axis_size("rows") - 1,
        row % 2 == 0,
        column % 2 == 0,
    )


def from_sides(even, first, second):
    first, second = first.astype(F32), second.astype(F32)
    return jnp.where(even, second, first), jnp.where(even, first, second)


def border_rows(ref, c0):
    return jnp.concatenate([ref[0:4, c0 : c0 + WIN], ref[12:16, c0 : c0 + WIN]], axis=0)


def halves(wide, count):
    left = lax.broadcasted_iota(jnp.int32, (1, 128), 1) < 64
    rest = wide.shape[0] - count
    out = jnp.where(left, wide[0:rest], pltpu.roll(wide[count:], 64, 1))
    return out if rest == count else jnp.concatenate([out, wide[rest:count]], axis=0)


def unhalve(packed, rows):
    count = packed.shape[0]
    return jnp.concatenate([packed, pltpu.roll(packed[0 : rows - count], 64, 1)], axis=0)


def split_kernel(own_ref, pay_one_ref, pay_two_ref, sem):
    even_row = at_edges()[4]
    high = own_ref.shape[0] - RIM
    one, two = jnp.where(even_row, high, 0), jnp.where(even_row, 0, high)
    copies = [
        pltpu.make_async_copy(own_ref.at[pl.ds(start, RIM)], pay_ref, sem.at[index])
        for index, (start, pay_ref) in enumerate(((two, pay_two_ref), (one, pay_one_ref)))
    ]
    for copy in copies:
        copy.start()
    for copy in copies:
        copy.wait()


def split(own):
    height, cols, chans = own.shape
    pay = jax.ShapeDtypeStruct((RIM, cols, chans), BF16)
    return call(
        split_kernel, (pay, pay), [pltpu.SemaphoreType.DMA((2,))], 1000, 1000, [pl.BlockSpec(memory_space=pl.ANY)]
    )(own)


def pack_kernel(own_ref, row_two_ref, row_one_ref, pay_one_ref, pay_two_ref, x_scr, flat):
    height, cols, chans = own_ref.shape
    even_row, even_col = at_edges()[4:]
    above, below = from_sides(even_row, row_one_ref[...], row_two_ref[...])
    x_scr[0:RIM] = above
    x_scr[RIM : RIM + height] = own_ref[...].astype(F32)
    x_scr[RIM + height :] = below
    for side, near, far in ((0, 0, WIN), (1, cols - WIN, cols - WIN - RIM)):
        for r in range(height + 2 * RIM):
            flat[side, WIN * r : WIN * (r + 1), 0:chans] = x_scr[r, near : near + WIN]
            place = WIN * (height + 2 * RIM) + RIM * r
            flat[side, place : place + RIM, 0:chans] = x_scr[r, far : far + RIM]
    count = flat.shape[1]
    for lanes in (slice(0, 128), slice(128, 256)):
        low, high = flat[0, :, lanes], flat[1, :, lanes]
        one, two = jnp.where(even_col, high, low), jnp.where(even_col, low, high)
        rows = slice(0, count)
        if lanes.start:
            one, two = halves(one, count // 2), halves(two, count // 2)
            rows = slice(count, count + count // 2)
        pay_one_ref[rows] = one.astype(BF16)
        pay_two_ref[rows] = two.astype(BF16)


def pack(own, row_one, row_two):
    height, cols, chans = own.shape
    pixels = (height + 2 * RIM) * (WIN + RIM)
    pay = jax.ShapeDtypeStruct((pixels * 3 // 2, 128), BF16)
    return call(
        pack_kernel,
        (pay, pay),
        [
            pltpu.VMEM((height + 2 * RIM, cols, chans), F32),
            pltpu.VMEM((2, pixels, 256), F32),
        ],
        1_000_000,
        1_000_000,
    )(own, row_two, row_one)


def inner_kernel(
    own_ref,
    row_two_ref,
    row_one_ref,
    gain_one_ref,
    qkv_ref,
    proj_ref,
    bias_ref,
    gain_two_ref,
    hidden_ref,
    output_ref,
    nrm_ref,
    wk_ref,
    wqv_ref,
    wp_ref,
    k_ref,
    v_ref,
    border_ref,
    mid_ref,
    q_scr,
    s_scr,
    p_scr,
    o_scr,
):
    height, cols, chans = own_ref.shape
    inner = cols // WIN - 2
    flags = at_edges()
    weights_into(qkv_ref, proj_ref, wk_ref, wqv_ref, wp_ref)
    gain_one = gain_one_ref[...]
    for r in range(RIM):
        above, below = from_sides(flags[4], row_one_ref[r], row_two_ref[r])
        nrm_ref[r] = layer_norm(above, gain_one)
        nrm_ref[RIM + height + r] = layer_norm(below, gain_one)
    for r in range(height):
        nrm_ref[RIM + r] = layer_norm(own_ref[r].astype(F32), gain_one)
    groups, first, queries = [], [], []
    for w in range(inner):
        c0 = WIN * (w + 1)
        project(nrm_ref[:, c0 - RIM : c0 - RIM + KWIN], wk_ref, wqv_ref, k_ref, v_ref, w)
        first.append(border_rows(own_ref, c0))
        queries.append(border_rows(nrm_ref.at[RIM : RIM + height], c0))
        groups.append((1, w))
    for w in range(inner - 1):
        c0 = WIN * (w + 1)
        first.append(own_ref[4:12, c0 : c0 + WIN])
        queries.append(nrm_ref[RIM + 4 : RIM + 12, c0 : c0 + WIN])
        groups.append((3, w))
    set_queries(q_scr, wqv_ref, queries)

    def finish(g, attended):
        one = first[g].astype(F32).reshape(128, chans) + attended
        one = feed_forward(one, gain_two_ref[...], hidden_ref, output_ref).reshape(8, WIN, chans)
        if g < inner:
            border_ref[:, WIN * g : WIN * (g + 1)] = one
        else:
            mid_ref[:, WIN * (g - inner) : WIN * (g - inner + 1)] = one

    attention(groups, q_scr, k_ref, v_ref, bias_ref, wp_ref, s_scr, p_scr, o_scr, finish)


def outer_kernel(
    own_ref,
    nrm_ref,
    col_two_ref,
    col_one_ref,
    gain_one_ref,
    wk_ref,
    wqv_ref,
    wp_ref,
    inner_k_ref,
    inner_v_ref,
    inner_border_ref,
    bias_ref,
    gain_two_ref,
    hidden_ref,
    output_ref,
    pay_one_ref,
    pay_two_ref,
    edge_ref,
    side_ref,
    strip_ref,
    k_ref,
    v_ref,
    side_scr,
    x_scr,
    n_scr,
    b_scr,
    q_scr,
    s_scr,
    p_scr,
    o_scr,
    image,
):
    height, cols, chans = own_ref.shape
    inner = cols // WIN - 2
    flags = at_edges()
    gain_one = gain_one_ref[...]
    rows = height + 2 * RIM
    pixels = rows * (WIN + RIM)
    both = from_sides(flags[5], col_one_ref[...], col_two_ref[...])
    for side in range(2):
        x_scr[side, :, 0:128] = both[side][0:pixels]
        x_scr[side, :, 128:256] = unhalve(both[side][pixels:], pixels)
        n_scr[...] = layer_norm(x_scr[side, :, 0:chans], gain_one)
        near, far = (EDGE - WIN, EDGE - WIN - RIM) if side == 0 else (EDGE, EDGE + WIN)
        for r in range(rows):
            side_scr[side, r, near : near + WIN] = n_scr[WIN * r : WIN * (r + 1)]
            place = WIN * rows + RIM * r
            side_scr[side, r, far : far + RIM] = n_scr[place : place + RIM]
        c0 = WIN - STRIP if side == 0 else 0
        x = x_scr[side, 0 : WIN * rows, 0:chans].reshape(rows, WIN, chans)
        strip_ref[side] = x[:, c0 : c0 + STRIP]
    side_scr[0, :, EDGE : 2 * EDGE] = nrm_ref[:, 0:EDGE]
    side_scr[1, :, 0:EDGE] = nrm_ref[:, cols - EDGE : cols]
    k_ref[2] = inner_k_ref[inner - 1]
    v_ref[2] = inner_v_ref[inner - 1]
    for index, side, c0 in ((0, 0, RIM), (1, 0, RIM + WIN), (3, 1, RIM), (4, 1, RIM + WIN)):
        project(side_scr[side, :, c0 : c0 + KWIN], wk_ref, wqv_ref, k_ref, v_ref, index)
    spots = (EDGE - STRIP, 0, cols - WIN, EDGE)
    first, queries = [], []
    for g in range(4):
        side, c0 = g // 2, spots[g]
        if g in (0, 3):
            x = strip_ref[side, RIM : RIM + height]
            queries.append(side_scr[side, RIM : RIM + height, c0 : c0 + STRIP])
        else:
            x = border_rows(own_ref, c0).astype(F32)
            queries.append(border_rows(nrm_ref.at[RIM : RIM + height], c0))
        first.append(x.reshape(128, chans))
    set_queries(q_scr, wqv_ref, queries)
    image[0:4, STRIP + WIN : STRIP + cols - WIN] = inner_border_ref[0:4]
    image[12:16, STRIP + WIN : STRIP + cols - WIN] = inner_border_ref[4:8]

    def finish(g, attended):
        one = feed_forward(first[g] + attended, gain_two_ref[...], hidden_ref, output_ref)
        if g in (0, 3):
            one = jnp.where(flags[g // 3], 0.0, one).reshape(height, STRIP, chans)
            c0 = 0 if g == 0 else STRIP + cols
            image[:, c0 : c0 + STRIP] = one
        else:
            one = one.reshape(8, WIN, chans)
            c0 = STRIP + spots[g]
            image[0:4, c0 : c0 + WIN] = one[0:4]
            image[12:16, c0 : c0 + WIN] = one[4:8]

    groups = [(0, 0), (1, 1), (1, 3), (2, 4)]
    attention(groups, q_scr, k_ref, v_ref, bias_ref, wp_ref, s_scr, p_scr, o_scr, finish)
    even = flags[4]
    count = 3 * image.shape[1]
    for pay_ref, rows in (
        (pay_one_ref, jnp.where(even, image[13:16], image[0:3])),
        (pay_two_ref, jnp.where(even, image[0:3], image[13:16])),
    ):
        b_scr[:, 0:chans] = rows.reshape(count, chans)
        pay_ref[0:count] = b_scr[:, 0:128].astype(BF16)
        pay_ref[count:] = halves(b_scr[:, 128:256], 128).astype(BF16)
    edge_ref[0:4] = image[0:4]
    edge_ref[4:8] = image[12:16]
    side_ref[:, 0:STRIP] = image[4:12, 0:STRIP]
    side_ref[:, STRIP : 2 * STRIP] = image[4:12, STRIP + cols :]


def middle_kernel(
    own_ref,
    nrm_ref,
    k_ref,
    v_ref,
    wqv_ref,
    wp_ref,
    inner_mid_ref,
    bias_ref,
    gain_two_ref,
    hidden_ref,
    output_ref,
    mid_ref,
    q_scr,
    s_scr,
    p_scr,
    o_scr,
):
    height, cols, chans = own_ref.shape
    spots = (0, cols - 2 * WIN, cols - WIN)
    set_queries(q_scr, wqv_ref, [nrm_ref[RIM + 4 : RIM + 12, c0 : c0 + WIN] for c0 in spots])
    mid_ref[:, WIN : cols - 2 * WIN] = inner_mid_ref[...]

    def finish(g, attended):
        c0 = spots[g]
        one = own_ref[4:12, c0 : c0 + WIN].astype(F32).reshape(128, chans) + attended
        one = feed_forward(one, gain_two_ref[...], hidden_ref, output_ref)
        mid_ref[:, c0 : c0 + WIN] = one.reshape(8, WIN, chans)

    groups = [(3, 1), (3, 2), (3, 3)]
    attention(groups, q_scr, k_ref, v_ref, bias_ref, wp_ref, s_scr, p_scr, o_scr, finish)


def attention_scratch(groups):
    return [
        pltpu.VMEM((groups, HEADS // 2, 2 * HP, 256), BF16),
        pltpu.VMEM((2, KEYS, 256), F32),
        pltpu.VMEM((2, KEYS, 256), BF16),
        pltpu.VMEM((6, 2 * HP, 256), F32),
    ]


def inner_block(*args):
    height, cols, chans = args[0].shape
    inner = cols // WIN - 2
    width = HEADS * HP
    groups = 2 * inner - 1
    return call(
        inner_kernel,
        (
            jax.ShapeDtypeStruct((height + 2 * RIM, cols, chans), F32),
            jax.ShapeDtypeStruct((chans, 3 * 128), BF16),
            jax.ShapeDtypeStruct((2 * width, chans), BF16),
            jax.ShapeDtypeStruct((width, chans), BF16),
            jax.ShapeDtypeStruct((inner, KEYS, 3 * 128), BF16),
            jax.ShapeDtypeStruct((inner, width, KEYS), BF16),
            jax.ShapeDtypeStruct((8, WIN * inner, chans), F32),
            jax.ShapeDtypeStruct((8, WIN * (inner - 1), chans), F32),
        ),
        attention_scratch(groups),
        5_000_000_000,
        4_000_000,
    )(*args)


def outer_block(*args):
    height, cols, chans = args[0].shape
    span = cols + 2 * STRIP
    return call(
        outer_kernel,
        (
            jax.ShapeDtypeStruct((3 * span + 128, 128), BF16),
            jax.ShapeDtypeStruct((3 * span + 128, 128), BF16),
            jax.ShapeDtypeStruct((8, span, chans), F32),
            jax.ShapeDtypeStruct((8, 2 * STRIP, chans), F32),
            jax.ShapeDtypeStruct((2, height + 2 * RIM, STRIP, chans), F32),
            jax.ShapeDtypeStruct((5, KEYS, 3 * 128), BF16),
            jax.ShapeDtypeStruct((5, HEADS * HP, KEYS), BF16),
        ),
        [
            pltpu.VMEM((2, height + 2 * RIM, 2 * EDGE, chans), F32),
            pltpu.VMEM((2, (height + 2 * RIM) * (WIN + RIM), 256), F32),
            pltpu.VMEM(((height + 2 * RIM) * (WIN + RIM), chans), F32),
            pltpu.VMEM((3 * span, 256), F32),
            *attention_scratch(4),
            pltpu.VMEM((height, span, chans), F32),
        ],
        5_000_000_000,
        4_000_000,
    )(*args)


def middle_block(*args):
    height, cols, chans = args[0].shape
    return call(
        middle_kernel,
        jax.ShapeDtypeStruct((8, cols, chans), F32),
        attention_scratch(3),
        5_000_000_000,
        4_000_000,
    )(*args)


def conv_kernel(
    own_ref,
    row_two_ref,
    row_one_ref,
    strip_ref,
    back_two_ref,
    back_one_ref,
    edge_ref,
    side_ref,
    mid_ref,
    group_ref,
    before_ref,
    upsample_ref,
    out_ref,
    base,
    image,
    taps,
    grouped,
    sums,
    lowfeat,
    low_taps,
    out_scr,
    wg_scr,
    wb_scr,
    wu_scr,
):
    height, cols, chans = own_ref.shape
    span = cols + 2 * STRIP
    at_left, at_right, at_top, at_bottom, even_row, _ = at_edges()

    feats = before_ref.shape[2]
    pad = chans // 16 * 16
    for a in range(3):
        wb_scr[256 * a + pad : 256 * (a + 1)] = jnp.zeros((256 - pad, 3 * feats), BF16)
        wu_scr[256 * a + 3 * feats : 256 * (a + 1)] = jnp.zeros((256 - 3 * feats, 4 * feats), BF16)
        for b in range(3):
            wg_scr[256 * (3 * a + b) + pad : 256 * (3 * a + b + 1)] = jnp.zeros((256 - pad, chans), BF16)
            wg_scr[256 * (3 * a + b) : 256 * (3 * a + b) + chans] = group_ref[a, b]
    same = one_hot((chans, chans), lambda row: row, lambda col: col)
    order = one_hot(
        (4 * feats, 4 * feats), lambda row: row, lambda col: col % feats * 4 + col // feats
    )
    for a in range(3):
        part = before_ref[a].reshape(3 * feats, chans)
        wb_scr[256 * a : 256 * a + chans] = dot_nt(same, part).astype(BF16)
        part = upsample_ref[a].reshape(3 * feats, 4 * feats)
        wu_scr[256 * a : 256 * a + 3 * feats] = dot(part, order).astype(BF16)

    above, below = from_sides(even_row, row_one_ref[...], row_two_ref[...])
    base[0:2, STRIP : STRIP + cols] = above[2:4]
    base[2 : 2 + height, STRIP : STRIP + cols] = own_ref[...].astype(F32)
    base[2 + height : 4 + height, STRIP : STRIP + cols] = below[0:2]
    rows = slice(2, height + 6)
    base[:, 0:STRIP] = strip_ref[0, rows]
    base[:, STRIP + cols : span] = strip_ref[1, rows]
    base[:, span:] = jnp.zeros((height + 4, STRIP, chans), F32)
    image[:, span:] = jnp.zeros((height + 6, STRIP, chans), F32)
    above, below = from_sides(even_row, back_one_ref[...], back_two_ref[...])
    for rows, packed in ((slice(0, 3), above), (slice(19, 22), below)):
        image[rows, 0:span, 0:128] = packed[0 : 3 * span].reshape(3, span, 128)
        rest = unhalve(packed[3 * span :], 3 * span).reshape(3, span, 128)
        image[rows, 0:span, 128:chans] = rest[:, :, 0 : chans - 128]
    image[3:7, 0:span] = edge_ref[0:4]
    image[7:15, 0:STRIP] = side_ref[:, 0:STRIP]
    image[7:15, STRIP : STRIP + cols] = mid_ref[...]
    image[7:15, STRIP + cols : span] = side_ref[:, STRIP : 2 * STRIP]
    image[15:19, 0:span] = edge_ref[4:8]
    taps[...] = jnp.zeros(taps.shape, BF16)
    grouped[...] = jnp.zeros(grouped.shape, BF16)
    part = 4
    col = lax.broadcasted_iota(jnp.int32, (span, chans), 0) - 2
    keep_grouped = (col < cols + 2) & ((col >= 0) | jnp.logical_not(at_left))
    keep_grouped = keep_grouped & ((col < cols) | jnp.logical_not(at_right))
    low_span = cols + 8
    col = lax.broadcasted_iota(jnp.int32, (low_span, 128), 0) - 1
    keep_low = (col <= cols) & ((col >= 0) | jnp.logical_not(at_left))
    keep_low = keep_low & ((col < cols) | jnp.logical_not(at_right))
    left_half = lax.broadcasted_iota(jnp.int32, (cols, 128), 1) < feats
    spot = lax.broadcasted_iota(jnp.int32, (256, 256), 0)
    place = lax.broadcasted_iota(jnp.int32, (256, 256), 1)
    spread = (spot % 128 // cols == place // 128) & (
        spot % cols * 2 + spot // 128 == place % 128
    )
    spread = spread.astype(F32).astype(BF16)

    def fill_taps(first, last):
        for b in range(3):
            start = STRIP - 3 + b
            taps[first:last, :, 256 * b : 256 * b + chans] = image[
                first:last, start : start + span, :
            ].astype(BF16)

    def group(h):
        lhs = jnp.concatenate(
            [taps[h + a : h + a + part].reshape(part * span, 768) for a in range(3)], axis=1
        )
        total = dot(lhs, wg_scr[...]).reshape(part, span, chans)
        total = total + base[h : h + part, STRIP - 2 : STRIP - 2 + span, :]
        for r in range(part):
            mask = keep_grouped
            if h + r < 2:
                mask = mask & jnp.logical_not(at_top)
            if h + r >= height + 2:
                mask = mask & jnp.logical_not(at_bottom)
            grouped[h + r, 0:span, 0:chans] = jnp.where(mask, total[r], 0.0).astype(BF16)

    def narrow(h, count):
        lhs = jnp.concatenate(
            [grouped[h + a : h + a + count].reshape(count * span, 256) for a in range(3)], axis=1
        )
        slot = h // part % 2
        sums[slot, 0:count, :, 0 : 3 * feats] = dot(lhs, wb_scr[...]).reshape(count, span, 3 * feats)
        for r in range(count):
            total = sums[slot, r, 0:low_span, 0:128]
            total = total + pltpu.roll(sums[slot, r, 1 : low_span + 1, 0:128], feats, 1)
            total = total + sums[slot, r, 2 : low_span + 2, 128:256]
            mask = keep_low
            if h + r == 0:
                mask = mask & jnp.logical_not(at_top)
            if h + r == height + 1:
                mask = mask & jnp.logical_not(at_bottom)
            lowfeat[h + r] = jnp.where(mask, jnp.where(total >= 0, total, 0.01 * total), 0.0)
            low_taps[h + r, :, 0:128] = jnp.where(
                left_half, lowfeat[h + r, 0:cols], pltpu.roll(lowfeat[h + r, 1 : cols + 1], feats, 1)
            ).astype(BF16)
            low_taps[h + r, :, 128:256] = jnp.where(
                left_half, lowfeat[h + r, 2 : cols + 2], 0.0
            ).astype(BF16)

    def expand(h):
        lhs = jnp.concatenate(
            [low_taps[h + a : h + a + part].reshape(part * cols, 256) for a in range(3)], axis=1
        )
        total = dot(lhs, wu_scr[...])
        for pair in range(part // 2):
            turned = total[2 * cols * pair : 2 * cols * (pair + 1)].T.astype(BF16)
            lhs = [
                jnp.concatenate(
                    [turned[(2 * a + b) * feats : (2 * a + b + 1) * feats] for b in range(2)], axis=1
                )
                for a in range(2)
            ]
            final = dot(jnp.concatenate(lhs, axis=0), spread)
            for r in range(2):
                for a in range(2):
                    row = 2 * (h + 2 * pair + r) + a
                    out_scr[pl.ds(row, feats, stride=2 * height), :] = final[
                        a * feats : (a + 1) * feats, 128 * r : 128 * (r + 1)
                    ]

    fill_taps(0, part + 2)
    narrowed = expanded = done = 0
    while expanded < height:
        expand_to, narrow_to = min(narrowed - 2, height), min(done - 2, height + 2)
        if done < height + 4:
            if done + part < height + 4:
                fill_taps(done + part + 2, done + 2 * part + 2)
            group(done)
            done += part
        while narrowed < narrow_to:
            count = min(part, height + 2 - narrowed)
            if narrowed + count > narrow_to:
                break
            narrow(narrowed, count)
            narrowed += count
        while expanded + part <= expand_to:
            expand(expanded)
            expanded += part
    out_ref[...] = out_scr[...].reshape(feats, 2 * height, 128).astype(BF16)


def convs(*args):
    height, cols, chans = args[0].shape
    span = cols + 2 * STRIP
    feats = args[-2].shape[2]
    return call(
        conv_kernel,
        jax.ShapeDtypeStruct((feats, 2 * height, 2 * cols), BF16),
        [
            pltpu.VMEM((height + 4, span + STRIP, chans), F32),
            pltpu.VMEM((height + 6, span + STRIP, chans), F32),
            pltpu.VMEM((height + 6, span, 768), BF16),
            pltpu.VMEM((height + 4, span, 256), BF16),
            pltpu.VMEM((2, 4, span, 256), F32),
            pltpu.VMEM((height + 2, cols + 8, 128), F32),
            pltpu.VMEM((height + 2, cols, 256), BF16),
            pltpu.VMEM((feats * 2 * height, 128), F32),
            pltpu.VMEM((9 * 256, chans), BF16),
            pltpu.VMEM((3 * 256, 3 * feats), BF16),
            pltpu.VMEM((3 * 256, 4 * feats), BF16),
        ],
        8_000_000_000,
        4_000_000,
    )(*args)


def swapped(axis, first, second):
    count = lax.axis_size(axis)
    out = []
    for start, payload in ((1, second), (0, first)):
        pairs = [(i, i + 1) for i in range(start, count - 1, 2)]
        pairs = pairs + [(b, a) for a, b in pairs]
        out.append(lax.ppermute(payload, axis, pairs))
    return out[::-1]


def on_device(
    features,
    gain_one,
    qkv_weight,
    bias_table,
    proj_weight,
    gain_two,
    hidden_weight,
    output_weight,
    group_conv,
    before_conv,
    upsample_conv,
):
    chans = features.shape[2]
    row_one, row_two = swapped("rows", *split(features))
    col_one, col_two = swapped("cols", *pack(features, row_one, row_two))

    bias = build_bias(bias_table)
    gain_one, gain_two = gain_one.reshape(1, chans), gain_two.reshape(1, chans)
    post = (gain_two, hidden_weight, output_weight.T)
    nrm, wk, wqv, wp, inner_k, inner_v, inner_border, inner_mid = inner_block(
        features,
        row_two,
        row_one,
        gain_one,
        qkv_weight,
        proj_weight,
        bias,
        *post,
    )
    back_one, back_two, edge, side, strips, keys, values = outer_block(
        features,
        nrm,
        col_two,
        col_one,
        gain_one,
        wk,
        wqv,
        wp,
        inner_k,
        inner_v,
        inner_border,
        bias,
        *post,
    )
    back_one, back_two = swapped("rows", back_one, back_two)
    mid = middle_block(features, nrm, keys, values, wqv, wp, inner_mid, bias, *post)
    return convs(
        features,
        row_two,
        row_one,
        strips,
        back_two,
        back_one,
        edge,
        side,
        mid,
        group_conv,
        before_conv.transpose(0, 1, 3, 2),
        upsample_conv,
    )


def solution(mesh):
    placed = (P("rows", "cols", None), P(), P(), P(), P(), P(), P(), P(), P(), P(), P())
    return jax.shard_map(
        on_device, mesh=mesh, in_specs=placed, out_specs=P(None, "rows", "cols"), check_vma=False
    )
```

```python
import functools

import jax
import jax.numpy as jnp
import numpy as np
from jax import lax
from jax.experimental import pallas as pl
from jax.experimental.pallas import tpu as pltpu
from jax.sharding import PartitionSpec as P

HEADS = 6
HD = 30
HP = 32
WIN = 16
KWIN = 24
KEYS = KWIN * KWIN
SIDE = WIN + KWIN - 1
RIM = (KWIN - WIN) // 2
EDGE = WIN + 2 * RIM
STRIP = 8
LOG2E = 1.4426950408889634
F32 = jnp.float32
BF16 = jnp.bfloat16
NT = (((1,), (1,)), ((), ()))
TN = (((0,), (0,)), ((), ()))


def dot(a, b):
    return jnp.dot(a, b, preferred_element_type=F32)


def dot_nt(a, b):
    return lax.dot_general(a, b, NT, preferred_element_type=F32)


def layer_norm(values, gain):
    center = values - jnp.mean(values, axis=-1, keepdims=True)
    spread = jnp.mean(center * center, axis=-1, keepdims=True)
    return center * lax.rsqrt(spread + 1e-05) * gain


def call(kernel, out_shape, scratch, flops, bytes_accessed):
    return pl.pallas_call(
        kernel,
        out_shape=out_shape,
        scratch_shapes=scratch,
        compiler_params=pltpu.CompilerParams(vmem_limit_bytes=24 * 2**20),
        cost_estimate=pl.CostEstimate(
            flops=flops, bytes_accessed=bytes_accessed, transcendentals=0
        ),
    )


def bias_kernel(table_ref, out_ref, t_scr, e_scr, w_scr, x_scr):
    for d in range(SIDE):
        t_scr[8 * d : 8 * d + HEADS, 0:SIDE] = jnp.exp(table_ref[:, SIDE * d : SIDE * (d + 1)])

    def head(h, carry):
        values = t_scr[pl.ds(h, SIDE, stride=8), 0:SIDE].astype(BF16)

        def expand(cols, first):
            width = -(-SIDE * cols // 128) * 128
            spot = lax.broadcasted_iota(jnp.int32, (SIDE, width), 1) // cols
            row = lax.broadcasted_iota(jnp.int32, (SIDE, width), 0)
            pick = (spot == SIDE - 1 - row).astype(F32).astype(BF16)
            e_scr[0:SIDE, 0:width] = lax.dot_general(values, pick, TN, preferred_element_type=F32)
            lane = lax.broadcasted_iota(jnp.int32, (KWIN, width), 1) % cols
            out = jnp.zeros((KWIN, width), F32)
            for jj in range(cols):
                start = WIN - 1 - first - jj
                out = jnp.where(lane == jj, e_scr[start : start + KWIN, 0:width], out)
            w_scr[:, 0:width] = out

        lanes = lax.broadcasted_iota(jnp.int32, (KWIN, 128), 1)
        expand(WIN, 0)
        whole = w_scr[...]
        for phase in range(8):
            turned = whole if phase == 0 else pltpu.roll(whole, 640 - WIN * phase, 1)
            for p in range(KWIN):
                rows = slice(p * KWIN, (p + 1) * KWIN)
                if (23 - p) % 8 == phase:
                    at = (23 - p) // 8 * 128
                    low, high = turned[:, at : at + 128], turned[:, at + 128 : at + 256]
                    x_scr[0, rows] = jnp.where(lanes < 64, low, high)
                if (27 - p) % 8 == phase:
                    at = (27 - p) // 8 * 128
                    x_scr[1, rows] = turned[:, at : at + 128]
        out_ref[1, h] = x_scr[0].astype(BF16)
        out_ref[3, h] = x_scr[1].astype(BF16)
        for kind, first in ((0, WIN - STRIP), (2, 0)):
            expand(STRIP, first)
            for p in range(KWIN):
                rows = slice(p * KWIN, (p + 1) * KWIN)
                x_scr[0, rows] = w_scr[:, (23 - p) * STRIP : (23 - p) * STRIP + 128]
            out_ref[kind, h] = x_scr[0].astype(BF16)
        return carry

    lax.fori_loop(0, HEADS, head, 0)


def build_bias(bias_table):
    return call(
        bias_kernel,
        jax.ShapeDtypeStruct((4, HEADS, KEYS, 128), BF16),
        [
            pltpu.VMEM((8 * SIDE, 128), F32),
            pltpu.VMEM((SIDE + 1, 640), F32),
            pltpu.VMEM((KWIN, 640), F32),
            pltpu.VMEM((2, KEYS, 128), F32),
        ],
        4_000_000_000,
        4_000_000,
    )(bias_table.T)


def one_hot(shape, row_of, col_of):
    row = lax.broadcasted_iota(jnp.int32, shape, 0)
    col = lax.broadcasted_iota(jnp.int32, shape, 1)
    return (row_of(row) == col_of(col)).astype(F32).astype(BF16)


def spread_head(place):
    return jnp.where(place % HP < HD, place // HP * HD + place % HP, -1)


def weights_into(qkv_ref, proj_ref, wk_ref, wqv_ref, wp_ref):
    chans = qkv_ref.shape[0]
    width = HEADS * HP
    qkv = qkv_ref[...]
    pick = one_hot(
        (3 * chans, 3 * 128),
        lambda row: row,
        lambda col: jnp.where(
            (col % 128 < 2 * HP) & (col % HP < HD),
            chans + (col // 128 * 2 + col % 128 // HP) * HD + col % HP,
            -1,
        ),
    )
    wk_ref[...] = dot(qkv, pick).astype(BF16)
    pick = one_hot(
        (2 * width, 3 * chans),
        lambda row: jnp.where(
            row % HP < HD, row // HP * HD + row % HP + jnp.where(row < width, 0, chans), -1
        ),
        lambda col: col,
    )
    wqv_ref[...] = dot_nt(pick, qkv).astype(BF16)
    pick = one_hot((width, chans), spread_head, lambda col: col)
    wp_ref[...] = dot(pick, proj_ref[...]).astype(BF16)


def set_queries(q_scr, wqv_ref, groups):
    scale = LOG2E / np.sqrt(HD)
    rows = jnp.concatenate([rows.reshape(128, rows.shape[2]) for rows in groups], axis=0)
    queries = (dot_nt(wqv_ref[0 : HEADS * HP], rows.astype(BF16)) * scale).astype(BF16)
    none = jnp.zeros((HP, 128), BF16)
    for g in range(len(groups)):
        lanes = slice(128 * g, 128 * g + 128)
        for t in range(HEADS // 2):
            one = queries[2 * t * HP : (2 * t + 1) * HP, lanes]
            two = queries[(2 * t + 1) * HP : (2 * t + 2) * HP, lanes]
            q_scr[g, t, 0:HP] = jnp.concatenate([one, none], axis=1)
            q_scr[g, t, HP : 2 * HP] = jnp.concatenate([none, two], axis=1)


def lookup(g, values):
    out = values[0]
    for index in range(1, len(values)):
        out = jnp.where(g >= index, values[index], out)
    return out


def attention(kinds, windows, q_scr, k_ref, v_ref, bias_ref, wp_ref, s_scr, m_scr, p_scr, o_scr):
    groups = len(kinds)
    pairs = HEADS // 2
    step = 192

    def keep(g, t, k0, top):
        keys = k_ref[lookup(g, windows), k0 : k0 + step, 128 * t : 128 * t + 2 * HP]
        one = dot(keys, q_scr[g, t])
        s_scr[t, k0 : k0 + step] = one
        part = jnp.max(one.reshape(step // 8, 8, 256), axis=0)
        return part if top is None else jnp.maximum(top, part)

    def sum_values(g, t):
        o_scr[g, t] = dot(v_ref[lookup(g, windows), 2 * t * HP : 2 * (t + 1) * HP], p_scr[t])

    for t in range(2):
        later = None
        for k0 in range(0, KEYS, step):
            later = keep(0, t, k0, later)
        m_scr[t] = jnp.broadcast_to(jnp.max(later, axis=0, keepdims=True), later.shape) if t == 0 else later
    p_scr[pairs - 1] = jnp.zeros((KEYS, 256), BF16)

    def attend(g, carry):
        kind = lookup(g, kinds)
        top, coming = m_scr[0, 0:1], m_scr[1]
        for t in range(pairs):
            if t == 0:
                sum_values(jnp.maximum(g - 1, 0), pairs - 1)
            else:
                sum_values(g, t - 1)
            following = g if t + 2 < pairs else jnp.minimum(g + 1, groups - 1)
            later = None
            for k0 in range(0, KEYS, step):
                prob = jnp.exp2(s_scr[t, k0 : k0 + step] - top).astype(BF16)
                for half in range(2):
                    lanes = slice(128 * half, 128 * half + 128)
                    p_scr[t, k0 : k0 + step, lanes] = (
                        prob[:, lanes] * bias_ref[kind, 2 * t + half, k0 : k0 + step]
                    )
                later = keep(following, (t + 2) % pairs, k0, later)
            top, coming = jnp.max(coming, axis=0, keepdims=True), later
        m_scr[0] = jnp.broadcast_to(top, coming.shape)
        m_scr[1] = coming
        return carry

    lax.fori_loop(0, groups, attend, 0)
    sum_values(groups - 1, pairs - 1)
    attended = []
    for g in range(groups):
        parts = []
        for t in range(pairs):
            for half in range(2):
                lanes = slice(128 * half, 128 * half + 128)
                one = o_scr[g, t, half * HP : (half + 1) * HP, lanes]
                parts.append((one * (1.0 / one[HD : HD + 1])).astype(BF16))
        attended.append(jnp.concatenate(parts, axis=0))
    attended = jnp.concatenate(attended, axis=1)
    return lax.dot_general(attended, wp_ref[...], TN, preferred_element_type=F32)


def feed_forward(first, gain, hidden_ref, output_ref):
    normed = layer_norm(first, gain).astype(BF16)
    inner = dot(normed, hidden_ref[...])
    inner = (0.5 * inner * (1.0 + lax.erf(inner * np.float32(np.sqrt(0.5))))).astype(BF16)
    return first + dot_nt(inner, output_ref[...])


def feed_groups(first, gain, hidden_ref, output_ref, batch):
    out = []
    for start in range(0, first.shape[0], 128 * batch):
        mixed = feed_forward(first[start : start + 128 * batch], gain, hidden_ref, output_ref)
        out += [mixed[128 * g : 128 * (g + 1)] for g in range(batch)]
    return out


def project(keys, wk_ref, wqv_ref, k_ref, v_ref, index):
    width = HEADS * HP
    one_row = (lax.broadcasted_iota(jnp.int32, (width, 1), 0) % HP == HD).astype(F32)
    keys = keys.reshape(KEYS, keys.shape[2]).astype(BF16)
    k_ref[index] = dot(keys, wk_ref[...]).astype(BF16)
    v_ref[index] = (dot_nt(wqv_ref[width : 2 * width], keys) + one_row).astype(BF16)


def at_edges():
    row, column = lax.axis_index("rows"), lax.axis_index("cols")
    return (
        column == 0,
        column == lax.axis_size("cols") - 1,
        row == 0,
        row == lax.axis_size("rows") - 1,
        row % 2 == 0,
        column % 2 == 0,
    )


def from_sides(even, first, second):
    first, second = first.astype(F32), second.astype(F32)
    return jnp.where(even, second, first), jnp.where(even, first, second)


def border_rows(ref, c0):
    return jnp.concatenate([ref[0:4, c0 : c0 + WIN], ref[12:16, c0 : c0 + WIN]], axis=0)


def halves(wide, count):
    left = lax.broadcasted_iota(jnp.int32, (1, 128), 1) < 64
    rest = wide.shape[0] - count
    out = jnp.where(left, wide[0:rest], pltpu.roll(wide[count:], 64, 1))
    return out if rest == count else jnp.concatenate([out, wide[rest:count]], axis=0)


def unhalve(packed, rows):
    count = packed.shape[0]
    return jnp.concatenate([packed, pltpu.roll(packed[0 : rows - count], 64, 1)], axis=0)


def pack_kernel(own_ref, row_one_ref, row_two_ref, pay_one_ref, pay_two_ref, x_scr, flat):
    height, cols, chans = own_ref.shape
    even_row, even_col = at_edges()[4:]
    above, below = from_sides(even_row, row_one_ref[...], row_two_ref[...])
    x_scr[0:RIM] = above
    x_scr[RIM : RIM + height] = own_ref[...].astype(F32)
    x_scr[RIM + height :] = below
    for side, near, far in ((0, 0, WIN), (1, cols - WIN, cols - WIN - RIM)):
        for r in range(height + 2 * RIM):
            flat[side, WIN * r : WIN * (r + 1), 0:chans] = x_scr[r, near : near + WIN]
            place = WIN * (height + 2 * RIM) + RIM * r
            flat[side, place : place + RIM, 0:chans] = x_scr[r, far : far + RIM]
    count = flat.shape[1]
    for lanes in (slice(0, 128), slice(128, 256)):
        low, high = flat[0, :, lanes], flat[1, :, lanes]
        one, two = jnp.where(even_col, high, low), jnp.where(even_col, low, high)
        rows = slice(0, count)
        if lanes.start:
            one, two = halves(one, count // 2), halves(two, count // 2)
            rows = slice(count, count + count // 2)
        pay_one_ref[rows] = one.astype(BF16)
        pay_two_ref[rows] = two.astype(BF16)


def pack(own, row_one, row_two):
    height, cols, chans = own.shape
    pixels = (height + 2 * RIM) * (WIN + RIM)
    pay = jax.ShapeDtypeStruct((pixels * 3 // 2, 128), BF16)
    return call(
        pack_kernel,
        (pay, pay),
        [
            pltpu.VMEM((height + 2 * RIM, cols, chans), F32),
            pltpu.VMEM((2, pixels, 256), F32),
        ],
        1_000_000,
        1_000_000,
    )(own, row_one, row_two)


def inner_kernel(
    own_ref,
    row_one_ref,
    row_two_ref,
    gain_one_ref,
    qkv_ref,
    proj_ref,
    bias_ref,
    gain_two_ref,
    hidden_ref,
    output_ref,
    nrm_ref,
    wk_ref,
    wqv_ref,
    wp_ref,
    k_ref,
    v_ref,
    border_ref,
    mid_ref,
    q_scr,
    s_scr,
    m_scr,
    p_scr,
    o_scr,
):
    height, cols, chans = own_ref.shape
    inner = cols // WIN - 2
    flags = at_edges()
    weights_into(qkv_ref, proj_ref, wk_ref, wqv_ref, wp_ref)
    gain_one = gain_one_ref[...]
    for r in range(RIM):
        above, below = from_sides(flags[4], row_one_ref[r], row_two_ref[r])
        nrm_ref[r] = layer_norm(above, gain_one)
        nrm_ref[RIM + height + r] = layer_norm(below, gain_one)
    for r in range(height):
        nrm_ref[RIM + r] = layer_norm(own_ref[r].astype(F32), gain_one)
    kinds, windows, first, queries = [], [], [], []
    for w in range(inner):
        c0 = WIN * (w + 1)
        project(nrm_ref[:, c0 - RIM : c0 - RIM + KWIN], wk_ref, wqv_ref, k_ref, v_ref, w)
        first.append(border_rows(own_ref, c0).reshape(128, chans))
        queries.append(border_rows(nrm_ref.at[RIM : RIM + height], c0))
        kinds.append(1)
        windows.append(w)
    for w in range(inner - 1):
        c0 = WIN * (w + 1)
        first.append(own_ref[4:12, c0 : c0 + WIN].reshape(128, chans))
        queries.append(nrm_ref[RIM + 4 : RIM + 12, c0 : c0 + WIN])
        kinds.append(3)
        windows.append(w)
    groups = len(kinds)
    set_queries(q_scr, wqv_ref, queries)
    first = jnp.concatenate(first, axis=0).astype(F32) + attention(
        kinds, windows, q_scr, k_ref, v_ref, bias_ref, wp_ref, s_scr, m_scr, p_scr, o_scr
    )
    mixed = feed_groups(first, gain_two_ref[...], hidden_ref, output_ref, len(kinds))
    for g in range(groups):
        one = mixed[g].reshape(8, WIN, chans)
        if g < inner:
            border_ref[:, WIN * g : WIN * (g + 1)] = one
        else:
            mid_ref[:, WIN * (g - inner) : WIN * (g - inner + 1)] = one


def outer_kernel(
    own_ref,
    nrm_ref,
    col_two_ref,
    col_one_ref,
    gain_one_ref,
    wk_ref,
    wqv_ref,
    wp_ref,
    inner_k_ref,
    inner_v_ref,
    inner_border_ref,
    bias_ref,
    gain_two_ref,
    hidden_ref,
    output_ref,
    pay_one_ref,
    pay_two_ref,
    edge_ref,
    side_ref,
    strip_ref,
    k_ref,
    v_ref,
    side_scr,
    x_scr,
    n_scr,
    b_scr,
    q_scr,
    s_scr,
    m_scr,
    p_scr,
    o_scr,
    image,
):
    height, cols, chans = own_ref.shape
    inner = cols // WIN - 2
    flags = at_edges()
    gain_one = gain_one_ref[...]
    rows = height + 2 * RIM
    pixels = rows * (WIN + RIM)
    both = from_sides(flags[5], col_one_ref[...], col_two_ref[...])
    for side in range(2):
        x_scr[side, :, 0:128] = both[side][0:pixels]
        x_scr[side, :, 128:256] = unhalve(both[side][pixels:], pixels)
        n_scr[...] = layer_norm(x_scr[side, :, 0:chans], gain_one)
        near, far = (EDGE - WIN, EDGE - WIN - RIM) if side == 0 else (EDGE, EDGE + WIN)
        for r in range(rows):
            side_scr[side, r, near : near + WIN] = n_scr[WIN * r : WIN * (r + 1)]
            place = WIN * rows + RIM * r
            side_scr[side, r, far : far + RIM] = n_scr[place : place + RIM]
        c0 = WIN - STRIP if side == 0 else 0
        x = x_scr[side, 0 : WIN * rows, 0:chans].reshape(rows, WIN, chans)
        strip_ref[side] = x[:, c0 : c0 + STRIP]
    side_scr[0, :, EDGE : 2 * EDGE] = nrm_ref[:, 0:EDGE]
    side_scr[1, :, 0:EDGE] = nrm_ref[:, cols - EDGE : cols]
    k_ref[2] = inner_k_ref[inner - 1]
    v_ref[2] = inner_v_ref[inner - 1]
    for index, side, c0 in ((0, 0, RIM), (1, 0, RIM + WIN), (3, 1, RIM), (4, 1, RIM + WIN)):
        project(side_scr[side, :, c0 : c0 + KWIN], wk_ref, wqv_ref, k_ref, v_ref, index)
    spots = (EDGE - STRIP, 0, cols - WIN, EDGE)
    first, queries = [], []
    for g in range(4):
        side, c0 = g // 2, spots[g]
        if g in (0, 3):
            x = strip_ref[side, RIM : RIM + height]
            queries.append(side_scr[side, RIM : RIM + height, c0 : c0 + STRIP])
        else:
            x = border_rows(own_ref, c0).astype(F32)
            queries.append(border_rows(nrm_ref.at[RIM : RIM + height], c0))
        first.append(x.reshape(128, chans))
    set_queries(q_scr, wqv_ref, queries)
    first = jnp.concatenate(first, axis=0) + attention(
        [0, 1, 1, 2], [0, 1, 3, 4], q_scr, k_ref, v_ref, bias_ref, wp_ref, s_scr, m_scr, p_scr, o_scr
    )
    image[0:4, STRIP + WIN : STRIP + cols - WIN] = inner_border_ref[0:4]
    image[12:16, STRIP + WIN : STRIP + cols - WIN] = inner_border_ref[4:8]
    mixed = feed_groups(first, gain_two_ref[...], hidden_ref, output_ref, 1)
    for g in range(4):
        if g in (0, 3):
            one = jnp.where(flags[g // 3], 0.0, mixed[g]).reshape(height, STRIP, chans)
            c0 = 0 if g == 0 else STRIP + cols
            image[:, c0 : c0 + STRIP] = one
        else:
            one = mixed[g].reshape(8, WIN, chans)
            c0 = STRIP + spots[g]
            image[0:4, c0 : c0 + WIN] = one[0:4]
            image[12:16, c0 : c0 + WIN] = one[4:8]
    even = flags[4]
    count = 3 * image.shape[1]
    for pay_ref, rows in (
        (pay_one_ref, jnp.where(even, image[13:16], image[0:3])),
        (pay_two_ref, jnp.where(even, image[0:3], image[13:16])),
    ):
        b_scr[:, 0:chans] = rows.reshape(count, chans)
        pay_ref[0:count] = b_scr[:, 0:128].astype(BF16)
        pay_ref[count:] = halves(b_scr[:, 128:256], 128).astype(BF16)
    edge_ref[0:4] = image[0:4]
    edge_ref[4:8] = image[12:16]
    side_ref[:, 0:STRIP] = image[4:12, 0:STRIP]
    side_ref[:, STRIP : 2 * STRIP] = image[4:12, STRIP + cols :]


def middle_kernel(
    own_ref,
    nrm_ref,
    k_ref,
    v_ref,
    wqv_ref,
    wp_ref,
    inner_mid_ref,
    bias_ref,
    gain_two_ref,
    hidden_ref,
    output_ref,
    mid_ref,
    q_scr,
    s_scr,
    m_scr,
    p_scr,
    o_scr,
):
    height, cols, chans = own_ref.shape
    spots = (0, cols - 2 * WIN, cols - WIN)
    set_queries(q_scr, wqv_ref, [nrm_ref[RIM + 4 : RIM + 12, c0 : c0 + WIN] for c0 in spots])
    first = [own_ref[4:12, c0 : c0 + WIN].reshape(128, chans) for c0 in spots]
    first = jnp.concatenate(first, axis=0).astype(F32) + attention(
        [3, 3, 3], [1, 2, 3], q_scr, k_ref, v_ref, bias_ref, wp_ref, s_scr, m_scr, p_scr, o_scr
    )
    mixed = feed_groups(first, gain_two_ref[...], hidden_ref, output_ref, 3)
    mid_ref[:, WIN : cols - 2 * WIN] = inner_mid_ref[...]
    for g in range(3):
        mid_ref[:, spots[g] : spots[g] + WIN] = mixed[g].reshape(8, WIN, chans)


def attention_scratch(groups):
    return [
        pltpu.VMEM((groups, HEADS // 2, 2 * HP, 256), BF16),
        pltpu.VMEM((HEADS // 2, KEYS, 256), F32),
        pltpu.VMEM((2, 8, 256), F32),
        pltpu.VMEM((HEADS // 2, KEYS, 256), BF16),
        pltpu.VMEM((groups, HEADS // 2, 2 * HP, 256), F32),
    ]


def inner_block(*args):
    height, cols, chans = args[0].shape
    inner = cols // WIN - 2
    width = HEADS * HP
    groups = 2 * inner - 1
    return call(
        inner_kernel,
        (
            jax.ShapeDtypeStruct((height + 2 * RIM, cols, chans), F32),
            jax.ShapeDtypeStruct((chans, 3 * 128), BF16),
            jax.ShapeDtypeStruct((2 * width, chans), BF16),
            jax.ShapeDtypeStruct((width, chans), BF16),
            jax.ShapeDtypeStruct((inner, KEYS, 3 * 128), BF16),
            jax.ShapeDtypeStruct((inner, width, KEYS), BF16),
            jax.ShapeDtypeStruct((8, WIN * inner, chans), F32),
            jax.ShapeDtypeStruct((8, WIN * (inner - 1), chans), F32),
        ),
        attention_scratch(groups),
        5_000_000_000,
        4_000_000,
    )(*args)


def outer_block(*args):
    height, cols, chans = args[0].shape
    span = cols + 2 * STRIP
    return call(
        outer_kernel,
        (
            jax.ShapeDtypeStruct((3 * span + 128, 128), BF16),
            jax.ShapeDtypeStruct((3 * span + 128, 128), BF16),
            jax.ShapeDtypeStruct((8, span, chans), F32),
            jax.ShapeDtypeStruct((8, 2 * STRIP, chans), F32),
            jax.ShapeDtypeStruct((2, height + 2 * RIM, STRIP, chans), F32),
            jax.ShapeDtypeStruct((5, KEYS, 3 * 128), BF16),
            jax.ShapeDtypeStruct((5, HEADS * HP, KEYS), BF16),
        ),
        [
            pltpu.VMEM((2, height + 2 * RIM, 2 * EDGE, chans), F32),
            pltpu.VMEM((2, (height + 2 * RIM) * (WIN + RIM), 256), F32),
            pltpu.VMEM(((height + 2 * RIM) * (WIN + RIM), chans), F32),
            pltpu.VMEM((3 * span, 256), F32),
            *attention_scratch(4),
            pltpu.VMEM((height, span, chans), F32),
        ],
        5_000_000_000,
        4_000_000,
    )(*args)


def middle_block(*args):
    height, cols, chans = args[0].shape
    return call(
        middle_kernel,
        jax.ShapeDtypeStruct((8, cols, chans), F32),
        attention_scratch(3),
        5_000_000_000,
        4_000_000,
    )(*args)


def conv_kernel(
    own_ref,
    row_one_ref,
    row_two_ref,
    strip_ref,
    back_two_ref,
    back_one_ref,
    edge_ref,
    side_ref,
    mid_ref,
    group_ref,
    before_ref,
    upsample_ref,
    out_ref,
    base,
    image,
    taps,
    grouped,
    sums,
    lowfeat,
    low_taps,
    out_scr,
    wg_scr,
    wb_scr,
    wu_scr,
):
    height, cols, chans = own_ref.shape
    span = cols + 2 * STRIP
    at_left, at_right, at_top, at_bottom, even_row, _ = at_edges()

    feats = before_ref.shape[2]
    pad = chans // 16 * 16
    for a in range(3):
        wb_scr[256 * a + pad : 256 * (a + 1)] = jnp.zeros((256 - pad, 3 * feats), BF16)
        wu_scr[256 * a + 3 * feats : 256 * (a + 1)] = jnp.zeros((256 - 3 * feats, 4 * feats), BF16)
        for b in range(3):
            wg_scr[256 * (3 * a + b) + pad : 256 * (3 * a + b + 1)] = jnp.zeros((256 - pad, chans), BF16)
            wg_scr[256 * (3 * a + b) : 256 * (3 * a + b) + chans] = group_ref[a, b]
    same = one_hot((chans, chans), lambda row: row, lambda col: col)
    order = one_hot(
        (4 * feats, 4 * feats), lambda row: row, lambda col: col % feats * 4 + col // feats
    )
    for a in range(3):
        part = before_ref[a].reshape(3 * feats, chans)
        wb_scr[256 * a : 256 * a + chans] = dot_nt(same, part).astype(BF16)
        part = upsample_ref[a].reshape(3 * feats, 4 * feats)
        wu_scr[256 * a : 256 * a + 3 * feats] = dot(part, order).astype(BF16)

    above, below = from_sides(even_row, row_one_ref[...], row_two_ref[...])
    base[0:2, STRIP : STRIP + cols] = above[2:4]
    base[2 : 2 + height, STRIP : STRIP + cols] = own_ref[...].astype(F32)
    base[2 + height : 4 + height, STRIP : STRIP + cols] = below[0:2]
    rows = slice(2, height + 6)
    base[:, 0:STRIP] = strip_ref[0, rows]
    base[:, STRIP + cols : span] = strip_ref[1, rows]
    base[:, span:] = jnp.zeros((height + 4, STRIP, chans), F32)
    image[:, span:] = jnp.zeros((height + 6, STRIP, chans), F32)
    above, below = from_sides(even_row, back_one_ref[...], back_two_ref[...])
    for rows, packed in ((slice(0, 3), above), (slice(19, 22), below)):
        image[rows, 0:span, 0:128] = packed[0 : 3 * span].reshape(3, span, 128)
        rest = unhalve(packed[3 * span :], 3 * span).reshape(3, span, 128)
        image[rows, 0:span, 128:chans] = rest[:, :, 0 : chans - 128]
    image[3:7, 0:span] = edge_ref[0:4]
    image[7:15, 0:STRIP] = side_ref[:, 0:STRIP]
    image[7:15, STRIP : STRIP + cols] = mid_ref[...]
    image[7:15, STRIP + cols : span] = side_ref[:, STRIP : 2 * STRIP]
    image[15:19, 0:span] = edge_ref[4:8]
    grouped[:, :, 128:256] = jnp.zeros((height + 4, span, 128), BF16)
    for b in range(3):
        taps[:, :, 256 * b + 128 : 256 * b + 256] = jnp.zeros((height + 6, span, 128), BF16)
    part = 4
    col = lax.broadcasted_iota(jnp.int32, (span, chans), 0) - 2
    keep_grouped = (col < cols + 2) & ((col >= 0) | jnp.logical_not(at_left))
    keep_grouped = keep_grouped & ((col < cols) | jnp.logical_not(at_right))
    low_span = cols + 8
    col = lax.broadcasted_iota(jnp.int32, (low_span, 128), 0) - 1
    keep_low = (col <= cols) & ((col >= 0) | jnp.logical_not(at_left))
    keep_low = keep_low & ((col < cols) | jnp.logical_not(at_right))
    left_half = lax.broadcasted_iota(jnp.int32, (cols, 128), 1) < feats
    spot = lax.broadcasted_iota(jnp.int32, (256, 256), 0)
    place = lax.broadcasted_iota(jnp.int32, (256, 256), 1)
    spread = (spot % 128 // cols == place // 128) & (
        spot % cols * 2 + spot // 128 == place % 128
    )
    spread = spread.astype(F32).astype(BF16)

    def fill_taps(first, last):
        for b in range(3):
            start = STRIP - 3 + b
            taps[first:last, :, 256 * b : 256 * b + chans] = image[
                first:last, start : start + span, :
            ].astype(BF16)

    def group(h):
        lhs = jnp.concatenate(
            [taps[h + a : h + a + part].reshape(part * span, 768) for a in range(3)], axis=1
        )
        total = dot(lhs, wg_scr[...]).reshape(part, span, chans)
        total = total + base[h : h + part, STRIP - 2 : STRIP - 2 + span, :]
        for r in range(part):
            mask = keep_grouped
            if h + r < 2:
                mask = mask & jnp.logical_not(at_top)
            if h + r >= height + 2:
                mask = mask & jnp.logical_not(at_bottom)
            grouped[h + r, 0:span, 0:chans] = jnp.where(mask, total[r], 0.0).astype(BF16)

    def narrow(h, count):
        lhs = jnp.concatenate(
            [grouped[h + a : h + a + count].reshape(count * span, 256) for a in range(3)], axis=1
        )
        slot = h // part % 2
        sums[slot, 0:count, :, 0 : 3 * feats] = dot(lhs, wb_scr[...]).reshape(count, span, 3 * feats)
        for r in range(count):
            total = sums[slot, r, 0:low_span, 0:128]
            total = total + pltpu.roll(sums[slot, r, 1 : low_span + 1, 0:128], feats, 1)
            total = total + sums[slot, r, 2 : low_span + 2, 128:256]
            mask = keep_low
            if h + r == 0:
                mask = mask & jnp.logical_not(at_top)
            if h + r == height + 1:
                mask = mask & jnp.logical_not(at_bottom)
            lowfeat[h + r] = jnp.where(mask, jnp.where(total >= 0, total, 0.01 * total), 0.0)
            low_taps[h + r, :, 0:128] = jnp.where(
                left_half, lowfeat[h + r, 0:cols], pltpu.roll(lowfeat[h + r, 1 : cols + 1], feats, 1)
            ).astype(BF16)
            low_taps[h + r, :, 128:256] = jnp.where(
                left_half, lowfeat[h + r, 2 : cols + 2], 0.0
            ).astype(BF16)

    def expand(h):
        lhs = jnp.concatenate(
            [low_taps[h + a : h + a + part].reshape(part * cols, 256) for a in range(3)], axis=1
        )
        total = dot(lhs, wu_scr[...])
        for pair in range(part // 2):
            turned = total[2 * cols * pair : 2 * cols * (pair + 1)].T.astype(BF16)
            lhs = [
                jnp.concatenate(
                    [turned[(2 * a + b) * feats : (2 * a + b + 1) * feats] for b in range(2)], axis=1
                )
                for a in range(2)
            ]
            final = dot(jnp.concatenate(lhs, axis=0), spread)
            for r in range(2):
                for a in range(2):
                    row = 2 * (h + 2 * pair + r) + a
                    out_scr[pl.ds(row, feats, stride=2 * height), :] = final[
                        a * feats : (a + 1) * feats, 128 * r : 128 * (r + 1)
                    ]

    fill_taps(0, part + 2)
    narrowed = expanded = done = 0
    while expanded < height:
        expand_to, narrow_to = min(narrowed - 2, height), min(done - 2, height + 2)
        if done < height + 4:
            if done + part < height + 4:
                fill_taps(done + part + 2, done + 2 * part + 2)
            group(done)
            done += part
        while narrowed < narrow_to:
            count = min(part, height + 2 - narrowed)
            if narrowed + count > narrow_to:
                break
            narrow(narrowed, count)
            narrowed += count
        while expanded + part <= expand_to:
            expand(expanded)
            expanded += part
    out_ref[...] = out_scr[...].reshape(feats, 2 * height, 128).astype(BF16)


def convs(*args):
    height, cols, chans = args[0].shape
    span = cols + 2 * STRIP
    feats = args[-2].shape[2]
    return call(
        conv_kernel,
        jax.ShapeDtypeStruct((feats, 2 * height, 2 * cols), BF16),
        [
            pltpu.VMEM((height + 4, span + STRIP, chans), F32),
            pltpu.VMEM((height + 6, span + STRIP, chans), F32),
            pltpu.VMEM((height + 6, span, 768), BF16),
            pltpu.VMEM((height + 4, span, 256), BF16),
            pltpu.VMEM((2, 4, span, 256), F32),
            pltpu.VMEM((height + 2, cols + 8, 128), F32),
            pltpu.VMEM((height + 2, cols, 256), BF16),
            pltpu.VMEM((feats * 2 * height, 128), F32),
            pltpu.VMEM((9 * 256, chans), BF16),
            pltpu.VMEM((3 * 256, 3 * feats), BF16),
            pltpu.VMEM((3 * 256, 4 * feats), BF16),
        ],
        8_000_000_000,
        4_000_000,
    )(*args)


def swapped(axis, first, second):
    count = lax.axis_size(axis)
    out = []
    for start, payload in ((1, second), (0, first)):
        pairs = [(i, i + 1) for i in range(start, count - 1, 2)]
        pairs = pairs + [(b, a) for a, b in pairs]
        out.append(lax.ppermute(payload, axis, pairs))
    return out[::-1]


def on_device(
    features,
    gain_one,
    qkv_weight,
    bias_table,
    proj_weight,
    gain_two,
    hidden_weight,
    output_weight,
    group_conv,
    before_conv,
    upsample_conv,
):
    height, cols, chans = features.shape
    even_row = lax.axis_index("rows") % 2 == 0
    low, high = features[:RIM], features[height - RIM :]
    row_one, row_two = swapped(
        "rows", jnp.where(even_row, high, low), jnp.where(even_row, low, high)
    )
    col_one, col_two = swapped("cols", *pack(features, row_one, row_two))

    bias = build_bias(bias_table)
    gain_one, gain_two = gain_one.reshape(1, chans), gain_two.reshape(1, chans)
    post = (gain_two, hidden_weight, output_weight.T)
    nrm, wk, wqv, wp, inner_k, inner_v, inner_border, inner_mid = inner_block(
        features,
        row_one,
        row_two,
        gain_one,
        qkv_weight,
        proj_weight,
        bias,
        *post,
    )
    back_one, back_two, edge, side, strips, keys, values = outer_block(
        features,
        nrm,
        col_two,
        col_one,
        gain_one,
        wk,
        wqv,
        wp,
        inner_k,
        inner_v,
        inner_border,
        bias,
        *post,
    )
    back_one, back_two = swapped("rows", back_one, back_two)
    mid = middle_block(features, nrm, keys, values, wqv, wp, inner_mid, bias, *post)
    return convs(
        features,
        row_one,
        row_two,
        strips,
        back_two,
        back_one,
        edge,
        side,
        mid,
        group_conv,
        before_conv.transpose(0, 1, 3, 2),
        upsample_conv,
    )


def solution(mesh):
    placed = (P("rows", "cols", None), P(), P(), P(), P(), P(), P(), P(), P(), P(), P())
    return jax.shard_map(
        on_device, mesh=mesh, in_specs=placed, out_specs=P(None, "rows", "cols"), check_vma=False
    )
```

```python
import functools

import jax
import jax.numpy as jnp
import numpy as np
from jax import lax
from jax.experimental import pallas as pl
from jax.experimental.pallas import tpu as pltpu
from jax.sharding import PartitionSpec as P

HEADS = 6
HD = 30
HP = 32
WIN = 16
KWIN = 24
KEYS = KWIN * KWIN
SIDE = WIN + KWIN - 1
RIM = (KWIN - WIN) // 2
EDGE = WIN + 2 * RIM
STRIP = 8
LOG2E = 1.4426950408889634
F32 = jnp.float32
BF16 = jnp.bfloat16
NT = (((1,), (1,)), ((), ()))
TN = (((0,), (0,)), ((), ()))


def dot(a, b):
    return jnp.dot(a, b, preferred_element_type=F32)


def dot_nt(a, b):
    return lax.dot_general(a, b, NT, preferred_element_type=F32)


def layer_norm(values, gain):
    center = values - jnp.mean(values, axis=-1, keepdims=True)
    spread = jnp.mean(center * center, axis=-1, keepdims=True)
    return center * lax.rsqrt(spread + 1e-05) * gain


def call(kernel, out_shape, scratch, flops, bytes_accessed):
    return pl.pallas_call(
        kernel,
        out_shape=out_shape,
        scratch_shapes=scratch,
        compiler_params=pltpu.CompilerParams(vmem_limit_bytes=24 * 2**20),
        cost_estimate=pl.CostEstimate(
            flops=flops, bytes_accessed=bytes_accessed, transcendentals=0
        ),
    )


def bias_kernel(table_ref, out_ref, t_scr, e_scr, w_scr, x_scr):
    for d in range(SIDE):
        t_scr[8 * d : 8 * d + HEADS, 0:SIDE] = jnp.exp(table_ref[:, SIDE * d : SIDE * (d + 1)])

    def head(h, carry):
        values = t_scr[pl.ds(h, SIDE, stride=8), 0:SIDE].astype(BF16)

        def expand(cols, first):
            width = -(-SIDE * cols // 128) * 128
            spot = lax.broadcasted_iota(jnp.int32, (SIDE, width), 1) // cols
            row = lax.broadcasted_iota(jnp.int32, (SIDE, width), 0)
            pick = (spot == SIDE - 1 - row).astype(F32).astype(BF16)
            e_scr[0:SIDE, 0:width] = lax.dot_general(values, pick, TN, preferred_element_type=F32)
            lane = lax.broadcasted_iota(jnp.int32, (KWIN, width), 1) % cols
            out = jnp.zeros((KWIN, width), F32)
            for jj in range(cols):
                start = WIN - 1 - first - jj
                out = jnp.where(lane == jj, e_scr[start : start + KWIN, 0:width], out)
            w_scr[:, 0:width] = out

        lanes = lax.broadcasted_iota(jnp.int32, (KWIN, 128), 1)
        expand(WIN, 0)
        whole = w_scr[...]
        for phase in range(8):
            turned = whole if phase == 0 else pltpu.roll(whole, 640 - WIN * phase, 1)
            for p in range(KWIN):
                rows = slice(p * KWIN, (p + 1) * KWIN)
                if (23 - p) % 8 == phase:
                    at = (23 - p) // 8 * 128
                    low, high = turned[:, at : at + 128], turned[:, at + 128 : at + 256]
                    x_scr[0, rows] = jnp.where(lanes < 64, low, high)
                if (27 - p) % 8 == phase:
                    at = (27 - p) // 8 * 128
                    x_scr[1, rows] = turned[:, at : at + 128]
        out_ref[1, h] = x_scr[0].astype(BF16)
        out_ref[3, h] = x_scr[1].astype(BF16)
        for kind, first in ((0, WIN - STRIP), (2, 0)):
            expand(STRIP, first)
            for p in range(KWIN):
                rows = slice(p * KWIN, (p + 1) * KWIN)
                x_scr[0, rows] = w_scr[:, (23 - p) * STRIP : (23 - p) * STRIP + 128]
            out_ref[kind, h] = x_scr[0].astype(BF16)
        return carry

    lax.fori_loop(0, HEADS, head, 0)


def build_bias(bias_table):
    return call(
        bias_kernel,
        jax.ShapeDtypeStruct((4, HEADS, KEYS, 128), BF16),
        [
            pltpu.VMEM((8 * SIDE, 128), F32),
            pltpu.VMEM((SIDE + 1, 640), F32),
            pltpu.VMEM((KWIN, 640), F32),
            pltpu.VMEM((2, KEYS, 128), F32),
        ],
        4_000_000_000,
        4_000_000,
    )(bias_table.T)


def one_hot(shape, row_of, col_of):
    row = lax.broadcasted_iota(jnp.int32, shape, 0)
    col = lax.broadcasted_iota(jnp.int32, shape, 1)
    return (row_of(row) == col_of(col)).astype(F32).astype(BF16)


def spread_head(place):
    return jnp.where(place % HP < HD, place // HP * HD + place % HP, -1)


def weights_into(qkv_ref, proj_ref, wk_ref, wqv_ref, wp_ref):
    chans = qkv_ref.shape[0]
    width = HEADS * HP
    qkv = qkv_ref[...]
    pick = one_hot(
        (3 * chans, 3 * 128),
        lambda row: row,
        lambda col: jnp.where(
            (col % 128 < 2 * HP) & (col % HP < HD),
            chans + (col // 128 * 2 + col % 128 // HP) * HD + col % HP,
            -1,
        ),
    )
    wk_ref[...] = dot(qkv, pick).astype(BF16)
    pick = one_hot(
        (2 * width, 3 * chans),
        lambda row: jnp.where(
            row % HP < HD, row // HP * HD + row % HP + jnp.where(row < width, 0, chans), -1
        ),
        lambda col: col,
    )
    wqv_ref[...] = dot_nt(pick, qkv).astype(BF16)
    pick = one_hot((width, chans), spread_head, lambda col: col)
    wp_ref[...] = dot(pick, proj_ref[...]).astype(BF16)


def set_queries(q_scr, wqv_ref, groups):
    scale = LOG2E / np.sqrt(HD)
    rows = jnp.concatenate([rows.reshape(128, rows.shape[2]) for rows in groups], axis=0)
    queries = (dot_nt(wqv_ref[0 : HEADS * HP], rows.astype(BF16)) * scale).astype(BF16)
    none = jnp.zeros((HP, 128), BF16)
    for g in range(len(groups)):
        lanes = slice(128 * g, 128 * g + 128)
        for t in range(HEADS // 2):
            one = queries[2 * t * HP : (2 * t + 1) * HP, lanes]
            two = queries[(2 * t + 1) * HP : (2 * t + 2) * HP, lanes]
            q_scr[g, t, 0:HP] = jnp.concatenate([one, none], axis=1)
            q_scr[g, t, HP : 2 * HP] = jnp.concatenate([none, two], axis=1)


def lookup(g, values):
    out = values[0]
    for index in range(1, len(values)):
        out = jnp.where(g >= index, values[index], out)
    return out


def attention(kinds, windows, q_scr, k_ref, v_ref, bias_ref, wp_ref, s_scr, m_scr, p_scr, o_scr):
    groups = len(kinds)
    pairs = HEADS // 2
    step = 144

    def keep(g, t, k0, top):
        keys = k_ref[lookup(g, windows), k0 : k0 + step, 128 * t : 128 * t + 2 * HP]
        one = dot(keys, q_scr[g, t])
        s_scr[t, k0 : k0 + step] = one
        part = jnp.max(one.reshape(step // 8, 8, 256), axis=0)
        return part if top is None else jnp.maximum(top, part)

    def sum_values(g, t):
        for half in range(2):
            head = 2 * t + half
            lanes = slice(128 * half, 128 * half + 128)
            o_scr[g, head] = dot(v_ref[lookup(g, windows), head * HP : (head + 1) * HP], p_scr[t, :, lanes])

    top = None
    for k0 in range(0, KEYS, step):
        top = keep(0, 0, k0, top)
    m_scr[...] = top
    p_scr[pairs - 1] = jnp.zeros((KEYS, 256), BF16)

    def attend(g, carry):
        kind = lookup(g, kinds)
        top = m_scr[...]
        for t in range(pairs):
            top = jnp.max(top, axis=0, keepdims=True)
            if t == 0:
                sum_values(jnp.maximum(g - 1, 0), pairs - 1)
            else:
                sum_values(g, t - 1)
            following = g if t + 1 < pairs else jnp.minimum(g + 1, groups - 1)
            later = None
            for k0 in range(0, KEYS, step):
                prob = jnp.exp2(s_scr[t, k0 : k0 + step] - top).astype(BF16)
                for half in range(2):
                    lanes = slice(128 * half, 128 * half + 128)
                    p_scr[t, k0 : k0 + step, lanes] = (
                        prob[:, lanes] * bias_ref[kind, 2 * t + half, k0 : k0 + step]
                    )
                later = keep(following, (t + 1) % pairs, k0, later)
            top = later
        m_scr[...] = top
        return carry

    lax.fori_loop(0, groups, attend, 0)
    sum_values(groups - 1, pairs - 1)
    attended = []
    for g in range(groups):
        parts = []
        for head in range(HEADS):
            one = o_scr[g, head]
            parts.append((one * (1.0 / one[HD : HD + 1])).astype(BF16))
        attended.append(jnp.concatenate(parts, axis=0))
    attended = jnp.concatenate(attended, axis=1)
    return lax.dot_general(attended, wp_ref[...], TN, preferred_element_type=F32)


def feed_forward(first, gain, hidden_ref, output_ref):
    normed = layer_norm(first, gain).astype(BF16)
    inner = dot(normed, hidden_ref[...])
    inner = (0.5 * inner * (1.0 + lax.erf(inner * np.float32(np.sqrt(0.5))))).astype(BF16)
    return first + dot_nt(inner, output_ref[...])


def feed_groups(first, gain, hidden_ref, output_ref, batch):
    out = []
    for start in range(0, first.shape[0], 128 * batch):
        mixed = feed_forward(first[start : start + 128 * batch], gain, hidden_ref, output_ref)
        out += [mixed[128 * g : 128 * (g + 1)] for g in range(batch)]
    return out


def project(keys, wk_ref, wqv_ref, k_ref, v_ref, index):
    width = HEADS * HP
    one_row = (lax.broadcasted_iota(jnp.int32, (width, 1), 0) % HP == HD).astype(F32)
    keys = keys.reshape(KEYS, keys.shape[2]).astype(BF16)
    k_ref[index] = dot(keys, wk_ref[...]).astype(BF16)
    v_ref[index] = (dot_nt(wqv_ref[width : 2 * width], keys) + one_row).astype(BF16)


def at_edges():
    row, column = lax.axis_index("rows"), lax.axis_index("cols")
    return (
        column == 0,
        column == lax.axis_size("cols") - 1,
        row == 0,
        row == lax.axis_size("rows") - 1,
        row % 2 == 0,
        column % 2 == 0,
    )


def from_sides(even, first, second):
    first, second = first.astype(F32), second.astype(F32)
    return jnp.where(even, second, first), jnp.where(even, first, second)


def border_rows(ref, c0):
    return jnp.concatenate([ref[0:4, c0 : c0 + WIN], ref[12:16, c0 : c0 + WIN]], axis=0)


def halves(wide, count):
    left = lax.broadcasted_iota(jnp.int32, (1, 128), 1) < 64
    rest = wide.shape[0] - count
    out = jnp.where(left, wide[0:rest], pltpu.roll(wide[count:], 64, 1))
    return out if rest == count else jnp.concatenate([out, wide[rest:count]], axis=0)


def unhalve(packed, rows):
    count = packed.shape[0]
    return jnp.concatenate([packed, pltpu.roll(packed[0 : rows - count], 64, 1)], axis=0)


def pack_kernel(own_ref, row_one_ref, row_two_ref, pay_one_ref, pay_two_ref, x_scr, flat):
    height, cols, chans = own_ref.shape
    even_row, even_col = at_edges()[4:]
    above, below = from_sides(even_row, row_one_ref[...], row_two_ref[...])
    x_scr[0:RIM] = above
    x_scr[RIM : RIM + height] = own_ref[...].astype(F32)
    x_scr[RIM + height :] = below
    for side, near, far in ((0, 0, WIN), (1, cols - WIN, cols - WIN - RIM)):
        for r in range(height + 2 * RIM):
            flat[side, WIN * r : WIN * (r + 1), 0:chans] = x_scr[r, near : near + WIN]
            place = WIN * (height + 2 * RIM) + RIM * r
            flat[side, place : place + RIM, 0:chans] = x_scr[r, far : far + RIM]
    count = flat.shape[1]
    for lanes in (slice(0, 128), slice(128, 256)):
        low, high = flat[0, :, lanes], flat[1, :, lanes]
        one, two = jnp.where(even_col, high, low), jnp.where(even_col, low, high)
        rows = slice(0, count)
        if lanes.start:
            one, two = halves(one, count // 2), halves(two, count // 2)
            rows = slice(count, count + count // 2)
        pay_one_ref[rows] = one.astype(BF16)
        pay_two_ref[rows] = two.astype(BF16)


def pack(own, row_one, row_two):
    height, cols, chans = own.shape
    pixels = (height + 2 * RIM) * (WIN + RIM)
    pay = jax.ShapeDtypeStruct((pixels * 3 // 2, 128), BF16)
    return call(
        pack_kernel,
        (pay, pay),
        [
            pltpu.VMEM((height + 2 * RIM, cols, chans), F32),
            pltpu.VMEM((2, pixels, 256), F32),
        ],
        1_000_000,
        1_000_000,
    )(own, row_one, row_two)


def inner_kernel(
    own_ref,
    row_one_ref,
    row_two_ref,
    gain_one_ref,
    qkv_ref,
    proj_ref,
    bias_ref,
    gain_two_ref,
    hidden_ref,
    output_ref,
    nrm_ref,
    wk_ref,
    wqv_ref,
    wp_ref,
    k_ref,
    v_ref,
    border_ref,
    mid_ref,
    q_scr,
    s_scr,
    m_scr,
    p_scr,
    o_scr,
):
    height, cols, chans = own_ref.shape
    inner = cols // WIN - 2
    flags = at_edges()
    weights_into(qkv_ref, proj_ref, wk_ref, wqv_ref, wp_ref)
    gain_one = gain_one_ref[...]
    for r in range(RIM):
        above, below = from_sides(flags[4], row_one_ref[r], row_two_ref[r])
        nrm_ref[r] = layer_norm(above, gain_one)
        nrm_ref[RIM + height + r] = layer_norm(below, gain_one)
    for r in range(height):
        nrm_ref[RIM + r] = layer_norm(own_ref[r].astype(F32), gain_one)
    kinds, windows, first, queries = [], [], [], []
    for w in range(inner):
        c0 = WIN * (w + 1)
        project(nrm_ref[:, c0 - RIM : c0 - RIM + KWIN], wk_ref, wqv_ref, k_ref, v_ref, w)
        first.append(border_rows(own_ref, c0).reshape(128, chans))
        queries.append(border_rows(nrm_ref.at[RIM : RIM + height], c0))
        kinds.append(1)
        windows.append(w)
    for w in range(inner - 1):
        c0 = WIN * (w + 1)
        first.append(own_ref[4:12, c0 : c0 + WIN].reshape(128, chans))
        queries.append(nrm_ref[RIM + 4 : RIM + 12, c0 : c0 + WIN])
        kinds.append(3)
        windows.append(w)
    groups = len(kinds)
    set_queries(q_scr, wqv_ref, queries)
    first = jnp.concatenate(first, axis=0).astype(F32) + attention(
        kinds, windows, q_scr, k_ref, v_ref, bias_ref, wp_ref, s_scr, m_scr, p_scr, o_scr
    )
    mixed = feed_groups(first, gain_two_ref[...], hidden_ref, output_ref, len(kinds))
    for g in range(groups):
        one = mixed[g].reshape(8, WIN, chans)
        if g < inner:
            border_ref[:, WIN * g : WIN * (g + 1)] = one
        else:
            mid_ref[:, WIN * (g - inner) : WIN * (g - inner + 1)] = one


def outer_kernel(
    own_ref,
    nrm_ref,
    col_two_ref,
    col_one_ref,
    gain_one_ref,
    wk_ref,
    wqv_ref,
    wp_ref,
    inner_k_ref,
    inner_v_ref,
    inner_border_ref,
    bias_ref,
    gain_two_ref,
    hidden_ref,
    output_ref,
    pay_one_ref,
    pay_two_ref,
    edge_ref,
    side_ref,
    strip_ref,
    k_ref,
    v_ref,
    side_scr,
    x_scr,
    n_scr,
    b_scr,
    q_scr,
    s_scr,
    m_scr,
    p_scr,
    o_scr,
    image,
):
    height, cols, chans = own_ref.shape
    inner = cols // WIN - 2
    flags = at_edges()
    gain_one = gain_one_ref[...]
    rows = height + 2 * RIM
    pixels = rows * (WIN + RIM)
    both = from_sides(flags[5], col_one_ref[...], col_two_ref[...])
    for side in range(2):
        x_scr[side, :, 0:128] = both[side][0:pixels]
        x_scr[side, :, 128:256] = unhalve(both[side][pixels:], pixels)
        n_scr[...] = layer_norm(x_scr[side, :, 0:chans], gain_one)
        near, far = (EDGE - WIN, EDGE - WIN - RIM) if side == 0 else (EDGE, EDGE + WIN)
        for r in range(rows):
            side_scr[side, r, near : near + WIN] = n_scr[WIN * r : WIN * (r + 1)]
            place = WIN * rows + RIM * r
            side_scr[side, r, far : far + RIM] = n_scr[place : place + RIM]
        c0 = WIN - STRIP if side == 0 else 0
        x = x_scr[side, 0 : WIN * rows, 0:chans].reshape(rows, WIN, chans)
        strip_ref[side] = x[:, c0 : c0 + STRIP]
    side_scr[0, :, EDGE : 2 * EDGE] = nrm_ref[:, 0:EDGE]
    side_scr[1, :, 0:EDGE] = nrm_ref[:, cols - EDGE : cols]
    k_ref[2] = inner_k_ref[inner - 1]
    v_ref[2] = inner_v_ref[inner - 1]
    for index, side, c0 in ((0, 0, RIM), (1, 0, RIM + WIN), (3, 1, RIM), (4, 1, RIM + WIN)):
        project(side_scr[side, :, c0 : c0 + KWIN], wk_ref, wqv_ref, k_ref, v_ref, index)
    spots = (EDGE - STRIP, 0, cols - WIN, EDGE)
    first, queries = [], []
    for g in range(4):
        side, c0 = g // 2, spots[g]
        if g in (0, 3):
            x = strip_ref[side, RIM : RIM + height]
            queries.append(side_scr[side, RIM : RIM + height, c0 : c0 + STRIP])
        else:
            x = border_rows(own_ref, c0).astype(F32)
            queries.append(border_rows(nrm_ref.at[RIM : RIM + height], c0))
        first.append(x.reshape(128, chans))
    set_queries(q_scr, wqv_ref, queries)
    first = jnp.concatenate(first, axis=0) + attention(
        [0, 1, 1, 2], [0, 1, 3, 4], q_scr, k_ref, v_ref, bias_ref, wp_ref, s_scr, m_scr, p_scr, o_scr
    )
    image[0:4, STRIP + WIN : STRIP + cols - WIN] = inner_border_ref[0:4]
    image[12:16, STRIP + WIN : STRIP + cols - WIN] = inner_border_ref[4:8]
    mixed = feed_groups(first, gain_two_ref[...], hidden_ref, output_ref, 2)
    for g in range(4):
        if g in (0, 3):
            one = jnp.where(flags[g // 3], 0.0, mixed[g]).reshape(height, STRIP, chans)
            c0 = 0 if g == 0 else STRIP + cols
            image[:, c0 : c0 + STRIP] = one
        else:
            one = mixed[g].reshape(8, WIN, chans)
            c0 = STRIP + spots[g]
            image[0:4, c0 : c0 + WIN] = one[0:4]
            image[12:16, c0 : c0 + WIN] = one[4:8]
    even = flags[4]
    count = 3 * image.shape[1]
    for pay_ref, rows in (
        (pay_one_ref, jnp.where(even, image[13:16], image[0:3])),
        (pay_two_ref, jnp.where(even, image[0:3], image[13:16])),
    ):
        b_scr[:, 0:chans] = rows.reshape(count, chans)
        pay_ref[0:count] = b_scr[:, 0:128].astype(BF16)
        pay_ref[count:] = halves(b_scr[:, 128:256], 128).astype(BF16)
    edge_ref[0:4] = image[0:4]
    edge_ref[4:8] = image[12:16]
    side_ref[:, 0:STRIP] = image[4:12, 0:STRIP]
    side_ref[:, STRIP : 2 * STRIP] = image[4:12, STRIP + cols :]


def middle_kernel(
    own_ref,
    nrm_ref,
    k_ref,
    v_ref,
    wqv_ref,
    wp_ref,
    inner_mid_ref,
    bias_ref,
    gain_two_ref,
    hidden_ref,
    output_ref,
    mid_ref,
    q_scr,
    s_scr,
    m_scr,
    p_scr,
    o_scr,
):
    height, cols, chans = own_ref.shape
    spots = (0, cols - 2 * WIN, cols - WIN)
    set_queries(q_scr, wqv_ref, [nrm_ref[RIM + 4 : RIM + 12, c0 : c0 + WIN] for c0 in spots])
    first = [own_ref[4:12, c0 : c0 + WIN].reshape(128, chans) for c0 in spots]
    first = jnp.concatenate(first, axis=0).astype(F32) + attention(
        [3, 3, 3], [1, 2, 3], q_scr, k_ref, v_ref, bias_ref, wp_ref, s_scr, m_scr, p_scr, o_scr
    )
    mixed = feed_groups(first, gain_two_ref[...], hidden_ref, output_ref, 3)
    mid_ref[:, WIN : cols - 2 * WIN] = inner_mid_ref[...]
    for g in range(3):
        mid_ref[:, spots[g] : spots[g] + WIN] = mixed[g].reshape(8, WIN, chans)


def attention_scratch(groups):
    return [
        pltpu.VMEM((groups, HEADS // 2, 2 * HP, 256), BF16),
        pltpu.VMEM((HEADS // 2, KEYS, 256), F32),
        pltpu.VMEM((8, 256), F32),
        pltpu.VMEM((HEADS // 2, KEYS, 256), BF16),
        pltpu.VMEM((groups, HEADS, HP, 128), F32),
    ]


def inner_block(*args):
    height, cols, chans = args[0].shape
    inner = cols // WIN - 2
    width = HEADS * HP
    groups = 2 * inner - 1
    return call(
        inner_kernel,
        (
            jax.ShapeDtypeStruct((height + 2 * RIM, cols, chans), F32),
            jax.ShapeDtypeStruct((chans, 3 * 128), BF16),
            jax.ShapeDtypeStruct((2 * width, chans), BF16),
            jax.ShapeDtypeStruct((width, chans), BF16),
            jax.ShapeDtypeStruct((inner, KEYS, 3 * 128), BF16),
            jax.ShapeDtypeStruct((inner, width, KEYS), BF16),
            jax.ShapeDtypeStruct((8, WIN * inner, chans), F32),
            jax.ShapeDtypeStruct((8, WIN * (inner - 1), chans), F32),
        ),
        attention_scratch(groups),
        5_000_000_000,
        4_000_000,
    )(*args)


def outer_block(*args):
    height, cols, chans = args[0].shape
    span = cols + 2 * STRIP
    return call(
        outer_kernel,
        (
            jax.ShapeDtypeStruct((3 * span + 128, 128), BF16),
            jax.ShapeDtypeStruct((3 * span + 128, 128), BF16),
            jax.ShapeDtypeStruct((8, span, chans), F32),
            jax.ShapeDtypeStruct((8, 2 * STRIP, chans), F32),
            jax.ShapeDtypeStruct((2, height + 2 * RIM, STRIP, chans), F32),
            jax.ShapeDtypeStruct((5, KEYS, 3 * 128), BF16),
            jax.ShapeDtypeStruct((5, HEADS * HP, KEYS), BF16),
        ),
        [
            pltpu.VMEM((2, height + 2 * RIM, 2 * EDGE, chans), F32),
            pltpu.VMEM((2, (height + 2 * RIM) * (WIN + RIM), 256), F32),
            pltpu.VMEM(((height + 2 * RIM) * (WIN + RIM), chans), F32),
            pltpu.VMEM((3 * span, 256), F32),
            *attention_scratch(4),
            pltpu.VMEM((height, span, chans), F32),
        ],
        5_000_000_000,
        4_000_000,
    )(*args)


def middle_block(*args):
    height, cols, chans = args[0].shape
    return call(
        middle_kernel,
        jax.ShapeDtypeStruct((8, cols, chans), F32),
        attention_scratch(3),
        5_000_000_000,
        4_000_000,
    )(*args)


def conv_kernel(
    own_ref,
    row_one_ref,
    row_two_ref,
    strip_ref,
    back_two_ref,
    back_one_ref,
    edge_ref,
    side_ref,
    mid_ref,
    group_ref,
    before_ref,
    upsample_ref,
    out_ref,
    base,
    image,
    taps,
    grouped,
    sums,
    lowfeat,
    low_taps,
    out_scr,
    wg_scr,
    wb_scr,
    wu_scr,
):
    height, cols, chans = own_ref.shape
    span = cols + 2 * STRIP
    at_left, at_right, at_top, at_bottom, even_row, _ = at_edges()

    feats = before_ref.shape[2]
    pad = chans // 16 * 16
    for a in range(3):
        wb_scr[256 * a + pad : 256 * (a + 1)] = jnp.zeros((256 - pad, 3 * feats), BF16)
        wu_scr[256 * a + 3 * feats : 256 * (a + 1)] = jnp.zeros((256 - 3 * feats, 4 * feats), BF16)
        for b in range(3):
            wg_scr[256 * (3 * a + b) + pad : 256 * (3 * a + b + 1)] = jnp.zeros((256 - pad, chans), BF16)
            wg_scr[256 * (3 * a + b) : 256 * (3 * a + b) + chans] = group_ref[a, b]
    same = one_hot((chans, chans), lambda row: row, lambda col: col)
    order = one_hot(
        (4 * feats, 4 * feats), lambda row: row, lambda col: col % feats * 4 + col // feats
    )
    for a in range(3):
        part = before_ref[a].reshape(3 * feats, chans)
        wb_scr[256 * a : 256 * a + chans] = dot_nt(same, part).astype(BF16)
        part = upsample_ref[a].reshape(3 * feats, 4 * feats)
        wu_scr[256 * a : 256 * a + 3 * feats] = dot(part, order).astype(BF16)

    above, below = from_sides(even_row, row_one_ref[...], row_two_ref[...])
    base[0:2, STRIP : STRIP + cols] = above[2:4]
    base[2 : 2 + height, STRIP : STRIP + cols] = own_ref[...].astype(F32)
    base[2 + height : 4 + height, STRIP : STRIP + cols] = below[0:2]
    rows = slice(2, height + 6)
    base[:, 0:STRIP] = strip_ref[0, rows]
    base[:, STRIP + cols : span] = strip_ref[1, rows]
    base[:, span:] = jnp.zeros((height + 4, STRIP, chans), F32)
    image[:, span:] = jnp.zeros((height + 6, STRIP, chans), F32)
    above, below = from_sides(even_row, back_one_ref[...], back_two_ref[...])
    for rows, packed in ((slice(0, 3), above), (slice(19, 22), below)):
        image[rows, 0:span, 0:128] = packed[0 : 3 * span].reshape(3, span, 128)
        rest = unhalve(packed[3 * span :], 3 * span).reshape(3, span, 128)
        image[rows, 0:span, 128:chans] = rest[:, :, 0 : chans - 128]
    image[3:7, 0:span] = edge_ref[0:4]
    image[7:15, 0:STRIP] = side_ref[:, 0:STRIP]
    image[7:15, STRIP : STRIP + cols] = mid_ref[...]
    image[7:15, STRIP + cols : span] = side_ref[:, STRIP : 2 * STRIP]
    image[15:19, 0:span] = edge_ref[4:8]
    grouped[:, :, 128:256] = jnp.zeros((height + 4, span, 128), BF16)
    for b in range(3):
        taps[:, :, 256 * b + 128 : 256 * b + 256] = jnp.zeros((height + 6, span, 128), BF16)
    part = 4
    col = lax.broadcasted_iota(jnp.int32, (span, chans), 0) - 2
    keep_grouped = (col < cols + 2) & ((col >= 0) | jnp.logical_not(at_left))
    keep_grouped = keep_grouped & ((col < cols) | jnp.logical_not(at_right))
    low_span = cols + 8
    col = lax.broadcasted_iota(jnp.int32, (low_span, 128), 0) - 1
    keep_low = (col <= cols) & ((col >= 0) | jnp.logical_not(at_left))
    keep_low = keep_low & ((col < cols) | jnp.logical_not(at_right))
    left_half = lax.broadcasted_iota(jnp.int32, (cols, 128), 1) < feats
    spot = lax.broadcasted_iota(jnp.int32, (256, 256), 0)
    place = lax.broadcasted_iota(jnp.int32, (256, 256), 1)
    spread = (spot % 128 // cols == place // 128) & (
        spot % cols * 2 + spot // 128 == place % 128
    )
    spread = spread.astype(F32).astype(BF16)

    def fill_taps(first, last):
        for b in range(3):
            start = STRIP - 3 + b
            taps[first:last, :, 256 * b : 256 * b + chans] = image[
                first:last, start : start + span, :
            ].astype(BF16)

    def group(h):
        totals = []
        for h2 in range(h, h + part, 2):
            lhs = jnp.concatenate(
                [taps[h2 + a : h2 + a + 2].reshape(2 * span, 768) for a in range(3)], axis=1
            )
            totals.append(dot(lhs, wg_scr[...]).reshape(2, span, chans))
        total = jnp.concatenate(totals, axis=0)
        total = total + base[h : h + part, STRIP - 2 : STRIP - 2 + span, :]
        for r in range(part):
            mask = keep_grouped
            if h + r < 2:
                mask = mask & jnp.logical_not(at_top)
            if h + r >= height + 2:
                mask = mask & jnp.logical_not(at_bottom)
            grouped[h + r, 0:span, 0:chans] = jnp.where(mask, total[r], 0.0).astype(BF16)

    def narrow(h, count):
        lhs = jnp.concatenate(
            [grouped[h + a : h + a + count].reshape(count * span, 256) for a in range(3)], axis=1
        )
        slot = h // part % 2
        sums[slot, 0:count, :, 0 : 3 * feats] = dot(lhs, wb_scr[...]).reshape(count, span, 3 * feats)
        for r in range(count):
            total = sums[slot, r, 0:low_span, 0:128]
            total = total + pltpu.roll(sums[slot, r, 1 : low_span + 1, 0:128], feats, 1)
            total = total + sums[slot, r, 2 : low_span + 2, 128:256]
            mask = keep_low
            if h + r == 0:
                mask = mask & jnp.logical_not(at_top)
            if h + r == height + 1:
                mask = mask & jnp.logical_not(at_bottom)
            lowfeat[h + r] = jnp.where(mask, jnp.where(total >= 0, total, 0.01 * total), 0.0)
            low_taps[h + r, :, 0:128] = jnp.where(
                left_half, lowfeat[h + r, 0:cols], pltpu.roll(lowfeat[h + r, 1 : cols + 1], feats, 1)
            ).astype(BF16)
            low_taps[h + r, :, 128:256] = jnp.where(
                left_half, lowfeat[h + r, 2 : cols + 2], 0.0
            ).astype(BF16)

    def expand(h):
        lhs = jnp.concatenate(
            [low_taps[h + a : h + a + part].reshape(part * cols, 256) for a in range(3)], axis=1
        )
        total = dot(lhs, wu_scr[...])
        for pair in range(part // 2):
            turned = total[2 * cols * pair : 2 * cols * (pair + 1)].T.astype(BF16)
            lhs = [
                jnp.concatenate(
                    [turned[(2 * a + b) * feats : (2 * a + b + 1) * feats] for b in range(2)], axis=1
                )
                for a in range(2)
            ]
            final = dot(jnp.concatenate(lhs, axis=0), spread)
            for r in range(2):
                for a in range(2):
                    row = 2 * (h + 2 * pair + r) + a
                    out_scr[pl.ds(row, feats, stride=2 * height), :] = final[
                        a * feats : (a + 1) * feats, 128 * r : 128 * (r + 1)
                    ]

    fill_taps(0, part + 2)
    narrowed = expanded = done = 0
    while expanded < height:
        expand_to, narrow_to = min(narrowed - 2, height), min(done - 2, height + 2)
        if done < height + 4:
            if done + part < height + 4:
                fill_taps(done + part + 2, done + 2 * part + 2)
            group(done)
            done += part
        while narrowed < narrow_to:
            count = min(part, height + 2 - narrowed)
            if narrowed + count > narrow_to:
                break
            narrow(narrowed, count)
            narrowed += count
        while expanded + part <= expand_to:
            expand(expanded)
            expanded += part
    out_ref[...] = out_scr[...].reshape(feats, 2 * height, 128).astype(BF16)


def convs(*args):
    height, cols, chans = args[0].shape
    span = cols + 2 * STRIP
    feats = args[-2].shape[2]
    return call(
        conv_kernel,
        jax.ShapeDtypeStruct((feats, 2 * height, 2 * cols), BF16),
        [
            pltpu.VMEM((height + 4, span + STRIP, chans), F32),
            pltpu.VMEM((height + 6, span + STRIP, chans), F32),
            pltpu.VMEM((height + 6, span, 768), BF16),
            pltpu.VMEM((height + 4, span, 256), BF16),
            pltpu.VMEM((2, 4, span, 256), F32),
            pltpu.VMEM((height + 2, cols + 8, 128), F32),
            pltpu.VMEM((height + 2, cols, 256), BF16),
            pltpu.VMEM((feats * 2 * height, 128), F32),
            pltpu.VMEM((9 * 256, chans), BF16),
            pltpu.VMEM((3 * 256, 3 * feats), BF16),
            pltpu.VMEM((3 * 256, 4 * feats), BF16),
        ],
        8_000_000_000,
        4_000_000,
    )(*args)


def swapped(axis, first, second):
    count = lax.axis_size(axis)
    out = []
    for start, payload in ((1, second), (0, first)):
        pairs = [(i, i + 1) for i in range(start, count - 1, 2)]
        pairs = pairs + [(b, a) for a, b in pairs]
        out.append(lax.ppermute(payload, axis, pairs))
    return out[::-1]


def on_device(
    features,
    gain_one,
    qkv_weight,
    bias_table,
    proj_weight,
    gain_two,
    hidden_weight,
    output_weight,
    group_conv,
    before_conv,
    upsample_conv,
):
    height, cols, chans = features.shape
    even_row = lax.axis_index("rows") % 2 == 0
    low, high = features[:RIM], features[height - RIM :]
    row_one, row_two = swapped(
        "rows", jnp.where(even_row, high, low), jnp.where(even_row, low, high)
    )
    col_one, col_two = swapped("cols", *pack(features, row_one, row_two))

    bias = build_bias(bias_table)
    gain_one, gain_two = gain_one.reshape(1, chans), gain_two.reshape(1, chans)
    post = (gain_two, hidden_weight, output_weight.T)
    nrm, wk, wqv, wp, inner_k, inner_v, inner_border, inner_mid = inner_block(
        features,
        row_one,
        row_two,
        gain_one,
        qkv_weight,
        proj_weight,
        bias,
        *post,
    )
    back_one, back_two, edge, side, strips, keys, values = outer_block(
        features,
        nrm,
        col_two,
        col_one,
        gain_one,
        wk,
        wqv,
        wp,
        inner_k,
        inner_v,
        inner_border,
        bias,
        *post,
    )
    back_one, back_two = swapped("rows", back_one, back_two)
    mid = middle_block(features, nrm, keys, values, wqv, wp, inner_mid, bias, *post)
    return convs(
        features,
        row_one,
        row_two,
        strips,
        back_two,
        back_one,
        edge,
        side,
        mid,
        group_conv,
        before_conv.transpose(0, 1, 3, 2),
        upsample_conv,
    )


def solution(mesh):
    placed = (P("rows", "cols", None), P(), P(), P(), P(), P(), P(), P(), P(), P(), P())
    return jax.shard_map(
        on_device, mesh=mesh, in_specs=placed, out_specs=P(None, "rows", "cols"), check_vma=False
    )
```

```python
import functools

import jax
import jax.numpy as jnp
import numpy as np
from jax import lax
from jax.experimental import pallas as pl
from jax.experimental.pallas import tpu as pltpu
from jax.sharding import PartitionSpec as P

HEADS = 6
HD = 30
HP = 32
WIN = 16
KWIN = 24
KEYS = KWIN * KWIN
SIDE = WIN + KWIN - 1
RIM = (KWIN - WIN) // 2
EDGE = WIN + 2 * RIM
STRIP = 8
LOG2E = 1.4426950408889634
F32 = jnp.float32
BF16 = jnp.bfloat16
NT = (((1,), (1,)), ((), ()))
TN = (((0,), (0,)), ((), ()))


def dot(a, b):
    return jnp.dot(a, b, preferred_element_type=F32)


def dot_nt(a, b):
    return lax.dot_general(a, b, NT, preferred_element_type=F32)


def layer_norm(values, gain):
    center = values - jnp.mean(values, axis=-1, keepdims=True)
    spread = jnp.mean(center * center, axis=-1, keepdims=True)
    return center * lax.rsqrt(spread + 1e-05) * gain


def call(kernel, out_shape, scratch, flops, bytes_accessed):
    return pl.pallas_call(
        kernel,
        out_shape=out_shape,
        scratch_shapes=scratch,
        compiler_params=pltpu.CompilerParams(vmem_limit_bytes=24 * 2**20),
        cost_estimate=pl.CostEstimate(
            flops=flops, bytes_accessed=bytes_accessed, transcendentals=0
        ),
    )


def bias_kernel(table_ref, out_ref, t_scr, e_scr, w_scr, x_scr):
    for d in range(SIDE):
        t_scr[8 * d : 8 * d + HEADS, 0:SIDE] = jnp.exp(table_ref[:, SIDE * d : SIDE * (d + 1)])

    def head(h, carry):
        values = t_scr[pl.ds(h, SIDE, stride=8), 0:SIDE].astype(BF16)

        def expand(cols, first):
            width = -(-SIDE * cols // 128) * 128
            spot = lax.broadcasted_iota(jnp.int32, (SIDE, width), 1) // cols
            row = lax.broadcasted_iota(jnp.int32, (SIDE, width), 0)
            pick = (spot == SIDE - 1 - row).astype(F32).astype(BF16)
            e_scr[0:SIDE, 0:width] = lax.dot_general(values, pick, TN, preferred_element_type=F32)
            lane = lax.broadcasted_iota(jnp.int32, (KWIN, width), 1) % cols
            out = jnp.zeros((KWIN, width), F32)
            for jj in range(cols):
                start = WIN - 1 - first - jj
                out = jnp.where(lane == jj, e_scr[start : start + KWIN, 0:width], out)
            w_scr[:, 0:width] = out

        lanes = lax.broadcasted_iota(jnp.int32, (KWIN, 128), 1)
        expand(WIN, 0)
        whole = w_scr[...]
        for phase in range(8):
            turned = whole if phase == 0 else pltpu.roll(whole, 640 - WIN * phase, 1)
            for p in range(KWIN):
                rows = slice(p * KWIN, (p + 1) * KWIN)
                if (23 - p) % 8 == phase:
                    at = (23 - p) // 8 * 128
                    low, high = turned[:, at : at + 128], turned[:, at + 128 : at + 256]
                    x_scr[0, rows] = jnp.where(lanes < 64, low, high)
                if (27 - p) % 8 == phase:
                    at = (27 - p) // 8 * 128
                    x_scr[1, rows] = turned[:, at : at + 128]
        out_ref[1, h] = x_scr[0].astype(BF16)
        out_ref[3, h] = x_scr[1].astype(BF16)
        for kind, first in ((0, WIN - STRIP), (2, 0)):
            expand(STRIP, first)
            for p in range(KWIN):
                rows = slice(p * KWIN, (p + 1) * KWIN)
                x_scr[0, rows] = w_scr[:, (23 - p) * STRIP : (23 - p) * STRIP + 128]
            out_ref[kind, h] = x_scr[0].astype(BF16)
        return carry

    lax.fori_loop(0, HEADS, head, 0)


def build_bias(bias_table):
    return call(
        bias_kernel,
        jax.ShapeDtypeStruct((4, HEADS, KEYS, 128), BF16),
        [
            pltpu.VMEM((8 * SIDE, 128), F32),
            pltpu.VMEM((SIDE + 1, 640), F32),
            pltpu.VMEM((KWIN, 640), F32),
            pltpu.VMEM((2, KEYS, 128), F32),
        ],
        4_000_000_000,
        4_000_000,
    )(bias_table.T)


def one_hot(shape, row_of, col_of):
    row = lax.broadcasted_iota(jnp.int32, shape, 0)
    col = lax.broadcasted_iota(jnp.int32, shape, 1)
    return (row_of(row) == col_of(col)).astype(F32).astype(BF16)


def spread_head(place):
    return jnp.where(place % HP < HD, place // HP * HD + place % HP, -1)


def weights_into(qkv_ref, proj_ref, wk_ref, wqv_ref, wp_ref):
    chans = qkv_ref.shape[0]
    width = HEADS * HP
    qkv = qkv_ref[...]
    pick = one_hot(
        (3 * chans, 3 * 128),
        lambda row: row,
        lambda col: jnp.where(
            (col % 128 < 2 * HP) & (col % HP < HD),
            chans + (col // 128 * 2 + col % 128 // HP) * HD + col % HP,
            -1,
        ),
    )
    wk_ref[...] = dot(qkv, pick).astype(BF16)
    pick = one_hot(
        (2 * width, 3 * chans),
        lambda row: jnp.where(
            row % HP < HD, row // HP * HD + row % HP + jnp.where(row < width, 0, chans), -1
        ),
        lambda col: col,
    )
    wqv_ref[...] = dot_nt(pick, qkv).astype(BF16)
    pick = one_hot((width, chans), spread_head, lambda col: col)
    wp_ref[...] = dot(pick, proj_ref[...]).astype(BF16)


def set_queries(q_scr, wqv_ref, groups):
    scale = LOG2E / np.sqrt(HD)
    rows = jnp.concatenate([rows.reshape(128, rows.shape[2]) for rows in groups], axis=0)
    queries = (dot_nt(wqv_ref[0 : HEADS * HP], rows.astype(BF16)) * scale).astype(BF16)
    none = jnp.zeros((HP, 128), BF16)
    for g in range(len(groups)):
        lanes = slice(128 * g, 128 * g + 128)
        for t in range(HEADS // 2):
            one = queries[2 * t * HP : (2 * t + 1) * HP, lanes]
            two = queries[(2 * t + 1) * HP : (2 * t + 2) * HP, lanes]
            q_scr[g, t, 0:HP] = jnp.concatenate([one, none], axis=1)
            q_scr[g, t, HP : 2 * HP] = jnp.concatenate([none, two], axis=1)


def lookup(g, values):
    out = values[0]
    for index in range(1, len(values)):
        out = jnp.where(g >= index, values[index], out)
    return out


def attention(kinds, windows, q_scr, k_ref, v_ref, bias_ref, wp_ref, s_scr, m_scr, p_scr, o_scr):
    groups = len(kinds)
    pairs = HEADS // 2
    step = 144

    def keep(g, t, k0, top):
        keys = k_ref[lookup(g, windows), k0 : k0 + step, 128 * t : 128 * t + 2 * HP]
        one = dot(keys, q_scr[g, t])
        s_scr[t, k0 : k0 + step] = one
        part = jnp.max(one.reshape(step // 8, 8, 256), axis=0)
        return part if top is None else jnp.maximum(top, part)

    def sum_values(g, t):
        for half in range(2):
            head = 2 * t + half
            lanes = slice(128 * half, 128 * half + 128)
            o_scr[g, head] = dot(v_ref[lookup(g, windows), head * HP : (head + 1) * HP], p_scr[t, :, lanes])

    top = None
    for k0 in range(0, KEYS, step):
        top = keep(0, 0, k0, top)
    m_scr[...] = top
    p_scr[pairs - 1] = jnp.zeros((KEYS, 256), BF16)

    def attend(g, carry):
        kind = lookup(g, kinds)
        top = m_scr[...]
        for t in range(pairs):
            top = jnp.max(top, axis=0, keepdims=True)
            if t == 0:
                sum_values(jnp.maximum(g - 1, 0), pairs - 1)
            else:
                sum_values(g, t - 1)
            following = g if t + 1 < pairs else jnp.minimum(g + 1, groups - 1)
            later = None
            for k0 in range(0, KEYS, step):
                prob = jnp.exp2(s_scr[t, k0 : k0 + step] - top).astype(BF16)
                for half in range(2):
                    lanes = slice(128 * half, 128 * half + 128)
                    p_scr[t, k0 : k0 + step, lanes] = (
                        prob[:, lanes] * bias_ref[kind, 2 * t + half, k0 : k0 + step]
                    )
                later = keep(following, (t + 1) % pairs, k0, later)
            top = later
        m_scr[...] = top
        return carry

    lax.fori_loop(0, groups, attend, 0)
    sum_values(groups - 1, pairs - 1)
    attended = []
    for g in range(groups):
        parts = []
        for head in range(HEADS):
            one = o_scr[g, head]
            parts.append((one * (1.0 / one[HD : HD + 1])).astype(BF16))
        attended.append(jnp.concatenate(parts, axis=0))
    attended = jnp.concatenate(attended, axis=1)
    return lax.dot_general(attended, wp_ref[...], TN, preferred_element_type=F32)


def feed_forward(first, gain, hidden_ref, output_ref):
    normed = layer_norm(first, gain).astype(BF16)
    inner = dot(normed, hidden_ref[...])
    inner = (0.5 * inner * (1.0 + lax.erf(inner * np.float32(np.sqrt(0.5))))).astype(BF16)
    return first + dot_nt(inner, output_ref[...])


def feed_groups(first, gain, hidden_ref, output_ref, batch):
    out = []
    for start in range(0, first.shape[0], 128 * batch):
        mixed = feed_forward(first[start : start + 128 * batch], gain, hidden_ref, output_ref)
        out += [mixed[128 * g : 128 * (g + 1)] for g in range(batch)]
    return out


def project(keys, wk_ref, wqv_ref, k_ref, v_ref, index):
    width = HEADS * HP
    one_row = (lax.broadcasted_iota(jnp.int32, (width, 1), 0) % HP == HD).astype(F32)
    keys = keys.reshape(KEYS, keys.shape[2]).astype(BF16)
    k_ref[index] = dot(keys, wk_ref[...]).astype(BF16)
    v_ref[index] = (dot_nt(wqv_ref[width : 2 * width], keys) + one_row).astype(BF16)


def at_edges():
    row, column = lax.axis_index("rows"), lax.axis_index("cols")
    return (
        column == 0,
        column == lax.axis_size("cols") - 1,
        row == 0,
        row == lax.axis_size("rows") - 1,
        row % 2 == 0,
        column % 2 == 0,
    )


def from_sides(even, first, second):
    first, second = first.astype(F32), second.astype(F32)
    return jnp.where(even, second, first), jnp.where(even, first, second)


def border_rows(ref, c0):
    return jnp.concatenate([ref[0:4, c0 : c0 + WIN], ref[12:16, c0 : c0 + WIN]], axis=0)


def halves(wide, count):
    left = lax.broadcasted_iota(jnp.int32, (1, 128), 1) < 64
    rest = wide.shape[0] - count
    out = jnp.where(left, wide[0:rest], pltpu.roll(wide[count:], 64, 1))
    return out if rest == count else jnp.concatenate([out, wide[rest:count]], axis=0)


def unhalve(packed, rows):
    count = packed.shape[0]
    return jnp.concatenate([packed, pltpu.roll(packed[0 : rows - count], 64, 1)], axis=0)


def pack_kernel(own_ref, row_one_ref, row_two_ref, pay_one_ref, pay_two_ref, x_scr, flat):
    height, cols, chans = own_ref.shape
    even_row, even_col = at_edges()[4:]
    above, below = from_sides(even_row, row_one_ref[...], row_two_ref[...])
    x_scr[0:RIM] = above
    x_scr[RIM : RIM + height] = own_ref[...].astype(F32)
    x_scr[RIM + height :] = below
    for side, near, far in ((0, 0, WIN), (1, cols - WIN, cols - WIN - RIM)):
        for r in range(height + 2 * RIM):
            flat[side, WIN * r : WIN * (r + 1), 0:chans] = x_scr[r, near : near + WIN]
            place = WIN * (height + 2 * RIM) + RIM * r
            flat[side, place : place + RIM, 0:chans] = x_scr[r, far : far + RIM]
    count = flat.shape[1]
    for lanes in (slice(0, 128), slice(128, 256)):
        low, high = flat[0, :, lanes], flat[1, :, lanes]
        one, two = jnp.where(even_col, high, low), jnp.where(even_col, low, high)
        rows = slice(0, count)
        if lanes.start:
            one, two = halves(one, count // 2), halves(two, count // 2)
            rows = slice(count, count + count // 2)
        pay_one_ref[rows] = one.astype(BF16)
        pay_two_ref[rows] = two.astype(BF16)


def pack(own, row_one, row_two):
    height, cols, chans = own.shape
    pixels = (height + 2 * RIM) * (WIN + RIM)
    pay = jax.ShapeDtypeStruct((pixels * 3 // 2, 128), BF16)
    return call(
        pack_kernel,
        (pay, pay),
        [
            pltpu.VMEM((height + 2 * RIM, cols, chans), F32),
            pltpu.VMEM((2, pixels, 256), F32),
        ],
        1_000_000,
        1_000_000,
    )(own, row_one, row_two)


def inner_kernel(
    own_ref,
    row_one_ref,
    row_two_ref,
    gain_one_ref,
    qkv_ref,
    proj_ref,
    bias_ref,
    gain_two_ref,
    hidden_ref,
    output_ref,
    nrm_ref,
    wk_ref,
    wqv_ref,
    wp_ref,
    k_ref,
    v_ref,
    border_ref,
    mid_ref,
    q_scr,
    s_scr,
    m_scr,
    p_scr,
    o_scr,
):
    height, cols, chans = own_ref.shape
    inner = cols // WIN - 2
    flags = at_edges()
    weights_into(qkv_ref, proj_ref, wk_ref, wqv_ref, wp_ref)
    gain_one = gain_one_ref[...]
    for r in range(RIM):
        above, below = from_sides(flags[4], row_one_ref[r], row_two_ref[r])
        nrm_ref[r] = layer_norm(above, gain_one)
        nrm_ref[RIM + height + r] = layer_norm(below, gain_one)
    for r in range(height):
        nrm_ref[RIM + r] = layer_norm(own_ref[r].astype(F32), gain_one)
    kinds, windows, first, queries = [], [], [], []
    for w in range(inner):
        c0 = WIN * (w + 1)
        project(nrm_ref[:, c0 - RIM : c0 - RIM + KWIN], wk_ref, wqv_ref, k_ref, v_ref, w)
        first.append(border_rows(own_ref, c0).reshape(128, chans))
        queries.append(border_rows(nrm_ref.at[RIM : RIM + height], c0))
        kinds.append(1)
        windows.append(w)
    for w in range(inner - 1):
        c0 = WIN * (w + 1)
        first.append(own_ref[4:12, c0 : c0 + WIN].reshape(128, chans))
        queries.append(nrm_ref[RIM + 4 : RIM + 12, c0 : c0 + WIN])
        kinds.append(3)
        windows.append(w)
    groups = len(kinds)
    set_queries(q_scr, wqv_ref, queries)
    first = jnp.concatenate(first, axis=0).astype(F32) + attention(
        kinds, windows, q_scr, k_ref, v_ref, bias_ref, wp_ref, s_scr, m_scr, p_scr, o_scr
    )
    mixed = feed_groups(first, gain_two_ref[...], hidden_ref, output_ref, len(kinds))
    for g in range(groups):
        one = mixed[g].reshape(8, WIN, chans)
        if g < inner:
            border_ref[:, WIN * g : WIN * (g + 1)] = one
        else:
            mid_ref[:, WIN * (g - inner) : WIN * (g - inner + 1)] = one


def outer_kernel(
    own_ref,
    nrm_ref,
    col_two_ref,
    col_one_ref,
    gain_one_ref,
    wk_ref,
    wqv_ref,
    wp_ref,
    inner_k_ref,
    inner_v_ref,
    inner_border_ref,
    bias_ref,
    gain_two_ref,
    hidden_ref,
    output_ref,
    pay_one_ref,
    pay_two_ref,
    edge_ref,
    side_ref,
    strip_ref,
    k_ref,
    v_ref,
    side_scr,
    x_scr,
    n_scr,
    b_scr,
    q_scr,
    s_scr,
    m_scr,
    p_scr,
    o_scr,
    image,
):
    height, cols, chans = own_ref.shape
    inner = cols // WIN - 2
    flags = at_edges()
    gain_one = gain_one_ref[...]
    rows = height + 2 * RIM
    pixels = rows * (WIN + RIM)
    both = from_sides(flags[5], col_one_ref[...], col_two_ref[...])
    for side in range(2):
        x_scr[side, :, 0:128] = both[side][0:pixels]
        x_scr[side, :, 128:256] = unhalve(both[side][pixels:], pixels)
        n_scr[...] = layer_norm(x_scr[side, :, 0:chans], gain_one)
        near, far = (EDGE - WIN, EDGE - WIN - RIM) if side == 0 else (EDGE, EDGE + WIN)
        for r in range(rows):
            side_scr[side, r, near : near + WIN] = n_scr[WIN * r : WIN * (r + 1)]
            place = WIN * rows + RIM * r
            side_scr[side, r, far : far + RIM] = n_scr[place : place + RIM]
        c0 = WIN - STRIP if side == 0 else 0
        x = x_scr[side, 0 : WIN * rows, 0:chans].reshape(rows, WIN, chans)
        strip_ref[side] = x[:, c0 : c0 + STRIP]
    side_scr[0, :, EDGE : 2 * EDGE] = nrm_ref[:, 0:EDGE]
    side_scr[1, :, 0:EDGE] = nrm_ref[:, cols - EDGE : cols]
    k_ref[2] = inner_k_ref[inner - 1]
    v_ref[2] = inner_v_ref[inner - 1]
    for index, side, c0 in ((0, 0, RIM), (1, 0, RIM + WIN), (3, 1, RIM), (4, 1, RIM + WIN)):
        project(side_scr[side, :, c0 : c0 + KWIN], wk_ref, wqv_ref, k_ref, v_ref, index)
    spots = (EDGE - STRIP, 0, cols - WIN, EDGE)
    first, queries = [], []
    for g in range(4):
        side, c0 = g // 2, spots[g]
        if g in (0, 3):
            x = strip_ref[side, RIM : RIM + height]
            queries.append(side_scr[side, RIM : RIM + height, c0 : c0 + STRIP])
        else:
            x = border_rows(own_ref, c0).astype(F32)
            queries.append(border_rows(nrm_ref.at[RIM : RIM + height], c0))
        first.append(x.reshape(128, chans))
    set_queries(q_scr, wqv_ref, queries)
    first = jnp.concatenate(first, axis=0) + attention(
        [0, 1, 1, 2], [0, 1, 3, 4], q_scr, k_ref, v_ref, bias_ref, wp_ref, s_scr, m_scr, p_scr, o_scr
    )
    image[0:4, STRIP + WIN : STRIP + cols - WIN] = inner_border_ref[0:4]
    image[12:16, STRIP + WIN : STRIP + cols - WIN] = inner_border_ref[4:8]
    mixed = feed_groups(first, gain_two_ref[...], hidden_ref, output_ref, 2)
    for g in range(4):
        if g in (0, 3):
            one = jnp.where(flags[g // 3], 0.0, mixed[g]).reshape(height, STRIP, chans)
            c0 = 0 if g == 0 else STRIP + cols
            image[:, c0 : c0 + STRIP] = one
        else:
            one = mixed[g].reshape(8, WIN, chans)
            c0 = STRIP + spots[g]
            image[0:4, c0 : c0 + WIN] = one[0:4]
            image[12:16, c0 : c0 + WIN] = one[4:8]
    even = flags[4]
    count = 3 * image.shape[1]
    for pay_ref, rows in (
        (pay_one_ref, jnp.where(even, image[13:16], image[0:3])),
        (pay_two_ref, jnp.where(even, image[0:3], image[13:16])),
    ):
        b_scr[:, 0:chans] = rows.reshape(count, chans)
        pay_ref[0:count] = b_scr[:, 0:128].astype(BF16)
        pay_ref[count:] = halves(b_scr[:, 128:256], 128).astype(BF16)
    edge_ref[0:4] = image[0:4]
    edge_ref[4:8] = image[12:16]
    side_ref[:, 0:STRIP] = image[4:12, 0:STRIP]
    side_ref[:, STRIP : 2 * STRIP] = image[4:12, STRIP + cols :]


def fill_taps(taps_ref, image, span):
    chans = image.shape[2]
    for b in range(3):
        start = STRIP - 3 + b
        lanes = slice(256 * b + 128, 256 * b + 256)
        taps_ref[:, :, lanes] = jnp.zeros((taps_ref.shape[0], span, 128), BF16)
        taps_ref[:, :, 256 * b : 256 * b + chans] = image[:, start : start + span].astype(BF16)


def conv_weights(group_ref, before_ref, upsample_ref, wg_scr, wb_scr, wu_scr):
    chans = group_ref.shape[2]
    feats = before_ref.shape[2]
    pad = chans // 16 * 16
    for a in range(3):
        wb_scr[256 * a + pad : 256 * (a + 1)] = jnp.zeros((256 - pad, 3 * feats), BF16)
        wu_scr[256 * a + 3 * feats : 256 * (a + 1)] = jnp.zeros((256 - 3 * feats, 4 * feats), BF16)
        for b in range(3):
            wg_scr[256 * (3 * a + b) + pad : 256 * (3 * a + b + 1)] = jnp.zeros((256 - pad, chans), BF16)
            wg_scr[256 * (3 * a + b) : 256 * (3 * a + b) + chans] = group_ref[a, b]
    same = one_hot((chans, chans), lambda row: row, lambda col: col)
    order = one_hot(
        (4 * feats, 4 * feats), lambda row: row, lambda col: col % feats * 4 + col // feats
    )
    for a in range(3):
        part = before_ref[a].reshape(3 * feats, chans)
        wb_scr[256 * a : 256 * a + chans] = dot_nt(same, part).astype(BF16)
        part = upsample_ref[a].reshape(3 * feats, 4 * feats)
        wu_scr[256 * a : 256 * a + 3 * feats] = dot(part, order).astype(BF16)


def middle_kernel(
    own_ref,
    nrm_ref,
    k_ref,
    v_ref,
    wqv_ref,
    wp_ref,
    inner_mid_ref,
    edge_ref,
    side_ref,
    strip_ref,
    row_two_ref,
    row_one_ref,
    group_ref,
    before_ref,
    upsample_ref,
    bias_ref,
    gain_two_ref,
    hidden_ref,
    output_ref,
    taps_ref,
    base_ref,
    wg_ref,
    wb_ref,
    wu_ref,
    q_scr,
    s_scr,
    m_scr,
    p_scr,
    o_scr,
    image,
):
    height, cols, chans = own_ref.shape
    spots = (0, cols - 2 * WIN, cols - WIN)
    set_queries(q_scr, wqv_ref, [nrm_ref[RIM + 4 : RIM + 12, c0 : c0 + WIN] for c0 in spots])
    first = [own_ref[4:12, c0 : c0 + WIN].reshape(128, chans) for c0 in spots]
    first = jnp.concatenate(first, axis=0).astype(F32) + attention(
        [3, 3, 3], [1, 2, 3], q_scr, k_ref, v_ref, bias_ref, wp_ref, s_scr, m_scr, p_scr, o_scr
    )
    mixed = feed_groups(first, gain_two_ref[...], hidden_ref, output_ref, 3)
    span = cols + 2 * STRIP
    image[:, span:] = jnp.zeros((height, STRIP, chans), F32)
    image[0:4, 0:span] = edge_ref[0:4]
    image[4:12, 0:STRIP] = side_ref[:, 0:STRIP]
    image[4:12, STRIP + WIN : STRIP + cols - 2 * WIN] = inner_mid_ref[...]
    for g in range(3):
        c0 = STRIP + spots[g]
        image[4:12, c0 : c0 + WIN] = mixed[g].reshape(8, WIN, chans)
    image[4:12, STRIP + cols : span] = side_ref[:, STRIP : 2 * STRIP]
    image[12:16, 0:span] = edge_ref[4:8]
    fill_taps(taps_ref, image, span)
    conv_weights(group_ref, before_ref, upsample_ref, wg_ref, wb_ref, wu_ref)
    even_row = at_edges()[4]
    above, below = from_sides(even_row, row_one_ref[...], row_two_ref[...])
    base_ref[0:2, STRIP : STRIP + cols] = above[2:4]
    base_ref[2 : 2 + height, STRIP : STRIP + cols] = own_ref[...].astype(F32)
    base_ref[2 + height : 4 + height, STRIP : STRIP + cols] = below[0:2]
    rows = slice(2, height + 6)
    base_ref[:, 0:STRIP] = strip_ref[0, rows]
    base_ref[:, STRIP + cols : span] = strip_ref[1, rows]
    base_ref[:, span:] = jnp.zeros((height + 4, STRIP, chans), F32)


def attention_scratch(groups):
    return [
        pltpu.VMEM((groups, HEADS // 2, 2 * HP, 256), BF16),
        pltpu.VMEM((HEADS // 2, KEYS, 256), F32),
        pltpu.VMEM((8, 256), F32),
        pltpu.VMEM((HEADS // 2, KEYS, 256), BF16),
        pltpu.VMEM((groups, HEADS, HP, 128), F32),
    ]


def inner_block(*args):
    height, cols, chans = args[0].shape
    inner = cols // WIN - 2
    width = HEADS * HP
    groups = 2 * inner - 1
    return call(
        inner_kernel,
        (
            jax.ShapeDtypeStruct((height + 2 * RIM, cols, chans), F32),
            jax.ShapeDtypeStruct((chans, 3 * 128), BF16),
            jax.ShapeDtypeStruct((2 * width, chans), BF16),
            jax.ShapeDtypeStruct((width, chans), BF16),
            jax.ShapeDtypeStruct((inner, KEYS, 3 * 128), BF16),
            jax.ShapeDtypeStruct((inner, width, KEYS), BF16),
            jax.ShapeDtypeStruct((8, WIN * inner, chans), F32),
            jax.ShapeDtypeStruct((8, WIN * (inner - 1), chans), F32),
        ),
        attention_scratch(groups),
        5_000_000_000,
        4_000_000,
    )(*args)


def outer_block(*args):
    height, cols, chans = args[0].shape
    span = cols + 2 * STRIP
    return call(
        outer_kernel,
        (
            jax.ShapeDtypeStruct((3 * span + 128, 128), BF16),
            jax.ShapeDtypeStruct((3 * span + 128, 128), BF16),
            jax.ShapeDtypeStruct((8, span, chans), F32),
            jax.ShapeDtypeStruct((8, 2 * STRIP, chans), F32),
            jax.ShapeDtypeStruct((2, height + 2 * RIM, STRIP, chans), F32),
            jax.ShapeDtypeStruct((5, KEYS, 3 * 128), BF16),
            jax.ShapeDtypeStruct((5, HEADS * HP, KEYS), BF16),
        ),
        [
            pltpu.VMEM((2, height + 2 * RIM, 2 * EDGE, chans), F32),
            pltpu.VMEM((2, (height + 2 * RIM) * (WIN + RIM), 256), F32),
            pltpu.VMEM(((height + 2 * RIM) * (WIN + RIM), chans), F32),
            pltpu.VMEM((3 * span, 256), F32),
            *attention_scratch(4),
            pltpu.VMEM((height, span, chans), F32),
        ],
        5_000_000_000,
        4_000_000,
    )(*args)


def middle_block(*args):
    height, cols, chans = args[0].shape
    span = cols + 2 * STRIP
    feats = args[-6].shape[2]
    return call(
        middle_kernel,
        (
            jax.ShapeDtypeStruct((height, span, 768), BF16),
            jax.ShapeDtypeStruct((height + 4, span + STRIP, chans), F32),
            jax.ShapeDtypeStruct((9 * 256, chans), BF16),
            jax.ShapeDtypeStruct((3 * 256, 3 * feats), BF16),
            jax.ShapeDtypeStruct((3 * 256, 4 * feats), BF16),
        ),
        [*attention_scratch(3), pltpu.VMEM((height, span + STRIP, chans), F32)],
        5_000_000_000,
        4_000_000,
    )(*args)


def conv_kernel(
    taps_ref,
    base,
    back_two_ref,
    back_one_ref,
    wg_scr,
    wb_scr,
    wu_scr,
    out_ref,
    image,
    halo_taps,
    grouped,
    sums,
    lowfeat,
    low_taps,
    out_scr,
):
    height, span = taps_ref.shape[:2]
    cols = span - 2 * STRIP
    chans = base.shape[2]
    feats = out_ref.shape[0]
    at_left, at_right, at_top, at_bottom, even_row, _ = at_edges()
    image[:, span:] = jnp.zeros((6, STRIP, chans), F32)
    sides = from_sides(even_row, back_one_ref[...], back_two_ref[...])
    for rows, packed in ((slice(0, 3), sides[0]), (slice(3, 6), sides[1])):
        image[rows, 0:span, 0:128] = packed[0 : 3 * span].reshape(3, span, 128)
        rest = unhalve(packed[3 * span :], 3 * span).reshape(3, span, 128)
        image[rows, 0:span, 128:chans] = rest[:, :, 0 : chans - 128]
    fill_taps(halo_taps, image, span)
    grouped[:, :, 128:256] = jnp.zeros((height + 4, span, 128), BF16)
    part = 4
    col = lax.broadcasted_iota(jnp.int32, (span, chans), 0) - 2
    keep_grouped = (col < cols + 2) & ((col >= 0) | jnp.logical_not(at_left))
    keep_grouped = keep_grouped & ((col < cols) | jnp.logical_not(at_right))
    low_span = cols + 8
    col = lax.broadcasted_iota(jnp.int32, (low_span, 128), 0) - 1
    keep_low = (col <= cols) & ((col >= 0) | jnp.logical_not(at_left))
    keep_low = keep_low & ((col < cols) | jnp.logical_not(at_right))
    left_half = lax.broadcasted_iota(jnp.int32, (cols, 128), 1) < feats
    spot = lax.broadcasted_iota(jnp.int32, (256, 256), 0)
    place = lax.broadcasted_iota(jnp.int32, (256, 256), 1)
    spread = (spot % 128 // cols == place // 128) & (
        spot % cols * 2 + spot // 128 == place % 128
    )
    spread = spread.astype(F32).astype(BF16)

    def tap_row(row):
        if 3 <= row < height + 3:
            return taps_ref[row - 3]
        return halo_taps[row if row < 3 else row - height]

    def group(h):
        totals = []
        for h2 in range(h, h + part, 2):
            lhs = jnp.concatenate(
                [
                    jnp.concatenate([tap_row(h2 + a), tap_row(h2 + a + 1)], axis=0)
                    for a in range(3)
                ],
                axis=1,
            )
            totals.append(dot(lhs, wg_scr[...]).reshape(2, span, chans))
        total = jnp.concatenate(totals, axis=0)
        total = total + base[h : h + part, STRIP - 2 : STRIP - 2 + span, :]
        for r in range(part):
            mask = keep_grouped
            if h + r < 2:
                mask = mask & jnp.logical_not(at_top)
            if h + r >= height + 2:
                mask = mask & jnp.logical_not(at_bottom)
            grouped[h + r, 0:span, 0:chans] = jnp.where(mask, total[r], 0.0).astype(BF16)

    def narrow(h, count):
        lhs = jnp.concatenate(
            [grouped[h + a : h + a + count].reshape(count * span, 256) for a in range(3)], axis=1
        )
        slot = h // part % 2
        sums[slot, 0:count, :, 0 : 3 * feats] = dot(lhs, wb_scr[...]).reshape(count, span, 3 * feats)
        for r in range(count):
            total = sums[slot, r, 0:low_span, 0:128]
            total = total + pltpu.roll(sums[slot, r, 1 : low_span + 1, 0:128], feats, 1)
            total = total + sums[slot, r, 2 : low_span + 2, 128:256]
            mask = keep_low
            if h + r == 0:
                mask = mask & jnp.logical_not(at_top)
            if h + r == height + 1:
                mask = mask & jnp.logical_not(at_bottom)
            lowfeat[h + r] = jnp.where(mask, jnp.where(total >= 0, total, 0.01 * total), 0.0)
            low_taps[h + r, :, 0:128] = jnp.where(
                left_half, lowfeat[h + r, 0:cols], pltpu.roll(lowfeat[h + r, 1 : cols + 1], feats, 1)
            ).astype(BF16)
            low_taps[h + r, :, 128:256] = jnp.where(
                left_half, lowfeat[h + r, 2 : cols + 2], 0.0
            ).astype(BF16)

    def expand(h):
        lhs = jnp.concatenate(
            [low_taps[h + a : h + a + part].reshape(part * cols, 256) for a in range(3)], axis=1
        )
        total = dot(lhs, wu_scr[...])
        for pair in range(part // 2):
            turned = total[2 * cols * pair : 2 * cols * (pair + 1)].T.astype(BF16)
            lhs = [
                jnp.concatenate(
                    [turned[(2 * a + b) * feats : (2 * a + b + 1) * feats] for b in range(2)], axis=1
                )
                for a in range(2)
            ]
            final = dot(jnp.concatenate(lhs, axis=0), spread)
            for r in range(2):
                for a in range(2):
                    row = 2 * (h + 2 * pair + r) + a
                    out_scr[pl.ds(row, feats, stride=2 * height), :] = final[
                        a * feats : (a + 1) * feats, 128 * r : 128 * (r + 1)
                    ]

    narrowed = expanded = done = 0
    while expanded < height:
        expand_to, narrow_to = min(narrowed - 2, height), min(done - 2, height + 2)
        if done < height + 4:
            group(done)
            done += part
        while narrowed < narrow_to:
            count = min(part, height + 2 - narrowed)
            if narrowed + count > narrow_to:
                break
            narrow(narrowed, count)
            narrowed += count
        while expanded + part <= expand_to:
            expand(expanded)
            expanded += part
    out_ref[...] = out_scr[...].reshape(feats, 2 * height, 128).astype(BF16)


def convs(*args):
    height, span = args[0].shape[:2]
    chans = args[1].shape[2]
    cols = span - 2 * STRIP
    feats = args[-1].shape[1] // 4
    return call(
        conv_kernel,
        jax.ShapeDtypeStruct((feats, 2 * height, 2 * cols), BF16),
        [
            pltpu.VMEM((6, span + STRIP, chans), F32),
            pltpu.VMEM((6, span, 768), BF16),
            pltpu.VMEM((height + 4, span, 256), BF16),
            pltpu.VMEM((2, 4, span, 256), F32),
            pltpu.VMEM((height + 2, cols + 8, 128), F32),
            pltpu.VMEM((height + 2, cols, 256), BF16),
            pltpu.VMEM((feats * 2 * height, 128), F32),
        ],
        8_000_000_000,
        4_000_000,
    )(*args)


def swapped(axis, first, second):
    count = lax.axis_size(axis)
    out = []
    for start, payload in ((1, second), (0, first)):
        pairs = [(i, i + 1) for i in range(start, count - 1, 2)]
        pairs = pairs + [(b, a) for a, b in pairs]
        out.append(lax.ppermute(payload, axis, pairs))
    return out[::-1]


def on_device(
    features,
    gain_one,
    qkv_weight,
    bias_table,
    proj_weight,
    gain_two,
    hidden_weight,
    output_weight,
    group_conv,
    before_conv,
    upsample_conv,
):
    height, cols, chans = features.shape
    even_row = lax.axis_index("rows") % 2 == 0
    low, high = features[:RIM], features[height - RIM :]
    row_one, row_two = swapped(
        "rows", jnp.where(even_row, high, low), jnp.where(even_row, low, high)
    )
    col_one, col_two = swapped("cols", *pack(features, row_one, row_two))

    bias = build_bias(bias_table)
    gain_one, gain_two = gain_one.reshape(1, chans), gain_two.reshape(1, chans)
    post = (gain_two, hidden_weight, output_weight.T)
    nrm, wk, wqv, wp, inner_k, inner_v, inner_border, inner_mid = inner_block(
        features,
        row_one,
        row_two,
        gain_one,
        qkv_weight,
        proj_weight,
        bias,
        *post,
    )
    back_one, back_two, edge, side, strips, keys, values = outer_block(
        features,
        nrm,
        col_two,
        col_one,
        gain_one,
        wk,
        wqv,
        wp,
        inner_k,
        inner_v,
        inner_border,
        bias,
        *post,
    )
    back_one, back_two = swapped("rows", back_one, back_two)
    taps, base, group, before, upsample = middle_block(
        features,
        nrm,
        keys,
        values,
        wqv,
        wp,
        inner_mid,
        edge,
        side,
        strips,
        row_two,
        row_one,
        group_conv,
        before_conv.transpose(0, 1, 3, 2),
        upsample_conv,
        bias,
        *post,
    )
    return convs(taps, base, back_two, back_one, group, before, upsample)


def solution(mesh):
    placed = (P("rows", "cols", None), P(), P(), P(), P(), P(), P(), P(), P(), P(), P())
    return jax.shard_map(
        on_device, mesh=mesh, in_specs=placed, out_specs=P(None, "rows", "cols"), check_vma=False
    )
```

```python
import functools

import jax
import jax.numpy as jnp
import numpy as np
from jax import lax
from jax.experimental import pallas as pl
from jax.experimental.pallas import tpu as pltpu
from jax.sharding import PartitionSpec as P

HEADS = 6
HD = 30
HP = 32
WIN = 16
KWIN = 24
KEYS = KWIN * KWIN
SIDE = WIN + KWIN - 1
RIM = (KWIN - WIN) // 2
EDGE = WIN + 2 * RIM
STRIP = 8
SIDE_COLS = 4
LOG2E = 1.4426950408889634
F32 = jnp.float32
BF16 = jnp.bfloat16
NT = (((1,), (1,)), ((), ()))
TN = (((0,), (0,)), ((), ()))


def dot(a, b):
    return jnp.dot(a, b, preferred_element_type=F32)


def dot_nt(a, b):
    return lax.dot_general(a, b, NT, preferred_element_type=F32)


def layer_norm(values, gain):
    center = values - jnp.mean(values, axis=-1, keepdims=True)
    spread = jnp.mean(center * center, axis=-1, keepdims=True)
    return center * lax.rsqrt(spread + 1e-05) * gain


def call(kernel, out_shape, scratch, flops, bytes_accessed):
    return pl.pallas_call(
        kernel,
        out_shape=out_shape,
        scratch_shapes=scratch,
        compiler_params=pltpu.CompilerParams(vmem_limit_bytes=24 * 2**20),
        cost_estimate=pl.CostEstimate(
            flops=flops, bytes_accessed=bytes_accessed, transcendentals=0
        ),
    )


def bias_kernel(table_ref, out_ref, t_scr, e_scr, w_scr, x_scr):
    for d in range(SIDE):
        t_scr[8 * d : 8 * d + HEADS, 0:SIDE] = jnp.exp(table_ref[:, SIDE * d : SIDE * (d + 1)])

    def head(h, carry):
        values = t_scr[pl.ds(h, SIDE, stride=8), 0:SIDE].astype(BF16)

        def expand(cols, first, shift=0):
            width = -(-(SIDE * cols + shift) // 128) * 128
            spot = (lax.broadcasted_iota(jnp.int32, (SIDE, width), 1) - shift) // cols
            row = lax.broadcasted_iota(jnp.int32, (SIDE, width), 0)
            pick = (spot == SIDE - 1 - row).astype(F32).astype(BF16)
            e_scr[0:SIDE, 0:width] = lax.dot_general(values, pick, TN, preferred_element_type=F32)
            lane = lax.broadcasted_iota(jnp.int32, (KWIN, width), 1) % cols
            out = jnp.zeros((KWIN, width), F32)
            for jj in range(cols):
                start = WIN - 1 - first - jj
                out = jnp.where(lane == jj, e_scr[start : start + KWIN, 0:width], out)
            w_scr[:, 0:width] = out

        lanes = lax.broadcasted_iota(jnp.int32, (KWIN, 128), 1)
        expand(WIN, 0)
        whole = w_scr[...]
        for phase in range(8):
            turned = whole if phase == 0 else pltpu.roll(whole, 640 - WIN * phase, 1)
            for p in range(KWIN):
                rows = slice(p * KWIN, (p + 1) * KWIN)
                if (23 - p) % 8 == phase:
                    at = (23 - p) // 8 * 128
                    low, high = turned[:, at : at + 128], turned[:, at + 128 : at + 256]
                    x_scr[0, rows] = jnp.where(lanes < 64, low, high)
                if (27 - p) % 8 == phase:
                    at = (27 - p) // 8 * 128
                    x_scr[1, rows] = turned[:, at : at + 128]
        out_ref[1, h] = x_scr[0].astype(BF16)
        out_ref[2, h] = x_scr[1].astype(BF16)
        expand(SIDE_COLS, WIN - SIDE_COLS)
        left = w_scr[:, 0:256]
        expand(SIDE_COLS, 0, 64)
        right = w_scr[:, 0:256]
        whole = jnp.concatenate([left, right], axis=0)
        for p in range(KWIN):
            rows = slice(p * KWIN, (p + 1) * KWIN)
            at = (23 - p) * SIDE_COLS
            turned = whole if at == 0 else pltpu.roll(whole, 256 - at, 1)
            x_scr[0, rows] = jnp.where(lanes < 64, turned[0:KWIN, 0:128], turned[KWIN:, 0:128])
        out_ref[0, h] = x_scr[0].astype(BF16)
        return carry

    lax.fori_loop(0, HEADS, head, 0)


def build_bias(bias_table):
    return call(
        bias_kernel,
        jax.ShapeDtypeStruct((3, HEADS, KEYS, 128), BF16),
        [
            pltpu.VMEM((8 * SIDE, 128), F32),
            pltpu.VMEM((SIDE + 1, 640), F32),
            pltpu.VMEM((KWIN, 640), F32),
            pltpu.VMEM((2, KEYS, 128), F32),
        ],
        4_000_000_000,
        4_000_000,
    )(bias_table.T)


def one_hot(shape, row_of, col_of):
    row = lax.broadcasted_iota(jnp.int32, shape, 0)
    col = lax.broadcasted_iota(jnp.int32, shape, 1)
    return (row_of(row) == col_of(col)).astype(F32).astype(BF16)


def spread_head(place):
    return jnp.where(place % HP < HD, place // HP * HD + place % HP, -1)


def weights_into(qkv_ref, proj_ref, wk_ref, wqv_ref, wp_ref):
    chans = qkv_ref.shape[0]
    width = HEADS * HP
    qkv = qkv_ref[...]
    pick = one_hot(
        (3 * chans, 3 * 128),
        lambda row: row,
        lambda col: jnp.where(
            (col % 128 < 2 * HP) & (col % HP < HD),
            chans + (col // 128 * 2 + col % 128 // HP) * HD + col % HP,
            -1,
        ),
    )
    wk_ref[...] = dot(qkv, pick).astype(BF16)
    pick = one_hot(
        (2 * width, 3 * chans),
        lambda row: jnp.where(
            row % HP < HD, row // HP * HD + row % HP + jnp.where(row < width, 0, chans), -1
        ),
        lambda col: col,
    )
    wqv_ref[...] = dot_nt(pick, qkv).astype(BF16)
    pick = one_hot((width, chans), spread_head, lambda col: col)
    wp_ref[...] = dot(pick, proj_ref[...]).astype(BF16)


def set_queries(q_scr, wqv_ref, groups, strips=None):
    scale = LOG2E / np.sqrt(HD)
    rows = jnp.concatenate([rows.reshape(128, rows.shape[-1]) for rows in groups], axis=0)
    queries = (dot_nt(wqv_ref[0 : HEADS * HP], rows.astype(BF16)) * scale).astype(BF16)
    none = jnp.zeros((HP, 128), BF16)
    left = lax.broadcasted_iota(jnp.int32, (HP, 128), 1) < 64
    for g in range(len(groups)):
        lanes = slice(128 * g, 128 * g + 128)
        for t in range(HEADS // 2):
            one = queries[2 * t * HP : (2 * t + 1) * HP, lanes]
            two = queries[(2 * t + 1) * HP : (2 * t + 2) * HP, lanes]
            if g == strips:
                q_scr[g, t, 2 * HP : 3 * HP] = jnp.concatenate([jnp.where(left, none, one), none], axis=1)
                q_scr[g, t, 3 * HP : 4 * HP] = jnp.concatenate([none, jnp.where(left, none, two)], axis=1)
                one, two = jnp.where(left, one, none), jnp.where(left, two, none)
            elif strips is not None:
                q_scr[g, t, 2 * HP : 4 * HP] = jnp.zeros((2 * HP, 256), BF16)
            q_scr[g, t, 0:HP] = jnp.concatenate([one, none], axis=1)
            q_scr[g, t, HP : 2 * HP] = jnp.concatenate([none, two], axis=1)


def lookup(g, values):
    out = values[0]
    for index in range(1, len(values)):
        out = jnp.where(g >= index, values[index], out)
    return out


def attention(kinds, windows, q_scr, k_ref, v_ref, bias_ref, wp_ref, s_scr, m_scr, p_scr, o_scr, v_right=None):
    groups = len(kinds)
    pairs = HEADS // 2
    step = 144
    depth = 2 * HP if v_right is None else 4 * HP
    left = lax.broadcasted_iota(jnp.int32, (HP, 128), 1) < 64

    def keep(g, t, k0, top):
        keys = k_ref[lookup(g, windows), k0 : k0 + step, 128 * t : 128 * t + depth]
        one = dot(keys, q_scr[g, t])
        s_scr[t, k0 : k0 + step] = one
        part = jnp.max(one.reshape(step // 8, 8, 256), axis=0)
        return part if top is None else jnp.maximum(top, part)

    def sum_values(g, t):
        for half in range(2):
            head = 2 * t + half
            lanes = slice(128 * half, 128 * half + 128)
            window, rows = lookup(g, windows), slice(head * HP, (head + 1) * HP)
            values = v_ref[window, rows]
            if v_right is None:
                o_scr[g, head] = dot(values, p_scr[t, :, lanes])
            else:
                values = jnp.concatenate([values, v_right[window, rows]], axis=0)
                both = dot(values, p_scr[t, :, lanes])
                o_scr[g, head] = jnp.where(left, both[0:HP], both[HP : 2 * HP])

    top = None
    for k0 in range(0, KEYS, step):
        top = keep(0, 0, k0, top)
    m_scr[...] = top
    p_scr[pairs - 1] = jnp.zeros((KEYS, 256), BF16)

    def attend(g, carry):
        kind = lookup(g, kinds)
        top = m_scr[...]
        for t in range(pairs):
            top = jnp.max(top, axis=0, keepdims=True)
            if t == 0:
                sum_values(jnp.maximum(g - 1, 0), pairs - 1)
            else:
                sum_values(g, t - 1)
            following = g if t + 1 < pairs else jnp.minimum(g + 1, groups - 1)
            later = None
            for k0 in range(0, KEYS, step):
                prob = jnp.exp2(s_scr[t, k0 : k0 + step] - top).astype(BF16)
                for half in range(2):
                    lanes = slice(128 * half, 128 * half + 128)
                    p_scr[t, k0 : k0 + step, lanes] = (
                        prob[:, lanes] * bias_ref[kind, 2 * t + half, k0 : k0 + step]
                    )
                later = keep(following, (t + 1) % pairs, k0, later)
            top = later
        m_scr[...] = top
        return carry

    lax.fori_loop(0, groups, attend, 0)
    sum_values(groups - 1, pairs - 1)
    attended = []
    for g in range(groups):
        parts = []
        for head in range(HEADS):
            one = o_scr[g, head]
            parts.append((one * (1.0 / one[HD : HD + 1])).astype(BF16))
        attended.append(jnp.concatenate(parts, axis=0))
    attended = jnp.concatenate(attended, axis=1)
    return lax.dot_general(attended, wp_ref[...], TN, preferred_element_type=F32)


def feed_forward(first, gain, hidden_ref, output_ref):
    normed = layer_norm(first, gain).astype(BF16)
    inner = dot(normed, hidden_ref[...])
    inner = (0.5 * inner * (1.0 + lax.erf(inner * np.float32(np.sqrt(0.5))))).astype(BF16)
    return first + dot_nt(inner, output_ref[...])


def feed_groups(first, gain, hidden_ref, output_ref, batch):
    out = []
    for start in range(0, first.shape[0], 128 * batch):
        mixed = feed_forward(first[start : start + 128 * batch], gain, hidden_ref, output_ref)
        out += [mixed[128 * g : 128 * (g + 1)] for g in range(batch)]
    return out


def project(keys, wk_ref, wqv_ref, k_ref, v_ref, index):
    keys = keys.reshape(KEYS, keys.shape[2]).astype(BF16)
    k_ref[index] = dot(keys, wk_ref[...]).astype(BF16)
    v_ref[index] = project_values(keys, wqv_ref)


def project_values(keys, wqv_ref):
    width = HEADS * HP
    one_row = (lax.broadcasted_iota(jnp.int32, (width, 1), 0) % HP == HD).astype(F32)
    return (dot_nt(wqv_ref[width : 2 * width], keys) + one_row).astype(BF16)


def at_edges():
    row, column = lax.axis_index("rows"), lax.axis_index("cols")
    return (
        column == 0,
        column == lax.axis_size("cols") - 1,
        row == 0,
        row == lax.axis_size("rows") - 1,
        row % 2 == 0,
        column % 2 == 0,
    )


def from_sides(even, first, second):
    first, second = first.astype(F32), second.astype(F32)
    return jnp.where(even, second, first), jnp.where(even, first, second)


def border_rows(ref, c0):
    return jnp.concatenate([ref[0:4, c0 : c0 + WIN], ref[12:16, c0 : c0 + WIN]], axis=0)


def halves(wide, count):
    left = lax.broadcasted_iota(jnp.int32, (1, 128), 1) < 64
    rest = wide.shape[0] - count
    out = jnp.where(left, wide[0:rest], pltpu.roll(wide[count:], 64, 1))
    return out if rest == count else jnp.concatenate([out, wide[rest:count]], axis=0)


def unhalve(packed, rows):
    count = packed.shape[0]
    return jnp.concatenate([packed, pltpu.roll(packed[0 : rows - count], 64, 1)], axis=0)


def pack_kernel(own_ref, row_one_ref, row_two_ref, pay_one_ref, pay_two_ref, x_scr, flat):
    height, cols, chans = own_ref.shape
    even_row, even_col = at_edges()[4:]
    above, below = from_sides(even_row, row_one_ref[...], row_two_ref[...])
    x_scr[0:RIM] = above
    x_scr[RIM : RIM + height] = own_ref[...].astype(F32)
    x_scr[RIM + height :] = below
    for side, near, far in ((0, 0, WIN), (1, cols - WIN, cols - WIN - RIM)):
        for r in range(height + 2 * RIM):
            flat[side, WIN * r : WIN * (r + 1), 0:chans] = x_scr[r, near : near + WIN]
            place = WIN * (height + 2 * RIM) + RIM * r
            flat[side, place : place + RIM, 0:chans] = x_scr[r, far : far + RIM]
    count = flat.shape[1]
    for lanes in (slice(0, 128), slice(128, 256)):
        low, high = flat[0, :, lanes], flat[1, :, lanes]
        one, two = jnp.where(even_col, high, low), jnp.where(even_col, low, high)
        rows = slice(0, count)
        if lanes.start:
            one, two = halves(one, count // 2), halves(two, count // 2)
            rows = slice(count, count + count // 2)
        pay_one_ref[rows] = one.astype(BF16)
        pay_two_ref[rows] = two.astype(BF16)


def pack(own, row_one, row_two):
    height, cols, chans = own.shape
    pixels = (height + 2 * RIM) * (WIN + RIM)
    pay = jax.ShapeDtypeStruct((pixels * 3 // 2, 128), BF16)
    return call(
        pack_kernel,
        (pay, pay),
        [
            pltpu.VMEM((height + 2 * RIM, cols, chans), F32),
            pltpu.VMEM((2, pixels, 256), F32),
        ],
        1_000_000,
        1_000_000,
    )(own, row_one, row_two)


def inner_kernel(
    own_ref,
    row_one_ref,
    row_two_ref,
    gain_one_ref,
    qkv_ref,
    proj_ref,
    bias_ref,
    gain_two_ref,
    hidden_ref,
    output_ref,
    nrm_ref,
    wk_ref,
    wqv_ref,
    wp_ref,
    k_ref,
    v_ref,
    border_ref,
    mid_ref,
    q_scr,
    s_scr,
    m_scr,
    p_scr,
    o_scr,
):
    height, cols, chans = own_ref.shape
    inner = cols // WIN - 2
    flags = at_edges()
    weights_into(qkv_ref, proj_ref, wk_ref, wqv_ref, wp_ref)
    gain_one = gain_one_ref[...]
    for r in range(RIM):
        above, below = from_sides(flags[4], row_one_ref[r], row_two_ref[r])
        nrm_ref[r] = layer_norm(above, gain_one)
        nrm_ref[RIM + height + r] = layer_norm(below, gain_one)
    for r in range(height):
        nrm_ref[RIM + r] = layer_norm(own_ref[r].astype(F32), gain_one)
    kinds, windows, first, queries = [], [], [], []
    for w in range(inner):
        c0 = WIN * (w + 1)
        project(nrm_ref[:, c0 - RIM : c0 - RIM + KWIN], wk_ref, wqv_ref, k_ref, v_ref, w)
        first.append(border_rows(own_ref, c0).reshape(128, chans))
        queries.append(border_rows(nrm_ref.at[RIM : RIM + height], c0))
        kinds.append(1)
        windows.append(w)
    for w in range(inner - 1):
        c0 = WIN * (w + 1)
        first.append(own_ref[4:12, c0 : c0 + WIN].reshape(128, chans))
        queries.append(nrm_ref[RIM + 4 : RIM + 12, c0 : c0 + WIN])
        kinds.append(2)
        windows.append(w)
    groups = len(kinds)
    set_queries(q_scr, wqv_ref, queries)
    first = jnp.concatenate(first, axis=0).astype(F32) + attention(
        kinds, windows, q_scr, k_ref, v_ref, bias_ref, wp_ref, s_scr, m_scr, p_scr, o_scr
    )
    mixed = feed_groups(first, gain_two_ref[...], hidden_ref, output_ref, len(kinds))
    for g in range(groups):
        one = mixed[g].reshape(8, WIN, chans)
        if g < inner:
            border_ref[:, WIN * g : WIN * (g + 1)] = one
        else:
            mid_ref[:, WIN * (g - inner) : WIN * (g - inner + 1)] = one


def outer_kernel(
    own_ref,
    nrm_ref,
    col_two_ref,
    col_one_ref,
    gain_one_ref,
    wk_ref,
    wqv_ref,
    wp_ref,
    inner_k_ref,
    inner_v_ref,
    inner_border_ref,
    bias_ref,
    gain_two_ref,
    hidden_ref,
    output_ref,
    pay_one_ref,
    pay_two_ref,
    edge_ref,
    side_ref,
    strip_ref,
    k_ref,
    v_ref,
    side_scr,
    x_scr,
    n_scr,
    b_scr,
    strips,
    v_right,
    q_scr,
    s_scr,
    m_scr,
    p_scr,
    o_scr,
    image,
):
    height, cols, chans = own_ref.shape
    inner = cols // WIN - 2
    flags = at_edges()
    gain_one = gain_one_ref[...]
    rows = height + 2 * RIM
    pixels = rows * (WIN + RIM)
    both = from_sides(flags[5], col_one_ref[...], col_two_ref[...])
    for side in range(2):
        x_scr[side, :, 0:128] = both[side][0:pixels]
        x_scr[side, :, 128:256] = unhalve(both[side][pixels:], pixels)
        n_scr[...] = layer_norm(x_scr[side, :, 0:chans], gain_one)
        near, far = (EDGE - WIN, EDGE - WIN - RIM) if side == 0 else (EDGE, EDGE + WIN)
        for r in range(rows):
            side_scr[side, r, near : near + WIN] = n_scr[WIN * r : WIN * (r + 1)]
            place = WIN * rows + RIM * r
            side_scr[side, r, far : far + RIM] = n_scr[place : place + RIM]
        c0 = WIN - STRIP if side == 0 else 0
        x = x_scr[side, 0 : WIN * rows, 0:chans].reshape(rows, WIN, chans)
        strip_ref[side] = x[:, c0 : c0 + STRIP]
    side_scr[0, :, EDGE : 2 * EDGE] = nrm_ref[:, 0:EDGE]
    side_scr[1, :, 0:EDGE] = nrm_ref[:, cols - EDGE : cols]
    k_ref[2] = inner_k_ref[inner - 1]
    v_ref[2] = inner_v_ref[inner - 1]
    for index, side, c0 in ((1, 0, RIM + WIN), (3, 1, RIM)):
        project(side_scr[side, :, c0 : c0 + KWIN], wk_ref, wqv_ref, k_ref, v_ref, index)
        v_right[index] = v_ref[index]
    strip_keys = [
        side_scr[side, :, c0 : c0 + KWIN].reshape(KEYS, chans).astype(BF16)
        for side, c0 in ((0, RIM), (1, RIM + WIN))
    ]
    moved = pltpu.roll(wk_ref[...].astype(F32), 2 * HP, 1).astype(BF16)
    k_ref[0] = (dot(strip_keys[0], wk_ref[...]) + dot(strip_keys[1], moved)).astype(BF16)
    v_ref[0] = project_values(strip_keys[0], wqv_ref)
    v_right[0] = project_values(strip_keys[1], wqv_ref)
    n = SIDE_COLS
    for r in range(height):
        for side, c0, c1 in ((0, STRIP - n, EDGE - n), (1, 0, EDGE)):
            place = slice(64 * side + n * r, 64 * side + n * (r + 1))
            strips[0, place] = strip_ref[side, RIM + r, c0 : c0 + n]
            strips[1, place] = side_scr[side, RIM + r, c1 : c1 + n]
    first, queries = [strips[0]], [strips[1]]
    spots = (0, cols - WIN)
    for c0 in spots:
        first.append(border_rows(own_ref, c0).astype(F32).reshape(128, chans))
        queries.append(border_rows(nrm_ref.at[RIM : RIM + height], c0))
    set_queries(q_scr, wqv_ref, queries, 0)
    first = jnp.concatenate(first, axis=0) + attention(
        [0, 1, 1], [0, 1, 3], q_scr, k_ref, v_ref, bias_ref, wp_ref, s_scr, m_scr, p_scr, o_scr, v_right
    )
    image[:, 0:STRIP] = jnp.zeros((height, STRIP, chans), F32)
    image[:, STRIP + cols :] = jnp.zeros((height, STRIP, chans), F32)
    image[0:4, STRIP + WIN : STRIP + cols - WIN] = inner_border_ref[0:4]
    image[12:16, STRIP + WIN : STRIP + cols - WIN] = inner_border_ref[4:8]
    mixed = feed_groups(first, gain_two_ref[...], hidden_ref, output_ref, 3)
    row = lax.broadcasted_iota(jnp.int32, (128, chans), 0)
    outside = (flags[0] & (row < 64)) | (flags[1] & (row >= 64))
    strips[0] = jnp.where(outside, 0.0, mixed[0])
    for r in range(height):
        for side, c0 in ((0, STRIP - n), (1, STRIP + cols)):
            place = 64 * side + n * r
            image[r, c0 : c0 + n] = strips[0, place : place + n]
    for g in range(2):
        one = mixed[1 + g].reshape(8, WIN, chans)
        c0 = STRIP + spots[g]
        image[0:4, c0 : c0 + WIN] = one[0:4]
        image[12:16, c0 : c0 + WIN] = one[4:8]
    even = flags[4]
    count = 3 * image.shape[1]
    for pay_ref, rows in (
        (pay_one_ref, jnp.where(even, image[13:16], image[0:3])),
        (pay_two_ref, jnp.where(even, image[0:3], image[13:16])),
    ):
        b_scr[:, 0:chans] = rows.reshape(count, chans)
        pay_ref[0:count] = b_scr[:, 0:128].astype(BF16)
        pay_ref[count:] = halves(b_scr[:, 128:256], 128).astype(BF16)
    edge_ref[0:4] = image[0:4]
    edge_ref[4:8] = image[12:16]
    side_ref[:, 0:STRIP] = image[4:12, 0:STRIP]
    side_ref[:, STRIP : 2 * STRIP] = image[4:12, STRIP + cols :]


def fill_taps(taps_ref, image, span):
    chans = image.shape[2]
    for b in range(3):
        start = STRIP - 3 + b
        lanes = slice(256 * b + 128, 256 * b + 256)
        taps_ref[:, :, lanes] = jnp.zeros((taps_ref.shape[0], span, 128), BF16)
        taps_ref[:, :, 256 * b : 256 * b + chans] = image[:, start : start + span].astype(BF16)


def conv_weights(group_ref, before_ref, upsample_ref, wg_scr, wb_scr, wu_scr):
    chans = group_ref.shape[2]
    feats = before_ref.shape[2]
    pad = chans // 16 * 16
    for a in range(3):
        wb_scr[256 * a + pad : 256 * (a + 1)] = jnp.zeros((256 - pad, 3 * feats), BF16)
        wu_scr[256 * a + 3 * feats : 256 * (a + 1)] = jnp.zeros((256 - 3 * feats, 4 * feats), BF16)
        for b in range(3):
            wg_scr[256 * (3 * a + b) + pad : 256 * (3 * a + b + 1)] = jnp.zeros((256 - pad, chans), BF16)
            wg_scr[256 * (3 * a + b) : 256 * (3 * a + b) + chans] = group_ref[a, b]
    same = one_hot((chans, chans), lambda row: row, lambda col: col)
    order = one_hot(
        (4 * feats, 4 * feats), lambda row: row, lambda col: col % feats * 4 + col // feats
    )
    for a in range(3):
        part = before_ref[a].reshape(3 * feats, chans)
        wb_scr[256 * a : 256 * a + chans] = dot_nt(same, part).astype(BF16)
        part = upsample_ref[a].reshape(3 * feats, 4 * feats)
        wu_scr[256 * a : 256 * a + 3 * feats] = dot(part, order).astype(BF16)


def middle_kernel(
    own_ref,
    nrm_ref,
    k_ref,
    v_ref,
    wqv_ref,
    wp_ref,
    inner_mid_ref,
    edge_ref,
    side_ref,
    strip_ref,
    row_two_ref,
    row_one_ref,
    group_ref,
    before_ref,
    upsample_ref,
    bias_ref,
    gain_two_ref,
    hidden_ref,
    output_ref,
    taps_ref,
    base_ref,
    wg_ref,
    wb_ref,
    wu_ref,
    q_scr,
    s_scr,
    m_scr,
    p_scr,
    o_scr,
    image,
):
    height, cols, chans = own_ref.shape
    spots = (0, cols - 2 * WIN, cols - WIN)
    set_queries(q_scr, wqv_ref, [nrm_ref[RIM + 4 : RIM + 12, c0 : c0 + WIN] for c0 in spots])
    first = [own_ref[4:12, c0 : c0 + WIN].reshape(128, chans) for c0 in spots]
    first = jnp.concatenate(first, axis=0).astype(F32) + attention(
        [2, 2, 2], [1, 2, 3], q_scr, k_ref, v_ref, bias_ref, wp_ref, s_scr, m_scr, p_scr, o_scr
    )
    mixed = feed_groups(first, gain_two_ref[...], hidden_ref, output_ref, 3)
    span = cols + 2 * STRIP
    image[:, span:] = jnp.zeros((height, STRIP, chans), F32)
    image[0:4, 0:span] = edge_ref[0:4]
    image[4:12, 0:STRIP] = side_ref[:, 0:STRIP]
    image[4:12, STRIP + WIN : STRIP + cols - 2 * WIN] = inner_mid_ref[...]
    for g in range(3):
        c0 = STRIP + spots[g]
        image[4:12, c0 : c0 + WIN] = mixed[g].reshape(8, WIN, chans)
    image[4:12, STRIP + cols : span] = side_ref[:, STRIP : 2 * STRIP]
    image[12:16, 0:span] = edge_ref[4:8]
    fill_taps(taps_ref, image, span)
    conv_weights(group_ref, before_ref, upsample_ref, wg_ref, wb_ref, wu_ref)
    even_row = at_edges()[4]
    above, below = from_sides(even_row, row_one_ref[...], row_two_ref[...])
    base_ref[0:2, STRIP : STRIP + cols] = above[2:4]
    base_ref[2 : 2 + height, STRIP : STRIP + cols] = own_ref[...].astype(F32)
    base_ref[2 + height : 4 + height, STRIP : STRIP + cols] = below[0:2]
    rows = slice(2, height + 6)
    base_ref[:, 0:STRIP] = strip_ref[0, rows]
    base_ref[:, STRIP + cols : span] = strip_ref[1, rows]
    base_ref[:, span:] = jnp.zeros((height + 4, STRIP, chans), F32)


def attention_scratch(groups, depth=2 * HP):
    return [
        pltpu.VMEM((groups, HEADS // 2, depth, 256), BF16),
        pltpu.VMEM((HEADS // 2, KEYS, 256), F32),
        pltpu.VMEM((8, 256), F32),
        pltpu.VMEM((HEADS // 2, KEYS, 256), BF16),
        pltpu.VMEM((groups, HEADS, HP, 128), F32),
    ]


def inner_block(*args):
    height, cols, chans = args[0].shape
    inner = cols // WIN - 2
    width = HEADS * HP
    groups = 2 * inner - 1
    return call(
        inner_kernel,
        (
            jax.ShapeDtypeStruct((height + 2 * RIM, cols, chans), F32),
            jax.ShapeDtypeStruct((chans, 3 * 128), BF16),
            jax.ShapeDtypeStruct((2 * width, chans), BF16),
            jax.ShapeDtypeStruct((width, chans), BF16),
            jax.ShapeDtypeStruct((inner, KEYS, 3 * 128), BF16),
            jax.ShapeDtypeStruct((inner, width, KEYS), BF16),
            jax.ShapeDtypeStruct((8, WIN * inner, chans), F32),
            jax.ShapeDtypeStruct((8, WIN * (inner - 1), chans), F32),
        ),
        attention_scratch(groups),
        5_000_000_000,
        4_000_000,
    )(*args)


def outer_block(*args):
    height, cols, chans = args[0].shape
    span = cols + 2 * STRIP
    return call(
        outer_kernel,
        (
            jax.ShapeDtypeStruct((3 * span + 128, 128), BF16),
            jax.ShapeDtypeStruct((3 * span + 128, 128), BF16),
            jax.ShapeDtypeStruct((8, span, chans), F32),
            jax.ShapeDtypeStruct((8, 2 * STRIP, chans), F32),
            jax.ShapeDtypeStruct((2, height + 2 * RIM, STRIP, chans), F32),
            jax.ShapeDtypeStruct((4, KEYS, 3 * 128), BF16),
            jax.ShapeDtypeStruct((4, HEADS * HP, KEYS), BF16),
        ),
        [
            pltpu.VMEM((2, height + 2 * RIM, 2 * EDGE, chans), F32),
            pltpu.VMEM((2, (height + 2 * RIM) * (WIN + RIM), 256), F32),
            pltpu.VMEM(((height + 2 * RIM) * (WIN + RIM), chans), F32),
            pltpu.VMEM((3 * span, 256), F32),
            pltpu.VMEM((2, 128, chans), F32),
            pltpu.VMEM((4, HEADS * HP, KEYS), BF16),
            *attention_scratch(3, 4 * HP),
            pltpu.VMEM((height, span, chans), F32),
        ],
        5_000_000_000,
        4_000_000,
    )(*args)


def middle_block(*args):
    height, cols, chans = args[0].shape
    span = cols + 2 * STRIP
    feats = args[-6].shape[2]
    return call(
        middle_kernel,
        (
            jax.ShapeDtypeStruct((height, span, 768), BF16),
            jax.ShapeDtypeStruct((height + 4, span + STRIP, chans), F32),
            jax.ShapeDtypeStruct((9 * 256, chans), BF16),
            jax.ShapeDtypeStruct((3 * 256, 3 * feats), BF16),
            jax.ShapeDtypeStruct((3 * 256, 4 * feats), BF16),
        ),
        [*attention_scratch(3), pltpu.VMEM((height, span + STRIP, chans), F32)],
        5_000_000_000,
        4_000_000,
    )(*args)


def conv_kernel(
    taps_ref,
    base,
    back_two_ref,
    back_one_ref,
    wg_scr,
    wb_scr,
    wu_scr,
    out_ref,
    image,
    halo_taps,
    grouped,
    sums,
    lowfeat,
    low_taps,
    out_scr,
):
    height, span = taps_ref.shape[:2]
    cols = span - 2 * STRIP
    chans = base.shape[2]
    feats = out_ref.shape[0]
    at_left, at_right, at_top, at_bottom, even_row, _ = at_edges()
    image[:, span:] = jnp.zeros((6, STRIP, chans), F32)
    sides = from_sides(even_row, back_one_ref[...], back_two_ref[...])
    for rows, packed in ((slice(0, 3), sides[0]), (slice(3, 6), sides[1])):
        image[rows, 0:span, 0:128] = packed[0 : 3 * span].reshape(3, span, 128)
        rest = unhalve(packed[3 * span :], 3 * span).reshape(3, span, 128)
        image[rows, 0:span, 128:chans] = rest[:, :, 0 : chans - 128]
    fill_taps(halo_taps, image, span)
    grouped[:, :, 128:256] = jnp.zeros((height + 4, span, 128), BF16)
    part = 4
    col = lax.broadcasted_iota(jnp.int32, (span, chans), 0) - 2
    keep_grouped = (col < cols + 2) & ((col >= 0) | jnp.logical_not(at_left))
    keep_grouped = keep_grouped & ((col < cols) | jnp.logical_not(at_right))
    low_span = cols + 8
    col = lax.broadcasted_iota(jnp.int32, (low_span, 128), 0) - 1
    keep_low = (col <= cols) & ((col >= 0) | jnp.logical_not(at_left))
    keep_low = keep_low & ((col < cols) | jnp.logical_not(at_right))
    left_half = lax.broadcasted_iota(jnp.int32, (cols, 128), 1) < feats
    spot = lax.broadcasted_iota(jnp.int32, (256, 256), 0)
    place = lax.broadcasted_iota(jnp.int32, (256, 256), 1)
    spread = (spot % 128 // cols == place // 128) & (
        spot % cols * 2 + spot // 128 == place % 128
    )
    spread = spread.astype(F32).astype(BF16)

    def tap_row(row):
        if 3 <= row < height + 3:
            return taps_ref[row - 3]
        return halo_taps[row if row < 3 else row - height]

    def group(h):
        totals = []
        for h2 in range(h, h + part, 2):
            lhs = jnp.concatenate(
                [
                    jnp.concatenate([tap_row(h2 + a), tap_row(h2 + a + 1)], axis=0)
                    for a in range(3)
                ],
                axis=1,
            )
            totals.append(dot(lhs, wg_scr[...]).reshape(2, span, chans))
        total = jnp.concatenate(totals, axis=0)
        total = total + base[h : h + part, STRIP - 2 : STRIP - 2 + span, :]
        for r in range(part):
            mask = keep_grouped
            if h + r < 2:
                mask = mask & jnp.logical_not(at_top)
            if h + r >= height + 2:
                mask = mask & jnp.logical_not(at_bottom)
            grouped[h + r, 0:span, 0:chans] = jnp.where(mask, total[r], 0.0).astype(BF16)

    def narrow(h, count):
        lhs = jnp.concatenate(
            [grouped[h + a : h + a + count].reshape(count * span, 256) for a in range(3)], axis=1
        )
        slot = h // part % 2
        sums[slot, 0:count, :, 0 : 3 * feats] = dot(lhs, wb_scr[...]).reshape(count, span, 3 * feats)
        for r in range(count):
            total = sums[slot, r, 0:low_span, 0:128]
            total = total + pltpu.roll(sums[slot, r, 1 : low_span + 1, 0:128], feats, 1)
            total = total + sums[slot, r, 2 : low_span + 2, 128:256]
            mask = keep_low
            if h + r == 0:
                mask = mask & jnp.logical_not(at_top)
            if h + r == height + 1:
                mask = mask & jnp.logical_not(at_bottom)
            lowfeat[h + r] = jnp.where(mask, jnp.where(total >= 0, total, 0.01 * total), 0.0)
            low_taps[h + r, :, 0:128] = jnp.where(
                left_half, lowfeat[h + r, 0:cols], pltpu.roll(lowfeat[h + r, 1 : cols + 1], feats, 1)
            ).astype(BF16)
            low_taps[h + r, :, 128:256] = jnp.where(
                left_half, lowfeat[h + r, 2 : cols + 2], 0.0
            ).astype(BF16)

    def expand(h):
        lhs = jnp.concatenate(
            [low_taps[h + a : h + a + part].reshape(part * cols, 256) for a in range(3)], axis=1
        )
        total = dot(lhs, wu_scr[...])
        for pair in range(part // 2):
            turned = total[2 * cols * pair : 2 * cols * (pair + 1)].T.astype(BF16)
            lhs = [
                jnp.concatenate(
                    [turned[(2 * a + b) * feats : (2 * a + b + 1) * feats] for b in range(2)], axis=1
                )
                for a in range(2)
            ]
            final = dot(jnp.concatenate(lhs, axis=0), spread)
            for r in range(2):
                for a in range(2):
                    row = 2 * (h + 2 * pair + r) + a
                    out_scr[pl.ds(row, feats, stride=2 * height), :] = final[
                        a * feats : (a + 1) * feats, 128 * r : 128 * (r + 1)
                    ]

    narrowed = expanded = done = 0
    while expanded < height:
        expand_to, narrow_to = min(narrowed - 2, height), min(done - 2, height + 2)
        if done < height + 4:
            group(done)
            done += part
        while narrowed < narrow_to:
            count = min(part, height + 2 - narrowed)
            if narrowed + count > narrow_to:
                break
            narrow(narrowed, count)
            narrowed += count
        while expanded + part <= expand_to:
            expand(expanded)
            expanded += part
    out_ref[...] = out_scr[...].reshape(feats, 2 * height, 128).astype(BF16)


def convs(*args):
    height, span = args[0].shape[:2]
    chans = args[1].shape[2]
    cols = span - 2 * STRIP
    feats = args[-1].shape[1] // 4
    return call(
        conv_kernel,
        jax.ShapeDtypeStruct((feats, 2 * height, 2 * cols), BF16),
        [
            pltpu.VMEM((6, span + STRIP, chans), F32),
            pltpu.VMEM((6, span, 768), BF16),
            pltpu.VMEM((height + 4, span, 256), BF16),
            pltpu.VMEM((2, 4, span, 256), F32),
            pltpu.VMEM((height + 2, cols + 8, 128), F32),
            pltpu.VMEM((height + 2, cols, 256), BF16),
            pltpu.VMEM((feats * 2 * height, 128), F32),
        ],
        8_000_000_000,
        4_000_000,
    )(*args)


def swapped(axis, first, second):
    count = lax.axis_size(axis)
    out = []
    for start, payload in ((1, second), (0, first)):
        pairs = [(i, i + 1) for i in range(start, count - 1, 2)]
        pairs = pairs + [(b, a) for a, b in pairs]
        out.append(lax.ppermute(payload, axis, pairs))
    return out[::-1]


def on_device(
    features,
    gain_one,
    qkv_weight,
    bias_table,
    proj_weight,
    gain_two,
    hidden_weight,
    output_weight,
    group_conv,
    before_conv,
    upsample_conv,
):
    height, cols, chans = features.shape
    even_row = lax.axis_index("rows") % 2 == 0
    low, high = features[:RIM], features[height - RIM :]
    row_one, row_two = swapped(
        "rows", jnp.where(even_row, high, low), jnp.where(even_row, low, high)
    )
    col_one, col_two = swapped("cols", *pack(features, row_one, row_two))

    bias = build_bias(bias_table)
    gain_one, gain_two = gain_one.reshape(1, chans), gain_two.reshape(1, chans)
    post = (gain_two, hidden_weight, output_weight.T)
    nrm, wk, wqv, wp, inner_k, inner_v, inner_border, inner_mid = inner_block(
        features,
        row_one,
        row_two,
        gain_one,
        qkv_weight,
        proj_weight,
        bias,
        *post,
    )
    back_one, back_two, edge, side, strips, keys, values = outer_block(
        features,
        nrm,
        col_two,
        col_one,
        gain_one,
        wk,
        wqv,
        wp,
        inner_k,
        inner_v,
        inner_border,
        bias,
        *post,
    )
    back_one, back_two = swapped("rows", back_one, back_two)
    taps, base, group, before, upsample = middle_block(
        features,
        nrm,
        keys,
        values,
        wqv,
        wp,
        inner_mid,
        edge,
        side,
        strips,
        row_two,
        row_one,
        group_conv,
        before_conv.transpose(0, 1, 3, 2),
        upsample_conv,
        bias,
        *post,
    )
    return convs(taps, base, back_two, back_one, group, before, upsample)


def solution(mesh):
    placed = (P("rows", "cols", None), P(), P(), P(), P(), P(), P(), P(), P(), P(), P())
    return jax.shard_map(
        on_device, mesh=mesh, in_specs=placed, out_specs=P(None, "rows", "cols"), check_vma=False
    )
```

```python
import functools

import jax
import jax.numpy as jnp
import numpy as np
from jax import lax
from jax.experimental import pallas as pl
from jax.experimental.pallas import tpu as pltpu
from jax.sharding import PartitionSpec as P

HEADS = 6
HD = 30
HP = 32
WIN = 16
KWIN = 24
KEYS = KWIN * KWIN
SIDE = WIN + KWIN - 1
RIM = (KWIN - WIN) // 2
EDGE = WIN + 2 * RIM
STRIP = 8
SIDE_COLS = 4
LOG2E = 1.4426950408889634
F32 = jnp.float32
BF16 = jnp.bfloat16
NT = (((1,), (1,)), ((), ()))
TN = (((0,), (0,)), ((), ()))


def dot(a, b):
    return jnp.dot(a, b, preferred_element_type=F32)


def dot_nt(a, b):
    return lax.dot_general(a, b, NT, preferred_element_type=F32)


def layer_norm(values, gain):
    center = values - jnp.mean(values, axis=-1, keepdims=True)
    spread = jnp.mean(center * center, axis=-1, keepdims=True)
    return center * lax.rsqrt(spread + 1e-05) * gain


def call(kernel, out_shape, scratch, flops, bytes_accessed):
    return pl.pallas_call(
        kernel,
        out_shape=out_shape,
        scratch_shapes=scratch,
        compiler_params=pltpu.CompilerParams(vmem_limit_bytes=24 * 2**20),
        cost_estimate=pl.CostEstimate(
            flops=flops, bytes_accessed=bytes_accessed, transcendentals=0
        ),
    )


def bias_kernel(table_ref, out_ref, t_scr, e_scr, w_scr, x_scr):
    for d in range(SIDE):
        t_scr[8 * d : 8 * d + HEADS, 0:SIDE] = jnp.exp(table_ref[:, SIDE * d : SIDE * (d + 1)])

    def head(h, carry):
        values = t_scr[pl.ds(h, SIDE, stride=8), 0:SIDE].astype(BF16)

        def expand(cols, first, shift=0):
            width = -(-(SIDE * cols + shift) // 128) * 128
            spot = (lax.broadcasted_iota(jnp.int32, (SIDE, width), 1) - shift) // cols
            row = lax.broadcasted_iota(jnp.int32, (SIDE, width), 0)
            pick = (spot == SIDE - 1 - row).astype(F32).astype(BF16)
            e_scr[0:SIDE, 0:width] = lax.dot_general(values, pick, TN, preferred_element_type=F32)
            lane = lax.broadcasted_iota(jnp.int32, (KWIN, width), 1) % cols
            out = jnp.zeros((KWIN, width), F32)
            for jj in range(cols):
                start = WIN - 1 - first - jj
                out = jnp.where(lane == jj, e_scr[start : start + KWIN, 0:width], out)
            w_scr[:, 0:width] = out

        lanes = lax.broadcasted_iota(jnp.int32, (KWIN, 128), 1)
        expand(WIN, 0)
        whole = w_scr[...]
        for phase in range(8):
            turned = whole if phase == 0 else pltpu.roll(whole, 640 - WIN * phase, 1)
            for p in range(KWIN):
                rows = slice(p * KWIN, (p + 1) * KWIN)
                if (23 - p) % 8 == phase:
                    at = (23 - p) // 8 * 128
                    low, high = turned[:, at : at + 128], turned[:, at + 128 : at + 256]
                    x_scr[0, rows] = jnp.where(lanes < 64, low, high)
                if (27 - p) % 8 == phase:
                    at = (27 - p) // 8 * 128
                    x_scr[1, rows] = turned[:, at : at + 128]
        out_ref[1, h] = x_scr[0].astype(BF16)
        out_ref[2, h] = x_scr[1].astype(BF16)
        expand(SIDE_COLS, WIN - SIDE_COLS)
        left = w_scr[:, 0:256]
        expand(SIDE_COLS, 0, 64)
        right = w_scr[:, 0:256]
        whole = jnp.concatenate([left, right], axis=0)
        for p in range(KWIN):
            rows = slice(p * KWIN, (p + 1) * KWIN)
            at = (23 - p) * SIDE_COLS
            turned = whole if at == 0 else pltpu.roll(whole, 256 - at, 1)
            x_scr[0, rows] = jnp.where(lanes < 64, turned[0:KWIN, 0:128], turned[KWIN:, 0:128])
        out_ref[0, h] = x_scr[0].astype(BF16)
        return carry

    lax.fori_loop(0, HEADS, head, 0)


def build_bias(bias_table):
    return call(
        bias_kernel,
        jax.ShapeDtypeStruct((3, HEADS, KEYS, 128), BF16),
        [
            pltpu.VMEM((8 * SIDE, 128), F32),
            pltpu.VMEM((SIDE + 1, 640), F32),
            pltpu.VMEM((KWIN, 640), F32),
            pltpu.VMEM((2, KEYS, 128), F32),
        ],
        4_000_000_000,
        4_000_000,
    )(bias_table.T)


def one_hot(shape, row_of, col_of):
    row = lax.broadcasted_iota(jnp.int32, shape, 0)
    col = lax.broadcasted_iota(jnp.int32, shape, 1)
    return (row_of(row) == col_of(col)).astype(F32).astype(BF16)


def spread_head(place):
    return jnp.where(place % HP < HD, place // HP * HD + place % HP, -1)


def weights_into(qkv_ref, proj_ref, wk_ref, wqv_ref, wp_ref):
    chans = qkv_ref.shape[0]
    width = HEADS * HP
    qkv = qkv_ref[...]
    pick = one_hot(
        (3 * chans, 3 * 128),
        lambda row: row,
        lambda col: jnp.where(
            (col % 128 < 2 * HP) & (col % HP < HD),
            chans + (col // 128 * 2 + col % 128 // HP) * HD + col % HP,
            -1,
        ),
    )
    wk_ref[...] = dot(qkv, pick).astype(BF16)
    pick = one_hot(
        (2 * width, 3 * chans),
        lambda row: jnp.where(
            row % HP < HD, row // HP * HD + row % HP + jnp.where(row < width, 0, chans), -1
        ),
        lambda col: col,
    )
    wqv_ref[...] = dot_nt(pick, qkv).astype(BF16)
    pick = one_hot((width, chans), spread_head, lambda col: col)
    wp_ref[...] = dot(pick, proj_ref[...]).astype(BF16)


def set_queries(q_scr, wqv_ref, groups, strips=None):
    scale = LOG2E / np.sqrt(HD)
    rows = jnp.concatenate([rows.reshape(128, rows.shape[-1]) for rows in groups], axis=0)
    queries = (dot_nt(wqv_ref[0 : HEADS * HP], rows.astype(BF16)) * scale).astype(BF16)
    none = jnp.zeros((HP, 128), BF16)
    left = lax.broadcasted_iota(jnp.int32, (HP, 128), 1) < 64
    for g in range(len(groups)):
        lanes = slice(128 * g, 128 * g + 128)
        for t in range(HEADS // 2):
            one = queries[2 * t * HP : (2 * t + 1) * HP, lanes]
            two = queries[(2 * t + 1) * HP : (2 * t + 2) * HP, lanes]
            if g == strips:
                q_scr[g, t, 2 * HP : 3 * HP] = jnp.concatenate([jnp.where(left, none, one), none], axis=1)
                q_scr[g, t, 3 * HP : 4 * HP] = jnp.concatenate([none, jnp.where(left, none, two)], axis=1)
                one, two = jnp.where(left, one, none), jnp.where(left, two, none)
            elif strips is not None:
                q_scr[g, t, 2 * HP : 4 * HP] = jnp.zeros((2 * HP, 256), BF16)
            q_scr[g, t, 0:HP] = jnp.concatenate([one, none], axis=1)
            q_scr[g, t, HP : 2 * HP] = jnp.concatenate([none, two], axis=1)


def lookup(g, values):
    out = values[0]
    for index in range(1, len(values)):
        out = jnp.where(g >= index, values[index], out)
    return out


def attention(kinds, windows, q_scr, k_ref, v_ref, bias_ref, wp_ref, s_scr, m_scr, p_scr, o_scr, v_right=None):
    groups = len(kinds)
    pairs = HEADS // 2
    step = 144
    depth = 2 * HP if v_right is None else 4 * HP
    left = lax.broadcasted_iota(jnp.int32, (HP, 128), 1) < 64

    def keep(g, t, k0, top):
        keys = k_ref[lookup(g, windows), k0 : k0 + step, 128 * t : 128 * t + depth]
        one = dot(keys, q_scr[g, t])
        s_scr[t, k0 : k0 + step] = one
        part = jnp.max(one.reshape(step // 8, 8, 256), axis=0)
        return part if top is None else jnp.maximum(top, part)

    def sum_values(g, t):
        for half in range(2):
            head = 2 * t + half
            lanes = slice(128 * half, 128 * half + 128)
            window, rows = lookup(g, windows), slice(head * HP, (head + 1) * HP)
            values = v_ref[window, rows]
            if v_right is None:
                o_scr[g, head] = dot(values, p_scr[t, :, lanes])
            else:
                values = jnp.concatenate([values, v_right[window, rows]], axis=0)
                both = dot(values, p_scr[t, :, lanes])
                o_scr[g, head] = jnp.where(left, both[0:HP], both[HP : 2 * HP])

    top = None
    for k0 in range(0, KEYS, step):
        top = keep(0, 0, k0, top)
    m_scr[...] = top
    p_scr[pairs - 1] = jnp.zeros((KEYS, 256), BF16)

    def attend(g, carry):
        kind = lookup(g, kinds)
        top = m_scr[...]
        for t in range(pairs):
            top = jnp.max(top, axis=0, keepdims=True)
            if t == 0:
                sum_values(jnp.maximum(g - 1, 0), pairs - 1)
            else:
                sum_values(g, t - 1)
            following = g if t + 1 < pairs else jnp.minimum(g + 1, groups - 1)
            later = None
            for k0 in range(0, KEYS, step):
                later = keep(following, (t + 1) % pairs, k0, later)
                prob = jnp.exp2(s_scr[t, k0 : k0 + step] - top).astype(BF16)
                for half in range(2):
                    lanes = slice(128 * half, 128 * half + 128)
                    p_scr[t, k0 : k0 + step, lanes] = (
                        prob[:, lanes] * bias_ref[kind, 2 * t + half, k0 : k0 + step]
                    )
            top = later
        m_scr[...] = top
        return carry

    lax.fori_loop(0, groups, attend, 0)
    sum_values(groups - 1, pairs - 1)
    attended = []
    for g in range(groups):
        parts = []
        for head in range(HEADS):
            one = o_scr[g, head]
            parts.append((one * (1.0 / one[HD : HD + 1])).astype(BF16))
        attended.append(jnp.concatenate(parts, axis=0))
    attended = jnp.concatenate(attended, axis=1)
    return lax.dot_general(attended, wp_ref[...], TN, preferred_element_type=F32)


def feed_forward(first, gain, hidden_ref, output_ref):
    normed = layer_norm(first, gain).astype(BF16)
    inner = dot(normed, hidden_ref[...])
    inner = (0.5 * inner * (1.0 + lax.erf(inner * np.float32(np.sqrt(0.5))))).astype(BF16)
    return first + dot_nt(inner, output_ref[...])


def feed_groups(first, gain, hidden_ref, output_ref, batch):
    out = []
    for start in range(0, first.shape[0], 128 * batch):
        mixed = feed_forward(first[start : start + 128 * batch], gain, hidden_ref, output_ref)
        out += [mixed[128 * g : 128 * (g + 1)] for g in range(batch)]
    return out


def project(keys, wk_ref, wqv_ref, k_ref, v_ref, index):
    keys = keys.reshape(KEYS, keys.shape[2]).astype(BF16)
    k_ref[index] = dot(keys, wk_ref[...]).astype(BF16)
    v_ref[index] = project_values(keys, wqv_ref)


def project_values(keys, wqv_ref):
    width = HEADS * HP
    one_row = (lax.broadcasted_iota(jnp.int32, (width, 1), 0) % HP == HD).astype(F32)
    return (dot_nt(wqv_ref[width : 2 * width], keys) + one_row).astype(BF16)


def at_edges():
    row, column = lax.axis_index("rows"), lax.axis_index("cols")
    return (
        column == 0,
        column == lax.axis_size("cols") - 1,
        row == 0,
        row == lax.axis_size("rows") - 1,
        row % 2 == 0,
        column % 2 == 0,
    )


def from_sides(even, first, second):
    first, second = first.astype(F32), second.astype(F32)
    return jnp.where(even, second, first), jnp.where(even, first, second)


def border_rows(ref, c0):
    return jnp.concatenate([ref[0:4, c0 : c0 + WIN], ref[12:16, c0 : c0 + WIN]], axis=0)


def halves(wide, count):
    left = lax.broadcasted_iota(jnp.int32, (1, 128), 1) < 64
    rest = wide.shape[0] - count
    out = jnp.where(left, wide[0:rest], pltpu.roll(wide[count:], 64, 1))
    return out if rest == count else jnp.concatenate([out, wide[rest:count]], axis=0)


def unhalve(packed, rows):
    count = packed.shape[0]
    return jnp.concatenate([packed, pltpu.roll(packed[0 : rows - count], 64, 1)], axis=0)


def pack_kernel(own_ref, row_one_ref, row_two_ref, pay_one_ref, pay_two_ref, x_scr, flat):
    height, cols, chans = own_ref.shape
    even_row, even_col = at_edges()[4:]
    above, below = from_sides(even_row, row_one_ref[...], row_two_ref[...])
    x_scr[0:RIM] = above
    x_scr[RIM : RIM + height] = own_ref[...].astype(F32)
    x_scr[RIM + height :] = below
    for side, near, far in ((0, 0, WIN), (1, cols - WIN, cols - WIN - RIM)):
        for r in range(height + 2 * RIM):
            flat[side, WIN * r : WIN * (r + 1), 0:chans] = x_scr[r, near : near + WIN]
            place = WIN * (height + 2 * RIM) + RIM * r
            flat[side, place : place + RIM, 0:chans] = x_scr[r, far : far + RIM]
    count = flat.shape[1]
    for lanes in (slice(0, 128), slice(128, 256)):
        low, high = flat[0, :, lanes], flat[1, :, lanes]
        one, two = jnp.where(even_col, high, low), jnp.where(even_col, low, high)
        rows = slice(0, count)
        if lanes.start:
            one, two = halves(one, count // 2), halves(two, count // 2)
            rows = slice(count, count + count // 2)
        pay_one_ref[rows] = one.astype(BF16)
        pay_two_ref[rows] = two.astype(BF16)


def pack(own, row_one, row_two):
    height, cols, chans = own.shape
    pixels = (height + 2 * RIM) * (WIN + RIM)
    pay = jax.ShapeDtypeStruct((pixels * 3 // 2, 128), BF16)
    return call(
        pack_kernel,
        (pay, pay),
        [
            pltpu.VMEM((height + 2 * RIM, cols, chans), F32),
            pltpu.VMEM((2, pixels, 256), F32),
        ],
        1_000_000,
        1_000_000,
    )(own, row_one, row_two)


def inner_kernel(
    own_ref,
    row_one_ref,
    row_two_ref,
    gain_one_ref,
    qkv_ref,
    proj_ref,
    bias_ref,
    gain_two_ref,
    hidden_ref,
    output_ref,
    nrm_ref,
    wk_ref,
    wqv_ref,
    wp_ref,
    k_ref,
    v_ref,
    border_ref,
    mid_ref,
    q_scr,
    s_scr,
    m_scr,
    p_scr,
    o_scr,
):
    height, cols, chans = own_ref.shape
    inner = cols // WIN - 2
    flags = at_edges()
    weights_into(qkv_ref, proj_ref, wk_ref, wqv_ref, wp_ref)
    gain_one = gain_one_ref[...]
    for r in range(RIM):
        above, below = from_sides(flags[4], row_one_ref[r], row_two_ref[r])
        nrm_ref[r] = layer_norm(above, gain_one)
        nrm_ref[RIM + height + r] = layer_norm(below, gain_one)
    for r in range(height):
        nrm_ref[RIM + r] = layer_norm(own_ref[r].astype(F32), gain_one)
    kinds, windows, first, queries = [], [], [], []
    for w in range(inner):
        c0 = WIN * (w + 1)
        project(nrm_ref[:, c0 - RIM : c0 - RIM + KWIN], wk_ref, wqv_ref, k_ref, v_ref, w)
        first.append(border_rows(own_ref, c0).reshape(128, chans))
        queries.append(border_rows(nrm_ref.at[RIM : RIM + height], c0))
        kinds.append(1)
        windows.append(w)
    for w in range(inner - 1):
        c0 = WIN * (w + 1)
        first.append(own_ref[4:12, c0 : c0 + WIN].reshape(128, chans))
        queries.append(nrm_ref[RIM + 4 : RIM + 12, c0 : c0 + WIN])
        kinds.append(2)
        windows.append(w)
    groups = len(kinds)
    set_queries(q_scr, wqv_ref, queries)
    first = jnp.concatenate(first, axis=0).astype(F32) + attention(
        kinds, windows, q_scr, k_ref, v_ref, bias_ref, wp_ref, s_scr, m_scr, p_scr, o_scr
    )
    mixed = feed_groups(first, gain_two_ref[...], hidden_ref, output_ref, len(kinds))
    for g in range(groups):
        one = mixed[g].reshape(8, WIN, chans)
        if g < inner:
            border_ref[:, WIN * g : WIN * (g + 1)] = one
        else:
            mid_ref[:, WIN * (g - inner) : WIN * (g - inner + 1)] = one


def outer_kernel(
    own_ref,
    nrm_ref,
    col_two_ref,
    col_one_ref,
    gain_one_ref,
    wk_ref,
    wqv_ref,
    wp_ref,
    inner_k_ref,
    inner_v_ref,
    inner_border_ref,
    bias_ref,
    gain_two_ref,
    hidden_ref,
    output_ref,
    pay_one_ref,
    pay_two_ref,
    edge_ref,
    side_ref,
    strip_ref,
    k_ref,
    v_ref,
    side_scr,
    x_scr,
    n_scr,
    b_scr,
    strips,
    v_right,
    q_scr,
    s_scr,
    m_scr,
    p_scr,
    o_scr,
    image,
):
    height, cols, chans = own_ref.shape
    inner = cols // WIN - 2
    flags = at_edges()
    gain_one = gain_one_ref[...]
    rows = height + 2 * RIM
    pixels = rows * (WIN + RIM)
    both = from_sides(flags[5], col_one_ref[...], col_two_ref[...])
    for side in range(2):
        x_scr[side, :, 0:128] = both[side][0:pixels]
        x_scr[side, :, 128:256] = unhalve(both[side][pixels:], pixels)
        n_scr[...] = layer_norm(x_scr[side, :, 0:chans], gain_one)
        near, far = (EDGE - WIN, EDGE - WIN - RIM) if side == 0 else (EDGE, EDGE + WIN)
        for r in range(rows):
            side_scr[side, r, near : near + WIN] = n_scr[WIN * r : WIN * (r + 1)]
            place = WIN * rows + RIM * r
            side_scr[side, r, far : far + RIM] = n_scr[place : place + RIM]
        c0 = WIN - STRIP if side == 0 else 0
        x = x_scr[side, 0 : WIN * rows, 0:chans].reshape(rows, WIN, chans)
        strip_ref[side] = x[:, c0 : c0 + STRIP]
    side_scr[0, :, EDGE : 2 * EDGE] = nrm_ref[:, 0:EDGE]
    side_scr[1, :, 0:EDGE] = nrm_ref[:, cols - EDGE : cols]
    k_ref[2] = inner_k_ref[inner - 1]
    v_ref[2] = inner_v_ref[inner - 1]
    for index, side, c0 in ((1, 0, RIM + WIN), (3, 1, RIM)):
        project(side_scr[side, :, c0 : c0 + KWIN], wk_ref, wqv_ref, k_ref, v_ref, index)
        v_right[index] = v_ref[index]
    strip_keys = [
        side_scr[side, :, c0 : c0 + KWIN].reshape(KEYS, chans).astype(BF16)
        for side, c0 in ((0, RIM), (1, RIM + WIN))
    ]
    moved = pltpu.roll(wk_ref[...].astype(F32), 2 * HP, 1).astype(BF16)
    k_ref[0] = (dot(strip_keys[0], wk_ref[...]) + dot(strip_keys[1], moved)).astype(BF16)
    v_ref[0] = project_values(strip_keys[0], wqv_ref)
    v_right[0] = project_values(strip_keys[1], wqv_ref)
    n = SIDE_COLS
    for r in range(height):
        for side, c0, c1 in ((0, STRIP - n, EDGE - n), (1, 0, EDGE)):
            place = slice(64 * side + n * r, 64 * side + n * (r + 1))
            strips[0, place] = strip_ref[side, RIM + r, c0 : c0 + n]
            strips[1, place] = side_scr[side, RIM + r, c1 : c1 + n]
    first, queries = [strips[0]], [strips[1]]
    spots = (0, cols - WIN)
    for c0 in spots:
        first.append(border_rows(own_ref, c0).astype(F32).reshape(128, chans))
        queries.append(border_rows(nrm_ref.at[RIM : RIM + height], c0))
    set_queries(q_scr, wqv_ref, queries, 0)
    first = jnp.concatenate(first, axis=0) + attention(
        [0, 1, 1], [0, 1, 3], q_scr, k_ref, v_ref, bias_ref, wp_ref, s_scr, m_scr, p_scr, o_scr, v_right
    )
    image[:, 0:STRIP] = jnp.zeros((height, STRIP, chans), F32)
    image[:, STRIP + cols :] = jnp.zeros((height, STRIP, chans), F32)
    image[0:4, STRIP + WIN : STRIP + cols - WIN] = inner_border_ref[0:4]
    image[12:16, STRIP + WIN : STRIP + cols - WIN] = inner_border_ref[4:8]
    mixed = feed_groups(first, gain_two_ref[...], hidden_ref, output_ref, 3)
    row = lax.broadcasted_iota(jnp.int32, (128, chans), 0)
    outside = (flags[0] & (row < 64)) | (flags[1] & (row >= 64))
    strips[0] = jnp.where(outside, 0.0, mixed[0])
    for r in range(height):
        for side, c0 in ((0, STRIP - n), (1, STRIP + cols)):
            place = 64 * side + n * r
            image[r, c0 : c0 + n] = strips[0, place : place + n]
    for g in range(2):
        one = mixed[1 + g].reshape(8, WIN, chans)
        c0 = STRIP + spots[g]
        image[0:4, c0 : c0 + WIN] = one[0:4]
        image[12:16, c0 : c0 + WIN] = one[4:8]
    even = flags[4]
    count = 3 * image.shape[1]
    for pay_ref, rows in (
        (pay_one_ref, jnp.where(even, image[13:16], image[0:3])),
        (pay_two_ref, jnp.where(even, image[0:3], image[13:16])),
    ):
        b_scr[:, 0:chans] = rows.reshape(count, chans)
        pay_ref[0:count] = b_scr[:, 0:128].astype(BF16)
        pay_ref[count:] = halves(b_scr[:, 128:256], 128).astype(BF16)
    edge_ref[0:4] = image[0:4]
    edge_ref[4:8] = image[12:16]
    side_ref[:, 0:STRIP] = image[4:12, 0:STRIP]
    side_ref[:, STRIP : 2 * STRIP] = image[4:12, STRIP + cols :]


def fill_taps(taps_ref, image, span):
    chans = image.shape[2]
    for b in range(3):
        start = STRIP - 3 + b
        lanes = slice(256 * b + 128, 256 * b + 256)
        taps_ref[:, :, lanes] = jnp.zeros((taps_ref.shape[0], span, 128), BF16)
        taps_ref[:, :, 256 * b : 256 * b + chans] = image[:, start : start + span].astype(BF16)


def conv_weights(group_ref, before_ref, upsample_ref, wg_scr, wb_scr, wu_scr):
    chans = group_ref.shape[2]
    feats = before_ref.shape[2]
    pad = chans // 16 * 16
    for a in range(3):
        wb_scr[256 * a + pad : 256 * (a + 1)] = jnp.zeros((256 - pad, 3 * feats), BF16)
        wu_scr[256 * a + 3 * feats : 256 * (a + 1)] = jnp.zeros((256 - 3 * feats, 4 * feats), BF16)
        for b in range(3):
            wg_scr[256 * (3 * a + b) + pad : 256 * (3 * a + b + 1)] = jnp.zeros((256 - pad, chans), BF16)
            wg_scr[256 * (3 * a + b) : 256 * (3 * a + b) + chans] = group_ref[a, b]
    same = one_hot((chans, chans), lambda row: row, lambda col: col)
    order = one_hot(
        (4 * feats, 4 * feats), lambda row: row, lambda col: col % feats * 4 + col // feats
    )
    for a in range(3):
        part = before_ref[a].reshape(3 * feats, chans)
        wb_scr[256 * a : 256 * a + chans] = dot_nt(same, part).astype(BF16)
        part = upsample_ref[a].reshape(3 * feats, 4 * feats)
        wu_scr[256 * a : 256 * a + 3 * feats] = dot(part, order).astype(BF16)


def middle_kernel(
    own_ref,
    nrm_ref,
    k_ref,
    v_ref,
    wqv_ref,
    wp_ref,
    inner_mid_ref,
    edge_ref,
    side_ref,
    strip_ref,
    row_two_ref,
    row_one_ref,
    group_ref,
    before_ref,
    upsample_ref,
    bias_ref,
    gain_two_ref,
    hidden_ref,
    output_ref,
    taps_ref,
    base_ref,
    wg_ref,
    wb_ref,
    wu_ref,
    q_scr,
    s_scr,
    m_scr,
    p_scr,
    o_scr,
    image,
):
    height, cols, chans = own_ref.shape
    spots = (0, cols - 2 * WIN, cols - WIN)
    set_queries(q_scr, wqv_ref, [nrm_ref[RIM + 4 : RIM + 12, c0 : c0 + WIN] for c0 in spots])
    first = [own_ref[4:12, c0 : c0 + WIN].reshape(128, chans) for c0 in spots]
    first = jnp.concatenate(first, axis=0).astype(F32) + attention(
        [2, 2, 2], [1, 2, 3], q_scr, k_ref, v_ref, bias_ref, wp_ref, s_scr, m_scr, p_scr, o_scr
    )
    mixed = feed_groups(first, gain_two_ref[...], hidden_ref, output_ref, 3)
    span = cols + 2 * STRIP
    image[:, span:] = jnp.zeros((height, STRIP, chans), F32)
    image[0:4, 0:span] = edge_ref[0:4]
    image[4:12, 0:STRIP] = side_ref[:, 0:STRIP]
    image[4:12, STRIP + WIN : STRIP + cols - 2 * WIN] = inner_mid_ref[...]
    for g in range(3):
        c0 = STRIP + spots[g]
        image[4:12, c0 : c0 + WIN] = mixed[g].reshape(8, WIN, chans)
    image[4:12, STRIP + cols : span] = side_ref[:, STRIP : 2 * STRIP]
    image[12:16, 0:span] = edge_ref[4:8]
    fill_taps(taps_ref, image, span)
    conv_weights(group_ref, before_ref, upsample_ref, wg_ref, wb_ref, wu_ref)
    even_row = at_edges()[4]
    above, below = from_sides(even_row, row_one_ref[...], row_two_ref[...])
    base_ref[0:2, STRIP : STRIP + cols] = above[2:4]
    base_ref[2 : 2 + height, STRIP : STRIP + cols] = own_ref[...].astype(F32)
    base_ref[2 + height : 4 + height, STRIP : STRIP + cols] = below[0:2]
    rows = slice(2, height + 6)
    base_ref[:, 0:STRIP] = strip_ref[0, rows]
    base_ref[:, STRIP + cols : span] = strip_ref[1, rows]
    base_ref[:, span:] = jnp.zeros((height + 4, STRIP, chans), F32)


def attention_scratch(groups, depth=2 * HP):
    return [
        pltpu.VMEM((groups, HEADS // 2, depth, 256), BF16),
        pltpu.VMEM((HEADS // 2, KEYS, 256), F32),
        pltpu.VMEM((8, 256), F32),
        pltpu.VMEM((HEADS // 2, KEYS, 256), BF16),
        pltpu.VMEM((groups, HEADS, HP, 128), F32),
    ]


def inner_block(*args):
    height, cols, chans = args[0].shape
    inner = cols // WIN - 2
    width = HEADS * HP
    groups = 2 * inner - 1
    return call(
        inner_kernel,
        (
            jax.ShapeDtypeStruct((height + 2 * RIM, cols, chans), F32),
            jax.ShapeDtypeStruct((chans, 3 * 128), BF16),
            jax.ShapeDtypeStruct((2 * width, chans), BF16),
            jax.ShapeDtypeStruct((width, chans), BF16),
            jax.ShapeDtypeStruct((inner, KEYS, 3 * 128), BF16),
            jax.ShapeDtypeStruct((inner, width, KEYS), BF16),
            jax.ShapeDtypeStruct((8, WIN * inner, chans), F32),
            jax.ShapeDtypeStruct((8, WIN * (inner - 1), chans), F32),
        ),
        attention_scratch(groups),
        5_000_000_000,
        4_000_000,
    )(*args)


def outer_block(*args):
    height, cols, chans = args[0].shape
    span = cols + 2 * STRIP
    return call(
        outer_kernel,
        (
            jax.ShapeDtypeStruct((3 * span + 128, 128), BF16),
            jax.ShapeDtypeStruct((3 * span + 128, 128), BF16),
            jax.ShapeDtypeStruct((8, span, chans), F32),
            jax.ShapeDtypeStruct((8, 2 * STRIP, chans), F32),
            jax.ShapeDtypeStruct((2, height + 2 * RIM, STRIP, chans), F32),
            jax.ShapeDtypeStruct((4, KEYS, 3 * 128), BF16),
            jax.ShapeDtypeStruct((4, HEADS * HP, KEYS), BF16),
        ),
        [
            pltpu.VMEM((2, height + 2 * RIM, 2 * EDGE, chans), F32),
            pltpu.VMEM((2, (height + 2 * RIM) * (WIN + RIM), 256), F32),
            pltpu.VMEM(((height + 2 * RIM) * (WIN + RIM), chans), F32),
            pltpu.VMEM((3 * span, 256), F32),
            pltpu.VMEM((2, 128, chans), F32),
            pltpu.VMEM((4, HEADS * HP, KEYS), BF16),
            *attention_scratch(3, 4 * HP),
            pltpu.VMEM((height, span, chans), F32),
        ],
        5_000_000_000,
        4_000_000,
    )(*args)


def middle_block(*args):
    height, cols, chans = args[0].shape
    span = cols + 2 * STRIP
    feats = args[-6].shape[2]
    return call(
        middle_kernel,
        (
            jax.ShapeDtypeStruct((height, span, 768), BF16),
            jax.ShapeDtypeStruct((height + 4, span + STRIP, chans), F32),
            jax.ShapeDtypeStruct((9 * 256, chans), BF16),
            jax.ShapeDtypeStruct((3 * 256, 3 * feats), BF16),
            jax.ShapeDtypeStruct((3 * 256, 4 * feats), BF16),
        ),
        [*attention_scratch(3), pltpu.VMEM((height, span + STRIP, chans), F32)],
        5_000_000_000,
        4_000_000,
    )(*args)


def conv_kernel(
    taps_ref,
    base,
    back_two_ref,
    back_one_ref,
    wg_scr,
    wb_scr,
    wu_scr,
    out_ref,
    image,
    halo_taps,
    grouped,
    sums,
    lowfeat,
    low_taps,
    out_scr,
):
    height, span = taps_ref.shape[:2]
    cols = span - 2 * STRIP
    chans = base.shape[2]
    feats = out_ref.shape[0]
    at_left, at_right, at_top, at_bottom, even_row, _ = at_edges()
    image[:, span:] = jnp.zeros((6, STRIP, chans), F32)
    sides = from_sides(even_row, back_one_ref[...], back_two_ref[...])
    for rows, packed in ((slice(0, 3), sides[0]), (slice(3, 6), sides[1])):
        image[rows, 0:span, 0:128] = packed[0 : 3 * span].reshape(3, span, 128)
        rest = unhalve(packed[3 * span :], 3 * span).reshape(3, span, 128)
        image[rows, 0:span, 128:chans] = rest[:, :, 0 : chans - 128]
    fill_taps(halo_taps, image, span)
    grouped[:, :, 128:256] = jnp.zeros((height + 4, span, 128), BF16)
    part = 2
    col = lax.broadcasted_iota(jnp.int32, (span, chans), 0) - 2
    keep_grouped = (col < cols + 2) & ((col >= 0) | jnp.logical_not(at_left))
    keep_grouped = keep_grouped & ((col < cols) | jnp.logical_not(at_right))
    low_span = cols + 8
    col = lax.broadcasted_iota(jnp.int32, (low_span, 128), 0) - 1
    keep_low = (col <= cols) & ((col >= 0) | jnp.logical_not(at_left))
    keep_low = keep_low & ((col < cols) | jnp.logical_not(at_right))
    left_half = lax.broadcasted_iota(jnp.int32, (cols, 128), 1) < feats
    spot = lax.broadcasted_iota(jnp.int32, (256, 256), 0)
    place = lax.broadcasted_iota(jnp.int32, (256, 256), 1)
    spread = (spot % 128 // cols == place // 128) & (
        spot % cols * 2 + spot // 128 == place % 128
    )
    spread = spread.astype(F32).astype(BF16)

    def tap_row(row):
        if 3 <= row < height + 3:
            return taps_ref[row - 3]
        return halo_taps[row if row < 3 else row - height]

    def group(h):
        totals = []
        for h2 in range(h, h + part, 2):
            lhs = jnp.concatenate(
                [
                    jnp.concatenate([tap_row(h2 + a), tap_row(h2 + a + 1)], axis=0)
                    for a in range(3)
                ],
                axis=1,
            )
            totals.append(dot(lhs, wg_scr[...]).reshape(2, span, chans))
        total = jnp.concatenate(totals, axis=0)
        total = total + base[h : h + part, STRIP - 2 : STRIP - 2 + span, :]
        for r in range(part):
            mask = keep_grouped
            if h + r < 2:
                mask = mask & jnp.logical_not(at_top)
            if h + r >= height + 2:
                mask = mask & jnp.logical_not(at_bottom)
            grouped[h + r, 0:span, 0:chans] = jnp.where(mask, total[r], 0.0).astype(BF16)

    def narrow(h, count):
        lhs = jnp.concatenate(
            [grouped[h + a : h + a + count].reshape(count * span, 256) for a in range(3)], axis=1
        )
        slot = h // part % 2
        sums[slot, 0:count, :, 0 : 3 * feats] = dot(lhs, wb_scr[...]).reshape(count, span, 3 * feats)
        for r in range(count):
            total = sums[slot, r, 0:low_span, 0:128]
            total = total + pltpu.roll(sums[slot, r, 1 : low_span + 1, 0:128], feats, 1)
            total = total + sums[slot, r, 2 : low_span + 2, 128:256]
            mask = keep_low
            if h + r == 0:
                mask = mask & jnp.logical_not(at_top)
            if h + r == height + 1:
                mask = mask & jnp.logical_not(at_bottom)
            lowfeat[h + r] = jnp.where(mask, jnp.where(total >= 0, total, 0.01 * total), 0.0)
            low_taps[h + r, :, 0:128] = jnp.where(
                left_half, lowfeat[h + r, 0:cols], pltpu.roll(lowfeat[h + r, 1 : cols + 1], feats, 1)
            ).astype(BF16)
            low_taps[h + r, :, 128:256] = jnp.where(
                left_half, lowfeat[h + r, 2 : cols + 2], 0.0
            ).astype(BF16)

    def expand(h):
        lhs = jnp.concatenate(
            [low_taps[h + a : h + a + part].reshape(part * cols, 256) for a in range(3)], axis=1
        )
        total = dot(lhs, wu_scr[...])
        for pair in range(part // 2):
            turned = total[2 * cols * pair : 2 * cols * (pair + 1)].T.astype(BF16)
            lhs = [
                jnp.concatenate(
                    [turned[(2 * a + b) * feats : (2 * a + b + 1) * feats] for b in range(2)], axis=1
                )
                for a in range(2)
            ]
            final = dot(jnp.concatenate(lhs, axis=0), spread)
            for r in range(2):
                for a in range(2):
                    row = 2 * (h + 2 * pair + r) + a
                    out_scr[pl.ds(row, feats, stride=2 * height), :] = final[
                        a * feats : (a + 1) * feats, 128 * r : 128 * (r + 1)
                    ]

    narrowed = expanded = done = 0
    while expanded < height:
        expand_to, narrow_to = min(narrowed - 2, height), min(done - 2, height + 2)
        if done < height + 4:
            group(done)
            done += part
        while narrowed < narrow_to:
            count = min(part, height + 2 - narrowed)
            if narrowed + count > narrow_to:
                break
            narrow(narrowed, count)
            narrowed += count
        while expanded + part <= expand_to:
            expand(expanded)
            expanded += part
    out_ref[...] = out_scr[...].reshape(feats, 2 * height, 128).astype(BF16)


def convs(*args):
    height, span = args[0].shape[:2]
    chans = args[1].shape[2]
    cols = span - 2 * STRIP
    feats = args[-1].shape[1] // 4
    return call(
        conv_kernel,
        jax.ShapeDtypeStruct((feats, 2 * height, 2 * cols), BF16),
        [
            pltpu.VMEM((6, span + STRIP, chans), F32),
            pltpu.VMEM((6, span, 768), BF16),
            pltpu.VMEM((height + 4, span, 256), BF16),
            pltpu.VMEM((2, 4, span, 256), F32),
            pltpu.VMEM((height + 2, cols + 8, 128), F32),
            pltpu.VMEM((height + 2, cols, 256), BF16),
            pltpu.VMEM((feats * 2 * height, 128), F32),
        ],
        8_000_000_000,
        4_000_000,
    )(*args)


def swapped(axis, first, second):
    count = lax.axis_size(axis)
    out = []
    for start, payload in ((1, second), (0, first)):
        pairs = [(i, i + 1) for i in range(start, count - 1, 2)]
        pairs = pairs + [(b, a) for a, b in pairs]
        out.append(lax.ppermute(payload, axis, pairs))
    return out[::-1]


def on_device(
    features,
    gain_one,
    qkv_weight,
    bias_table,
    proj_weight,
    gain_two,
    hidden_weight,
    output_weight,
    group_conv,
    before_conv,
    upsample_conv,
):
    height, cols, chans = features.shape
    even_row = lax.axis_index("rows") % 2 == 0
    low, high = features[:RIM], features[height - RIM :]
    row_one, row_two = swapped(
        "rows", jnp.where(even_row, high, low), jnp.where(even_row, low, high)
    )
    col_one, col_two = swapped("cols", *pack(features, row_one, row_two))

    bias = build_bias(bias_table)
    gain_one, gain_two = gain_one.reshape(1, chans), gain_two.reshape(1, chans)
    post = (gain_two, hidden_weight, output_weight.T)
    nrm, wk, wqv, wp, inner_k, inner_v, inner_border, inner_mid = inner_block(
        features,
        row_one,
        row_two,
        gain_one,
        qkv_weight,
        proj_weight,
        bias,
        *post,
    )
    back_one, back_two, edge, side, strips, keys, values = outer_block(
        features,
        nrm,
        col_two,
        col_one,
        gain_one,
        wk,
        wqv,
        wp,
        inner_k,
        inner_v,
        inner_border,
        bias,
        *post,
    )
    back_one, back_two = swapped("rows", back_one, back_two)
    taps, base, group, before, upsample = middle_block(
        features,
        nrm,
        keys,
        values,
        wqv,
        wp,
        inner_mid,
        edge,
        side,
        strips,
        row_two,
        row_one,
        group_conv,
        before_conv.transpose(0, 1, 3, 2),
        upsample_conv,
        bias,
        *post,
    )
    return convs(taps, base, back_two, back_one, group, before, upsample)


def solution(mesh):
    placed = (P("rows", "cols", None), P(), P(), P(), P(), P(), P(), P(), P(), P(), P())
    return jax.shard_map(
        on_device, mesh=mesh, in_specs=placed, out_specs=P(None, "rows", "cols"), check_vma=False
    )
```

```python
import functools

import jax
import jax.numpy as jnp
import numpy as np
from jax import lax
from jax.experimental import pallas as pl
from jax.experimental.pallas import tpu as pltpu
from jax.sharding import PartitionSpec as P

HEADS = 6
HD = 30
HP = 32
WIN = 16
KWIN = 24
KEYS = KWIN * KWIN
SIDE = WIN + KWIN - 1
RIM = (KWIN - WIN) // 2
EDGE = WIN + 2 * RIM
STRIP = 8
SIDE_COLS = 4
LOG2E = 1.4426950408889634
F32 = jnp.float32
BF16 = jnp.bfloat16
NT = (((1,), (1,)), ((), ()))
TN = (((0,), (0,)), ((), ()))


def dot(a, b):
    return jnp.dot(a, b, preferred_element_type=F32)


def dot_nt(a, b):
    return lax.dot_general(a, b, NT, preferred_element_type=F32)


def layer_norm(values, gain):
    center = values - jnp.mean(values, axis=-1, keepdims=True)
    spread = jnp.mean(center * center, axis=-1, keepdims=True)
    return center * lax.rsqrt(spread + 1e-05) * gain


def call(kernel, out_shape, scratch, flops, bytes_accessed):
    return pl.pallas_call(
        kernel,
        out_shape=out_shape,
        scratch_shapes=scratch,
        compiler_params=pltpu.CompilerParams(vmem_limit_bytes=24 * 2**20),
        cost_estimate=pl.CostEstimate(
            flops=flops, bytes_accessed=bytes_accessed, transcendentals=0
        ),
    )


def bias_kernel(table_ref, out_ref, t_scr, e_scr, w_scr, x_scr):
    for d in range(SIDE):
        t_scr[8 * d : 8 * d + HEADS, 0:SIDE] = jnp.exp(table_ref[:, SIDE * d : SIDE * (d + 1)])

    def head(h, carry):
        values = t_scr[pl.ds(h, SIDE, stride=8), 0:SIDE].astype(BF16)

        def expand(cols, first, shift=0):
            width = -(-(SIDE * cols + shift) // 128) * 128
            spot = (lax.broadcasted_iota(jnp.int32, (SIDE, width), 1) - shift) // cols
            row = lax.broadcasted_iota(jnp.int32, (SIDE, width), 0)
            pick = (spot == SIDE - 1 - row).astype(F32).astype(BF16)
            e_scr[0:SIDE, 0:width] = lax.dot_general(values, pick, TN, preferred_element_type=F32)
            lane = lax.broadcasted_iota(jnp.int32, (KWIN, width), 1) % cols
            out = jnp.zeros((KWIN, width), F32)
            for jj in range(cols):
                start = WIN - 1 - first - jj
                out = jnp.where(lane == jj, e_scr[start : start + KWIN, 0:width], out)
            w_scr[:, 0:width] = out

        lanes = lax.broadcasted_iota(jnp.int32, (KWIN, 128), 1)
        expand(WIN, 0)
        whole = w_scr[...]
        for phase in range(8):
            turned = whole if phase == 0 else pltpu.roll(whole, 640 - WIN * phase, 1)
            for p in range(KWIN):
                rows = slice(p * KWIN, (p + 1) * KWIN)
                if (23 - p) % 8 == phase:
                    at = (23 - p) // 8 * 128
                    low, high = turned[:, at : at + 128], turned[:, at + 128 : at + 256]
                    x_scr[0, rows] = jnp.where(lanes < 64, low, high)
                if (27 - p) % 8 == phase:
                    at = (27 - p) // 8 * 128
                    x_scr[1, rows] = turned[:, at : at + 128]
        out_ref[1, h] = x_scr[0].astype(BF16)
        out_ref[2, h] = x_scr[1].astype(BF16)
        expand(SIDE_COLS, WIN - SIDE_COLS)
        left = w_scr[:, 0:256]
        expand(SIDE_COLS, 0, 64)
        right = w_scr[:, 0:256]
        whole = jnp.concatenate([left, right], axis=0)
        for p in range(KWIN):
            rows = slice(p * KWIN, (p + 1) * KWIN)
            at = (23 - p) * SIDE_COLS
            turned = whole if at == 0 else pltpu.roll(whole, 256 - at, 1)
            x_scr[0, rows] = jnp.where(lanes < 64, turned[0:KWIN, 0:128], turned[KWIN:, 0:128])
        out_ref[0, h] = x_scr[0].astype(BF16)
        return carry

    lax.fori_loop(0, HEADS, head, 0)


def build_bias(bias_table):
    return call(
        bias_kernel,
        jax.ShapeDtypeStruct((3, HEADS, KEYS, 128), BF16),
        [
            pltpu.VMEM((8 * SIDE, 128), F32),
            pltpu.VMEM((SIDE + 1, 640), F32),
            pltpu.VMEM((KWIN, 640), F32),
            pltpu.VMEM((2, KEYS, 128), F32),
        ],
        4_000_000_000,
        4_000_000,
    )(bias_table.T)


def one_hot(shape, row_of, col_of):
    row = lax.broadcasted_iota(jnp.int32, shape, 0)
    col = lax.broadcasted_iota(jnp.int32, shape, 1)
    return (row_of(row) == col_of(col)).astype(F32).astype(BF16)


def spread_head(place):
    return jnp.where(place % HP < HD, place // HP * HD + place % HP, -1)


def weights_into(qkv_ref, proj_ref, wk_ref, wqv_ref, wp_ref):
    chans = qkv_ref.shape[0]
    width = HEADS * HP
    qkv = qkv_ref[...]
    pick = one_hot(
        (3 * chans, 3 * 128),
        lambda row: row,
        lambda col: jnp.where(
            (col % 128 < 2 * HP) & (col % HP < HD),
            chans + (col // 128 * 2 + col % 128 // HP) * HD + col % HP,
            -1,
        ),
    )
    wk_ref[...] = dot(qkv, pick).astype(BF16)
    pick = one_hot(
        (2 * width, 3 * chans),
        lambda row: jnp.where(
            row % HP < HD, row // HP * HD + row % HP + jnp.where(row < width, 0, chans), -1
        ),
        lambda col: col,
    )
    wqv_ref[...] = dot_nt(pick, qkv).astype(BF16)
    pick = one_hot((width, chans), spread_head, lambda col: col)
    wp_ref[...] = dot(pick, proj_ref[...]).astype(BF16)


def set_queries(q_scr, wqv_ref, groups, strips=None):
    scale = LOG2E / np.sqrt(HD)
    rows = jnp.concatenate([rows.reshape(128, rows.shape[-1]) for rows in groups], axis=0)
    queries = (dot_nt(wqv_ref[0 : HEADS * HP], rows.astype(BF16)) * scale).astype(BF16)
    none = jnp.zeros((HP, 128), BF16)
    left = lax.broadcasted_iota(jnp.int32, (HP, 128), 1) < 64
    for g in range(len(groups)):
        lanes = slice(128 * g, 128 * g + 128)
        for t in range(HEADS // 2):
            one = queries[2 * t * HP : (2 * t + 1) * HP, lanes]
            two = queries[(2 * t + 1) * HP : (2 * t + 2) * HP, lanes]
            if g == strips:
                q_scr[g, t, 2 * HP : 3 * HP] = jnp.concatenate([jnp.where(left, none, one), none], axis=1)
                q_scr[g, t, 3 * HP : 4 * HP] = jnp.concatenate([none, jnp.where(left, none, two)], axis=1)
                one, two = jnp.where(left, one, none), jnp.where(left, two, none)
            elif strips is not None:
                q_scr[g, t, 2 * HP : 4 * HP] = jnp.zeros((2 * HP, 256), BF16)
            q_scr[g, t, 0:HP] = jnp.concatenate([one, none], axis=1)
            q_scr[g, t, HP : 2 * HP] = jnp.concatenate([none, two], axis=1)


def lookup(g, values):
    out = values[0]
    for index in range(1, len(values)):
        out = jnp.where(g >= index, values[index], out)
    return out


def attention(kinds, windows, q_scr, k_ref, v_ref, bias_ref, wp_ref, s_scr, m_scr, p_scr, o_scr, v_right=None):
    groups = len(kinds)
    pairs = HEADS // 2
    step = 144
    depth = 2 * HP if v_right is None else 4 * HP
    left = lax.broadcasted_iota(jnp.int32, (HP, 128), 1) < 64

    def keep(g, t, k0, top):
        keys = k_ref[lookup(g, windows), k0 : k0 + step, 128 * t : 128 * t + depth]
        one = dot(keys, q_scr[g, t])
        s_scr[t, k0 : k0 + step] = one
        part = jnp.max(one.reshape(step // 8, 8, 256), axis=0)
        return part if top is None else jnp.maximum(top, part)

    def sum_values(g, t):
        for half in range(2):
            head = 2 * t + half
            lanes = slice(128 * half, 128 * half + 128)
            window, rows = lookup(g, windows), slice(head * HP, (head + 1) * HP)
            values = v_ref[window, rows]
            if v_right is None:
                o_scr[g, head] = dot(values, p_scr[t, :, lanes])
            else:
                values = jnp.concatenate([values, v_right[window, rows]], axis=0)
                both = dot(values, p_scr[t, :, lanes])
                o_scr[g, head] = jnp.where(left, both[0:HP], both[HP : 2 * HP])

    top = None
    for k0 in range(0, KEYS, step):
        top = keep(0, 0, k0, top)
    m_scr[...] = top
    p_scr[pairs - 1] = jnp.zeros((KEYS, 256), BF16)

    def attend(g, carry):
        kind = lookup(g, kinds)
        top = m_scr[...]
        for t in range(pairs):
            top = jnp.max(top, axis=0, keepdims=True)
            if t == 0:
                sum_values(jnp.maximum(g - 1, 0), pairs - 1)
            else:
                sum_values(g, t - 1)
            following = g if t + 1 < pairs else jnp.minimum(g + 1, groups - 1)
            later = None
            for k0 in range(0, KEYS, step):
                later = keep(following, (t + 1) % pairs, k0, later)
                prob = jnp.exp2(s_scr[t, k0 : k0 + step] - top).astype(BF16)
                for half in range(2):
                    lanes = slice(128 * half, 128 * half + 128)
                    p_scr[t, k0 : k0 + step, lanes] = (
                        prob[:, lanes] * bias_ref[kind, 2 * t + half, k0 : k0 + step]
                    )
            top = later
        m_scr[...] = top
        return carry

    lax.fori_loop(0, groups, attend, 0)
    sum_values(groups - 1, pairs - 1)
    attended = []
    for g in range(groups):
        parts = []
        for head in range(HEADS):
            one = o_scr[g, head]
            parts.append((one * (1.0 / one[HD : HD + 1])).astype(BF16))
        attended.append(jnp.concatenate(parts, axis=0))
    attended = jnp.concatenate(attended, axis=1)
    return lax.dot_general(attended, wp_ref[...], TN, preferred_element_type=F32)


def feed_forward(first, gain, hidden_ref, output_ref):
    normed = layer_norm(first, gain).astype(BF16)
    inner = dot(normed, hidden_ref[...])
    inner = (0.5 * inner * (1.0 + lax.erf(inner * np.float32(np.sqrt(0.5))))).astype(BF16)
    return first + dot_nt(inner, output_ref[...])


def feed_groups(first, gain, hidden_ref, output_ref, batch):
    out = []
    for start in range(0, first.shape[0], 128 * batch):
        mixed = feed_forward(first[start : start + 128 * batch], gain, hidden_ref, output_ref)
        out += [mixed[128 * g : 128 * (g + 1)] for g in range(batch)]
    return out


def project(keys, wk_ref, wqv_ref, k_ref, v_ref, index):
    keys = keys.reshape(KEYS, keys.shape[2]).astype(BF16)
    k_ref[index] = dot(keys, wk_ref[...]).astype(BF16)
    v_ref[index] = project_values(keys, wqv_ref)


def project_values(keys, wqv_ref):
    width = HEADS * HP
    one_row = (lax.broadcasted_iota(jnp.int32, (width, 1), 0) % HP == HD).astype(F32)
    return (dot_nt(wqv_ref[width : 2 * width], keys) + one_row).astype(BF16)


def at_edges():
    row, column = lax.axis_index("rows"), lax.axis_index("cols")
    return (
        column == 0,
        column == lax.axis_size("cols") - 1,
        row == 0,
        row == lax.axis_size("rows") - 1,
        row % 2 == 0,
        column % 2 == 0,
    )


def from_sides(even, first, second):
    first, second = first.astype(F32), second.astype(F32)
    return jnp.where(even, second, first), jnp.where(even, first, second)


def border_rows(ref, c0):
    return jnp.concatenate([ref[0:4, c0 : c0 + WIN], ref[12:16, c0 : c0 + WIN]], axis=0)


def halves(wide, count):
    left = lax.broadcasted_iota(jnp.int32, (1, 128), 1) < 64
    rest = wide.shape[0] - count
    out = jnp.where(left, wide[0:rest], pltpu.roll(wide[count:], 64, 1))
    return out if rest == count else jnp.concatenate([out, wide[rest:count]], axis=0)


def unhalve(packed, rows):
    count = packed.shape[0]
    return jnp.concatenate([packed, pltpu.roll(packed[0 : rows - count], 64, 1)], axis=0)


def pack_kernel(own_ref, row_one_ref, row_two_ref, pay_one_ref, pay_two_ref, x_scr, flat):
    height, cols, chans = own_ref.shape
    even_row, even_col = at_edges()[4:]
    above, below = from_sides(even_row, row_one_ref[...], row_two_ref[...])
    x_scr[0:RIM] = above
    x_scr[RIM : RIM + height] = own_ref[...].astype(F32)
    x_scr[RIM + height :] = below
    for side, near, far in ((0, 0, WIN), (1, cols - WIN, cols - WIN - RIM)):
        for r in range(height + 2 * RIM):
            flat[side, WIN * r : WIN * (r + 1), 0:chans] = x_scr[r, near : near + WIN]
            place = WIN * (height + 2 * RIM) + RIM * r
            flat[side, place : place + RIM, 0:chans] = x_scr[r, far : far + RIM]
    count = flat.shape[1]
    for lanes in (slice(0, 128), slice(128, 256)):
        low, high = flat[0, :, lanes], flat[1, :, lanes]
        one, two = jnp.where(even_col, high, low), jnp.where(even_col, low, high)
        rows = slice(0, count)
        if lanes.start:
            one, two = halves(one, count // 2), halves(two, count // 2)
            rows = slice(count, count + count // 2)
        pay_one_ref[rows] = one.astype(BF16)
        pay_two_ref[rows] = two.astype(BF16)


def pack(own, row_one, row_two):
    height, cols, chans = own.shape
    pixels = (height + 2 * RIM) * (WIN + RIM)
    pay = jax.ShapeDtypeStruct((pixels * 3 // 2, 128), BF16)
    return call(
        pack_kernel,
        (pay, pay),
        [
            pltpu.VMEM((height + 2 * RIM, cols, chans), F32),
            pltpu.VMEM((2, pixels, 256), F32),
        ],
        1_000_000,
        1_000_000,
    )(own, row_one, row_two)


def inner_kernel(
    own_ref,
    row_one_ref,
    row_two_ref,
    gain_one_ref,
    qkv_ref,
    proj_ref,
    bias_ref,
    gain_two_ref,
    hidden_ref,
    output_ref,
    nrm_ref,
    wk_ref,
    wqv_ref,
    wp_ref,
    k_ref,
    v_ref,
    border_ref,
    mid_ref,
    q_scr,
    s_scr,
    m_scr,
    p_scr,
    o_scr,
):
    height, cols, chans = own_ref.shape
    inner = cols // WIN - 2
    flags = at_edges()
    weights_into(qkv_ref, proj_ref, wk_ref, wqv_ref, wp_ref)
    gain_one = gain_one_ref[...]
    for r in range(RIM):
        above, below = from_sides(flags[4], row_one_ref[r], row_two_ref[r])
        nrm_ref[r] = layer_norm(above, gain_one)
        nrm_ref[RIM + height + r] = layer_norm(below, gain_one)
    for r in range(height):
        nrm_ref[RIM + r] = layer_norm(own_ref[r].astype(F32), gain_one)
    kinds, windows, first, queries = [], [], [], []
    for w in range(inner):
        c0 = WIN * (w + 1)
        project(nrm_ref[:, c0 - RIM : c0 - RIM + KWIN], wk_ref, wqv_ref, k_ref, v_ref, w)
        first.append(border_rows(own_ref, c0).reshape(128, chans))
        queries.append(border_rows(nrm_ref.at[RIM : RIM + height], c0))
        kinds.append(1)
        windows.append(w)
    for w in range(inner - 1):
        c0 = WIN * (w + 1)
        first.append(own_ref[4:12, c0 : c0 + WIN].reshape(128, chans))
        queries.append(nrm_ref[RIM + 4 : RIM + 12, c0 : c0 + WIN])
        kinds.append(2)
        windows.append(w)
    groups = len(kinds)
    set_queries(q_scr, wqv_ref, queries)
    first = jnp.concatenate(first, axis=0).astype(F32) + attention(
        kinds, windows, q_scr, k_ref, v_ref, bias_ref, wp_ref, s_scr, m_scr, p_scr, o_scr
    )
    mixed = feed_groups(first, gain_two_ref[...], hidden_ref, output_ref, len(kinds))
    for g in range(groups):
        one = mixed[g].reshape(8, WIN, chans)
        if g < inner:
            border_ref[:, WIN * g : WIN * (g + 1)] = one
        else:
            mid_ref[:, WIN * (g - inner) : WIN * (g - inner + 1)] = one


def outer_kernel(
    own_ref,
    nrm_ref,
    col_two_ref,
    col_one_ref,
    gain_one_ref,
    wk_ref,
    wqv_ref,
    wp_ref,
    inner_k_ref,
    inner_v_ref,
    inner_border_ref,
    bias_ref,
    gain_two_ref,
    hidden_ref,
    output_ref,
    pay_one_ref,
    pay_two_ref,
    edge_ref,
    side_ref,
    strip_ref,
    k_ref,
    v_ref,
    side_scr,
    x_scr,
    n_scr,
    b_scr,
    strips,
    v_right,
    q_scr,
    s_scr,
    m_scr,
    p_scr,
    o_scr,
    image,
):
    height, cols, chans = own_ref.shape
    inner = cols // WIN - 2
    flags = at_edges()
    gain_one = gain_one_ref[...]
    rows = height + 2 * RIM
    pixels = rows * (WIN + RIM)
    both = from_sides(flags[5], col_one_ref[...], col_two_ref[...])
    for side in range(2):
        x_scr[side, :, 0:128] = both[side][0:pixels]
        x_scr[side, :, 128:256] = unhalve(both[side][pixels:], pixels)
        n_scr[...] = layer_norm(x_scr[side, :, 0:chans], gain_one)
        near, far = (EDGE - WIN, EDGE - WIN - RIM) if side == 0 else (EDGE, EDGE + WIN)
        for r in range(rows):
            side_scr[side, r, near : near + WIN] = n_scr[WIN * r : WIN * (r + 1)]
            place = WIN * rows + RIM * r
            side_scr[side, r, far : far + RIM] = n_scr[place : place + RIM]
        c0 = WIN - STRIP if side == 0 else 0
        x = x_scr[side, 0 : WIN * rows, 0:chans].reshape(rows, WIN, chans)
        strip_ref[side] = x[:, c0 : c0 + STRIP]
    side_scr[0, :, EDGE : 2 * EDGE] = nrm_ref[:, 0:EDGE]
    side_scr[1, :, 0:EDGE] = nrm_ref[:, cols - EDGE : cols]
    k_ref[2] = inner_k_ref[inner - 1]
    v_ref[2] = inner_v_ref[inner - 1]
    for index, side, c0 in ((1, 0, RIM + WIN), (3, 1, RIM)):
        project(side_scr[side, :, c0 : c0 + KWIN], wk_ref, wqv_ref, k_ref, v_ref, index)
        v_right[index] = v_ref[index]
    strip_keys = [
        side_scr[side, :, c0 : c0 + KWIN].reshape(KEYS, chans).astype(BF16)
        for side, c0 in ((0, RIM), (1, RIM + WIN))
    ]
    moved = pltpu.roll(wk_ref[...].astype(F32), 2 * HP, 1).astype(BF16)
    k_ref[0] = (dot(strip_keys[0], wk_ref[...]) + dot(strip_keys[1], moved)).astype(BF16)
    v_ref[0] = project_values(strip_keys[0], wqv_ref)
    v_right[0] = project_values(strip_keys[1], wqv_ref)
    n = SIDE_COLS
    for r in range(height):
        for side, c0, c1 in ((0, STRIP - n, EDGE - n), (1, 0, EDGE)):
            place = slice(64 * side + n * r, 64 * side + n * (r + 1))
            strips[0, place] = strip_ref[side, RIM + r, c0 : c0 + n]
            strips[1, place] = side_scr[side, RIM + r, c1 : c1 + n]
    first, queries = [strips[0]], [strips[1]]
    spots = (0, cols - WIN)
    for c0 in spots:
        first.append(border_rows(own_ref, c0).astype(F32).reshape(128, chans))
        queries.append(border_rows(nrm_ref.at[RIM : RIM + height], c0))
    set_queries(q_scr, wqv_ref, queries, 0)
    first = jnp.concatenate(first, axis=0) + attention(
        [0, 1, 1], [0, 1, 3], q_scr, k_ref, v_ref, bias_ref, wp_ref, s_scr, m_scr, p_scr, o_scr, v_right
    )
    image[:, 0:STRIP] = jnp.zeros((height, STRIP, chans), F32)
    image[:, STRIP + cols :] = jnp.zeros((height, STRIP, chans), F32)
    image[0:4, STRIP + WIN : STRIP + cols - WIN] = inner_border_ref[0:4]
    image[12:16, STRIP + WIN : STRIP + cols - WIN] = inner_border_ref[4:8]
    mixed = feed_groups(first, gain_two_ref[...], hidden_ref, output_ref, 3)
    row = lax.broadcasted_iota(jnp.int32, (128, chans), 0)
    outside = (flags[0] & (row < 64)) | (flags[1] & (row >= 64))
    strips[0] = jnp.where(outside, 0.0, mixed[0])
    for r in range(height):
        for side, c0 in ((0, STRIP - n), (1, STRIP + cols)):
            place = 64 * side + n * r
            image[r, c0 : c0 + n] = strips[0, place : place + n]
    for g in range(2):
        one = mixed[1 + g].reshape(8, WIN, chans)
        c0 = STRIP + spots[g]
        image[0:4, c0 : c0 + WIN] = one[0:4]
        image[12:16, c0 : c0 + WIN] = one[4:8]
    even = flags[4]
    count = 3 * image.shape[1]
    for pay_ref, rows in (
        (pay_one_ref, jnp.where(even, image[13:16], image[0:3])),
        (pay_two_ref, jnp.where(even, image[0:3], image[13:16])),
    ):
        b_scr[:, 0:chans] = rows.reshape(count, chans)
        pay_ref[0:count] = b_scr[:, 0:128].astype(BF16)
        pay_ref[count:] = halves(b_scr[:, 128:256], 128).astype(BF16)
    edge_ref[0:4] = image[0:4]
    edge_ref[4:8] = image[12:16]
    side_ref[:, 0:STRIP] = image[4:12, 0:STRIP]
    side_ref[:, STRIP : 2 * STRIP] = image[4:12, STRIP + cols :]


def fill_taps(taps_ref, image, span):
    chans = image.shape[2]
    for b in range(3):
        start = STRIP - 3 + b
        lanes = slice(256 * b + 128, 256 * b + 256)
        taps_ref[:, :, lanes] = jnp.zeros((taps_ref.shape[0], span, 128), BF16)
        taps_ref[:, :, 256 * b : 256 * b + chans] = image[:, start : start + span].astype(BF16)


def conv_weights(group_ref, before_ref, upsample_ref, wg_scr, wb_scr, wu_scr):
    chans = group_ref.shape[2]
    feats = before_ref.shape[2]
    pad = chans // 16 * 16
    for a in range(3):
        wb_scr[256 * a + pad : 256 * (a + 1)] = jnp.zeros((256 - pad, 3 * feats), BF16)
        wu_scr[256 * a + 3 * feats : 256 * (a + 1)] = jnp.zeros((256 - 3 * feats, 4 * feats), BF16)
        for b in range(3):
            wg_scr[256 * (3 * a + b) + pad : 256 * (3 * a + b + 1)] = jnp.zeros((256 - pad, chans), BF16)
            wg_scr[256 * (3 * a + b) : 256 * (3 * a + b) + chans] = group_ref[a, b]
    same = one_hot((chans, chans), lambda row: row, lambda col: col)
    order = one_hot(
        (4 * feats, 4 * feats), lambda row: row, lambda col: col % feats * 4 + col // feats
    )
    for a in range(3):
        part = before_ref[a].reshape(3 * feats, chans)
        wb_scr[256 * a : 256 * a + chans] = dot_nt(same, part).astype(BF16)
        part = upsample_ref[a].reshape(3 * feats, 4 * feats)
        wu_scr[256 * a : 256 * a + 3 * feats] = dot(part, order).astype(BF16)


def middle_kernel(
    own_ref,
    nrm_ref,
    k_ref,
    v_ref,
    wqv_ref,
    wp_ref,
    inner_mid_ref,
    edge_ref,
    side_ref,
    strip_ref,
    row_two_ref,
    row_one_ref,
    group_ref,
    before_ref,
    upsample_ref,
    bias_ref,
    gain_two_ref,
    hidden_ref,
    output_ref,
    taps_ref,
    base_ref,
    wg_ref,
    wb_ref,
    wu_ref,
    q_scr,
    s_scr,
    m_scr,
    p_scr,
    o_scr,
    image,
):
    height, cols, chans = own_ref.shape
    spots = (0, cols - 2 * WIN, cols - WIN)
    set_queries(q_scr, wqv_ref, [nrm_ref[RIM + 4 : RIM + 12, c0 : c0 + WIN] for c0 in spots])
    first = [own_ref[4:12, c0 : c0 + WIN].reshape(128, chans) for c0 in spots]
    first = jnp.concatenate(first, axis=0).astype(F32) + attention(
        [2, 2, 2], [1, 2, 3], q_scr, k_ref, v_ref, bias_ref, wp_ref, s_scr, m_scr, p_scr, o_scr
    )
    mixed = feed_groups(first, gain_two_ref[...], hidden_ref, output_ref, 3)
    span = cols + 2 * STRIP
    image[:, span:] = jnp.zeros((height, STRIP, chans), F32)
    image[0:4, 0:span] = edge_ref[0:4]
    image[4:12, 0:STRIP] = side_ref[:, 0:STRIP]
    image[4:12, STRIP + WIN : STRIP + cols - 2 * WIN] = inner_mid_ref[...]
    for g in range(3):
        c0 = STRIP + spots[g]
        image[4:12, c0 : c0 + WIN] = mixed[g].reshape(8, WIN, chans)
    image[4:12, STRIP + cols : span] = side_ref[:, STRIP : 2 * STRIP]
    image[12:16, 0:span] = edge_ref[4:8]
    fill_taps(taps_ref, image, span)
    conv_weights(group_ref, before_ref, upsample_ref, wg_ref, wb_ref, wu_ref)
    even_row = at_edges()[4]
    above, below = from_sides(even_row, row_one_ref[...], row_two_ref[...])
    base_ref[0:2, STRIP : STRIP + cols] = above[2:4]
    base_ref[2 : 2 + height, STRIP : STRIP + cols] = own_ref[...].astype(F32)
    base_ref[2 + height : 4 + height, STRIP : STRIP + cols] = below[0:2]
    rows = slice(2, height + 6)
    base_ref[:, 0:STRIP] = strip_ref[0, rows]
    base_ref[:, STRIP + cols : span] = strip_ref[1, rows]
    base_ref[:, span:] = jnp.zeros((height + 4, STRIP, chans), F32)


def attention_scratch(groups, depth=2 * HP):
    return [
        pltpu.VMEM((groups, HEADS // 2, depth, 256), BF16),
        pltpu.VMEM((HEADS // 2, KEYS, 256), F32),
        pltpu.VMEM((8, 256), F32),
        pltpu.VMEM((HEADS // 2, KEYS, 256), BF16),
        pltpu.VMEM((groups, HEADS, HP, 128), F32),
    ]


def inner_block(*args):
    height, cols, chans = args[0].shape
    inner = cols // WIN - 2
    width = HEADS * HP
    groups = 2 * inner - 1
    return call(
        inner_kernel,
        (
            jax.ShapeDtypeStruct((height + 2 * RIM, cols, chans), F32),
            jax.ShapeDtypeStruct((chans, 3 * 128), BF16),
            jax.ShapeDtypeStruct((2 * width, chans), BF16),
            jax.ShapeDtypeStruct((width, chans), BF16),
            jax.ShapeDtypeStruct((inner, KEYS, 3 * 128), BF16),
            jax.ShapeDtypeStruct((inner, width, KEYS), BF16),
            jax.ShapeDtypeStruct((8, WIN * inner, chans), F32),
            jax.ShapeDtypeStruct((8, WIN * (inner - 1), chans), F32),
        ),
        attention_scratch(groups),
        5_000_000_000,
        4_000_000,
    )(*args)


def outer_block(*args):
    height, cols, chans = args[0].shape
    span = cols + 2 * STRIP
    return call(
        outer_kernel,
        (
            jax.ShapeDtypeStruct((3 * span + 128, 128), BF16),
            jax.ShapeDtypeStruct((3 * span + 128, 128), BF16),
            jax.ShapeDtypeStruct((8, span, chans), F32),
            jax.ShapeDtypeStruct((8, 2 * STRIP, chans), F32),
            jax.ShapeDtypeStruct((2, height + 2 * RIM, STRIP, chans), F32),
            jax.ShapeDtypeStruct((4, KEYS, 3 * 128), BF16),
            jax.ShapeDtypeStruct((4, HEADS * HP, KEYS), BF16),
        ),
        [
            pltpu.VMEM((2, height + 2 * RIM, 2 * EDGE, chans), F32),
            pltpu.VMEM((2, (height + 2 * RIM) * (WIN + RIM), 256), F32),
            pltpu.VMEM(((height + 2 * RIM) * (WIN + RIM), chans), F32),
            pltpu.VMEM((3 * span, 256), F32),
            pltpu.VMEM((2, 128, chans), F32),
            pltpu.VMEM((4, HEADS * HP, KEYS), BF16),
            *attention_scratch(3, 4 * HP),
            pltpu.VMEM((height, span, chans), F32),
        ],
        5_000_000_000,
        4_000_000,
    )(*args)


def middle_block(*args):
    height, cols, chans = args[0].shape
    span = cols + 2 * STRIP
    feats = args[-6].shape[2]
    return call(
        middle_kernel,
        (
            jax.ShapeDtypeStruct((height, span, 768), BF16),
            jax.ShapeDtypeStruct((height + 4, span + STRIP, chans), F32),
            jax.ShapeDtypeStruct((9 * 256, chans), BF16),
            jax.ShapeDtypeStruct((3 * 256, 3 * feats), BF16),
            jax.ShapeDtypeStruct((3 * 256, 4 * feats), BF16),
        ),
        [*attention_scratch(3), pltpu.VMEM((height, span + STRIP, chans), F32)],
        5_000_000_000,
        4_000_000,
    )(*args)


def conv_kernel(
    taps_ref,
    base,
    back_two_ref,
    back_one_ref,
    wg_scr,
    wb_scr,
    wu_scr,
    out_ref,
    image,
    halo_taps,
    grouped,
    sums,
    lowfeat,
    low_taps,
    out_scr,
):
    height, span = taps_ref.shape[:2]
    cols = span - 2 * STRIP
    chans = base.shape[2]
    feats = out_ref.shape[0]
    at_left, at_right, at_top, at_bottom, even_row, _ = at_edges()
    image[:, span:] = jnp.zeros((6, STRIP, chans), F32)
    sides = from_sides(even_row, back_one_ref[...], back_two_ref[...])
    for rows, packed in ((slice(0, 3), sides[0]), (slice(3, 6), sides[1])):
        image[rows, 0:span, 0:128] = packed[0 : 3 * span].reshape(3, span, 128)
        rest = unhalve(packed[3 * span :], 3 * span).reshape(3, span, 128)
        image[rows, 0:span, 128:chans] = rest[:, :, 0 : chans - 128]
    fill_taps(halo_taps, image, span)
    grouped[:, :, 128:256] = jnp.zeros((height + 4, span, 128), BF16)
    col = lax.broadcasted_iota(jnp.int32, (span, chans), 0) - 2
    keep_grouped = (col < cols + 2) & ((col >= 0) | jnp.logical_not(at_left))
    keep_grouped = keep_grouped & ((col < cols) | jnp.logical_not(at_right))
    low_span = cols + 8
    col = lax.broadcasted_iota(jnp.int32, (low_span, 128), 0) - 1
    keep_low = (col <= cols) & ((col >= 0) | jnp.logical_not(at_left))
    keep_low = keep_low & ((col < cols) | jnp.logical_not(at_right))
    left_half = lax.broadcasted_iota(jnp.int32, (cols, 128), 1) < feats
    spot = lax.broadcasted_iota(jnp.int32, (256, 256), 0)
    place = lax.broadcasted_iota(jnp.int32, (256, 256), 1)
    spread = (spot % 128 // cols == place // 128) & (
        spot % cols * 2 + spot // 128 == place % 128
    )
    spread = spread.astype(F32).astype(BF16)

    def tap_row(row):
        if 3 <= row < height + 3:
            return taps_ref[row - 3]
        return halo_taps[row if row < 3 else row - height]

    def group(h, part):
        lhs = jnp.concatenate(
            [
                jnp.concatenate([tap_row(h + a + r) for r in range(part)], axis=0)
                for a in range(3)
            ],
            axis=1,
        )
        total = dot(lhs, wg_scr[...]).reshape(part, span, chans)
        total = total + base[h : h + part, STRIP - 2 : STRIP - 2 + span, :]
        for r in range(part):
            mask = keep_grouped
            if h + r < 2:
                mask = mask & jnp.logical_not(at_top)
            if h + r >= height + 2:
                mask = mask & jnp.logical_not(at_bottom)
            grouped[h + r, 0:span, 0:chans] = jnp.where(mask, total[r], 0.0).astype(BF16)

    def narrow(h, count):
        lhs = jnp.concatenate(
            [grouped[h + a : h + a + count].reshape(count * span, 256) for a in range(3)], axis=1
        )
        slot = h // count % 2
        sums[slot, 0:count, :, 0 : 3 * feats] = dot(lhs, wb_scr[...]).reshape(count, span, 3 * feats)
        for r in range(count):
            total = sums[slot, r, 0:low_span, 0:128]
            total = total + pltpu.roll(sums[slot, r, 1 : low_span + 1, 0:128], feats, 1)
            total = total + sums[slot, r, 2 : low_span + 2, 128:256]
            mask = keep_low
            if h + r == 0:
                mask = mask & jnp.logical_not(at_top)
            if h + r == height + 1:
                mask = mask & jnp.logical_not(at_bottom)
            lowfeat[h + r] = jnp.where(mask, jnp.where(total >= 0, total, 0.01 * total), 0.0)
            low_taps[h + r, :, 0:128] = jnp.where(
                left_half, lowfeat[h + r, 0:cols], pltpu.roll(lowfeat[h + r, 1 : cols + 1], feats, 1)
            ).astype(BF16)
            low_taps[h + r, :, 128:256] = jnp.where(
                left_half, lowfeat[h + r, 2 : cols + 2], 0.0
            ).astype(BF16)

    def expand(h, part):
        lhs = jnp.concatenate(
            [low_taps[h + a : h + a + part].reshape(part * cols, 256) for a in range(3)], axis=1
        )
        total = dot(lhs, wu_scr[...])
        for pair in range(part // 2):
            turned = total[2 * cols * pair : 2 * cols * (pair + 1)].T.astype(BF16)
            lhs = [
                jnp.concatenate(
                    [turned[(2 * a + b) * feats : (2 * a + b + 1) * feats] for b in range(2)], axis=1
                )
                for a in range(2)
            ]
            final = dot(jnp.concatenate(lhs, axis=0), spread)
            for r in range(2):
                for a in range(2):
                    row = 2 * (h + 2 * pair + r) + a
                    out_scr[pl.ds(row, feats, stride=2 * height), :] = final[
                        a * feats : (a + 1) * feats, 128 * r : 128 * (r + 1)
                    ]

    half, third = (height + 4) // 2, (height + 2) // 3
    group(0, half)
    group(half, half)
    narrow(0, third)
    narrow(third, third)
    narrow(2 * third, third)
    expand(0, height // 2)
    expand(height // 2, height // 2)
    out_ref[...] = out_scr[...].reshape(feats, 2 * height, 128).astype(BF16)


def convs(*args):
    height, span = args[0].shape[:2]
    chans = args[1].shape[2]
    cols = span - 2 * STRIP
    feats = args[-1].shape[1] // 4
    return call(
        conv_kernel,
        jax.ShapeDtypeStruct((feats, 2 * height, 2 * cols), BF16),
        [
            pltpu.VMEM((6, span + STRIP, chans), F32),
            pltpu.VMEM((6, span, 768), BF16),
            pltpu.VMEM((height + 4, span, 256), BF16),
            pltpu.VMEM((2, 6, span, 256), F32),
            pltpu.VMEM((height + 2, cols + 8, 128), F32),
            pltpu.VMEM((height + 2, cols, 256), BF16),
            pltpu.VMEM((feats * 2 * height, 128), F32),
        ],
        8_000_000_000,
        4_000_000,
    )(*args)


def swapped(axis, first, second):
    count = lax.axis_size(axis)
    out = []
    for start, payload in ((1, second), (0, first)):
        pairs = [(i, i + 1) for i in range(start, count - 1, 2)]
        pairs = pairs + [(b, a) for a, b in pairs]
        out.append(lax.ppermute(payload, axis, pairs))
    return out[::-1]


def on_device(
    features,
    gain_one,
    qkv_weight,
    bias_table,
    proj_weight,
    gain_two,
    hidden_weight,
    output_weight,
    group_conv,
    before_conv,
    upsample_conv,
):
    height, cols, chans = features.shape
    even_row = lax.axis_index("rows") % 2 == 0
    low, high = features[:RIM], features[height - RIM :]
    row_one, row_two = swapped(
        "rows", jnp.where(even_row, high, low), jnp.where(even_row, low, high)
    )
    col_one, col_two = swapped("cols", *pack(features, row_one, row_two))

    bias = build_bias(bias_table)
    gain_one, gain_two = gain_one.reshape(1, chans), gain_two.reshape(1, chans)
    post = (gain_two, hidden_weight, output_weight.T)
    nrm, wk, wqv, wp, inner_k, inner_v, inner_border, inner_mid = inner_block(
        features,
        row_one,
        row_two,
        gain_one,
        qkv_weight,
        proj_weight,
        bias,
        *post,
    )
    back_one, back_two, edge, side, strips, keys, values = outer_block(
        features,
        nrm,
        col_two,
        col_one,
        gain_one,
        wk,
        wqv,
        wp,
        inner_k,
        inner_v,
        inner_border,
        bias,
        *post,
    )
    back_one, back_two = swapped("rows", back_one, back_two)
    taps, base, group, before, upsample = middle_block(
        features,
        nrm,
        keys,
        values,
        wqv,
        wp,
        inner_mid,
        edge,
        side,
        strips,
        row_two,
        row_one,
        group_conv,
        before_conv.transpose(0, 1, 3, 2),
        upsample_conv,
        bias,
        *post,
    )
    return convs(taps, base, back_two, back_one, group, before, upsample)


def solution(mesh):
    placed = (P("rows", "cols", None), P(), P(), P(), P(), P(), P(), P(), P(), P(), P())
    return jax.shard_map(
        on_device, mesh=mesh, in_specs=placed, out_specs=P(None, "rows", "cols"), check_vma=False
    )
```

```python
import functools

import jax
import jax.numpy as jnp
import numpy as np
from jax import lax
from jax.experimental import pallas as pl
from jax.experimental.pallas import tpu as pltpu
from jax.sharding import PartitionSpec as P

HEADS = 6
HD = 30
HP = 32
WIN = 16
KWIN = 24
KEYS = KWIN * KWIN
SIDE = WIN + KWIN - 1
RIM = (KWIN - WIN) // 2
EDGE = WIN + 2 * RIM
STRIP = 8
SIDE_COLS = 4
LOG2E = 1.4426950408889634
F32 = jnp.float32
BF16 = jnp.bfloat16
NT = (((1,), (1,)), ((), ()))
TN = (((0,), (0,)), ((), ()))


def dot(a, b):
    return jnp.dot(a, b, preferred_element_type=F32)


def dot_nt(a, b):
    return lax.dot_general(a, b, NT, preferred_element_type=F32)


def layer_norm(values, gain):
    center = values - jnp.mean(values, axis=-1, keepdims=True)
    spread = jnp.mean(center * center, axis=-1, keepdims=True)
    return center * lax.rsqrt(spread + 1e-05) * gain


def call(kernel, out_shape, scratch, flops, bytes_accessed):
    return pl.pallas_call(
        kernel,
        out_shape=out_shape,
        scratch_shapes=scratch,
        compiler_params=pltpu.CompilerParams(vmem_limit_bytes=24 * 2**20),
        cost_estimate=pl.CostEstimate(
            flops=flops, bytes_accessed=bytes_accessed, transcendentals=0
        ),
    )


def bias_kernel(
    table_ref, qkv_ref, proj_ref, out_ref, wk_ref, wqv_ref, wp_ref, t_scr, e_scr, w_scr, x_scr
):
    for d in range(SIDE):
        t_scr[8 * d : 8 * d + HEADS, 0:SIDE] = jnp.exp(table_ref[:, SIDE * d : SIDE * (d + 1)])

    def head(h, carry):
        values = t_scr[pl.ds(h, SIDE, stride=8), 0:SIDE].astype(BF16)

        def expand(cols, first, shift=0):
            width = -(-(SIDE * cols + shift) // 128) * 128
            spot = (lax.broadcasted_iota(jnp.int32, (SIDE, width), 1) - shift) // cols
            row = lax.broadcasted_iota(jnp.int32, (SIDE, width), 0)
            pick = (spot == SIDE - 1 - row).astype(F32).astype(BF16)
            e_scr[0:SIDE, 0:width] = lax.dot_general(values, pick, TN, preferred_element_type=F32)
            lane = lax.broadcasted_iota(jnp.int32, (KWIN, width), 1) % cols
            out = jnp.zeros((KWIN, width), F32)
            for jj in range(cols):
                start = WIN - 1 - first - jj
                out = jnp.where(lane == jj, e_scr[start : start + KWIN, 0:width], out)
            w_scr[:, 0:width] = out

        lanes = lax.broadcasted_iota(jnp.int32, (KWIN, 128), 1)
        expand(WIN, 0)
        whole = w_scr[...]
        for phase in range(8):
            turned = whole if phase == 0 else pltpu.roll(whole, 640 - WIN * phase, 1)
            for p in range(KWIN):
                rows = slice(p * KWIN, (p + 1) * KWIN)
                if (23 - p) % 8 == phase:
                    at = (23 - p) // 8 * 128
                    low, high = turned[:, at : at + 128], turned[:, at + 128 : at + 256]
                    x_scr[0, rows] = jnp.where(lanes < 64, low, high)
                if (27 - p) % 8 == phase:
                    at = (27 - p) // 8 * 128
                    x_scr[1, rows] = turned[:, at : at + 128]
        out_ref[1, h] = x_scr[0].astype(BF16)
        out_ref[2, h] = x_scr[1].astype(BF16)
        expand(SIDE_COLS, WIN - SIDE_COLS)
        left = w_scr[:, 0:256]
        expand(SIDE_COLS, 0, 64)
        right = w_scr[:, 0:256]
        whole = jnp.concatenate([left, right], axis=0)
        for p in range(KWIN):
            rows = slice(p * KWIN, (p + 1) * KWIN)
            at = (23 - p) * SIDE_COLS
            turned = whole if at == 0 else pltpu.roll(whole, 256 - at, 1)
            x_scr[0, rows] = jnp.where(lanes < 64, turned[0:KWIN, 0:128], turned[KWIN:, 0:128])
        out_ref[0, h] = x_scr[0].astype(BF16)
        return carry

    lax.fori_loop(0, HEADS, head, 0)
    weights_into(qkv_ref, proj_ref, wk_ref, wqv_ref, wp_ref)


def build_bias(bias_table, qkv_weight, proj_weight):
    chans = qkv_weight.shape[0]
    width = HEADS * HP
    return call(
        bias_kernel,
        (
            jax.ShapeDtypeStruct((3, HEADS, KEYS, 128), BF16),
            jax.ShapeDtypeStruct((chans, 3 * 128), BF16),
            jax.ShapeDtypeStruct((2 * width, chans), BF16),
            jax.ShapeDtypeStruct((width, chans), BF16),
        ),
        [
            pltpu.VMEM((8 * SIDE, 128), F32),
            pltpu.VMEM((SIDE + 1, 640), F32),
            pltpu.VMEM((KWIN, 640), F32),
            pltpu.VMEM((2, KEYS, 128), F32),
        ],
        4_000_000_000,
        4_000_000,
    )(bias_table.T, qkv_weight, proj_weight)


def one_hot(shape, row_of, col_of):
    row = lax.broadcasted_iota(jnp.int32, shape, 0)
    col = lax.broadcasted_iota(jnp.int32, shape, 1)
    return (row_of(row) == col_of(col)).astype(F32).astype(BF16)


def spread_head(place):
    return jnp.where(place % HP < HD, place // HP * HD + place % HP, -1)


def weights_into(qkv_ref, proj_ref, wk_ref, wqv_ref, wp_ref):
    chans = qkv_ref.shape[0]
    width = HEADS * HP
    qkv = qkv_ref[...]
    pick = one_hot(
        (3 * chans, 3 * 128),
        lambda row: row,
        lambda col: jnp.where(
            (col % 128 < 2 * HP) & (col % HP < HD),
            chans + (col // 128 * 2 + col % 128 // HP) * HD + col % HP,
            -1,
        ),
    )
    wk_ref[...] = dot(qkv, pick).astype(BF16)
    pick = one_hot(
        (2 * width, 3 * chans),
        lambda row: jnp.where(
            row % HP < HD, row // HP * HD + row % HP + jnp.where(row < width, 0, chans), -1
        ),
        lambda col: col,
    )
    wqv_ref[...] = dot_nt(pick, qkv).astype(BF16)
    pick = one_hot((width, chans), spread_head, lambda col: col)
    wp_ref[...] = dot(pick, proj_ref[...]).astype(BF16)


def set_queries(q_scr, wqv_ref, groups, strips=None):
    scale = LOG2E / np.sqrt(HD)
    rows = jnp.concatenate([rows.reshape(128, rows.shape[-1]) for rows in groups], axis=0)
    queries = (dot_nt(wqv_ref[0 : HEADS * HP], rows.astype(BF16)) * scale).astype(BF16)
    none = jnp.zeros((HP, 128), BF16)
    left = lax.broadcasted_iota(jnp.int32, (HP, 128), 1) < 64
    for g in range(len(groups)):
        lanes = slice(128 * g, 128 * g + 128)
        for t in range(HEADS // 2):
            one = queries[2 * t * HP : (2 * t + 1) * HP, lanes]
            two = queries[(2 * t + 1) * HP : (2 * t + 2) * HP, lanes]
            if g == strips:
                q_scr[g, t, 2 * HP : 3 * HP] = jnp.concatenate([jnp.where(left, none, one), none], axis=1)
                q_scr[g, t, 3 * HP : 4 * HP] = jnp.concatenate([none, jnp.where(left, none, two)], axis=1)
                one, two = jnp.where(left, one, none), jnp.where(left, two, none)
            elif strips is not None:
                q_scr[g, t, 2 * HP : 4 * HP] = jnp.zeros((2 * HP, 256), BF16)
            q_scr[g, t, 0:HP] = jnp.concatenate([one, none], axis=1)
            q_scr[g, t, HP : 2 * HP] = jnp.concatenate([none, two], axis=1)


def lookup(g, values):
    out = values[0]
    for index in range(1, len(values)):
        out = jnp.where(g >= index, values[index], out)
    return out


def attention(kinds, windows, q_scr, k_ref, v_ref, bias_ref, wp_ref, s_scr, m_scr, p_scr, o_scr, v_right=None):
    groups = len(kinds)
    pairs = HEADS // 2
    step = 144
    depth = 2 * HP if v_right is None else 4 * HP
    left = lax.broadcasted_iota(jnp.int32, (HP, 128), 1) < 64

    def keep(g, t, k0, top):
        keys = k_ref[lookup(g, windows), k0 : k0 + step, 128 * t : 128 * t + depth]
        one = dot(keys, q_scr[g, t])
        s_scr[t, k0 : k0 + step] = one
        part = jnp.max(one.reshape(step // 8, 8, 256), axis=0)
        return part if top is None else jnp.maximum(top, part)

    def sum_values(g, t):
        for half in range(2):
            head = 2 * t + half
            lanes = slice(128 * half, 128 * half + 128)
            window, rows = lookup(g, windows), slice(head * HP, (head + 1) * HP)
            values = v_ref[window, rows]
            if v_right is None:
                o_scr[g, head] = dot(values, p_scr[t, :, lanes])
            else:
                values = jnp.concatenate([values, v_right[window, rows]], axis=0)
                both = dot(values, p_scr[t, :, lanes])
                o_scr[g, head] = jnp.where(left, both[0:HP], both[HP : 2 * HP])

    top = None
    for k0 in range(0, KEYS, step):
        top = keep(0, 0, k0, top)
    m_scr[...] = top
    p_scr[pairs - 1] = jnp.zeros((KEYS, 256), BF16)

    def attend(g, carry):
        kind = lookup(g, kinds)
        top = m_scr[...]
        for t in range(pairs):
            top = jnp.max(top, axis=0, keepdims=True)
            if t == 0:
                sum_values(jnp.maximum(g - 1, 0), pairs - 1)
            else:
                sum_values(g, t - 1)
            following = g if t + 1 < pairs else jnp.minimum(g + 1, groups - 1)
            later = None
            for k0 in range(0, KEYS, step):
                later = keep(following, (t + 1) % pairs, k0, later)
                prob = jnp.exp2(s_scr[t, k0 : k0 + step] - top).astype(BF16)
                for half in range(2):
                    lanes = slice(128 * half, 128 * half + 128)
                    p_scr[t, k0 : k0 + step, lanes] = (
                        prob[:, lanes] * bias_ref[kind, 2 * t + half, k0 : k0 + step]
                    )
            top = later
        m_scr[...] = top
        return carry

    lax.fori_loop(0, groups, attend, 0)
    sum_values(groups - 1, pairs - 1)
    attended = []
    for g in range(groups):
        parts = []
        for head in range(HEADS):
            one = o_scr[g, head]
            parts.append((one * (1.0 / one[HD : HD + 1])).astype(BF16))
        attended.append(jnp.concatenate(parts, axis=0))
    attended = jnp.concatenate(attended, axis=1)
    return lax.dot_general(attended, wp_ref[...], TN, preferred_element_type=F32)


def feed_forward(first, gain, hidden_ref, output_ref):
    normed = layer_norm(first, gain).astype(BF16)
    inner = dot(normed, hidden_ref[...])
    inner = (0.5 * inner * (1.0 + lax.erf(inner * np.float32(np.sqrt(0.5))))).astype(BF16)
    return first + dot_nt(inner, output_ref[...])


def feed_groups(first, gain, hidden_ref, output_ref, batch):
    out = []
    for start in range(0, first.shape[0], 128 * batch):
        mixed = feed_forward(first[start : start + 128 * batch], gain, hidden_ref, output_ref)
        out += [mixed[128 * g : 128 * (g + 1)] for g in range(batch)]
    return out


def project(keys, wk_ref, wqv_ref, k_ref, v_ref, index):
    keys = keys.reshape(KEYS, keys.shape[2]).astype(BF16)
    k_ref[index] = dot(keys, wk_ref[...]).astype(BF16)
    v_ref[index] = project_values(keys, wqv_ref)


def project_values(keys, wqv_ref):
    width = HEADS * HP
    one_row = (lax.broadcasted_iota(jnp.int32, (width, 1), 0) % HP == HD).astype(F32)
    return (dot_nt(wqv_ref[width : 2 * width], keys) + one_row).astype(BF16)


def at_edges():
    row, column = lax.axis_index("rows"), lax.axis_index("cols")
    return (
        column == 0,
        column == lax.axis_size("cols") - 1,
        row == 0,
        row == lax.axis_size("rows") - 1,
        row % 2 == 0,
        column % 2 == 0,
    )


def from_sides(even, first, second):
    first, second = first.astype(F32), second.astype(F32)
    return jnp.where(even, second, first), jnp.where(even, first, second)


def border_rows(ref, c0):
    return jnp.concatenate([ref[0:4, c0 : c0 + WIN], ref[12:16, c0 : c0 + WIN]], axis=0)


def halves(wide, count):
    left = lax.broadcasted_iota(jnp.int32, (1, 128), 1) < 64
    rest = wide.shape[0] - count
    out = jnp.where(left, wide[0:rest], pltpu.roll(wide[count:], 64, 1))
    return out if rest == count else jnp.concatenate([out, wide[rest:count]], axis=0)


def unhalve(packed, rows):
    count = packed.shape[0]
    return jnp.concatenate([packed, pltpu.roll(packed[0 : rows - count], 64, 1)], axis=0)


def pack_kernel(own_ref, row_one_ref, row_two_ref, pay_one_ref, pay_two_ref, x_scr, flat):
    height, cols, chans = own_ref.shape
    even_row, even_col = at_edges()[4:]
    above, below = from_sides(even_row, row_one_ref[...], row_two_ref[...])
    x_scr[0:RIM] = above
    x_scr[RIM : RIM + height] = own_ref[...].astype(F32)
    x_scr[RIM + height :] = below
    for side, near, far in ((0, 0, WIN), (1, cols - WIN, cols - WIN - RIM)):
        for r in range(height + 2 * RIM):
            flat[side, WIN * r : WIN * (r + 1), 0:chans] = x_scr[r, near : near + WIN]
            place = WIN * (height + 2 * RIM) + RIM * r
            flat[side, place : place + RIM, 0:chans] = x_scr[r, far : far + RIM]
    count = flat.shape[1]
    for lanes in (slice(0, 128), slice(128, 256)):
        low, high = flat[0, :, lanes], flat[1, :, lanes]
        one, two = jnp.where(even_col, high, low), jnp.where(even_col, low, high)
        rows = slice(0, count)
        if lanes.start:
            one, two = halves(one, count // 2), halves(two, count // 2)
            rows = slice(count, count + count // 2)
        pay_one_ref[rows] = one.astype(BF16)
        pay_two_ref[rows] = two.astype(BF16)


def pack(own, row_one, row_two):
    height, cols, chans = own.shape
    pixels = (height + 2 * RIM) * (WIN + RIM)
    pay = jax.ShapeDtypeStruct((pixels * 3 // 2, 128), BF16)
    return call(
        pack_kernel,
        (pay, pay),
        [
            pltpu.VMEM((height + 2 * RIM, cols, chans), F32),
            pltpu.VMEM((2, pixels, 256), F32),
        ],
        1_000_000,
        1_000_000,
    )(own, row_one, row_two)


def inner_kernel(
    own_ref,
    row_one_ref,
    row_two_ref,
    gain_one_ref,
    wk_ref,
    wqv_ref,
    wp_ref,
    bias_ref,
    gain_two_ref,
    hidden_ref,
    output_ref,
    nrm_ref,
    k_ref,
    v_ref,
    border_ref,
    mid_ref,
    q_scr,
    s_scr,
    m_scr,
    p_scr,
    o_scr,
):
    height, cols, chans = own_ref.shape
    inner = cols // WIN - 2
    flags = at_edges()
    gain_one = gain_one_ref[...]
    for r in range(RIM):
        above, below = from_sides(flags[4], row_one_ref[r], row_two_ref[r])
        nrm_ref[r] = layer_norm(above, gain_one)
        nrm_ref[RIM + height + r] = layer_norm(below, gain_one)
    for r in range(height):
        nrm_ref[RIM + r] = layer_norm(own_ref[r].astype(F32), gain_one)
    kinds, windows, first, queries = [], [], [], []
    for w in range(inner):
        c0 = WIN * (w + 1)
        project(nrm_ref[:, c0 - RIM : c0 - RIM + KWIN], wk_ref, wqv_ref, k_ref, v_ref, w)
        first.append(border_rows(own_ref, c0).reshape(128, chans))
        queries.append(border_rows(nrm_ref.at[RIM : RIM + height], c0))
        kinds.append(1)
        windows.append(w)
    for w in range(inner - 1):
        c0 = WIN * (w + 1)
        first.append(own_ref[4:12, c0 : c0 + WIN].reshape(128, chans))
        queries.append(nrm_ref[RIM + 4 : RIM + 12, c0 : c0 + WIN])
        kinds.append(2)
        windows.append(w)
    groups = len(kinds)
    set_queries(q_scr, wqv_ref, queries)
    first = jnp.concatenate(first, axis=0).astype(F32) + attention(
        kinds, windows, q_scr, k_ref, v_ref, bias_ref, wp_ref, s_scr, m_scr, p_scr, o_scr
    )
    mixed = feed_groups(first, gain_two_ref[...], hidden_ref, output_ref, len(kinds))
    for g in range(groups):
        one = mixed[g].reshape(8, WIN, chans)
        if g < inner:
            border_ref[:, WIN * g : WIN * (g + 1)] = one
        else:
            mid_ref[:, WIN * (g - inner) : WIN * (g - inner + 1)] = one


def outer_kernel(
    own_ref,
    nrm_ref,
    col_two_ref,
    col_one_ref,
    gain_one_ref,
    wk_ref,
    wqv_ref,
    wp_ref,
    inner_k_ref,
    inner_v_ref,
    inner_border_ref,
    bias_ref,
    gain_two_ref,
    hidden_ref,
    output_ref,
    pay_one_ref,
    pay_two_ref,
    edge_ref,
    side_ref,
    strip_ref,
    k_ref,
    v_ref,
    side_scr,
    x_scr,
    n_scr,
    b_scr,
    strips,
    v_right,
    q_scr,
    s_scr,
    m_scr,
    p_scr,
    o_scr,
    image,
):
    height, cols, chans = own_ref.shape
    inner = cols // WIN - 2
    flags = at_edges()
    gain_one = gain_one_ref[...]
    rows = height + 2 * RIM
    pixels = rows * (WIN + RIM)
    both = from_sides(flags[5], col_one_ref[...], col_two_ref[...])
    for side in range(2):
        x_scr[side, :, 0:128] = both[side][0:pixels]
        x_scr[side, :, 128:256] = unhalve(both[side][pixels:], pixels)
        n_scr[...] = layer_norm(x_scr[side, :, 0:chans], gain_one)
        near, far = (EDGE - WIN, EDGE - WIN - RIM) if side == 0 else (EDGE, EDGE + WIN)
        for r in range(rows):
            side_scr[side, r, near : near + WIN] = n_scr[WIN * r : WIN * (r + 1)]
            place = WIN * rows + RIM * r
            side_scr[side, r, far : far + RIM] = n_scr[place : place + RIM]
        c0 = WIN - STRIP if side == 0 else 0
        x = x_scr[side, 0 : WIN * rows, 0:chans].reshape(rows, WIN, chans)
        strip_ref[side] = x[:, c0 : c0 + STRIP]
    side_scr[0, :, EDGE : 2 * EDGE] = nrm_ref[:, 0:EDGE]
    side_scr[1, :, 0:EDGE] = nrm_ref[:, cols - EDGE : cols]
    k_ref[2] = inner_k_ref[inner - 1]
    v_ref[2] = inner_v_ref[inner - 1]
    for index, side, c0 in ((1, 0, RIM + WIN), (3, 1, RIM)):
        project(side_scr[side, :, c0 : c0 + KWIN], wk_ref, wqv_ref, k_ref, v_ref, index)
        v_right[index] = v_ref[index]
    strip_keys = [
        side_scr[side, :, c0 : c0 + KWIN].reshape(KEYS, chans).astype(BF16)
        for side, c0 in ((0, RIM), (1, RIM + WIN))
    ]
    moved = pltpu.roll(wk_ref[...].astype(F32), 2 * HP, 1).astype(BF16)
    k_ref[0] = (dot(strip_keys[0], wk_ref[...]) + dot(strip_keys[1], moved)).astype(BF16)
    v_ref[0] = project_values(strip_keys[0], wqv_ref)
    v_right[0] = project_values(strip_keys[1], wqv_ref)
    n = SIDE_COLS
    for r in range(height):
        for side, c0, c1 in ((0, STRIP - n, EDGE - n), (1, 0, EDGE)):
            place = slice(64 * side + n * r, 64 * side + n * (r + 1))
            strips[0, place] = strip_ref[side, RIM + r, c0 : c0 + n]
            strips[1, place] = side_scr[side, RIM + r, c1 : c1 + n]
    first, queries = [strips[0]], [strips[1]]
    spots = (0, cols - WIN)
    for c0 in spots:
        first.append(border_rows(own_ref, c0).astype(F32).reshape(128, chans))
        queries.append(border_rows(nrm_ref.at[RIM : RIM + height], c0))
    set_queries(q_scr, wqv_ref, queries, 0)
    first = jnp.concatenate(first, axis=0) + attention(
        [0, 1, 1], [0, 1, 3], q_scr, k_ref, v_ref, bias_ref, wp_ref, s_scr, m_scr, p_scr, o_scr, v_right
    )
    image[:, 0:STRIP] = jnp.zeros((height, STRIP, chans), F32)
    image[:, STRIP + cols :] = jnp.zeros((height, STRIP, chans), F32)
    image[0:4, STRIP + WIN : STRIP + cols - WIN] = inner_border_ref[0:4]
    image[12:16, STRIP + WIN : STRIP + cols - WIN] = inner_border_ref[4:8]
    mixed = feed_groups(first, gain_two_ref[...], hidden_ref, output_ref, 3)
    row = lax.broadcasted_iota(jnp.int32, (128, chans), 0)
    outside = (flags[0] & (row < 64)) | (flags[1] & (row >= 64))
    strips[0] = jnp.where(outside, 0.0, mixed[0])
    for r in range(height):
        for side, c0 in ((0, STRIP - n), (1, STRIP + cols)):
            place = 64 * side + n * r
            image[r, c0 : c0 + n] = strips[0, place : place + n]
    for g in range(2):
        one = mixed[1 + g].reshape(8, WIN, chans)
        c0 = STRIP + spots[g]
        image[0:4, c0 : c0 + WIN] = one[0:4]
        image[12:16, c0 : c0 + WIN] = one[4:8]
    even = flags[4]
    count = 3 * image.shape[1]
    for pay_ref, rows in (
        (pay_one_ref, jnp.where(even, image[13:16], image[0:3])),
        (pay_two_ref, jnp.where(even, image[0:3], image[13:16])),
    ):
        b_scr[:, 0:chans] = rows.reshape(count, chans)
        pay_ref[0:count] = b_scr[:, 0:128].astype(BF16)
        pay_ref[count:] = halves(b_scr[:, 128:256], 128).astype(BF16)
    edge_ref[0:4] = image[0:4]
    edge_ref[4:8] = image[12:16]
    side_ref[:, 0:STRIP] = image[4:12, 0:STRIP]
    side_ref[:, STRIP : 2 * STRIP] = image[4:12, STRIP + cols :]


def fill_taps(taps_ref, image, span):
    chans = image.shape[2]
    for b in range(3):
        start = STRIP - 3 + b
        lanes = slice(256 * b + 128, 256 * b + 256)
        taps_ref[:, :, lanes] = jnp.zeros((taps_ref.shape[0], span, 128), BF16)
        taps_ref[:, :, 256 * b : 256 * b + chans] = image[:, start : start + span].astype(BF16)


def conv_weights(group_ref, before_ref, upsample_ref, wg_scr, wb_scr, wu_scr):
    chans = group_ref.shape[2]
    feats = before_ref.shape[2]
    pad = chans // 16 * 16
    for a in range(3):
        wb_scr[256 * a + pad : 256 * (a + 1)] = jnp.zeros((256 - pad, 3 * feats), BF16)
        wu_scr[256 * a + 3 * feats : 256 * (a + 1)] = jnp.zeros((256 - 3 * feats, 4 * feats), BF16)
        for b in range(3):
            wg_scr[256 * (3 * a + b) + pad : 256 * (3 * a + b + 1)] = jnp.zeros((256 - pad, chans), BF16)
            wg_scr[256 * (3 * a + b) : 256 * (3 * a + b) + chans] = group_ref[a, b]
    same = one_hot((chans, chans), lambda row: row, lambda col: col)
    order = one_hot(
        (4 * feats, 4 * feats), lambda row: row, lambda col: col % feats * 4 + col // feats
    )
    for a in range(3):
        part = before_ref[a].reshape(3 * feats, chans)
        wb_scr[256 * a : 256 * a + chans] = dot_nt(same, part).astype(BF16)
        part = upsample_ref[a].reshape(3 * feats, 4 * feats)
        wu_scr[256 * a : 256 * a + 3 * feats] = dot(part, order).astype(BF16)


def middle_kernel(
    own_ref,
    nrm_ref,
    k_ref,
    v_ref,
    wqv_ref,
    wp_ref,
    inner_mid_ref,
    edge_ref,
    side_ref,
    strip_ref,
    row_two_ref,
    row_one_ref,
    group_ref,
    before_ref,
    upsample_ref,
    bias_ref,
    gain_two_ref,
    hidden_ref,
    output_ref,
    taps_ref,
    base_ref,
    wg_ref,
    wb_ref,
    wu_ref,
    q_scr,
    s_scr,
    m_scr,
    p_scr,
    o_scr,
    image,
):
    height, cols, chans = own_ref.shape
    spots = (0, cols - 2 * WIN, cols - WIN)
    set_queries(q_scr, wqv_ref, [nrm_ref[RIM + 4 : RIM + 12, c0 : c0 + WIN] for c0 in spots])
    first = [own_ref[4:12, c0 : c0 + WIN].reshape(128, chans) for c0 in spots]
    first = jnp.concatenate(first, axis=0).astype(F32) + attention(
        [2, 2, 2], [1, 2, 3], q_scr, k_ref, v_ref, bias_ref, wp_ref, s_scr, m_scr, p_scr, o_scr
    )
    mixed = feed_groups(first, gain_two_ref[...], hidden_ref, output_ref, 3)
    span = cols + 2 * STRIP
    image[:, span:] = jnp.zeros((height, STRIP, chans), F32)
    image[0:4, 0:span] = edge_ref[0:4]
    image[4:12, 0:STRIP] = side_ref[:, 0:STRIP]
    image[4:12, STRIP + WIN : STRIP + cols - 2 * WIN] = inner_mid_ref[...]
    for g in range(3):
        c0 = STRIP + spots[g]
        image[4:12, c0 : c0 + WIN] = mixed[g].reshape(8, WIN, chans)
    image[4:12, STRIP + cols : span] = side_ref[:, STRIP : 2 * STRIP]
    image[12:16, 0:span] = edge_ref[4:8]
    fill_taps(taps_ref, image, span)
    conv_weights(group_ref, before_ref, upsample_ref, wg_ref, wb_ref, wu_ref)
    even_row = at_edges()[4]
    above, below = from_sides(even_row, row_one_ref[...], row_two_ref[...])
    base_ref[0:2, STRIP : STRIP + cols] = above[2:4]
    base_ref[2 : 2 + height, STRIP : STRIP + cols] = own_ref[...].astype(F32)
    base_ref[2 + height : 4 + height, STRIP : STRIP + cols] = below[0:2]
    rows = slice(2, height + 6)
    base_ref[:, 0:STRIP] = strip_ref[0, rows]
    base_ref[:, STRIP + cols : span] = strip_ref[1, rows]
    base_ref[:, span:] = jnp.zeros((height + 4, STRIP, chans), F32)


def attention_scratch(groups, depth=2 * HP):
    return [
        pltpu.VMEM((groups, HEADS // 2, depth, 256), BF16),
        pltpu.VMEM((HEADS // 2, KEYS, 256), F32),
        pltpu.VMEM((8, 256), F32),
        pltpu.VMEM((HEADS // 2, KEYS, 256), BF16),
        pltpu.VMEM((groups, HEADS, HP, 128), F32),
    ]


def inner_block(*args):
    height, cols, chans = args[0].shape
    inner = cols // WIN - 2
    width = HEADS * HP
    groups = 2 * inner - 1
    return call(
        inner_kernel,
        (
            jax.ShapeDtypeStruct((height + 2 * RIM, cols, chans), F32),
            jax.ShapeDtypeStruct((inner, KEYS, 3 * 128), BF16),
            jax.ShapeDtypeStruct((inner, width, KEYS), BF16),
            jax.ShapeDtypeStruct((8, WIN * inner, chans), F32),
            jax.ShapeDtypeStruct((8, WIN * (inner - 1), chans), F32),
        ),
        attention_scratch(groups),
        5_000_000_000,
        4_000_000,
    )(*args)


def outer_block(*args):
    height, cols, chans = args[0].shape
    span = cols + 2 * STRIP
    return call(
        outer_kernel,
        (
            jax.ShapeDtypeStruct((3 * span + 128, 128), BF16),
            jax.ShapeDtypeStruct((3 * span + 128, 128), BF16),
            jax.ShapeDtypeStruct((8, span, chans), F32),
            jax.ShapeDtypeStruct((8, 2 * STRIP, chans), F32),
            jax.ShapeDtypeStruct((2, height + 2 * RIM, STRIP, chans), F32),
            jax.ShapeDtypeStruct((4, KEYS, 3 * 128), BF16),
            jax.ShapeDtypeStruct((4, HEADS * HP, KEYS), BF16),
        ),
        [
            pltpu.VMEM((2, height + 2 * RIM, 2 * EDGE, chans), F32),
            pltpu.VMEM((2, (height + 2 * RIM) * (WIN + RIM), 256), F32),
            pltpu.VMEM(((height + 2 * RIM) * (WIN + RIM), chans), F32),
            pltpu.VMEM((3 * span, 256), F32),
            pltpu.VMEM((2, 128, chans), F32),
            pltpu.VMEM((4, HEADS * HP, KEYS), BF16),
            *attention_scratch(3, 4 * HP),
            pltpu.VMEM((height, span, chans), F32),
        ],
        5_000_000_000,
        4_000_000,
    )(*args)


def middle_block(*args):
    height, cols, chans = args[0].shape
    span = cols + 2 * STRIP
    feats = args[-6].shape[2]
    return call(
        middle_kernel,
        (
            jax.ShapeDtypeStruct((height, span, 768), BF16),
            jax.ShapeDtypeStruct((height + 4, span + STRIP, chans), F32),
            jax.ShapeDtypeStruct((9 * 256, chans), BF16),
            jax.ShapeDtypeStruct((3 * 256, 3 * feats), BF16),
            jax.ShapeDtypeStruct((3 * 256, 4 * feats), BF16),
        ),
        [*attention_scratch(3), pltpu.VMEM((height, span + STRIP, chans), F32)],
        5_000_000_000,
        4_000_000,
    )(*args)


def conv_kernel(
    taps_ref,
    base,
    back_two_ref,
    back_one_ref,
    wg_scr,
    wb_scr,
    wu_scr,
    out_ref,
    image,
    halo_taps,
    grouped,
    sums,
    lowfeat,
    low_taps,
    out_scr,
):
    height, span = taps_ref.shape[:2]
    cols = span - 2 * STRIP
    chans = base.shape[2]
    feats = out_ref.shape[0]
    at_left, at_right, at_top, at_bottom, even_row, _ = at_edges()
    image[:, span:] = jnp.zeros((6, STRIP, chans), F32)
    sides = from_sides(even_row, back_one_ref[...], back_two_ref[...])
    for rows, packed in ((slice(0, 3), sides[0]), (slice(3, 6), sides[1])):
        image[rows, 0:span, 0:128] = packed[0 : 3 * span].reshape(3, span, 128)
        rest = unhalve(packed[3 * span :], 3 * span).reshape(3, span, 128)
        image[rows, 0:span, 128:chans] = rest[:, :, 0 : chans - 128]
    fill_taps(halo_taps, image, span)
    grouped[:, :, 128:256] = jnp.zeros((height + 4, span, 128), BF16)
    col = lax.broadcasted_iota(jnp.int32, (span, chans), 0) - 2
    keep_grouped = (col < cols + 2) & ((col >= 0) | jnp.logical_not(at_left))
    keep_grouped = keep_grouped & ((col < cols) | jnp.logical_not(at_right))
    low_span = cols + 8
    col = lax.broadcasted_iota(jnp.int32, (low_span, 128), 0) - 1
    keep_low = (col <= cols) & ((col >= 0) | jnp.logical_not(at_left))
    keep_low = keep_low & ((col < cols) | jnp.logical_not(at_right))
    left_half = lax.broadcasted_iota(jnp.int32, (cols, 128), 1) < feats
    spot = lax.broadcasted_iota(jnp.int32, (256, 256), 0)
    place = lax.broadcasted_iota(jnp.int32, (256, 256), 1)
    spread = (spot % 128 // cols == place // 128) & (
        spot % cols * 2 + spot // 128 == place % 128
    )
    spread = spread.astype(F32).astype(BF16)

    def tap_row(row):
        if 3 <= row < height + 3:
            return taps_ref[row - 3]
        return halo_taps[row if row < 3 else row - height]

    def group(h, part):
        lhs = jnp.concatenate(
            [
                jnp.concatenate([tap_row(h + a + r) for r in range(part)], axis=0)
                for a in range(3)
            ],
            axis=1,
        )
        total = dot(lhs, wg_scr[...]).reshape(part, span, chans)
        total = total + base[h : h + part, STRIP - 2 : STRIP - 2 + span, :]
        for r in range(part):
            mask = keep_grouped
            if h + r < 2:
                mask = mask & jnp.logical_not(at_top)
            if h + r >= height + 2:
                mask = mask & jnp.logical_not(at_bottom)
            grouped[h + r, 0:span, 0:chans] = jnp.where(mask, total[r], 0.0).astype(BF16)

    def narrow(h, count):
        lhs = jnp.concatenate(
            [grouped[h + a : h + a + count].reshape(count * span, 256) for a in range(3)], axis=1
        )
        slot = h // count % 2
        sums[slot, 0:count, :, 0 : 3 * feats] = dot(lhs, wb_scr[...]).reshape(count, span, 3 * feats)
        for r in range(count):
            total = sums[slot, r, 0:low_span, 0:128]
            total = total + pltpu.roll(sums[slot, r, 1 : low_span + 1, 0:128], feats, 1)
            total = total + sums[slot, r, 2 : low_span + 2, 128:256]
            mask = keep_low
            if h + r == 0:
                mask = mask & jnp.logical_not(at_top)
            if h + r == height + 1:
                mask = mask & jnp.logical_not(at_bottom)
            lowfeat[h + r] = jnp.where(mask, jnp.where(total >= 0, total, 0.01 * total), 0.0)
            low_taps[h + r, :, 0:128] = jnp.where(
                left_half, lowfeat[h + r, 0:cols], pltpu.roll(lowfeat[h + r, 1 : cols + 1], feats, 1)
            ).astype(BF16)
            low_taps[h + r, :, 128:256] = jnp.where(
                left_half, lowfeat[h + r, 2 : cols + 2], 0.0
            ).astype(BF16)

    def expand(h, part):
        lhs = jnp.concatenate(
            [low_taps[h + a : h + a + part].reshape(part * cols, 256) for a in range(3)], axis=1
        )
        total = dot(lhs, wu_scr[...])
        for pair in range(part // 2):
            turned = total[2 * cols * pair : 2 * cols * (pair + 1)].T.astype(BF16)
            lhs = [
                jnp.concatenate(
                    [turned[(2 * a + b) * feats : (2 * a + b + 1) * feats] for b in range(2)], axis=1
                )
                for a in range(2)
            ]
            final = dot(jnp.concatenate(lhs, axis=0), spread)
            for r in range(2):
                for a in range(2):
                    row = 2 * (h + 2 * pair + r) + a
                    out_scr[pl.ds(row, feats, stride=2 * height), :] = final[
                        a * feats : (a + 1) * feats, 128 * r : 128 * (r + 1)
                    ]

    half, third = (height + 4) // 2, (height + 2) // 3
    group(0, half)
    group(half, half)
    narrow(0, third)
    narrow(third, third)
    expand(0, height // 2)
    narrow(2 * third, third)
    expand(height // 2, height // 2)
    out_ref[...] = out_scr[...].reshape(feats, 2 * height, 128).astype(BF16)


def convs(*args):
    height, span = args[0].shape[:2]
    chans = args[1].shape[2]
    cols = span - 2 * STRIP
    feats = args[-1].shape[1] // 4
    return call(
        conv_kernel,
        jax.ShapeDtypeStruct((feats, 2 * height, 2 * cols), BF16),
        [
            pltpu.VMEM((6, span + STRIP, chans), F32),
            pltpu.VMEM((6, span, 768), BF16),
            pltpu.VMEM((height + 4, span, 256), BF16),
            pltpu.VMEM((2, 6, span, 256), F32),
            pltpu.VMEM((height + 2, cols + 8, 128), F32),
            pltpu.VMEM((height + 2, cols, 256), BF16),
            pltpu.VMEM((feats * 2 * height, 128), F32),
        ],
        8_000_000_000,
        4_000_000,
    )(*args)


def swapped(axis, first, second):
    count = lax.axis_size(axis)
    out = []
    for start, payload in ((1, second), (0, first)):
        pairs = [(i, i + 1) for i in range(start, count - 1, 2)]
        pairs = pairs + [(b, a) for a, b in pairs]
        out.append(lax.ppermute(payload, axis, pairs))
    return out[::-1]


def on_device(
    features,
    gain_one,
    qkv_weight,
    bias_table,
    proj_weight,
    gain_two,
    hidden_weight,
    output_weight,
    group_conv,
    before_conv,
    upsample_conv,
):
    height, cols, chans = features.shape
    even_row = lax.axis_index("rows") % 2 == 0
    low, high = features[:RIM], features[height - RIM :]
    row_one, row_two = swapped(
        "rows", jnp.where(even_row, high, low), jnp.where(even_row, low, high)
    )
    col_one, col_two = swapped("cols", *pack(features, row_one, row_two))

    bias, wk, wqv, wp = build_bias(bias_table, qkv_weight, proj_weight)
    gain_one, gain_two = gain_one.reshape(1, chans), gain_two.reshape(1, chans)
    post = (gain_two, hidden_weight, output_weight.T)
    nrm, inner_k, inner_v, inner_border, inner_mid = inner_block(
        features,
        row_one,
        row_two,
        gain_one,
        wk,
        wqv,
        wp,
        bias,
        *post,
    )
    back_one, back_two, edge, side, strips, keys, values = outer_block(
        features,
        nrm,
        col_two,
        col_one,
        gain_one,
        wk,
        wqv,
        wp,
        inner_k,
        inner_v,
        inner_border,
        bias,
        *post,
    )
    back_one, back_two = swapped("rows", back_one, back_two)
    taps, base, group, before, upsample = middle_block(
        features,
        nrm,
        keys,
        values,
        wqv,
        wp,
        inner_mid,
        edge,
        side,
        strips,
        row_two,
        row_one,
        group_conv,
        before_conv.transpose(0, 1, 3, 2),
        upsample_conv,
        bias,
        *post,
    )
    return convs(taps, base, back_two, back_one, group, before, upsample)


def solution(mesh):
    placed = (P("rows", "cols", None), P(), P(), P(), P(), P(), P(), P(), P(), P(), P())
    return jax.shard_map(
        on_device, mesh=mesh, in_specs=placed, out_specs=P(None, "rows", "cols"), check_vma=False
    )
```

```python
import functools

import jax
import jax.numpy as jnp
import numpy as np
from jax import lax
from jax.experimental import pallas as pl
from jax.experimental.pallas import tpu as pltpu
from jax.sharding import PartitionSpec as P

HEADS = 6
HD = 30
HP = 32
WIN = 16
KWIN = 24
KEYS = KWIN * KWIN
SIDE = WIN + KWIN - 1
RIM = (KWIN - WIN) // 2
EDGE = WIN + 2 * RIM
STRIP = 8
SIDE_COLS = 4
LOG2E = 1.4426950408889634
F32 = jnp.float32
BF16 = jnp.bfloat16
NT = (((1,), (1,)), ((), ()))
TN = (((0,), (0,)), ((), ()))


def dot(a, b):
    return jnp.dot(a, b, preferred_element_type=F32)


def dot_nt(a, b):
    return lax.dot_general(a, b, NT, preferred_element_type=F32)


def layer_norm(values, gain):
    center = values - jnp.mean(values, axis=-1, keepdims=True)
    spread = jnp.mean(center * center, axis=-1, keepdims=True)
    return center * lax.rsqrt(spread + 1e-05) * gain


def call(kernel, out_shape, scratch, flops, bytes_accessed):
    return pl.pallas_call(
        kernel,
        out_shape=out_shape,
        scratch_shapes=scratch,
        compiler_params=pltpu.CompilerParams(vmem_limit_bytes=24 * 2**20),
        cost_estimate=pl.CostEstimate(
            flops=flops, bytes_accessed=bytes_accessed, transcendentals=0
        ),
    )


def bias_kernel(table_ref, out_ref, t_scr, e_scr, w_scr, x_scr):
    for d in range(SIDE):
        t_scr[8 * d : 8 * d + HEADS, 0:SIDE] = jnp.exp(table_ref[:, SIDE * d : SIDE * (d + 1)])

    def head(h, carry):
        values = t_scr[pl.ds(h, SIDE, stride=8), 0:SIDE].astype(BF16)

        def expand(cols, first, shift=0):
            width = -(-(SIDE * cols + shift) // 128) * 128
            spot = (lax.broadcasted_iota(jnp.int32, (SIDE, width), 1) - shift) // cols
            row = lax.broadcasted_iota(jnp.int32, (SIDE, width), 0)
            pick = (spot == SIDE - 1 - row).astype(F32).astype(BF16)
            e_scr[0:SIDE, 0:width] = lax.dot_general(values, pick, TN, preferred_element_type=F32)
            lane = lax.broadcasted_iota(jnp.int32, (KWIN, width), 1) % cols
            out = jnp.zeros((KWIN, width), F32)
            for jj in range(cols):
                start = WIN - 1 - first - jj
                out = jnp.where(lane == jj, e_scr[start : start + KWIN, 0:width], out)
            w_scr[:, 0:width] = out

        lanes = lax.broadcasted_iota(jnp.int32, (KWIN, 128), 1)
        expand(WIN, 0)
        whole = w_scr[...]
        for phase in range(8):
            turned = whole if phase == 0 else pltpu.roll(whole, 640 - WIN * phase, 1)
            for p in range(KWIN):
                rows = slice(p * KWIN, (p + 1) * KWIN)
                if (23 - p) % 8 == phase:
                    at = (23 - p) // 8 * 128
                    low, high = turned[:, at : at + 128], turned[:, at + 128 : at + 256]
                    x_scr[0, rows] = jnp.where(lanes < 64, low, high)
                if (27 - p) % 8 == phase:
                    at = (27 - p) // 8 * 128
                    x_scr[1, rows] = turned[:, at : at + 128]
        out_ref[1, h] = x_scr[0].astype(BF16)
        out_ref[2, h] = x_scr[1].astype(BF16)
        expand(SIDE_COLS, WIN - SIDE_COLS)
        left = w_scr[:, 0:256]
        expand(SIDE_COLS, 0, 64)
        right = w_scr[:, 0:256]
        whole = jnp.concatenate([left, right], axis=0)
        for p in range(KWIN):
            rows = slice(p * KWIN, (p + 1) * KWIN)
            at = (23 - p) * SIDE_COLS
            turned = whole if at == 0 else pltpu.roll(whole, 256 - at, 1)
            x_scr[0, rows] = jnp.where(lanes < 64, turned[0:KWIN, 0:128], turned[KWIN:, 0:128])
        out_ref[0, h] = x_scr[0].astype(BF16)
        return carry

    lax.fori_loop(0, HEADS, head, 0)


def build_bias(bias_table):
    return call(
        bias_kernel,
        jax.ShapeDtypeStruct((3, HEADS, KEYS, 128), BF16),
        [
            pltpu.VMEM((8 * SIDE, 128), F32),
            pltpu.VMEM((SIDE + 1, 640), F32),
            pltpu.VMEM((KWIN, 640), F32),
            pltpu.VMEM((2, KEYS, 128), F32),
        ],
        4_000_000_000,
        4_000_000,
    )(bias_table.T)


def one_hot(shape, row_of, col_of):
    row = lax.broadcasted_iota(jnp.int32, shape, 0)
    col = lax.broadcasted_iota(jnp.int32, shape, 1)
    return (row_of(row) == col_of(col)).astype(F32).astype(BF16)


def spread_head(place):
    return jnp.where(place % HP < HD, place // HP * HD + place % HP, -1)


def weights_into(qkv_ref, proj_ref, wk_ref, wqv_ref, wp_ref):
    chans = qkv_ref.shape[0]
    width = HEADS * HP
    qkv = qkv_ref[...]
    pick = one_hot(
        (3 * chans, 3 * 128),
        lambda row: row,
        lambda col: jnp.where(
            (col % 128 < 2 * HP) & (col % HP < HD),
            chans + (col // 128 * 2 + col % 128 // HP) * HD + col % HP,
            -1,
        ),
    )
    wk_ref[...] = dot(qkv, pick).astype(BF16)
    pick = one_hot(
        (2 * width, 3 * chans),
        lambda row: jnp.where(
            row % HP < HD, row // HP * HD + row % HP + jnp.where(row < width, 0, chans), -1
        ),
        lambda col: col,
    )
    wqv_ref[...] = dot_nt(pick, qkv).astype(BF16)
    pick = one_hot((width, chans), spread_head, lambda col: col)
    wp_ref[...] = dot(pick, proj_ref[...]).astype(BF16)


def set_queries(q_scr, wqv_ref, groups, strips=None):
    scale = LOG2E / np.sqrt(HD)
    rows = jnp.concatenate([rows.reshape(128, rows.shape[-1]) for rows in groups], axis=0)
    queries = (dot_nt(wqv_ref[0 : HEADS * HP], rows.astype(BF16)) * scale).astype(BF16)
    none = jnp.zeros((HP, 128), BF16)
    left = lax.broadcasted_iota(jnp.int32, (HP, 128), 1) < 64
    for g in range(len(groups)):
        lanes = slice(128 * g, 128 * g + 128)
        for t in range(HEADS // 2):
            one = queries[2 * t * HP : (2 * t + 1) * HP, lanes]
            two = queries[(2 * t + 1) * HP : (2 * t + 2) * HP, lanes]
            if g == strips:
                q_scr[g, t, 2 * HP : 3 * HP] = jnp.concatenate([jnp.where(left, none, one), none], axis=1)
                q_scr[g, t, 3 * HP : 4 * HP] = jnp.concatenate([none, jnp.where(left, none, two)], axis=1)
                one, two = jnp.where(left, one, none), jnp.where(left, two, none)
            elif strips is not None:
                q_scr[g, t, 2 * HP : 4 * HP] = jnp.zeros((2 * HP, 256), BF16)
            q_scr[g, t, 0:HP] = jnp.concatenate([one, none], axis=1)
            q_scr[g, t, HP : 2 * HP] = jnp.concatenate([none, two], axis=1)


def lookup(g, values):
    out = values[0]
    for index in range(1, len(values)):
        out = jnp.where(g >= index, values[index], out)
    return out


def attention(kinds, windows, q_scr, k_ref, v_ref, bias_ref, wp_ref, s_scr, m_scr, p_scr, o_scr, v_right=None):
    groups = len(kinds)
    pairs = HEADS // 2
    step = 144
    depth = 2 * HP if v_right is None else 4 * HP
    left = lax.broadcasted_iota(jnp.int32, (HP, 128), 1) < 64

    def keep(g, t, k0, top):
        keys = k_ref[lookup(g, windows), k0 : k0 + step, 128 * t : 128 * t + depth]
        one = dot(keys, q_scr[g, t])
        s_scr[t, k0 : k0 + step] = one
        part = jnp.max(one.reshape(step // 8, 8, 256), axis=0)
        return part if top is None else jnp.maximum(top, part)

    def sum_values(g, t):
        for half in range(2):
            head = 2 * t + half
            lanes = slice(128 * half, 128 * half + 128)
            window, rows = lookup(g, windows), slice(head * HP, (head + 1) * HP)
            values = v_ref[window, rows]
            if v_right is None:
                o_scr[g, head] = dot(values, p_scr[t, :, lanes])
            else:
                values = jnp.concatenate([values, v_right[window, rows]], axis=0)
                both = dot(values, p_scr[t, :, lanes])
                o_scr[g, head] = jnp.where(left, both[0:HP], both[HP : 2 * HP])

    top = None
    for k0 in range(0, KEYS, step):
        top = keep(0, 0, k0, top)
    m_scr[...] = top
    p_scr[pairs - 1] = jnp.zeros((KEYS, 256), BF16)

    def attend(g, carry):
        kind = lookup(g, kinds)
        top = m_scr[...]
        for t in range(pairs):
            top = jnp.max(top, axis=0, keepdims=True)
            if t == 0:
                sum_values(jnp.maximum(g - 1, 0), pairs - 1)
            else:
                sum_values(g, t - 1)
            following = g if t + 1 < pairs else jnp.minimum(g + 1, groups - 1)
            later = None
            for k0 in range(0, KEYS, step):
                later = keep(following, (t + 1) % pairs, k0, later)
                prob = jnp.exp2(s_scr[t, k0 : k0 + step] - top).astype(BF16)
                for half in range(2):
                    lanes = slice(128 * half, 128 * half + 128)
                    p_scr[t, k0 : k0 + step, lanes] = (
                        prob[:, lanes] * bias_ref[kind, 2 * t + half, k0 : k0 + step]
                    )
            top = later
        m_scr[...] = top
        return carry

    lax.fori_loop(0, groups, attend, 0)
    sum_values(groups - 1, pairs - 1)
    attended = []
    for g in range(groups):
        parts = []
        for head in range(HEADS):
            one = o_scr[g, head]
            parts.append((one * (1.0 / one[HD : HD + 1])).astype(BF16))
        attended.append(jnp.concatenate(parts, axis=0))
    attended = jnp.concatenate(attended, axis=1)
    return lax.dot_general(attended, wp_ref[...], TN, preferred_element_type=F32)


def feed_forward(first, gain, hidden_ref, output_ref):
    normed = layer_norm(first, gain).astype(BF16)
    inner = dot(normed, hidden_ref[...])
    inner = (0.5 * inner * (1.0 + lax.erf(inner * np.float32(np.sqrt(0.5))))).astype(BF16)
    return first + dot_nt(inner, output_ref[...])


def feed_groups(first, gain, hidden_ref, output_ref, batch):
    out = []
    for start in range(0, first.shape[0], 128 * batch):
        mixed = feed_forward(first[start : start + 128 * batch], gain, hidden_ref, output_ref)
        out += [mixed[128 * g : 128 * (g + 1)] for g in range(batch)]
    return out


def project(keys, wk_ref, wqv_ref, k_ref, v_ref, index):
    keys = keys.reshape(KEYS, keys.shape[2]).astype(BF16)
    k_ref[index] = dot(keys, wk_ref[...]).astype(BF16)
    v_ref[index] = project_values(keys, wqv_ref)


def project_values(keys, wqv_ref):
    width = HEADS * HP
    one_row = (lax.broadcasted_iota(jnp.int32, (width, 1), 0) % HP == HD).astype(F32)
    return (dot_nt(wqv_ref[width : 2 * width], keys) + one_row).astype(BF16)


def at_edges():
    row, column = lax.axis_index("rows"), lax.axis_index("cols")
    return (
        column == 0,
        column == lax.axis_size("cols") - 1,
        row == 0,
        row == lax.axis_size("rows") - 1,
        row % 2 == 0,
        column % 2 == 0,
    )


def from_sides(even, first, second):
    first, second = first.astype(F32), second.astype(F32)
    return jnp.where(even, second, first), jnp.where(even, first, second)


def border_rows(ref, c0):
    return jnp.concatenate([ref[0:4, c0 : c0 + WIN], ref[12:16, c0 : c0 + WIN]], axis=0)


def halves(wide, count):
    left = lax.broadcasted_iota(jnp.int32, (1, 128), 1) < 64
    rest = wide.shape[0] - count
    out = jnp.where(left, wide[0:rest], pltpu.roll(wide[count:], 64, 1))
    return out if rest == count else jnp.concatenate([out, wide[rest:count]], axis=0)


def unhalve(packed, rows):
    count = packed.shape[0]
    return jnp.concatenate([packed, pltpu.roll(packed[0 : rows - count], 64, 1)], axis=0)


def pack_kernel(own_ref, row_one_ref, row_two_ref, pay_one_ref, pay_two_ref, x_scr, flat):
    height, cols, chans = own_ref.shape
    even_row, even_col = at_edges()[4:]
    above, below = from_sides(even_row, row_one_ref[...], row_two_ref[...])
    x_scr[0:RIM] = above
    x_scr[RIM : RIM + height] = own_ref[...].astype(F32)
    x_scr[RIM + height :] = below
    for side, near, far in ((0, 0, WIN), (1, cols - WIN, cols - WIN - RIM)):
        for r in range(height + 2 * RIM):
            flat[side, WIN * r : WIN * (r + 1), 0:chans] = x_scr[r, near : near + WIN]
            place = WIN * (height + 2 * RIM) + RIM * r
            flat[side, place : place + RIM, 0:chans] = x_scr[r, far : far + RIM]
    count = flat.shape[1]
    for lanes in (slice(0, 128), slice(128, 256)):
        low, high = flat[0, :, lanes], flat[1, :, lanes]
        one, two = jnp.where(even_col, high, low), jnp.where(even_col, low, high)
        rows = slice(0, count)
        if lanes.start:
            one, two = halves(one, count // 2), halves(two, count // 2)
            rows = slice(count, count + count // 2)
        pay_one_ref[rows] = one.astype(BF16)
        pay_two_ref[rows] = two.astype(BF16)


def pack(own, row_one, row_two):
    height, cols, chans = own.shape
    pixels = (height + 2 * RIM) * (WIN + RIM)
    pay = jax.ShapeDtypeStruct((pixels * 3 // 2, 128), BF16)
    return call(
        pack_kernel,
        (pay, pay),
        [
            pltpu.VMEM((height + 2 * RIM, cols, chans), F32),
            pltpu.VMEM((2, pixels, 256), F32),
        ],
        1_000_000,
        1_000_000,
    )(own, row_one, row_two)


def inner_kernel(
    own_ref,
    row_one_ref,
    row_two_ref,
    gain_one_ref,
    qkv_ref,
    proj_ref,
    bias_ref,
    gain_two_ref,
    hidden_ref,
    output_ref,
    nrm_ref,
    wk_ref,
    wqv_ref,
    wp_ref,
    k_ref,
    v_ref,
    border_ref,
    mid_ref,
    q_scr,
    s_scr,
    m_scr,
    p_scr,
    o_scr,
):
    height, cols, chans = own_ref.shape
    inner = cols // WIN - 2
    flags = at_edges()
    weights_into(qkv_ref, proj_ref, wk_ref, wqv_ref, wp_ref)
    gain_one = gain_one_ref[...]
    for r in range(RIM):
        above, below = from_sides(flags[4], row_one_ref[r], row_two_ref[r])
        nrm_ref[r] = layer_norm(above, gain_one)
        nrm_ref[RIM + height + r] = layer_norm(below, gain_one)
    for r in range(height):
        nrm_ref[RIM + r] = layer_norm(own_ref[r].astype(F32), gain_one)
    kinds, windows, first, queries = [], [], [], []
    for w in range(inner):
        c0 = WIN * (w + 1)
        project(nrm_ref[:, c0 - RIM : c0 - RIM + KWIN], wk_ref, wqv_ref, k_ref, v_ref, w)
        first.append(border_rows(own_ref, c0).reshape(128, chans))
        queries.append(border_rows(nrm_ref.at[RIM : RIM + height], c0))
        kinds.append(1)
        windows.append(w)
    for w in range(inner - 1):
        c0 = WIN * (w + 1)
        first.append(own_ref[4:12, c0 : c0 + WIN].reshape(128, chans))
        queries.append(nrm_ref[RIM + 4 : RIM + 12, c0 : c0 + WIN])
        kinds.append(2)
        windows.append(w)
    groups = len(kinds)
    set_queries(q_scr, wqv_ref, queries)
    first = jnp.concatenate(first, axis=0).astype(F32) + attention(
        kinds, windows, q_scr, k_ref, v_ref, bias_ref, wp_ref, s_scr, m_scr, p_scr, o_scr
    )
    mixed = feed_groups(first, gain_two_ref[...], hidden_ref, output_ref, len(kinds))
    for g in range(groups):
        one = mixed[g].reshape(8, WIN, chans)
        if g < inner:
            border_ref[:, WIN * g : WIN * (g + 1)] = one
        else:
            mid_ref[:, WIN * (g - inner) : WIN * (g - inner + 1)] = one


def outer_kernel(
    own_ref,
    nrm_ref,
    col_two_ref,
    col_one_ref,
    gain_one_ref,
    wk_ref,
    wqv_ref,
    wp_ref,
    inner_k_ref,
    inner_v_ref,
    inner_border_ref,
    bias_ref,
    gain_two_ref,
    hidden_ref,
    output_ref,
    pay_one_ref,
    pay_two_ref,
    edge_ref,
    side_ref,
    strip_ref,
    k_ref,
    v_ref,
    side_scr,
    x_scr,
    n_scr,
    b_scr,
    strips,
    v_right,
    q_scr,
    s_scr,
    m_scr,
    p_scr,
    o_scr,
    image,
):
    height, cols, chans = own_ref.shape
    inner = cols // WIN - 2
    flags = at_edges()
    gain_one = gain_one_ref[...]
    rows = height + 2 * RIM
    pixels = rows * (WIN + RIM)
    both = from_sides(flags[5], col_one_ref[...], col_two_ref[...])
    for side in range(2):
        x_scr[side, :, 0:128] = both[side][0:pixels]
        x_scr[side, :, 128:256] = unhalve(both[side][pixels:], pixels)
        n_scr[...] = layer_norm(x_scr[side, :, 0:chans], gain_one)
        near, far = (EDGE - WIN, EDGE - WIN - RIM) if side == 0 else (EDGE, EDGE + WIN)
        for r in range(rows):
            side_scr[side, r, near : near + WIN] = n_scr[WIN * r : WIN * (r + 1)]
            place = WIN * rows + RIM * r
            side_scr[side, r, far : far + RIM] = n_scr[place : place + RIM]
        c0 = WIN - STRIP if side == 0 else 0
        x = x_scr[side, 0 : WIN * rows, 0:chans].reshape(rows, WIN, chans)
        strip_ref[side] = x[:, c0 : c0 + STRIP]
    side_scr[0, :, EDGE : 2 * EDGE] = nrm_ref[:, 0:EDGE]
    side_scr[1, :, 0:EDGE] = nrm_ref[:, cols - EDGE : cols]
    k_ref[2] = inner_k_ref[inner - 1]
    v_ref[2] = inner_v_ref[inner - 1]
    for index, side, c0 in ((1, 0, RIM + WIN), (3, 1, RIM)):
        project(side_scr[side, :, c0 : c0 + KWIN], wk_ref, wqv_ref, k_ref, v_ref, index)
        v_right[index] = v_ref[index]
    strip_keys = [
        side_scr[side, :, c0 : c0 + KWIN].reshape(KEYS, chans).astype(BF16)
        for side, c0 in ((0, RIM), (1, RIM + WIN))
    ]
    moved = pltpu.roll(wk_ref[...].astype(F32), 2 * HP, 1).astype(BF16)
    k_ref[0] = (dot(strip_keys[0], wk_ref[...]) + dot(strip_keys[1], moved)).astype(BF16)
    v_ref[0] = project_values(strip_keys[0], wqv_ref)
    v_right[0] = project_values(strip_keys[1], wqv_ref)
    n = SIDE_COLS
    for r in range(height):
        for side, c0, c1 in ((0, STRIP - n, EDGE - n), (1, 0, EDGE)):
            place = slice(64 * side + n * r, 64 * side + n * (r + 1))
            strips[0, place] = strip_ref[side, RIM + r, c0 : c0 + n]
            strips[1, place] = side_scr[side, RIM + r, c1 : c1 + n]
    first, queries = [strips[0]], [strips[1]]
    spots = (0, cols - WIN)
    for c0 in spots:
        first.append(border_rows(own_ref, c0).astype(F32).reshape(128, chans))
        queries.append(border_rows(nrm_ref.at[RIM : RIM + height], c0))
    set_queries(q_scr, wqv_ref, queries, 0)
    first = jnp.concatenate(first, axis=0) + attention(
        [0, 1, 1], [0, 1, 3], q_scr, k_ref, v_ref, bias_ref, wp_ref, s_scr, m_scr, p_scr, o_scr, v_right
    )
    image[:, 0:STRIP] = jnp.zeros((height, STRIP, chans), F32)
    image[:, STRIP + cols :] = jnp.zeros((height, STRIP, chans), F32)
    image[0:4, STRIP + WIN : STRIP + cols - WIN] = inner_border_ref[0:4]
    image[12:16, STRIP + WIN : STRIP + cols - WIN] = inner_border_ref[4:8]
    mixed = feed_groups(first, gain_two_ref[...], hidden_ref, output_ref, 3)
    row = lax.broadcasted_iota(jnp.int32, (128, chans), 0)
    outside = (flags[0] & (row < 64)) | (flags[1] & (row >= 64))
    strips[0] = jnp.where(outside, 0.0, mixed[0])
    for r in range(height):
        for side, c0 in ((0, STRIP - n), (1, STRIP + cols)):
            place = 64 * side + n * r
            image[r, c0 : c0 + n] = strips[0, place : place + n]
    for g in range(2):
        one = mixed[1 + g].reshape(8, WIN, chans)
        c0 = STRIP + spots[g]
        image[0:4, c0 : c0 + WIN] = one[0:4]
        image[12:16, c0 : c0 + WIN] = one[4:8]
    even = flags[4]
    count = 3 * image.shape[1]
    for pay_ref, rows in (
        (pay_one_ref, jnp.where(even, image[13:16], image[0:3])),
        (pay_two_ref, jnp.where(even, image[0:3], image[13:16])),
    ):
        b_scr[:, 0:chans] = rows.reshape(count, chans)
        pay_ref[0:count] = b_scr[:, 0:128].astype(BF16)
        pay_ref[count:] = halves(b_scr[:, 128:256], 128).astype(BF16)
    edge_ref[0:4] = image[0:4]
    edge_ref[4:8] = image[12:16]
    side_ref[:, 0:STRIP] = image[4:12, 0:STRIP]
    side_ref[:, STRIP : 2 * STRIP] = image[4:12, STRIP + cols :]


def fill_taps(taps_ref, image, span):
    chans = image.shape[2]
    for b in range(3):
        start = STRIP - 3 + b
        lanes = slice(256 * b + 128, 256 * b + 256)
        taps_ref[:, :, lanes] = jnp.zeros((taps_ref.shape[0], span, 128), BF16)
        taps_ref[:, :, 256 * b : 256 * b + chans] = image[:, start : start + span].astype(BF16)


def conv_weights(group_ref, before_ref, upsample_ref, wg_scr, wb_scr, wu_scr):
    chans = group_ref.shape[2]
    feats = before_ref.shape[2]
    pad = chans // 16 * 16
    for a in range(3):
        wb_scr[256 * a + pad : 256 * (a + 1)] = jnp.zeros((256 - pad, 3 * feats), BF16)
        wu_scr[256 * a + 3 * feats : 256 * (a + 1)] = jnp.zeros((256 - 3 * feats, 4 * feats), BF16)
        for b in range(3):
            wg_scr[256 * (3 * a + b) + pad : 256 * (3 * a + b + 1)] = jnp.zeros((256 - pad, chans), BF16)
            wg_scr[256 * (3 * a + b) : 256 * (3 * a + b) + chans] = group_ref[a, b]
    same = one_hot((chans, chans), lambda row: row, lambda col: col)
    order = one_hot(
        (4 * feats, 4 * feats), lambda row: row, lambda col: col % feats * 4 + col // feats
    )
    for a in range(3):
        part = before_ref[a].reshape(3 * feats, chans)
        wb_scr[256 * a : 256 * a + chans] = dot_nt(same, part).astype(BF16)
        part = upsample_ref[a].reshape(3 * feats, 4 * feats)
        wu_scr[256 * a : 256 * a + 3 * feats] = dot(part, order).astype(BF16)


def middle_kernel(
    own_ref,
    nrm_ref,
    k_ref,
    v_ref,
    wqv_ref,
    wp_ref,
    inner_mid_ref,
    edge_ref,
    side_ref,
    strip_ref,
    row_two_ref,
    row_one_ref,
    group_ref,
    before_ref,
    upsample_ref,
    bias_ref,
    gain_two_ref,
    hidden_ref,
    output_ref,
    taps_ref,
    base_ref,
    wg_ref,
    wb_ref,
    wu_ref,
    q_scr,
    s_scr,
    m_scr,
    p_scr,
    o_scr,
    image,
):
    height, cols, chans = own_ref.shape
    spots = (0, cols - 2 * WIN, cols - WIN)
    set_queries(q_scr, wqv_ref, [nrm_ref[RIM + 4 : RIM + 12, c0 : c0 + WIN] for c0 in spots])
    first = [own_ref[4:12, c0 : c0 + WIN].reshape(128, chans) for c0 in spots]
    first = jnp.concatenate(first, axis=0).astype(F32) + attention(
        [2, 2, 2], [1, 2, 3], q_scr, k_ref, v_ref, bias_ref, wp_ref, s_scr, m_scr, p_scr, o_scr
    )
    mixed = feed_groups(first, gain_two_ref[...], hidden_ref, output_ref, 3)
    span = cols + 2 * STRIP
    image[:, span:] = jnp.zeros((height, STRIP, chans), F32)
    image[0:4, 0:span] = edge_ref[0:4]
    image[4:12, 0:STRIP] = side_ref[:, 0:STRIP]
    image[4:12, STRIP + WIN : STRIP + cols - 2 * WIN] = inner_mid_ref[...]
    for g in range(3):
        c0 = STRIP + spots[g]
        image[4:12, c0 : c0 + WIN] = mixed[g].reshape(8, WIN, chans)
    image[4:12, STRIP + cols : span] = side_ref[:, STRIP : 2 * STRIP]
    image[12:16, 0:span] = edge_ref[4:8]
    fill_taps(taps_ref, image, span)
    conv_weights(group_ref, before_ref, upsample_ref, wg_ref, wb_ref, wu_ref)
    even_row = at_edges()[4]
    above, below = from_sides(even_row, row_one_ref[...], row_two_ref[...])
    base_ref[0:2, STRIP : STRIP + cols] = above[2:4]
    base_ref[2 : 2 + height, STRIP : STRIP + cols] = own_ref[...].astype(F32)
    base_ref[2 + height : 4 + height, STRIP : STRIP + cols] = below[0:2]
    rows = slice(2, height + 6)
    base_ref[:, 0:STRIP] = strip_ref[0, rows]
    base_ref[:, STRIP + cols : span] = strip_ref[1, rows]
    base_ref[:, span:] = jnp.zeros((height + 4, STRIP, chans), F32)


def attention_scratch(groups, depth=2 * HP):
    return [
        pltpu.VMEM((groups, HEADS // 2, depth, 256), BF16),
        pltpu.VMEM((HEADS // 2, KEYS, 256), F32),
        pltpu.VMEM((8, 256), F32),
        pltpu.VMEM((HEADS // 2, KEYS, 256), BF16),
        pltpu.VMEM((groups, HEADS, HP, 128), F32),
    ]


def inner_block(*args):
    height, cols, chans = args[0].shape
    inner = cols // WIN - 2
    width = HEADS * HP
    groups = 2 * inner - 1
    return call(
        inner_kernel,
        (
            jax.ShapeDtypeStruct((height + 2 * RIM, cols, chans), F32),
            jax.ShapeDtypeStruct((chans, 3 * 128), BF16),
            jax.ShapeDtypeStruct((2 * width, chans), BF16),
            jax.ShapeDtypeStruct((width, chans), BF16),
            jax.ShapeDtypeStruct((inner, KEYS, 3 * 128), BF16),
            jax.ShapeDtypeStruct((inner, width, KEYS), BF16),
            jax.ShapeDtypeStruct((8, WIN * inner, chans), F32),
            jax.ShapeDtypeStruct((8, WIN * (inner - 1), chans), F32),
        ),
        attention_scratch(groups),
        5_000_000_000,
        4_000_000,
    )(*args)


def outer_block(*args):
    height, cols, chans = args[0].shape
    span = cols + 2 * STRIP
    return call(
        outer_kernel,
        (
            jax.ShapeDtypeStruct((3 * span + 128, 128), BF16),
            jax.ShapeDtypeStruct((3 * span + 128, 128), BF16),
            jax.ShapeDtypeStruct((8, span, chans), F32),
            jax.ShapeDtypeStruct((8, 2 * STRIP, chans), F32),
            jax.ShapeDtypeStruct((2, height + 2 * RIM, STRIP, chans), F32),
            jax.ShapeDtypeStruct((4, KEYS, 3 * 128), BF16),
            jax.ShapeDtypeStruct((4, HEADS * HP, KEYS), BF16),
        ),
        [
            pltpu.VMEM((2, height + 2 * RIM, 2 * EDGE, chans), F32),
            pltpu.VMEM((2, (height + 2 * RIM) * (WIN + RIM), 256), F32),
            pltpu.VMEM(((height + 2 * RIM) * (WIN + RIM), chans), F32),
            pltpu.VMEM((3 * span, 256), F32),
            pltpu.VMEM((2, 128, chans), F32),
            pltpu.VMEM((4, HEADS * HP, KEYS), BF16),
            *attention_scratch(3, 4 * HP),
            pltpu.VMEM((height, span, chans), F32),
        ],
        5_000_000_000,
        4_000_000,
    )(*args)


def middle_block(*args):
    height, cols, chans = args[0].shape
    span = cols + 2 * STRIP
    feats = args[-6].shape[2]
    return call(
        middle_kernel,
        (
            jax.ShapeDtypeStruct((height, span, 768), BF16),
            jax.ShapeDtypeStruct((height + 4, span + STRIP, chans), F32),
            jax.ShapeDtypeStruct((9 * 256, chans), BF16),
            jax.ShapeDtypeStruct((3 * 256, 3 * feats), BF16),
            jax.ShapeDtypeStruct((3 * 256, 4 * feats), BF16),
        ),
        [*attention_scratch(3), pltpu.VMEM((height, span + STRIP, chans), F32)],
        5_000_000_000,
        4_000_000,
    )(*args)


def conv_kernel(
    taps_ref,
    base,
    back_two_ref,
    back_one_ref,
    wg_scr,
    wb_scr,
    wu_scr,
    out_ref,
    image,
    halo_taps,
    grouped,
    sums,
    lowfeat,
    low_taps,
    out_scr,
):
    height, span = taps_ref.shape[:2]
    cols = span - 2 * STRIP
    chans = base.shape[2]
    feats = out_ref.shape[0]
    at_left, at_right, at_top, at_bottom, even_row, _ = at_edges()
    image[:, span:] = jnp.zeros((6, STRIP, chans), F32)
    sides = from_sides(even_row, back_one_ref[...], back_two_ref[...])
    for rows, packed in ((slice(0, 3), sides[0]), (slice(3, 6), sides[1])):
        image[rows, 0:span, 0:128] = packed[0 : 3 * span].reshape(3, span, 128)
        rest = unhalve(packed[3 * span :], 3 * span).reshape(3, span, 128)
        image[rows, 0:span, 128:chans] = rest[:, :, 0 : chans - 128]
    fill_taps(halo_taps, image, span)
    grouped[:, :, 128:256] = jnp.zeros((height + 4, span, 128), BF16)
    col = lax.broadcasted_iota(jnp.int32, (span, chans), 0) - 2
    keep_grouped = (col < cols + 2) & ((col >= 0) | jnp.logical_not(at_left))
    keep_grouped = keep_grouped & ((col < cols) | jnp.logical_not(at_right))
    low_span = cols + 8
    col = lax.broadcasted_iota(jnp.int32, (low_span, 128), 0) - 1
    keep_low = (col <= cols) & ((col >= 0) | jnp.logical_not(at_left))
    keep_low = keep_low & ((col < cols) | jnp.logical_not(at_right))
    left_half = lax.broadcasted_iota(jnp.int32, (cols, 128), 1) < feats
    spot = lax.broadcasted_iota(jnp.int32, (256, 256), 0)
    place = lax.broadcasted_iota(jnp.int32, (256, 256), 1)
    spread = (spot % 128 // cols == place // 128) & (
        spot % cols * 2 + spot // 128 == place % 128
    )
    spread = spread.astype(F32).astype(BF16)

    def tap_row(row):
        if 3 <= row < height + 3:
            return taps_ref[row - 3]
        return halo_taps[row if row < 3 else row - height]

    def group(h, part):
        lhs = jnp.concatenate(
            [
                jnp.concatenate([tap_row(h + a + r) for r in range(part)], axis=0)
                for a in range(3)
            ],
            axis=1,
        )
        total = dot(lhs, wg_scr[...]).reshape(part, span, chans)
        total = total + base[h : h + part, STRIP - 2 : STRIP - 2 + span, :]
        for r in range(part):
            mask = keep_grouped
            if h + r < 2:
                mask = mask & jnp.logical_not(at_top)
            if h + r >= height + 2:
                mask = mask & jnp.logical_not(at_bottom)
            grouped[h + r, 0:span, 0:chans] = jnp.where(mask, total[r], 0.0).astype(BF16)

    def narrow(h, count):
        lhs = jnp.concatenate(
            [grouped[h + a : h + a + count].reshape(count * span, 256) for a in range(3)], axis=1
        )
        slot = h // count % 2
        sums[slot, 0:count, :, 0 : 3 * feats] = dot(lhs, wb_scr[...]).reshape(count, span, 3 * feats)
        for r in range(count):
            total = sums[slot, r, 0:low_span, 0:128]
            total = total + pltpu.roll(sums[slot, r, 1 : low_span + 1, 0:128], feats, 1)
            total = total + sums[slot, r, 2 : low_span + 2, 128:256]
            mask = keep_low
            if h + r == 0:
                mask = mask & jnp.logical_not(at_top)
            if h + r == height + 1:
                mask = mask & jnp.logical_not(at_bottom)
            lowfeat[h + r] = jnp.where(mask, jnp.where(total >= 0, total, 0.01 * total), 0.0)
            low_taps[h + r, :, 0:128] = jnp.where(
                left_half, lowfeat[h + r, 0:cols], pltpu.roll(lowfeat[h + r, 1 : cols + 1], feats, 1)
            ).astype(BF16)
            low_taps[h + r, :, 128:256] = jnp.where(
                left_half, lowfeat[h + r, 2 : cols + 2], 0.0
            ).astype(BF16)

    def expand(h, part):
        lhs = jnp.concatenate(
            [low_taps[h + a : h + a + part].reshape(part * cols, 256) for a in range(3)], axis=1
        )
        total = dot(lhs, wu_scr[...])
        for pair in range(part // 2):
            turned = total[2 * cols * pair : 2 * cols * (pair + 1)].T.astype(BF16)
            lhs = [
                jnp.concatenate(
                    [turned[(2 * a + b) * feats : (2 * a + b + 1) * feats] for b in range(2)], axis=1
                )
                for a in range(2)
            ]
            final = dot(jnp.concatenate(lhs, axis=0), spread)
            for r in range(2):
                for a in range(2):
                    row = 2 * (h + 2 * pair + r) + a
                    out_scr[pl.ds(row, feats, stride=2 * height), :] = final[
                        a * feats : (a + 1) * feats, 128 * r : 128 * (r + 1)
                    ]

    quarter, third = (height + 4) // 4, (height + 2) // 3
    for step in range(4):
        group(quarter * step, quarter)
    for step in range(3):
        narrow(third * step, third)
    for step in range(4):
        expand(height // 4 * step, height // 4)
    out_ref[...] = out_scr[...].reshape(feats, 2 * height, 128).astype(BF16)


def convs(*args):
    height, span = args[0].shape[:2]
    chans = args[1].shape[2]
    cols = span - 2 * STRIP
    feats = args[-1].shape[1] // 4
    return call(
        conv_kernel,
        jax.ShapeDtypeStruct((feats, 2 * height, 2 * cols), BF16),
        [
            pltpu.VMEM((6, span + STRIP, chans), F32),
            pltpu.VMEM((6, span, 768), BF16),
            pltpu.VMEM((height + 4, span, 256), BF16),
            pltpu.VMEM((2, 6, span, 256), F32),
            pltpu.VMEM((height + 2, cols + 8, 128), F32),
            pltpu.VMEM((height + 2, cols, 256), BF16),
            pltpu.VMEM((feats * 2 * height, 128), F32),
        ],
        8_000_000_000,
        4_000_000,
    )(*args)


def swapped(axis, first, second):
    count = lax.axis_size(axis)
    out = []
    for start, payload in ((1, second), (0, first)):
        pairs = [(i, i + 1) for i in range(start, count - 1, 2)]
        pairs = pairs + [(b, a) for a, b in pairs]
        out.append(lax.ppermute(payload, axis, pairs))
    return out[::-1]


def on_device(
    features,
    gain_one,
    qkv_weight,
    bias_table,
    proj_weight,
    gain_two,
    hidden_weight,
    output_weight,
    group_conv,
    before_conv,
    upsample_conv,
):
    height, cols, chans = features.shape
    even_row = lax.axis_index("rows") % 2 == 0
    low, high = features[:RIM], features[height - RIM :]
    row_one, row_two = swapped(
        "rows", jnp.where(even_row, high, low), jnp.where(even_row, low, high)
    )
    col_one, col_two = swapped("cols", *pack(features, row_one, row_two))

    bias = build_bias(bias_table)
    gain_one, gain_two = gain_one.reshape(1, chans), gain_two.reshape(1, chans)
    post = (gain_two, hidden_weight, output_weight.T)
    nrm, wk, wqv, wp, inner_k, inner_v, inner_border, inner_mid = inner_block(
        features,
        row_one,
        row_two,
        gain_one,
        qkv_weight,
        proj_weight,
        bias,
        *post,
    )
    back_one, back_two, edge, side, strips, keys, values = outer_block(
        features,
        nrm,
        col_two,
        col_one,
        gain_one,
        wk,
        wqv,
        wp,
        inner_k,
        inner_v,
        inner_border,
        bias,
        *post,
    )
    back_one, back_two = swapped("rows", back_one, back_two)
    taps, base, group, before, upsample = middle_block(
        features,
        nrm,
        keys,
        values,
        wqv,
        wp,
        inner_mid,
        edge,
        side,
        strips,
        row_two,
        row_one,
        group_conv,
        before_conv.transpose(0, 1, 3, 2),
        upsample_conv,
        bias,
        *post,
    )
    return convs(taps, base, back_two, back_one, group, before, upsample)


def solution(mesh):
    placed = (P("rows", "cols", None), P(), P(), P(), P(), P(), P(), P(), P(), P(), P())
    return jax.shard_map(
        on_device, mesh=mesh, in_specs=placed, out_specs=P(None, "rows", "cols"), check_vma=False
    )
```

```python
import functools

import jax
import jax.numpy as jnp
import numpy as np
from jax import lax
from jax.experimental import pallas as pl
from jax.experimental.pallas import tpu as pltpu
from jax.sharding import PartitionSpec as P

HEADS = 6
HD = 30
HP = 32
WIN = 16
KWIN = 24
KEYS = KWIN * KWIN
SIDE = WIN + KWIN - 1
RIM = (KWIN - WIN) // 2
EDGE = WIN + 2 * RIM
STRIP = 8
SIDE_COLS = 4
LOG2E = 1.4426950408889634
F32 = jnp.float32
BF16 = jnp.bfloat16
NT = (((1,), (1,)), ((), ()))
TN = (((0,), (0,)), ((), ()))


def dot(a, b):
    return jnp.dot(a, b, preferred_element_type=F32)


def dot_nt(a, b):
    return lax.dot_general(a, b, NT, preferred_element_type=F32)


def layer_norm(values, gain):
    center = values - jnp.mean(values, axis=-1, keepdims=True)
    spread = jnp.mean(center * center, axis=-1, keepdims=True)
    return center * lax.rsqrt(spread + 1e-05) * gain


def call(kernel, out_shape, scratch, flops, bytes_accessed):
    return pl.pallas_call(
        kernel,
        out_shape=out_shape,
        scratch_shapes=scratch,
        compiler_params=pltpu.CompilerParams(vmem_limit_bytes=24 * 2**20),
        cost_estimate=pl.CostEstimate(
            flops=flops, bytes_accessed=bytes_accessed, transcendentals=0
        ),
    )


def bias_kernel(table_ref, out_ref, t_scr, e_scr, w_scr, x_scr):
    for d in range(SIDE):
        t_scr[8 * d : 8 * d + HEADS, 0:SIDE] = jnp.exp(table_ref[:, SIDE * d : SIDE * (d + 1)])

    def head(h, carry):
        values = t_scr[pl.ds(h, SIDE, stride=8), 0:SIDE].astype(BF16)

        def expand(cols, first, shift=0):
            width = -(-(SIDE * cols + shift) // 128) * 128
            spot = (lax.broadcasted_iota(jnp.int32, (SIDE, width), 1) - shift) // cols
            row = lax.broadcasted_iota(jnp.int32, (SIDE, width), 0)
            pick = (spot == SIDE - 1 - row).astype(F32).astype(BF16)
            e_scr[0:SIDE, 0:width] = lax.dot_general(values, pick, TN, preferred_element_type=F32)
            lane = lax.broadcasted_iota(jnp.int32, (KWIN, width), 1) % cols
            out = jnp.zeros((KWIN, width), F32)
            for jj in range(cols):
                start = WIN - 1 - first - jj
                out = jnp.where(lane == jj, e_scr[start : start + KWIN, 0:width], out)
            w_scr[:, 0:width] = out

        lanes = lax.broadcasted_iota(jnp.int32, (KWIN, 128), 1)
        expand(WIN, 0)
        whole = w_scr[...]
        for phase in range(8):
            turned = whole if phase == 0 else pltpu.roll(whole, 640 - WIN * phase, 1)
            for p in range(KWIN):
                rows = slice(p * KWIN, (p + 1) * KWIN)
                if (23 - p) % 8 == phase:
                    at = (23 - p) // 8 * 128
                    low, high = turned[:, at : at + 128], turned[:, at + 128 : at + 256]
                    x_scr[0, rows] = jnp.where(lanes < 64, low, high)
                if (27 - p) % 8 == phase:
                    at = (27 - p) // 8 * 128
                    x_scr[1, rows] = turned[:, at : at + 128]
        out_ref[1, h] = x_scr[0].astype(BF16)
        out_ref[2, h] = x_scr[1].astype(BF16)
        expand(SIDE_COLS, WIN - SIDE_COLS)
        left = w_scr[:, 0:256]
        expand(SIDE_COLS, 0, 64)
        right = w_scr[:, 0:256]
        whole = jnp.concatenate([left, right], axis=0)
        for p in range(KWIN):
            rows = slice(p * KWIN, (p + 1) * KWIN)
            at = (23 - p) * SIDE_COLS
            turned = whole if at == 0 else pltpu.roll(whole, 256 - at, 1)
            x_scr[0, rows] = jnp.where(lanes < 64, turned[0:KWIN, 0:128], turned[KWIN:, 0:128])
        out_ref[0, h] = x_scr[0].astype(BF16)
        return carry

    lax.fori_loop(0, HEADS, head, 0)


def build_bias(bias_table):
    return call(
        bias_kernel,
        jax.ShapeDtypeStruct((3, HEADS, KEYS, 128), BF16),
        [
            pltpu.VMEM((8 * SIDE, 128), F32),
            pltpu.VMEM((SIDE + 1, 640), F32),
            pltpu.VMEM((KWIN, 640), F32),
            pltpu.VMEM((2, KEYS, 128), F32),
        ],
        4_000_000_000,
        4_000_000,
    )(bias_table.T)


def one_hot(shape, row_of, col_of):
    row = lax.broadcasted_iota(jnp.int32, shape, 0)
    col = lax.broadcasted_iota(jnp.int32, shape, 1)
    return (row_of(row) == col_of(col)).astype(F32).astype(BF16)


def spread_head(place):
    return jnp.where(place % HP < HD, place // HP * HD + place % HP, -1)


def weights_into(qkv_ref, proj_ref, wk_ref, wqv_ref, wp_ref):
    chans = qkv_ref.shape[0]
    width = HEADS * HP
    qkv = qkv_ref[...]
    pick = one_hot(
        (3 * chans, 3 * 128),
        lambda row: row,
        lambda col: jnp.where(
            (col % 128 < 2 * HP) & (col % HP < HD),
            chans + (col // 128 * 2 + col % 128 // HP) * HD + col % HP,
            -1,
        ),
    )
    wk_ref[...] = dot(qkv, pick).astype(BF16)
    pick = one_hot(
        (2 * width, 3 * chans),
        lambda row: jnp.where(
            row % HP < HD, row // HP * HD + row % HP + jnp.where(row < width, 0, chans), -1
        ),
        lambda col: col,
    )
    wqv_ref[...] = dot_nt(pick, qkv).astype(BF16)
    pick = one_hot((width, chans), spread_head, lambda col: col)
    wp_ref[...] = dot(pick, proj_ref[...]).astype(BF16)


def set_queries(q_scr, wqv_ref, groups, strips=None):
    scale = LOG2E / np.sqrt(HD)
    rows = jnp.concatenate([rows.reshape(128, rows.shape[-1]) for rows in groups], axis=0)
    queries = (dot_nt(wqv_ref[0 : HEADS * HP], rows.astype(BF16)) * scale).astype(BF16)
    none = jnp.zeros((HP, 128), BF16)
    left = lax.broadcasted_iota(jnp.int32, (HP, 128), 1) < 64
    for g in range(len(groups)):
        lanes = slice(128 * g, 128 * g + 128)
        for t in range(HEADS // 2):
            one = queries[2 * t * HP : (2 * t + 1) * HP, lanes]
            two = queries[(2 * t + 1) * HP : (2 * t + 2) * HP, lanes]
            if g == strips:
                q_scr[g, t, 2 * HP : 3 * HP] = jnp.concatenate([jnp.where(left, none, one), none], axis=1)
                q_scr[g, t, 3 * HP : 4 * HP] = jnp.concatenate([none, jnp.where(left, none, two)], axis=1)
                one, two = jnp.where(left, one, none), jnp.where(left, two, none)
            elif strips is not None:
                q_scr[g, t, 2 * HP : 4 * HP] = jnp.zeros((2 * HP, 256), BF16)
            q_scr[g, t, 0:HP] = jnp.concatenate([one, none], axis=1)
            q_scr[g, t, HP : 2 * HP] = jnp.concatenate([none, two], axis=1)


def lookup(g, values):
    out = values[0]
    for index in range(1, len(values)):
        out = jnp.where(g >= index, values[index], out)
    return out


def attention(kinds, windows, q_scr, k_ref, v_ref, bias_ref, wp_ref, s_scr, m_scr, p_scr, o_scr, v_right=None):
    groups = len(kinds)
    pairs = HEADS // 2
    step = 144
    depth = 2 * HP if v_right is None else 4 * HP
    left = lax.broadcasted_iota(jnp.int32, (HP, 128), 1) < 64

    def keep(g, t, k0, top):
        keys = k_ref[lookup(g, windows), k0 : k0 + step, 128 * t : 128 * t + depth]
        one = dot(keys, q_scr[g, t])
        s_scr[t, k0 : k0 + step] = one
        part = jnp.max(one.reshape(step // 8, 8, 256), axis=0)
        return part if top is None else jnp.maximum(top, part)

    def sum_values(g, t):
        for half in range(2):
            head = 2 * t + half
            lanes = slice(128 * half, 128 * half + 128)
            window, rows = lookup(g, windows), slice(head * HP, (head + 1) * HP)
            values = v_ref[window, rows]
            if v_right is None:
                o_scr[g, head] = dot(values, p_scr[t, :, lanes])
            else:
                values = jnp.concatenate([values, v_right[window, rows]], axis=0)
                both = dot(values, p_scr[t, :, lanes])
                o_scr[g, head] = jnp.where(left, both[0:HP], both[HP : 2 * HP])

    top = None
    for k0 in range(0, KEYS, step):
        top = keep(0, 0, k0, top)
    m_scr[...] = top
    p_scr[pairs - 1] = jnp.zeros((KEYS, 256), BF16)

    def attend(g, carry):
        kind = lookup(g, kinds)
        top = m_scr[...]
        for t in range(pairs):
            top = jnp.max(top, axis=0, keepdims=True)
            if t == 0:
                sum_values(jnp.maximum(g - 1, 0), pairs - 1)
            else:
                sum_values(g, t - 1)
            following = g if t + 1 < pairs else jnp.minimum(g + 1, groups - 1)
            later = None
            for k0 in range(0, KEYS, step):
                later = keep(following, (t + 1) % pairs, k0, later)
                prob = jnp.exp2(s_scr[t, k0 : k0 + step] - top).astype(BF16)
                for half in range(2):
                    lanes = slice(128 * half, 128 * half + 128)
                    p_scr[t, k0 : k0 + step, lanes] = (
                        prob[:, lanes] * bias_ref[kind, 2 * t + half, k0 : k0 + step]
                    )
            top = later
        m_scr[...] = top
        return carry

    lax.fori_loop(0, groups, attend, 0)
    sum_values(groups - 1, pairs - 1)
    attended = []
    for g in range(groups):
        parts = []
        for head in range(HEADS):
            one = o_scr[g, head]
            parts.append((one * (1.0 / one[HD : HD + 1])).astype(BF16))
        attended.append(jnp.concatenate(parts, axis=0))
    attended = jnp.concatenate(attended, axis=1)
    return lax.dot_general(attended, wp_ref[...], TN, preferred_element_type=F32)


def feed_forward(first, gain, hidden_ref, output_ref):
    normed = layer_norm(first, gain).astype(BF16)
    inner = dot(normed, hidden_ref[...])
    inner = (0.5 * inner * (1.0 + lax.erf(inner * np.float32(np.sqrt(0.5))))).astype(BF16)
    return first + dot_nt(inner, output_ref[...])


def feed_groups(first, gain, hidden_ref, output_ref, batch):
    out = []
    for start in range(0, first.shape[0], 128 * batch):
        mixed = feed_forward(first[start : start + 128 * batch], gain, hidden_ref, output_ref)
        out += [mixed[128 * g : 128 * (g + 1)] for g in range(batch)]
    return out


def project(keys, wk_ref, wqv_ref, k_ref, v_ref, index):
    keys = keys.reshape(KEYS, keys.shape[2]).astype(BF16)
    k_ref[index] = dot(keys, wk_ref[...]).astype(BF16)
    v_ref[index] = project_values(keys, wqv_ref)


def project_values(keys, wqv_ref):
    width = HEADS * HP
    one_row = (lax.broadcasted_iota(jnp.int32, (width, 1), 0) % HP == HD).astype(F32)
    return (dot_nt(wqv_ref[width : 2 * width], keys) + one_row).astype(BF16)


def at_edges():
    row, column = lax.axis_index("rows"), lax.axis_index("cols")
    return (
        column == 0,
        column == lax.axis_size("cols") - 1,
        row == 0,
        row == lax.axis_size("rows") - 1,
        row % 2 == 0,
        column % 2 == 0,
    )


def from_sides(even, first, second):
    first, second = first.astype(F32), second.astype(F32)
    return jnp.where(even, second, first), jnp.where(even, first, second)


def border_rows(ref, c0):
    return jnp.concatenate([ref[0:4, c0 : c0 + WIN], ref[12:16, c0 : c0 + WIN]], axis=0)


def halves(wide, count):
    left = lax.broadcasted_iota(jnp.int32, (1, 128), 1) < 64
    rest = wide.shape[0] - count
    out = jnp.where(left, wide[0:rest], pltpu.roll(wide[count:], 64, 1))
    return out if rest == count else jnp.concatenate([out, wide[rest:count]], axis=0)


def unhalve(packed, rows):
    count = packed.shape[0]
    return jnp.concatenate([packed, pltpu.roll(packed[0 : rows - count], 64, 1)], axis=0)


def pack_kernel(own_ref, row_one_ref, row_two_ref, pay_one_ref, pay_two_ref, x_scr, flat):
    height, cols, chans = own_ref.shape
    even_row, even_col = at_edges()[4:]
    above, below = from_sides(even_row, row_one_ref[...], row_two_ref[...])
    x_scr[0:RIM] = above
    x_scr[RIM : RIM + height] = own_ref[...].astype(F32)
    x_scr[RIM + height :] = below
    for side, near, far in ((0, 0, WIN), (1, cols - WIN, cols - WIN - RIM)):
        for r in range(height + 2 * RIM):
            flat[side, WIN * r : WIN * (r + 1), 0:chans] = x_scr[r, near : near + WIN]
            place = WIN * (height + 2 * RIM) + RIM * r
            flat[side, place : place + RIM, 0:chans] = x_scr[r, far : far + RIM]
    count = flat.shape[1]
    for lanes in (slice(0, 128), slice(128, 256)):
        low, high = flat[0, :, lanes], flat[1, :, lanes]
        one, two = jnp.where(even_col, high, low), jnp.where(even_col, low, high)
        rows = slice(0, count)
        if lanes.start:
            one, two = halves(one, count // 2), halves(two, count // 2)
            rows = slice(count, count + count // 2)
        pay_one_ref[rows] = one.astype(BF16)
        pay_two_ref[rows] = two.astype(BF16)


def pack(own, row_one, row_two):
    height, cols, chans = own.shape
    pixels = (height + 2 * RIM) * (WIN + RIM)
    pay = jax.ShapeDtypeStruct((pixels * 3 // 2, 128), BF16)
    return call(
        pack_kernel,
        (pay, pay),
        [
            pltpu.VMEM((height + 2 * RIM, cols, chans), F32),
            pltpu.VMEM((2, pixels, 256), F32),
        ],
        1_000_000,
        1_000_000,
    )(own, row_one, row_two)


def inner_kernel(
    own_ref,
    row_one_ref,
    row_two_ref,
    gain_one_ref,
    qkv_ref,
    proj_ref,
    bias_ref,
    gain_two_ref,
    hidden_ref,
    output_ref,
    nrm_ref,
    wk_ref,
    wqv_ref,
    wp_ref,
    k_ref,
    v_ref,
    border_ref,
    mid_ref,
    q_scr,
    s_scr,
    m_scr,
    p_scr,
    o_scr,
):
    height, cols, chans = own_ref.shape
    inner = cols // WIN - 2
    flags = at_edges()
    weights_into(qkv_ref, proj_ref, wk_ref, wqv_ref, wp_ref)
    gain_one = gain_one_ref[...]
    for r in range(RIM):
        above, below = from_sides(flags[4], row_one_ref[r], row_two_ref[r])
        nrm_ref[r] = layer_norm(above, gain_one)
        nrm_ref[RIM + height + r] = layer_norm(below, gain_one)
    for r in range(height):
        nrm_ref[RIM + r] = layer_norm(own_ref[r].astype(F32), gain_one)
    kinds, windows, first, queries = [], [], [], []
    for w in range(inner):
        c0 = WIN * (w + 1)
        project(nrm_ref[:, c0 - RIM : c0 - RIM + KWIN], wk_ref, wqv_ref, k_ref, v_ref, w)
        first.append(border_rows(own_ref, c0).reshape(128, chans))
        queries.append(border_rows(nrm_ref.at[RIM : RIM + height], c0))
        kinds.append(1)
        windows.append(w)
    for w in range(inner - 1):
        c0 = WIN * (w + 1)
        first.append(own_ref[4:12, c0 : c0 + WIN].reshape(128, chans))
        queries.append(nrm_ref[RIM + 4 : RIM + 12, c0 : c0 + WIN])
        kinds.append(2)
        windows.append(w)
    groups = len(kinds)
    set_queries(q_scr, wqv_ref, queries)
    first = jnp.concatenate(first, axis=0).astype(F32) + attention(
        kinds, windows, q_scr, k_ref, v_ref, bias_ref, wp_ref, s_scr, m_scr, p_scr, o_scr
    )
    mixed = feed_groups(first, gain_two_ref[...], hidden_ref, output_ref, len(kinds))
    for g in range(groups):
        one = mixed[g].reshape(8, WIN, chans)
        if g < inner:
            border_ref[:, WIN * g : WIN * (g + 1)] = one
        else:
            mid_ref[:, WIN * (g - inner) : WIN * (g - inner + 1)] = one


def outer_kernel(
    own_ref,
    nrm_ref,
    col_two_ref,
    col_one_ref,
    gain_one_ref,
    wk_ref,
    wqv_ref,
    wp_ref,
    inner_k_ref,
    inner_v_ref,
    inner_border_ref,
    bias_ref,
    gain_two_ref,
    hidden_ref,
    output_ref,
    pay_one_ref,
    pay_two_ref,
    edge_ref,
    side_ref,
    strip_ref,
    k_ref,
    v_ref,
    side_scr,
    x_scr,
    n_scr,
    b_scr,
    strips,
    v_right,
    q_scr,
    s_scr,
    m_scr,
    p_scr,
    o_scr,
    image,
):
    height, cols, chans = own_ref.shape
    inner = cols // WIN - 2
    flags = at_edges()
    gain_one = gain_one_ref[...]
    rows = height + 2 * RIM
    pixels = rows * (WIN + RIM)
    both = from_sides(flags[5], col_one_ref[...], col_two_ref[...])
    for side in range(2):
        x_scr[side, :, 0:128] = both[side][0:pixels]
        x_scr[side, :, 128:256] = unhalve(both[side][pixels:], pixels)
        n_scr[...] = layer_norm(x_scr[side, :, 0:chans], gain_one)
        near, far = (EDGE - WIN, EDGE - WIN - RIM) if side == 0 else (EDGE, EDGE + WIN)
        for r in range(rows):
            side_scr[side, r, near : near + WIN] = n_scr[WIN * r : WIN * (r + 1)]
            place = WIN * rows + RIM * r
            side_scr[side, r, far : far + RIM] = n_scr[place : place + RIM]
        c0 = WIN - STRIP if side == 0 else 0
        x = x_scr[side, 0 : WIN * rows, 0:chans].reshape(rows, WIN, chans)
        strip_ref[side] = x[:, c0 : c0 + STRIP]
    side_scr[0, :, EDGE : 2 * EDGE] = nrm_ref[:, 0:EDGE]
    side_scr[1, :, 0:EDGE] = nrm_ref[:, cols - EDGE : cols]
    k_ref[2] = inner_k_ref[inner - 1]
    v_ref[2] = inner_v_ref[inner - 1]
    for index, side, c0 in ((1, 0, RIM + WIN), (3, 1, RIM)):
        project(side_scr[side, :, c0 : c0 + KWIN], wk_ref, wqv_ref, k_ref, v_ref, index)
        v_right[index] = v_ref[index]
    strip_keys = [
        side_scr[side, :, c0 : c0 + KWIN].reshape(KEYS, chans).astype(BF16)
        for side, c0 in ((0, RIM), (1, RIM + WIN))
    ]
    moved = pltpu.roll(wk_ref[...].astype(F32), 2 * HP, 1).astype(BF16)
    k_ref[0] = (dot(strip_keys[0], wk_ref[...]) + dot(strip_keys[1], moved)).astype(BF16)
    v_ref[0] = project_values(strip_keys[0], wqv_ref)
    v_right[0] = project_values(strip_keys[1], wqv_ref)
    n = SIDE_COLS
    for r in range(height):
        for side, c0, c1 in ((0, STRIP - n, EDGE - n), (1, 0, EDGE)):
            place = slice(64 * side + n * r, 64 * side + n * (r + 1))
            strips[0, place] = strip_ref[side, RIM + r, c0 : c0 + n]
            strips[1, place] = side_scr[side, RIM + r, c1 : c1 + n]
    first, queries = [strips[0]], [strips[1]]
    spots = (0, cols - WIN)
    for c0 in spots:
        first.append(border_rows(own_ref, c0).astype(F32).reshape(128, chans))
        queries.append(border_rows(nrm_ref.at[RIM : RIM + height], c0))
    set_queries(q_scr, wqv_ref, queries, 0)
    first = jnp.concatenate(first, axis=0) + attention(
        [0, 1, 1], [0, 1, 3], q_scr, k_ref, v_ref, bias_ref, wp_ref, s_scr, m_scr, p_scr, o_scr, v_right
    )
    image[:, 0:STRIP] = jnp.zeros((height, STRIP, chans), F32)
    image[:, STRIP + cols :] = jnp.zeros((height, STRIP, chans), F32)
    image[0:4, STRIP + WIN : STRIP + cols - WIN] = inner_border_ref[0:4]
    image[12:16, STRIP + WIN : STRIP + cols - WIN] = inner_border_ref[4:8]
    mixed = feed_groups(first, gain_two_ref[...], hidden_ref, output_ref, 3)
    row = lax.broadcasted_iota(jnp.int32, (128, chans), 0)
    outside = (flags[0] & (row < 64)) | (flags[1] & (row >= 64))
    strips[0] = jnp.where(outside, 0.0, mixed[0])
    for r in range(height):
        for side, c0 in ((0, STRIP - n), (1, STRIP + cols)):
            place = 64 * side + n * r
            image[r, c0 : c0 + n] = strips[0, place : place + n]
    for g in range(2):
        one = mixed[1 + g].reshape(8, WIN, chans)
        c0 = STRIP + spots[g]
        image[0:4, c0 : c0 + WIN] = one[0:4]
        image[12:16, c0 : c0 + WIN] = one[4:8]
    even = flags[4]
    count = 3 * image.shape[1]
    for pay_ref, rows in (
        (pay_one_ref, jnp.where(even, image[13:16], image[0:3])),
        (pay_two_ref, jnp.where(even, image[0:3], image[13:16])),
    ):
        b_scr[:, 0:chans] = rows.reshape(count, chans)
        pay_ref[0:count] = b_scr[:, 0:128].astype(BF16)
        pay_ref[count:] = halves(b_scr[:, 128:256], 128).astype(BF16)
    edge_ref[0:4] = image[0:4]
    edge_ref[4:8] = image[12:16]
    side_ref[:, 0:STRIP] = image[4:12, 0:STRIP]
    side_ref[:, STRIP : 2 * STRIP] = image[4:12, STRIP + cols :]


def fill_taps(taps_ref, image, span):
    chans = image.shape[2]
    for b in range(3):
        start = STRIP - 3 + b
        lanes = slice(256 * b + 128, 256 * b + 256)
        taps_ref[:, :, lanes] = jnp.zeros((taps_ref.shape[0], span, 128), BF16)
        taps_ref[:, :, 256 * b : 256 * b + chans] = image[:, start : start + span].astype(BF16)


def conv_weights(group_ref, before_ref, upsample_ref, wg_scr, wb_scr, wu_scr):
    chans = group_ref.shape[2]
    feats = before_ref.shape[2]
    pad = chans // 16 * 16
    for a in range(3):
        wb_scr[256 * a + pad : 256 * (a + 1)] = jnp.zeros((256 - pad, 3 * feats), BF16)
        wu_scr[256 * a + 3 * feats : 256 * (a + 1)] = jnp.zeros((256 - 3 * feats, 4 * feats), BF16)
        for b in range(3):
            wg_scr[256 * (3 * a + b) + pad : 256 * (3 * a + b + 1)] = jnp.zeros((256 - pad, chans), BF16)
            wg_scr[256 * (3 * a + b) : 256 * (3 * a + b) + chans] = group_ref[a, b]
    same = one_hot((chans, chans), lambda row: row, lambda col: col)
    order = one_hot(
        (4 * feats, 4 * feats), lambda row: row, lambda col: col % feats * 4 + col // feats
    )
    for a in range(3):
        part = before_ref[a].reshape(3 * feats, chans)
        wb_scr[256 * a : 256 * a + chans] = dot_nt(same, part).astype(BF16)
        part = upsample_ref[a].reshape(3 * feats, 4 * feats)
        wu_scr[256 * a : 256 * a + 3 * feats] = dot(part, order).astype(BF16)


def middle_kernel(
    own_ref,
    nrm_ref,
    k_ref,
    v_ref,
    wqv_ref,
    wp_ref,
    inner_mid_ref,
    edge_ref,
    side_ref,
    strip_ref,
    row_two_ref,
    row_one_ref,
    group_ref,
    before_ref,
    upsample_ref,
    bias_ref,
    gain_two_ref,
    hidden_ref,
    output_ref,
    taps_ref,
    base_ref,
    wg_ref,
    wb_ref,
    wu_ref,
    q_scr,
    s_scr,
    m_scr,
    p_scr,
    o_scr,
    image,
):
    height, cols, chans = own_ref.shape
    spots = (0, cols - 2 * WIN, cols - WIN)
    set_queries(q_scr, wqv_ref, [nrm_ref[RIM + 4 : RIM + 12, c0 : c0 + WIN] for c0 in spots])
    first = [own_ref[4:12, c0 : c0 + WIN].reshape(128, chans) for c0 in spots]
    first = jnp.concatenate(first, axis=0).astype(F32) + attention(
        [2, 2, 2], [1, 2, 3], q_scr, k_ref, v_ref, bias_ref, wp_ref, s_scr, m_scr, p_scr, o_scr
    )
    mixed = feed_groups(first, gain_two_ref[...], hidden_ref, output_ref, 3)
    span = cols + 2 * STRIP
    image[:, span:] = jnp.zeros((height, STRIP, chans), F32)
    image[0:4, 0:span] = edge_ref[0:4]
    image[4:12, 0:STRIP] = side_ref[:, 0:STRIP]
    image[4:12, STRIP + WIN : STRIP + cols - 2 * WIN] = inner_mid_ref[...]
    for g in range(3):
        c0 = STRIP + spots[g]
        image[4:12, c0 : c0 + WIN] = mixed[g].reshape(8, WIN, chans)
    image[4:12, STRIP + cols : span] = side_ref[:, STRIP : 2 * STRIP]
    image[12:16, 0:span] = edge_ref[4:8]
    fill_taps(taps_ref, image, span)
    conv_weights(group_ref, before_ref, upsample_ref, wg_ref, wb_ref, wu_ref)
    even_row = at_edges()[4]
    above, below = from_sides(even_row, row_one_ref[...], row_two_ref[...])
    base_ref[0:2, STRIP : STRIP + cols] = above[2:4]
    base_ref[2 : 2 + height, STRIP : STRIP + cols] = own_ref[...].astype(F32)
    base_ref[2 + height : 4 + height, STRIP : STRIP + cols] = below[0:2]
    rows = slice(2, height + 6)
    base_ref[:, 0:STRIP] = strip_ref[0, rows]
    base_ref[:, STRIP + cols : span] = strip_ref[1, rows]
    base_ref[:, span:] = jnp.zeros((height + 4, STRIP, chans), F32)


def attention_scratch(groups, depth=2 * HP):
    return [
        pltpu.VMEM((groups, HEADS // 2, depth, 256), BF16),
        pltpu.VMEM((HEADS // 2, KEYS, 256), F32),
        pltpu.VMEM((8, 256), F32),
        pltpu.VMEM((HEADS // 2, KEYS, 256), BF16),
        pltpu.VMEM((groups, HEADS, HP, 128), F32),
    ]


def inner_block(*args):
    height, cols, chans = args[0].shape
    inner = cols // WIN - 2
    width = HEADS * HP
    groups = 2 * inner - 1
    return call(
        inner_kernel,
        (
            jax.ShapeDtypeStruct((height + 2 * RIM, cols, chans), F32),
            jax.ShapeDtypeStruct((chans, 3 * 128), BF16),
            jax.ShapeDtypeStruct((2 * width, chans), BF16),
            jax.ShapeDtypeStruct((width, chans), BF16),
            jax.ShapeDtypeStruct((inner, KEYS, 3 * 128), BF16),
            jax.ShapeDtypeStruct((inner, width, KEYS), BF16),
            jax.ShapeDtypeStruct((8, WIN * inner, chans), F32),
            jax.ShapeDtypeStruct((8, WIN * (inner - 1), chans), F32),
        ),
        attention_scratch(groups),
        5_000_000_000,
        4_000_000,
    )(*args)


def outer_block(*args):
    height, cols, chans = args[0].shape
    span = cols + 2 * STRIP
    return call(
        outer_kernel,
        (
            jax.ShapeDtypeStruct((3 * span + 128, 128), BF16),
            jax.ShapeDtypeStruct((3 * span + 128, 128), BF16),
            jax.ShapeDtypeStruct((8, span, chans), F32),
            jax.ShapeDtypeStruct((8, 2 * STRIP, chans), F32),
            jax.ShapeDtypeStruct((2, height + 2 * RIM, STRIP, chans), F32),
            jax.ShapeDtypeStruct((4, KEYS, 3 * 128), BF16),
            jax.ShapeDtypeStruct((4, HEADS * HP, KEYS), BF16),
        ),
        [
            pltpu.VMEM((2, height + 2 * RIM, 2 * EDGE, chans), F32),
            pltpu.VMEM((2, (height + 2 * RIM) * (WIN + RIM), 256), F32),
            pltpu.VMEM(((height + 2 * RIM) * (WIN + RIM), chans), F32),
            pltpu.VMEM((3 * span, 256), F32),
            pltpu.VMEM((2, 128, chans), F32),
            pltpu.VMEM((4, HEADS * HP, KEYS), BF16),
            *attention_scratch(3, 4 * HP),
            pltpu.VMEM((height, span, chans), F32),
        ],
        5_000_000_000,
        4_000_000,
    )(*args)


def middle_block(*args):
    height, cols, chans = args[0].shape
    span = cols + 2 * STRIP
    feats = args[-6].shape[2]
    return call(
        middle_kernel,
        (
            jax.ShapeDtypeStruct((height, span, 768), BF16),
            jax.ShapeDtypeStruct((height + 4, span + STRIP, chans), F32),
            jax.ShapeDtypeStruct((9 * 256, chans), BF16),
            jax.ShapeDtypeStruct((3 * 256, 3 * feats), BF16),
            jax.ShapeDtypeStruct((3 * 256, 4 * feats), BF16),
        ),
        [*attention_scratch(3), pltpu.VMEM((height, span + STRIP, chans), F32)],
        5_000_000_000,
        4_000_000,
    )(*args)


def conv_kernel(
    taps_ref,
    base,
    back_two_ref,
    back_one_ref,
    wg_scr,
    wb_scr,
    wu_scr,
    out_ref,
    image,
    halo_taps,
    grouped,
    sums,
    lowfeat,
    low_taps,
    out_scr,
):
    height, span = taps_ref.shape[:2]
    cols = span - 2 * STRIP
    chans = base.shape[2]
    feats = out_ref.shape[0]
    at_left, at_right, at_top, at_bottom, even_row, _ = at_edges()
    image[:, span:] = jnp.zeros((6, STRIP, chans), F32)
    sides = from_sides(even_row, back_one_ref[...], back_two_ref[...])
    for rows, packed in ((slice(0, 3), sides[0]), (slice(3, 6), sides[1])):
        image[rows, 0:span, 0:128] = packed[0 : 3 * span].reshape(3, span, 128)
        rest = unhalve(packed[3 * span :], 3 * span).reshape(3, span, 128)
        image[rows, 0:span, 128:chans] = rest[:, :, 0 : chans - 128]
    fill_taps(halo_taps, image, span)
    grouped[:, :, 128:256] = jnp.zeros((height + 4, span, 128), BF16)
    col = lax.broadcasted_iota(jnp.int32, (span, chans), 0) - 2
    keep_grouped = (col < cols + 2) & ((col >= 0) | jnp.logical_not(at_left))
    keep_grouped = keep_grouped & ((col < cols) | jnp.logical_not(at_right))
    low_span = cols + 8
    col = lax.broadcasted_iota(jnp.int32, (low_span, 128), 0) - 1
    keep_low = (col <= cols) & ((col >= 0) | jnp.logical_not(at_left))
    keep_low = keep_low & ((col < cols) | jnp.logical_not(at_right))
    left_half = lax.broadcasted_iota(jnp.int32, (cols, 128), 1) < feats
    spot = lax.broadcasted_iota(jnp.int32, (256, 256), 0)
    place = lax.broadcasted_iota(jnp.int32, (256, 256), 1)
    spread = (spot % 128 // cols == place // 128) & (
        spot % cols * 2 + spot // 128 == place % 128
    )
    spread = spread.astype(F32).astype(BF16)

    def tap_row(row):
        if 3 <= row < height + 3:
            return taps_ref[row - 3]
        return halo_taps[row if row < 3 else row - height]

    def group(h, part):
        lhs = jnp.concatenate(
            [
                jnp.concatenate([tap_row(h + a + r) for r in range(part)], axis=0)
                for a in range(3)
            ],
            axis=1,
        )
        total = dot(lhs, wg_scr[...]).reshape(part, span, chans)
        total = total + base[h : h + part, STRIP - 2 : STRIP - 2 + span, :]
        for r in range(part):
            mask = keep_grouped
            if h + r < 2:
                mask = mask & jnp.logical_not(at_top)
            if h + r >= height + 2:
                mask = mask & jnp.logical_not(at_bottom)
            grouped[h + r, 0:span, 0:chans] = jnp.where(mask, total[r], 0.0).astype(BF16)

    def narrow(h, count):
        lhs = jnp.concatenate(
            [grouped[h + a : h + a + count].reshape(count * span, 256) for a in range(3)], axis=1
        )
        slot = h // count % 2
        sums[slot, 0:count, :, 0 : 3 * feats] = dot(lhs, wb_scr[...]).reshape(count, span, 3 * feats)
        for r in range(count):
            total = sums[slot, r, 0:low_span, 0:128]
            total = total + pltpu.roll(sums[slot, r, 1 : low_span + 1, 0:128], feats, 1)
            total = total + sums[slot, r, 2 : low_span + 2, 128:256]
            mask = keep_low
            if h + r == 0:
                mask = mask & jnp.logical_not(at_top)
            if h + r == height + 1:
                mask = mask & jnp.logical_not(at_bottom)
            lowfeat[h + r] = jnp.where(mask, jnp.where(total >= 0, total, 0.01 * total), 0.0)
            low_taps[h + r, :, 0:128] = jnp.where(
                left_half, lowfeat[h + r, 0:cols], pltpu.roll(lowfeat[h + r, 1 : cols + 1], feats, 1)
            ).astype(BF16)
            low_taps[h + r, :, 128:256] = jnp.where(
                left_half, lowfeat[h + r, 2 : cols + 2], 0.0
            ).astype(BF16)

    def expand(h, part):
        lhs = jnp.concatenate(
            [low_taps[h + a : h + a + part].reshape(part * cols, 256) for a in range(3)], axis=1
        )
        total = dot(lhs, wu_scr[...])
        for pair in range(part // 2):
            turned = total[2 * cols * pair : 2 * cols * (pair + 1)].T.astype(BF16)
            lhs = [
                jnp.concatenate(
                    [turned[(2 * a + b) * feats : (2 * a + b + 1) * feats] for b in range(2)], axis=1
                )
                for a in range(2)
            ]
            final = dot(jnp.concatenate(lhs, axis=0), spread)
            for r in range(2):
                for a in range(2):
                    row = 2 * (h + 2 * pair + r) + a
                    out_scr[pl.ds(row, feats, stride=2 * height), :] = final[
                        a * feats : (a + 1) * feats, 128 * r : 128 * (r + 1)
                    ]

    group_part, narrow_part = (height + 4) // 2, (height + 2) // 2
    group(0, group_part)
    group(group_part, group_part)
    narrow(0, narrow_part)
    narrow(narrow_part, narrow_part)
    expand(0, height // 2)
    expand(height // 2, height // 2)
    out_ref[...] = out_scr[...].reshape(feats, 2 * height, 128).astype(BF16)


def convs(*args):
    height, span = args[0].shape[:2]
    chans = args[1].shape[2]
    cols = span - 2 * STRIP
    feats = args[-1].shape[1] // 4
    return call(
        conv_kernel,
        jax.ShapeDtypeStruct((feats, 2 * height, 2 * cols), BF16),
        [
            pltpu.VMEM((6, span + STRIP, chans), F32),
            pltpu.VMEM((6, span, 768), BF16),
            pltpu.VMEM((height + 4, span, 256), BF16),
            pltpu.VMEM((2, 9, span, 256), F32),
            pltpu.VMEM((height + 2, cols + 8, 128), F32),
            pltpu.VMEM((height + 2, cols, 256), BF16),
            pltpu.VMEM((feats * 2 * height, 128), F32),
        ],
        8_000_000_000,
        4_000_000,
    )(*args)


def swapped(axis, first, second):
    count = lax.axis_size(axis)
    out = []
    for start, payload in ((1, second), (0, first)):
        pairs = [(i, i + 1) for i in range(start, count - 1, 2)]
        pairs = pairs + [(b, a) for a, b in pairs]
        out.append(lax.ppermute(payload, axis, pairs))
    return out[::-1]


def on_device(
    features,
    gain_one,
    qkv_weight,
    bias_table,
    proj_weight,
    gain_two,
    hidden_weight,
    output_weight,
    group_conv,
    before_conv,
    upsample_conv,
):
    height, cols, chans = features.shape
    even_row = lax.axis_index("rows") % 2 == 0
    low, high = features[:RIM], features[height - RIM :]
    row_one, row_two = swapped(
        "rows", jnp.where(even_row, high, low), jnp.where(even_row, low, high)
    )
    col_one, col_two = swapped("cols", *pack(features, row_one, row_two))

    bias = build_bias(bias_table)
    gain_one, gain_two = gain_one.reshape(1, chans), gain_two.reshape(1, chans)
    post = (gain_two, hidden_weight, output_weight.T)
    nrm, wk, wqv, wp, inner_k, inner_v, inner_border, inner_mid = inner_block(
        features,
        row_one,
        row_two,
        gain_one,
        qkv_weight,
        proj_weight,
        bias,
        *post,
    )
    back_one, back_two, edge, side, strips, keys, values = outer_block(
        features,
        nrm,
        col_two,
        col_one,
        gain_one,
        wk,
        wqv,
        wp,
        inner_k,
        inner_v,
        inner_border,
        bias,
        *post,
    )
    back_one, back_two = swapped("rows", back_one, back_two)
    taps, base, group, before, upsample = middle_block(
        features,
        nrm,
        keys,
        values,
        wqv,
        wp,
        inner_mid,
        edge,
        side,
        strips,
        row_two,
        row_one,
        group_conv,
        before_conv.transpose(0, 1, 3, 2),
        upsample_conv,
        bias,
        *post,
    )
    return convs(taps, base, back_two, back_one, group, before, upsample)


def solution(mesh):
    placed = (P("rows", "cols", None), P(), P(), P(), P(), P(), P(), P(), P(), P(), P())
    return jax.shard_map(
        on_device, mesh=mesh, in_specs=placed, out_specs=P(None, "rows", "cols"), check_vma=False
    )
```
